32 devices in a mesh: dp: 8 (over y, x, core), tensor: 4 (over z).
Axes of the slice: x: 2, y: 2, z: 4, core: 2. Of those that a mesh axis runs over, the one named last changes fastest.
Arguments:
- latents: bfloat16 [4096, 1536], P('dp'), may hold values from -6 to 6
- context: bfloat16 [1024, 1536], P('dp'), may hold values from -6 to 6
- time_embed: float32 [2, 6, 1536], replicated, may hold values from -3 to 3
- teacher: bfloat16 [4096, 1536], P('dp'), may hold values from -6 to 6
- lengths: int32 [2], replicated, may hold values from 1844 to 2048, as said below
- block_order: int32 [8], P('dp'), may hold values from 0 to 3, as said below
- positions: int32 [3, 4096], P(None, 'dp'), may hold values from 0 to 63
- self_proj: bfloat16 [2, 3, 1536, 1536], P(None, None, 'dp', 'tensor'), may hold values from -0.15625 to 0.15625
- cross_proj: bfloat16 [2, 3, 1536, 1536], P(None, None, 'dp', 'tensor'), may hold values from -0.15625 to 0.15625
- out_proj: bfloat16 [2, 2, 1536, 1536], P(None, None, 'tensor', 'dp'), may hold values from -0.625 to 0.625
- ffn_up: bfloat16 [2, 1536, 8960], P(None, 'dp', 'tensor'), may hold values from -0.15625 to 0.15625
- ffn_down: bfloat16 [2, 8960, 1536], P(None, 'tensor', 'dp'), may hold values from -0.0625 to 0.0625
- proj_bias: float32 [2, 5, 1536], P(None, None, 'tensor'), may hold values from -2 to 2
- key_bias: float32 [2, 1536], P(None, 'tensor'), may hold values from -2 to 2
- norm_gains: float32 [2, 4, 1536], P(None, None, 'tensor'), may hold values from 0.25 to 1.75
- ffn_bias: float32 [2, 8960], P(None, 'tensor'), may hold values from -2 to 2
- out_bias: float32 [2, 3, 1536], replicated, may hold values from -2 to 2
- cross_gain: float32 [2, 1536], replicated, may hold values from 0.25 to 1.75
- cross_shift: float32 [2, 1536], replicated, may hold values from -2 to 2
- modulation: float32 [2, 6, 1536], replicated, may hold values from -3 to 3
Outputs:
- output: float32 [4096, 1536], P('dp')
- loss: float32 [], replicated
- latents_grad: float32 [4096, 1536], P('dp')
- context_grad: float32 [1024, 1536], P('dp')
- time_grad: float32 [2, 6, 1536], replicated
- self_proj_grad: float32 [2, 3, 1536, 1536], P(None, None, 'dp', 'tensor')
- cross_proj_grad: float32 [2, 3, 1536, 1536], P(None, None, 'dp', 'tensor')
- out_proj_grad: float32 [2, 2, 1536, 1536], P(None, None, 'tensor', 'dp')
- ffn_up_grad: float32 [2, 1536, 8960], P(None, 'dp', 'tensor')
- ffn_down_grad: float32 [2, 8960, 1536], P(None, 'tensor', 'dp')
- proj_bias_grad: float32 [2, 5, 1536], P(None, None, 'tensor')
- key_bias_grad: float32 [2, 1536], P(None, 'tensor')
- norm_gains_grad: float32 [2, 4, 1536], P(None, None, 'tensor')
- ffn_bias_grad: float32 [2, 8960], P(None, 'tensor')
- out_bias_grad: float32 [2, 3, 1536], replicated
- cross_gain_grad: float32 [2, 1536], replicated
- cross_shift_grad: float32 [2, 1536], replicated
- modulation_grad: float32 [2, 6, 1536], replicated
The draws below stay inside these ranges and needn't reach their ends.
Inputs may be any that keep to these rules, and one draw needn't show every extreme that they name: `lengths`: every clip has at least 1844 valid slots; in every draw exactly one clip has all 2048 slots valid. `block_order`: within each group of 4 consecutive devices of dp the values are a permutation of 0 to 3.
All inputs are finite; a program needn't handle non-finite values.
Results may differ from the reference program's by a relative error of at most 0.038.
Values may be sent and summed in bfloat16 or wider, within the bound.
A program may use at most 320 MiB of HBM per device.

```python
import math
import jax
import jax.numpy as jnp
import numpy as np
from jax import lax

D = 1536
HEADS = 12
HEAD_DIM = 128
FF = 8960
TEXT = 512
HOLD = 4
TOK_DEV = 512
LAYERS = 2
CLIPS = 2
TOKENS = 4096


def draw_lengths(key, part):
    seq_total = HOLD * TOK_DEV
    lowest = seq_total - seq_total // 10
    drawn = jax.random.randint(jax.random.fold_in(key, 11), (CLIPS,), lowest, seq_total)
    chosen = jax.random.randint(jax.random.fold_in(key, 12), (), 0, CLIPS)
    clip_ids = jnp.arange(CLIPS, dtype=jnp.int32)
    result = jnp.where(clip_ids == chosen, seq_total, drawn)
    return result.astype(jnp.int32)


def draw_block_order(key, part):
    clip_keys = jax.random.split(jax.random.fold_in(key, 13), CLIPS)
    orders = jax.vmap(lambda single: jax.random.permutation(single, HOLD))(clip_keys)
    return orders.reshape(CLIPS * HOLD).astype(jnp.int32)


def plant(values, key, least, top_value):
    longest = values.shape.index(max(values.shape))
    spots = []
    for shift in (0, 1):
        where = [jax.random.randint(jax.random.fold_in(key, axis), (), 0, length) for axis, length in enumerate(values.shape)]
        where[longest] = (where[longest] + shift) % values.shape[longest]
        spots.append(tuple(where))
    return values.at[spots[0]].set(least).at[spots[1]].set(top_value)


def steps_of(stream_key, shape, cuts, smallest, largest):
    loudness = 1.0
    for position, shards_of in cuts:
        draws = jax.random.uniform(jax.random.fold_in(jax.random.fold_in(stream_key, 6), position), (shards_of,), jnp.float32, smallest / len(cuts), largest / len(cuts))
        loudness = loudness * jnp.repeat(jnp.exp(draws), shape[position] // shards_of).reshape((-1,) + (1,) * (len(shape) - 1 - position))
    return loudness


def centred(rng, dims, scale, bound, shards=(), kind=jnp.bfloat16):
    entries = scale * jax.random.normal(rng, dims, jnp.float32)
    if shards:
        entries = entries * steps_of(rng, dims, shards, -0.22, 0.18)
    return jnp.clip(entries, -bound, bound).astype(kind)


def setup_inputs(seed: int = 0) -> dict:
    splits = jax.random.split(jax.random.key(seed), 21)
    latents = centred(splits[0], (TOKENS, D), 1.0, 6.0, ((0, 8),))
    context = centred(splits[1], (CLIPS * TEXT, D), 1.0, 6.0, ((0, 8),))
    time_embed = centred(splits[2], (CLIPS, 6, D), 0.5, 3.0, (), jnp.float32)
    teacher = centred(splits[3], (TOKENS, D), 1.0, 6.0, ((0, 8),))
    lengths = draw_lengths(jax.random.fold_in(splits[20], 71), 0)
    block_order = draw_block_order(jax.random.fold_in(splits[20], 71), 0)
    positions = plant(jax.random.randint(splits[6], (3, TOKENS), 0, 64), jax.random.fold_in(splits[6], 1), 0, 63).astype(jnp.int32)
    self_proj = centred(splits[7], (LAYERS, 3, D, D), D ** -0.5, 0.15625, ((2, 8), (3, 4)))
    cross_proj = centred(splits[8], (LAYERS, 3, D, D), D ** -0.5, 0.15625, ((2, 8), (3, 4)))
    out_proj = centred(splits[9], (LAYERS, 2, D, D), (D // 16) ** -0.5, 0.625, ((2, 4), (3, 8)))
    ffn_up = centred(splits[10], (LAYERS, D, FF), D ** -0.5, 0.15625, ((1, 8), (2, 4)))
    ffn_down = centred(splits[11], (LAYERS, FF, D), FF ** -0.5, 0.0625, ((1, 4), (2, 8)))
    proj_bias = centred(splits[12], (LAYERS, 5, D), 0.3, 2.0, ((2, 4),), jnp.float32)
    key_bias = centred(splits[13], (LAYERS, D), 0.3, 2.0, ((1, 4),), jnp.float32)
    norm_gains = jnp.clip(1.0 + 0.15 * jax.random.normal(splits[14], (LAYERS, 4, D), jnp.float32), 0.25, 1.75)
    ffn_bias = centred(splits[15], (LAYERS, FF), 0.3, 2.0, ((1, 4),), jnp.float32)
    out_bias = centred(splits[16], (LAYERS, 3, D), 0.3, 2.0, (), jnp.float32)
    cross_gain = jnp.clip(1.0 + 0.15 * jax.random.normal(splits[17], (LAYERS, D), jnp.float32), 0.25, 1.75)
    cross_shift = centred(splits[18], (LAYERS, D), 0.3, 2.0, (), jnp.float32)
    modulation = centred(splits[19], (LAYERS, 6, D), 0.5, 3.0, (), jnp.float32)
    return {"latents": latents, "context": context, "time_embed": time_embed, "teacher": teacher, "lengths": lengths, "block_order": block_order, "positions": positions, "self_proj": self_proj, "cross_proj": cross_proj, "out_proj": out_proj, "ffn_up": ffn_up, "ffn_down": ffn_down, "proj_bias": proj_bias, "key_bias": key_bias, "norm_gains": norm_gains, "ffn_bias": ffn_bias, "out_bias": out_bias, "cross_gain": cross_gain, "cross_shift": cross_shift, "modulation": modulation}


@jax.custom_vjp
def low(v):
    return lax.optimization_barrier(v.astype(jnp.bfloat16)).astype(jnp.float32)

@jax.custom_vjp
def low_back(v):
    return v

def low_keep(v):
    return (low(v), None)

def low_pass(kept, grad):
    return (grad,)

def back_keep(v):
    return (v, None)

def back_low(kept, grad):
    return (low(grad),)
low.defvjp(low_keep, low_pass)
low_back.defvjp(back_keep, back_low)
highest = lax.Precision.HIGHEST
epsilon = 1e-06

def rope_table(head_size):
    third = head_size // 6
    spans = [head_size - 4 * third, 2 * third, 2 * third]
    table = np.zeros((3, head_size), np.float32)
    start_col = 0
    for component in range(3):
        for pair_index in range(spans[component] // 2):
            freq_value = 10000.0 ** (-(2.0 * pair_index) / spans[component])
            table[component, start_col + 2 * pair_index] = freq_value
            table[component, start_col + 2 * pair_index + 1] = freq_value
        start_col += spans[component]
    return table

def turn_matrix(head_size):
    matrix = np.zeros((head_size, head_size), np.float32)
    for pair_index in range(head_size // 2):
        matrix[2 * pair_index + 1, 2 * pair_index] = -1.0
        matrix[2 * pair_index, 2 * pair_index + 1] = 1.0
    return matrix

def rope_angles(positions, head_size):
    table = rope_table(head_size)
    places = positions.astype(jnp.float32)
    angles = places[0][:, None] * table[0][None, :] + places[1][:, None] * table[1][None, :] + places[2][:, None] * table[2][None, :]
    return (jnp.cos(angles), jnp.sin(angles))

def rotate(values, cosine, sine_rows):
    turned = jnp.einsum('nhd,de->nhe', values, turn_matrix(values.shape[-1]), precision=highest)
    return values * cosine[:, None, :] + turned * sine_rows[:, None, :]

def layer_norm(values):
    center = values - lax.optimization_barrier(jnp.mean(values, axis=-1, keepdims=True))
    return center * lax.rsqrt(lax.optimization_barrier(jnp.mean(center * center, axis=-1, keepdims=True)) + epsilon)

def modulated(values, shift_row, scale_row):
    return layer_norm(values) * (1.0 + scale_row) + shift_row

def affine_norm(values, gain_row, shift_row):
    return layer_norm(values) * gain_row + shift_row

def rms_norm(values, gain_row):
    return values * lax.rsqrt(lax.optimization_barrier(jnp.mean(values * values, axis=-1, keepdims=True)) + epsilon) * gain_row

def gelu_tanh(values):
    return 0.5 * values * (1.0 + jnp.tanh(0.7978845608028654 * (values + 0.044715 * values * values * values)))

def attend(queries, key_rows, value_rows, key_valid):
    scaling = 1.0 / math.sqrt(queries.shape[-1])

    def one_head(operands):
        query_head, key_head, value_head = operands
        scores = low_back(jnp.dot(query_head, key_head.T, precision=highest)) * scaling
        if key_valid is not None:
            scores = jnp.where(key_valid[None, :], scores, -1e+30)
        shifted = jnp.exp(scores - lax.optimization_barrier(jnp.max(scores, axis=-1, keepdims=True)))
        weights = low(shifted / lax.optimization_barrier(jnp.sum(shifted, axis=-1, keepdims=True)))
        return jnp.dot(weights, value_head, precision=highest)
    stacked = lax.map(jax.checkpoint(one_head), (jnp.swapaxes(queries, 0, 1), jnp.swapaxes(key_rows, 0, 1), jnp.swapaxes(value_rows, 0, 1)))
    return jnp.swapaxes(stacked, 0, 1)

def block(hidden, text_rows, time_row, key_valid, cosine, sine_rows, params, layer_index):
    self_weight, cross_weight, out_weight, up_weight, down_weight, bias_rows, key_row, gain_rows, up_bias, out_rows, norm_gain, norm_shift, mod_rows = [item[layer_index] for item in params]
    tok_count = hidden.shape[0]
    text_count = text_rows.shape[0]
    mod_terms = mod_rows + time_row
    first_in = low(modulated(hidden, mod_terms[0], mod_terms[1]))
    self_bias = jnp.stack([bias_rows[0], key_row, bias_rows[1]])
    projected = jnp.einsum('td,cdh->cth', first_in, self_weight, precision=highest) + self_bias[:, None, :]
    query_proj = low_back(projected[0])
    key_proj = low_back(projected[1])
    value_proj = low_back(projected[2])
    query_rot = low(rotate(rms_norm(query_proj, gain_rows[0]).reshape(tok_count, HEADS, HEAD_DIM), cosine, sine_rows))
    key_rot = low(rotate(rms_norm(key_proj, gain_rows[1]).reshape(tok_count, HEADS, HEAD_DIM), cosine, sine_rows))
    value_heads = low(value_proj).reshape(tok_count, HEADS, HEAD_DIM)
    attended = attend(query_rot, key_rot, value_heads, key_valid).reshape(tok_count, D)
    attended = low(low_back(attended))
    self_branch = low_back(jnp.dot(attended, out_weight[0], precision=highest) + out_rows[0])
    hidden = hidden + self_branch * mod_terms[2]
    cross_in = low(affine_norm(hidden, norm_gain, norm_shift))
    cross_query = low_back(jnp.dot(cross_in, cross_weight[0], precision=highest) + bias_rows[2])
    text_proj = jnp.einsum('td,cdh->cth', text_rows, cross_weight[1:3], precision=highest) + bias_rows[3:5][:, None, :]
    text_key = low_back(text_proj[0])
    text_value = low_back(text_proj[1])
    cross_heads = low(rms_norm(cross_query, gain_rows[2])).reshape(tok_count, HEADS, HEAD_DIM)
    text_keys = low(rms_norm(text_key, gain_rows[3])).reshape(text_count, HEADS, HEAD_DIM)
    text_values = low(text_value).reshape(text_count, HEADS, HEAD_DIM)
    cross_out = low(low_back(attend(cross_heads, text_keys, text_values, None).reshape(tok_count, D)))
    cross_branch = low_back(jnp.dot(cross_out, out_weight[1], precision=highest) + out_rows[1])
    hidden = hidden + cross_branch
    ffn_in = low(modulated(hidden, mod_terms[3], mod_terms[4]))
    inner = low_back(jnp.dot(ffn_in, up_weight, precision=highest) + up_bias)
    gelu_out = low(gelu_tanh(inner))
    ffn_branch = low_back(jnp.dot(gelu_out, down_weight, precision=highest) + out_rows[2])
    return hidden + ffn_branch * mod_terms[5]

def reference(latents, context, time_embed, teacher, lengths, block_order, positions, self_proj, cross_proj, out_proj, ffn_up, ffn_down, proj_bias, key_bias, norm_gains, ffn_bias, out_bias, cross_gain, cross_shift, modulation):
    seq_len = HOLD * TOK_DEV
    row_index = jnp.arange(TOKENS, dtype=jnp.int32)
    device_of = row_index // TOK_DEV
    seq_place = block_order[device_of] * TOK_DEV + row_index % TOK_DEV
    token_valid = seq_place < lengths[device_of // HOLD]
    cosine, sine_rows = rope_angles(positions, HEAD_DIM)
    params = tuple((item.astype(jnp.float32) for item in (self_proj, cross_proj, out_proj, ffn_up, ffn_down, proj_bias, key_bias, norm_gains, ffn_bias, out_bias, cross_gain, cross_shift, modulation)))

    def forward(hidden, text_all, time_all, weights_all):

        def one_clip(operands):
            clip_hidden, clip_text, clip_time, clip_valid, clip_cos, clip_sin = operands
            for layer_index in range(LAYERS):
                clip_hidden = block(clip_hidden, clip_text, clip_time, clip_valid, clip_cos, clip_sin, weights_all, layer_index)
            return clip_hidden
        result = lax.map(jax.checkpoint(one_clip), (hidden.reshape(CLIPS, seq_len, D), text_all.reshape(CLIPS, TEXT, D), time_all, token_valid.reshape(CLIPS, seq_len), cosine.reshape(CLIPS, seq_len, HEAD_DIM), sine_rows.reshape(CLIPS, seq_len, HEAD_DIM)))
        return result.reshape(TOKENS, D)
    output, pullback = jax.vjp(forward, latents.astype(jnp.float32), context.astype(jnp.float32), time_embed, params)
    error = output - teacher.astype(jnp.float32)
    mask_rows = token_valid.astype(jnp.float32)[:, None]
    latents_grad, context_grad, time_grad, weight_grads = pullback(mask_rows * error)
    loss = jnp.sum(mask_rows * error * error) / (jnp.sum(lengths).astype(jnp.float32) * D)
    return (output, loss, latents_grad, context_grad, time_grad) + tuple(weight_grads)
```

```python
import functools
import math

import jax
import jax.numpy as jnp
import numpy as np
from jax import lax
from jax.experimental import pallas as pl
from jax.experimental.pallas import tpu as pltpu
from jax.sharding import PartitionSpec as P

MESH = pl.DeviceIdType.MESH
F32, BF16 = jnp.float32, jnp.bfloat16
NN = (((1,), (0,)), ((), ()))
NT = (((1,), (1,)), ((), ()))
TN = (((0,), (0,)), ((), ()))
HEAD_DIM = 128
HOLD = 4
LAYERS = 2
CHAIN = 4
CHUNK = 32
EPS = 1e-06
LOG2E = math.log2(math.e)
SCALE = 1.0 / math.sqrt(HEAD_DIM)
VMEM_BYTES = 60 * 2**20


def dot(left, right, dims=NN, exact=False):
    precision = lax.Precision.HIGHEST if exact else None
    return lax.dot_general(left, right, dims, precision=precision, preferred_element_type=F32)


def rope_table(head_size):
    third = head_size // 6
    spans = [head_size - 4 * third, 2 * third, 2 * third]
    table = np.zeros((3, head_size), np.float32)
    start_col = 0
    for component in range(3):
        for pair_index in range(spans[component] // 2):
            freq_value = 10000.0 ** (-(2.0 * pair_index) / spans[component])
            table[component, start_col + 2 * pair_index] = freq_value
            table[component, start_col + 2 * pair_index + 1] = freq_value
        start_col += spans[component]
    return table


def rope_angles(positions, head_size):
    table = rope_table(head_size)
    places = positions.astype(F32)
    angles = (
        places[0][:, None] * table[0][None, :]
        + places[1][:, None] * table[1][None, :]
        + places[2][:, None] * table[2][None, :]
    )
    return (jnp.cos(angles), jnp.sin(angles))


def signal(**device):
    pl.semaphore_signal(
        pltpu.get_barrier_semaphore(), inc=1, device_id=device, device_id_type=MESH
    )


def bits_of_dp():
    return max(lax.axis_size("dp").bit_length() - 1, 1)


def flip(index, mask):
    result, bit = index, 0
    while mask >> bit:
        if mask >> bit & 1:
            half = 1 << bit
            result = result + half - 2 * half * lax.rem(index // half, 2)
        bit += 1
    return result


def greet(tensor, masks):
    place, me = lax.axis_index("tensor"), lax.axis_index("dp")
    if tensor:
        for step in range(1, CHAIN):
            signal(tensor=lax.rem(place + step, CHAIN))
    for mask in masks:
        signal(dp=flip(me, mask))
    pl.semaphore_wait(
        pltpu.get_barrier_semaphore(), (CHAIN - 1 if tensor else 0) + len(masks)
    )


def holders():
    me = lax.axis_index("dp")
    return flip(me, 1), flip(me, 2)


def send(src, dst, send_sem, recv_sem, **device):
    return pltpu.make_async_remote_copy(
        src_ref=src,
        dst_ref=dst,
        send_sem=send_sem,
        recv_sem=recv_sem,
        device_id=device,
        device_id_type=MESH,
    )


def masks_over(bits):
    masks = [0]
    for bit in bits:
        masks += [mask | 1 << bit for mask in masks]
    return masks


def halves_of(size):
    cut = (size // 2 + 15) // 16 * 16
    return ((0, cut), (cut, size - cut))


def half_orders(bits):
    rising = list(range(1, bits))
    return (rising, rising[::-1])


class Gather:
    def __init__(self, source, layer):
        self.layer = layer
        self.operands = [source]
        shape = source.shape[1:]
        self.lead = shape[:-2]
        self.size = shape[-2]
        devices = lax.axis_size("dp")
        self.outs = [(self.lead + (self.size * devices, shape[-1]), source.dtype)]
        self.spaces = [pl.ANY]
        self.bits = bits_of_dp()
        plan = []
        for half, order in enumerate(half_orders(self.bits)):
            for phase, bit in enumerate(order):
                for mask in masks_over(order[:phase]):
                    plan.append((phase, half, bit, mask))
        for mask in masks_over(range(1, self.bits)):
            plan.append((self.bits - 1, None, 0, mask))
        self.plan = plan
        count = len(plan)
        self.scratch = [
            pltpu.SemaphoreType.DMA((count,)),
            pltpu.SemaphoreType.DMA((count,)),
            pltpu.SemaphoreType.DMA,
        ]

    def key(self):
        return ("gather", self.layer, self.outs[0][0])

    def bind(self, sources, outs, scratch):
        self.source = sources[0].at[self.layer]
        self.out = outs[0]
        self.send_sems, self.recv_sems, self.own_sem = scratch

    def block(self, ref, index, half):
        low, size = (0, self.size) if half is None else halves_of(self.size)[half]
        start = low if index is None else index * self.size + low
        rows = pl.ds(pl.multiple_of(start, 16), size)
        return ref.at[:, rows] if self.lead else ref.at[rows]

    def copies(self, phase, own=None):
        me = lax.axis_index("dp")
        for number, (step, half, bit, mask) in enumerate(self.plan):
            if step == phase and own in (None, mask == 0):
                index = flip(me, mask)
                source = (
                    self.block(self.source, None, half)
                    if mask == 0
                    else self.block(self.out, index, half)
                )
                yield send(
                    source,
                    self.block(self.out, index, half),
                    self.send_sems.at[number],
                    self.recv_sems.at[number],
                    dp=flip(me, 1 << bit),
                )

    def own_copy(self):
        me = lax.axis_index("dp")
        return pltpu.make_async_copy(
            self.source, self.block(self.out, me, None), self.own_sem
        )

    def start(self):
        for phase in range(self.bits):
            for copy in self.copies(phase, True):
                copy.start()
        self.own_copy().start()

    def advance(self, phase):
        for copy in self.copies(phase - 1):
            copy.wait_recv()
        for copy in self.copies(phase, False):
            copy.start()

    def finish(self):
        for copy in self.copies(self.bits - 1):
            copy.wait_recv()
        for phase in range(self.bits):
            for copy in self.copies(phase):
                copy.wait_send()
        self.own_copy().wait()


class Scatter:
    def __init__(self, source):
        self.operands = [source]
        self.bits = bits_of_dp()
        self.size = source.shape[0] // lax.axis_size("dp")
        self.width = source.shape[1]
        self.outs = [((self.size, self.width), F32)]
        self.spaces = [pltpu.VMEM]
        self.slots = 1 << self.bits - 1
        orders = [order[::-1] for order in half_orders(self.bits)]
        plan = [(0, None, 0, mask, mask >> 1) for mask in masks_over(range(1, self.bits))]
        for half, order in enumerate(orders):
            for phase, bit in enumerate(order):
                kept = masks_over(order[phase + 1 :])
                for place, mask in enumerate(kept):
                    plan.append((phase + 1, half, bit, mask, place))
        self.plan = plan
        count = len(plan)
        buffers = [pltpu.VMEM((self.slots, self.size, self.width), BF16)] * 2
        for phase in range(1, self.bits):
            places = 1 << self.bits - 1 - phase
            buffers += [
                pltpu.VMEM((places, size, self.width), BF16)
                for _, size in halves_of(self.size)
            ]
        self.scratch = buffers + [
            pltpu.SemaphoreType.DMA((count,)),
            pltpu.SemaphoreType.DMA((count,)),
            pltpu.SemaphoreType.DMA((self.slots,)),
        ]

    def key(self):
        return ("scatter", self.width)

    def bind(self, sources, outs, scratch):
        self.source, self.out = sources[0], outs[0]
        self.held, self.landed = scratch[:2]
        self.parts = scratch[2:-3]
        self.send_sems, self.recv_sems, self.own_sems = scratch[-3:]

    def rows(self, index):
        return pl.ds(pl.multiple_of(index * self.size, 16), self.size)

    def copies(self, phase):
        me = lax.axis_index("dp")
        for number, (step, half, bit, mask, place) in enumerate(self.plan):
            if step != phase:
                continue
            if phase == 0:
                source = self.source.at[self.rows(flip(me, mask | 1))]
                target = self.landed.at[mask >> 1]
            else:
                low, size = halves_of(self.size)[half]
                source = self.held.at[(mask | 1 << bit) >> 1, pl.ds(low, size)]
                target = self.parts[2 * (phase - 1) + half].at[place]
            yield send(
                source,
                target,
                self.send_sems.at[number],
                self.recv_sems.at[number],
                dp=flip(me, 1 << bit),
            )

    def own_copies(self):
        me = lax.axis_index("dp")
        for slot in range(self.slots):
            yield pltpu.make_async_copy(
                self.source.at[self.rows(flip(me, slot << 1))],
                self.held.at[slot],
                self.own_sems.at[slot],
            )

    def start(self):
        for copy in self.copies(0):
            copy.start()
        for copy in self.own_copies():
            copy.start()

    def add(self, phase):
        for copy in self.copies(phase):
            copy.wait_recv()
        if phase == 0:
            for copy in self.own_copies():
                copy.wait()
            for slot in range(self.slots):

                def step(rows, index, slot=slot):
                    self.held[slot, rows] = self.held[slot, rows] + self.landed[slot, rows]

                loop_rows(self.size, 16, step)
            return
        for number, (step, half, bit, mask, place) in enumerate(self.plan):
            if step == phase:
                low, size = halves_of(self.size)[half]
                part = self.parts[2 * (phase - 1) + half]

                def step(index, carry, mask=mask, place=place, low=low, part=part):
                    near = pl.ds(pl.multiple_of(index * 16, 16), 16)
                    rows = pl.ds(pl.multiple_of(low + index * 16, 16), 16)
                    if phase == self.bits - 1:
                        self.out[rows] = self.held[0, rows].astype(F32) + part[place, near].astype(
                            F32
                        )
                    else:
                        self.held[mask >> 1, rows] = (
                            self.held[mask >> 1, rows] + part[place, near]
                        )
                    return carry

                lax.fori_loop(0, size // 16, step, 0)

    def advance(self, phase):
        self.add(phase - 1)
        for copy in self.copies(phase):
            copy.start()

    def finish(self):
        self.add(self.bits - 1)
        for phase in range(self.bits):
            for copy in self.copies(phase):
                copy.wait_send()


class Side:
    def __init__(self, jobs):
        self.jobs = jobs
        self.masks = [1 << bit for bit in range(bits_of_dp())] if jobs else []

    def start(self):
        for job in self.jobs:
            job.start()

    def early(self):
        for phase in range(1, bits_of_dp() - 1):
            for job in self.jobs:
                job.advance(phase)

    def early_first(self):
        if bits_of_dp() > 2:
            for job in self.jobs:
                job.advance(1)

    def early_rest(self):
        for phase in range(2, bits_of_dp() - 1):
            for job in self.jobs:
                job.advance(phase)

    def late(self):
        for job in self.jobs:
            job.advance(bits_of_dp() - 1)

    def finish(self):
        for job in self.jobs:
            job.finish()


class Exchange:
    def __init__(self, slots, send_sems, recv_sems):
        self.slots = slots
        place = lax.axis_index("tensor")
        self.place = place
        self.copies = [
            send(
                slots.at[place],
                slots.at[place],
                send_sems.at[step - 1],
                recv_sems.at[step - 1],
                tensor=lax.rem(place + step, CHAIN),
            )
            for step in range(1, CHAIN)
        ]

    def start(self, rows):
        self.slots[self.place] = rows
        for copy in self.copies:
            copy.start()

    def finish(self):
        for copy in self.copies:
            copy.wait()


def stat_rows(squares, row):
    count, width = squares.shape
    ones = jnp.ones((8, width), F32)
    sums = dot(ones, squares, NT, exact=True)
    index = lax.broadcasted_iota(jnp.int32, sums.shape, 0)
    return jnp.where(index == row, sums, 0.0)


def stat_column(slots, row, lanes):
    gathered = jnp.concatenate([slots[place] for place in range(CHAIN)], axis=0)
    index = lax.broadcasted_iota(jnp.int32, (8 * CHAIN, lanes), 0)
    pick = jnp.where(lax.rem(index, 8) == row, 1.0, 0.0)
    return dot(gathered, pick, TN, exact=True)


class Chain:
    def __init__(self, part, total, buffers, sems):
        self.part, self.total = part, total
        self.came, self.pair, self.peers = buffers
        self.sems = sems
        place = lax.axis_index("tensor")
        self.is_end = (place == 0) | (place == 3)
        self.is_mid = jnp.logical_not(self.is_end)
        self.inner = jnp.where(place == 0, 1, 2)
        self.outer = jnp.where(place == 1, 0, 3)
        self.peer = 3 - place
        self.chunks = part.shape[0] // CHUNK

    @staticmethod
    def scratch(rows, width):
        chunks = rows // CHUNK
        return [pltpu.VMEM((rows, width), BF16)] * 4 + [pltpu.SemaphoreType.DMA((6, chunks))]

    def rows(self, k):
        return pl.ds(pl.multiple_of(k * CHUNK, CHUNK), CHUNK)

    def copy(self, src, dst, kind, k, device):
        return send(
            src.at[self.rows(k)],
            dst.at[self.rows(k)],
            self.sems.at[2 * kind, k],
            self.sems.at[2 * kind + 1, k],
            tensor=device,
        )

    def inward(self, k, device):
        return self.copy(self.part, self.came, 0, k, device)

    def across(self, k):
        return self.copy(self.pair, self.peers, 1, k, self.peer)

    def outward(self, k, device):
        return self.copy(self.total, self.total, 2, k, device)

    def begin(self, low, count):
        @pl.when(self.is_end)
        def _():
            def step(k, carry):
                self.inward(low + k, self.inner).start()
                return carry

            lax.fori_loop(0, count, step, 0)

    def first(self, k):
        self.inward(k, self.outer).wait_recv()
        rows = self.rows(k)
        self.pair[rows] = (self.part[rows].astype(F32) + self.came[rows].astype(F32)).astype(BF16)
        self.across(k).start()

    def second(self, k):
        self.across(k).wait_recv()
        rows = self.rows(k)
        self.total[rows] = (self.pair[rows].astype(F32) + self.peers[rows].astype(F32)).astype(
            BF16
        )
        self.outward(k, self.outer).start()

    def serve(self, k):
        @pl.when(self.is_mid)
        def _():
            self.first(k)

            @pl.when(k > 0)
            def _():
                self.second(jnp.maximum(k - 1, 0))

    def segment(self, low, high, closed, upto):
        @pl.when(self.is_mid)
        def _():
            def both(k, carry):
                self.first(k)

                @pl.when(k > 0)
                def _():
                    self.second(jnp.maximum(k - 1, 0))

                return carry

            lax.fori_loop(low, high, both, 0)
            if high == self.chunks:
                self.second(self.chunks - 1)

        @pl.when(self.is_end)
        def _():
            def close(k, carry):
                self.inward(k, self.inner).wait_send()
                self.outward(k, self.inner).wait_recv()
                return carry

            lax.fori_loop(closed, upto, close, 0)

    def drain(self, low, early=None, late=None):
        done, last = 0, self.chunks
        if early is not None:
            cut = low + (last - low) // 4
            self.segment(low, cut, done, cut - 1)
            low, done = cut, cut - 1
            early()
        if late is not None:
            cut = low + (last - low) * 5 // 8
            self.segment(low, cut, done, cut - 1)
            low, done = cut, cut - 1
            late()
        self.segment(low, last, done, last)

        @pl.when(self.is_mid)
        def _():
            def close(k, carry):
                self.across(k).wait_send()
                self.outward(k, self.outer).wait_send()
                return carry

            lax.fori_loop(0, self.chunks, close, 0)


COLLECTIVES = {}


def collective_of(key):
    return COLLECTIVES.setdefault(key, 1 + len(COLLECTIVES))


def run(name, kernel, ins, outs, scratch=(), remote=True, jobs=(), scalars=0, micros=0):
    whole = pl.BlockSpec(memory_space=pltpu.VMEM)
    far = pl.BlockSpec(memory_space=pl.ANY)
    job_ins = [item for job in jobs for item in job.operands]
    job_outs = [item for job in jobs for item in job.outs]
    job_spaces = [pl.BlockSpec(memory_space=space) for job in jobs for space in job.spaces]
    job_scratch = [item for job in jobs for item in job.scratch]
    side = Side(jobs)

    def body(*refs):
        refs = list(refs)

        def take(count):
            taken = refs[:count]
            del refs[:count]
            return taken

        own_in, side_in = take(len(ins)), take(len(job_ins))
        own_out, side_out = take(len(outs)), take(len(job_outs))
        own_scratch = take(len(scratch))
        for job in jobs:
            job.bind(
                [side_in.pop(0) for _ in job.operands],
                [side_out.pop(0) for _ in job.outs],
                take(len(job.scratch)),
            )
        kernel(side, *own_in, *own_out, *own_scratch)

    key = (name,) + tuple(job.key() for job in jobs)
    results = pl.pallas_call(
        body,
        out_shape=tuple(jax.ShapeDtypeStruct(shape, kind) for shape, kind in outs + tuple(job_outs)),
        in_specs=[pl.BlockSpec(memory_space=pltpu.SMEM)] * scalars
        + [whole] * (len(ins) - scalars)
        + [far] * len(job_ins),
        out_specs=tuple([whole] * len(outs) + job_spaces),
        scratch_shapes=list(scratch) + job_scratch,
        cost_estimate=pl.CostEstimate(
            flops=0, bytes_accessed=micros * 3000000, transcendentals=0
        ),
        compiler_params=pltpu.CompilerParams(
            collective_id=collective_of(key) if remote else None,
            has_side_effects=remote,
            vmem_limit_bytes=VMEM_BYTES,
        ),
    )(*ins, *job_ins)
    return results[: len(outs)], results[len(outs) :]


def normed(hidden):
    center = hidden - jnp.mean(hidden, axis=-1, keepdims=True)
    inverse = lax.rsqrt(jnp.mean(center * center, axis=-1, keepdims=True) + EPS)
    return center * inverse, inverse


def norm_back(hidden, scale_row, grad):
    hat, inverse = normed(hidden)
    inner = grad * scale_row
    back = inverse * (
        inner
        - jnp.mean(inner, axis=-1, keepdims=True)
        - hat * jnp.mean(inner * hat, axis=-1, keepdims=True)
    )
    return back, hat


def loop_rows(total, size, body):
    def step(index, carry):
        body(pl.ds(pl.multiple_of(index * size, size), size), index)
        return carry

    lax.fori_loop(0, total // size, step, 0)


def add_sum(ref, row, block):
    ref[row : row + 1] += jnp.sum(block, axis=0, keepdims=True)


def turned(rows):
    lane = lax.broadcasted_iota(jnp.int32, rows.shape, 1)
    width = rows.shape[1]
    return jnp.where(
        lax.rem(lane, 2) == 0, -pltpu.roll(rows, width - 1, 1), pltpu.roll(rows, 1, 1)
    )


def head_cols(head):
    return slice(head * HEAD_DIM, (head + 1) * HEAD_DIM)


def inverse_rms(sums, features):
    return lax.rsqrt(sums / features + EPS)


MODS, OUT_BIAS, CROSS_GAIN, CROSS_SHIFT = 0, 6, 9, 10
KEY_BIAS, GAINS = 5, 6


def row_of(ref, index):
    return ref[index : index + 1]


def entry_kernel(
    side,
    lengths,
    block_order,
    time_embed,
    modulation,
    out_bias,
    cross_gain,
    cross_shift,
    proj_bias,
    key_bias,
    norm_gains,
    ffn_bias,
    counts,
    *rest,
):
    packs, (send_sems, recv_sems) = rest[:-2], rest[-2:]
    greet(False, side.masks)
    near, far = holders()
    tokens = counts.shape[2]
    clip = lax.axis_index("dp") // HOLD
    mine = (lengths[clip] - block_order[0] * tokens).astype(F32)
    counts[0] = jnp.full(counts.shape[1:], mine, F32)

    def copy(number, source, target, device):
        return send(
            counts.at[source],
            counts.at[target],
            send_sems.at[number],
            recv_sems.at[number],
            dp=device,
        )

    to_near, to_far, onward = copy(0, 0, 1, near), copy(1, 0, 2, far), copy(2, 2, 3, near)
    side.start()
    to_near.start()
    to_far.start()
    for layer in range(LAYERS):
        rows_d, rows_w, rows_f = packs[3 * layer : 3 * layer + 3]
        rows_d[...] = jnp.zeros(rows_d.shape, F32)
        rows_w[...] = jnp.zeros(rows_w.shape, F32)
        rows_d[MODS : MODS + 6] = modulation[layer] + time_embed[clip]
        rows_d[OUT_BIAS : OUT_BIAS + 3] = out_bias[layer]
        rows_d[CROSS_GAIN : CROSS_GAIN + 1] = row_of(cross_gain, layer)
        rows_d[CROSS_SHIFT : CROSS_SHIFT + 1] = row_of(cross_shift, layer)
        rows_w[0:5] = proj_bias[layer]
        rows_w[KEY_BIAS : KEY_BIAS + 1] = row_of(key_bias, layer)
        rows_w[GAINS : GAINS + 4] = norm_gains[layer]
        rows_f[...] = row_of(ffn_bias, layer)
    to_far.wait_recv()
    onward.start()
    side.early()
    side.late()
    to_near.wait_recv()
    onward.wait_recv()
    for copy in (to_near, to_far, onward):
        copy.wait_send()
    side.finish()


def add_branch(base, tot, bias_row, gate_row):
    return base + (tot.astype(F32) + bias_row) * gate_row


def qkv_kernel(
    first,
    side,
    base,
    tot,
    rows_before,
    rows_d,
    rows_w,
    weight,
    cosine,
    sine,
    hidden,
    normal,
    query,
    key,
    query_rot,
    key_value,
    slots,
    send_sems,
    recv_sems,
):
    greet(True, side.masks)
    side.start()
    tokens, width = query.shape
    features = hidden.shape[1]
    heads = width // HEAD_DIM
    scale_row = 1.0 + row_of(rows_d, MODS + 1)
    shift_row = row_of(rows_d, MODS)

    def project(rows, index):
        if first:
            block = base[rows].astype(F32)
        else:
            block = add_branch(
                base[rows], tot[rows], row_of(rows_before, OUT_BIAS + 2), row_of(rows_before, MODS + 5)
            )
        hidden[rows] = block
        block = (normed(block)[0] * scale_row + shift_row).astype(BF16)
        normal[rows] = block
        query[rows] = dot(block, weight[0]) + row_of(rows_w, 0)
        key[rows] = dot(block, weight[1]) + row_of(rows_w, KEY_BIAS)
        value = (dot(block, weight[2]) + row_of(rows_w, 1)).astype(BF16)
        for head in range(heads):
            key_value[head, 1, rows] = value[:, head_cols(head)]

    loop_rows(tokens, 256, project)
    exchange = Exchange(slots, send_sems, recv_sems)
    exchange.start(
        stat_rows(query[...] * query[...], 0) + stat_rows(key[...] * key[...], 1)
    )
    side.early()
    exchange.finish()
    query_inv = inverse_rms(stat_column(slots, 0, HEAD_DIM), features)
    key_inv = inverse_rms(stat_column(slots, 1, HEAD_DIM), features)
    for head in range(heads):
        cols = head_cols(head)
        rows = query[:, cols] * query_inv * rows_w[GAINS : GAINS + 1, cols]
        query_rot[:, cols] = (rows * cosine[...] + turned(rows) * sine[...]).astype(BF16)
        rows = key[:, cols] * key_inv * rows_w[GAINS + 1 : GAINS + 2, cols]
        key_value[head, 0] = (rows * cosine[...] + turned(rows) * sine[...]).astype(BF16)
    side.late()
    side.finish()


def below(counts, slot, shape):
    index = lax.broadcasted_iota(jnp.int32, shape, 0).astype(F32)
    return index < counts[slot, 0:1]


def softmax_back(scores, lse_row, mask):
    probs = jnp.exp2(scores * (SCALE * LOG2E) - lse_row)
    return probs if mask is None else jnp.where(mask, probs, 0.0)


def attend_kernel(with_context, side, counts, query, key_value, *refs):
    refs = list(refs)
    context = refs.pop(0) if with_context else None
    others, result, lse = refs[:3]
    clip_context = refs[3] if with_context else None
    scores, send_sems, recv_sems = refs[-3:]
    greet(False, [1, 2])
    near, far = holders()
    tokens, width = query.shape
    heads = width // HEAD_DIM

    def copy(source, target, number, device):
        return send(source, target, send_sems.at[number], recv_sems.at[number], dp=device)

    to_near = copy(key_value, others.at[0], 0, near)
    to_far = [
        copy(key_value.at[head], others.at[1, head], 1 + head, far) for head in range(heads)
    ]
    onward = [
        copy(others.at[1, head], others.at[2, head], 1 + heads + head, near)
        for head in range(heads)
    ]
    for item in to_far:
        item.start()
    to_near.start()
    text = []
    if with_context:
        place = lax.rem(lax.axis_index("dp"), HOLD)
        size = context.shape[0]

        def block(index):
            return clip_context.at[pl.ds(pl.multiple_of(index * size, 16), size)]

        low = 1 + 2 * heads
        clip_context[pl.ds(pl.multiple_of(place * size, 16), size)] = context[...]
        text = [
            copy(block(place), block(place), low, near),
            copy(block(place), block(place), low + 1, far),
            copy(block(flip(place, 2)), block(flip(place, 2)), low + 2, near),
        ]
        text[0].start()
        text[1].start()

    def score(head, slot, keys):
        block = dot(keys, query[:, head_cols(head)], NT) * (SCALE * LOG2E)
        scores[head, slot] = jnp.where(below(counts, slot, block.shape), block, -1e30)

    for head in range(heads):
        score(head, 0, key_value[head, 0])
    to_near.wait_recv()
    for head in range(heads):
        score(head, 1, others[0, head, 0])
    lse[...] = jnp.zeros(lse.shape, F32)
    for head in range(heads):
        to_far[head].wait_recv()
        onward[head].start()
        score(head, 2, others[1, head, 0])
        onward[head].wait_recv()
        score(head, 3, others[2, head, 0])
        top = jnp.max(scores[head, 0], axis=0, keepdims=True)
        for slot in range(1, HOLD):
            top = jnp.maximum(top, jnp.max(scores[head, slot], axis=0, keepdims=True))
        total = jnp.zeros_like(top)
        summed = jnp.zeros((HEAD_DIM, tokens), F32)
        for slot in range(HOLD):
            values = key_value[head, 1] if slot == 0 else others[slot - 1, head, 1]
            probs = jnp.exp2(scores[head, slot] - top)
            total = total + jnp.sum(probs, axis=0, keepdims=True)
            summed = summed + dot(values, probs.astype(BF16), TN)
        result[:, head_cols(head)] = (summed / total).T.astype(BF16)
        lse[head : head + 1] = top + jnp.log2(total)
    if with_context:
        text[1].wait_recv()
        text[2].start()
        text[0].wait_recv()
        text[2].wait_recv()
    for item in [to_near] + to_far + onward + text:
        item.wait_send()


def out_sum_kernel(
    side,
    rows_in,
    weight,
    context,
    text_weight,
    rows_w,
    total,
    text_key,
    text_kb,
    text_vb,
    slots,
    send_sems,
    recv_sems,
    part,
    came,
    pair,
    peers,
    sems,
):
    greet(True, side.masks)
    side.start()
    chain = Chain(part, total, (came, pair, peers), sems)
    tokens, features = total.shape
    per_block = 128 // CHUNK

    def project(rows, index):
        part[rows] = dot(rows_in[rows], weight[0], NT).astype(BF16)
        chain.begin(index * per_block, per_block)

    loop_rows(tokens, 128, project)
    text_count, width = text_key.shape
    blocks = text_count // 128

    def text(rows, index):
        block = context[rows]
        text_key[rows] = dot(block, text_weight[1]) + row_of(rows_w, 3)
        chain.serve(2 * index)
        text_vb[rows] = (dot(block, text_weight[2]) + row_of(rows_w, 4)).astype(BF16)
        chain.serve(2 * index + 1)

    loop_rows(text_count, 128, text)
    exchange = Exchange(slots, send_sems, recv_sems)

    def early():
        side.early()
        exchange.start(stat_rows(text_key[...] * text_key[...], 0))

    def late():
        exchange.finish()
        text_inv = inverse_rms(stat_column(slots, 0, HEAD_DIM), features)
        for head in range(width // HEAD_DIM):
            cols = head_cols(head)
            text_kb[:, cols] = (
                text_key[:, cols] * text_inv * rows_w[GAINS + 3 : GAINS + 4, cols]
            ).astype(BF16)
        side.late()

    chain.drain(2 * blocks, early, late)
    side.finish()


def cross_kernel(
    side,
    base,
    tot,
    rows_d,
    rows_w,
    weight,
    text_kb,
    text_vb,
    out_weight,
    hidden,
    normal,
    query,
    query_b,
    result,
    lse,
    slots,
    total,
    send_sems,
    recv_sems,
    part,
    came,
    pair,
    peers,
    sems,
):
    greet(True, side.masks)
    side.start()
    chain = Chain(part, total, (came, pair, peers), sems)
    tokens, width = query.shape
    features = hidden.shape[1]
    heads = width // HEAD_DIM

    def project(rows, index):
        block = add_branch(
            base[rows], tot[rows], row_of(rows_d, OUT_BIAS), row_of(rows_d, MODS + 2)
        )
        hidden[rows] = block
        block = normed(block)[0] * row_of(rows_d, CROSS_GAIN) + row_of(rows_d, CROSS_SHIFT)
        block = block.astype(BF16)
        normal[rows] = block
        query[rows] = dot(block, weight[0]) + row_of(rows_w, 2)

    loop_rows(tokens, 256, project)
    exchange = Exchange(slots, send_sems, recv_sems)
    exchange.start(stat_rows(query[...] * query[...], 0))
    exchange.finish()
    query_inv = inverse_rms(stat_column(slots, 0, HEAD_DIM), features)
    lse[...] = jnp.zeros(lse.shape, F32)
    for head in range(heads):
        cols = head_cols(head)
        query_b[:, cols] = (
            query[:, cols] * query_inv * rows_w[GAINS + 2 : GAINS + 3, cols]
        ).astype(BF16)
        scores = dot(text_kb[:, cols], query_b[:, cols], NT) * (SCALE * LOG2E)
        top = jnp.max(scores, axis=0, keepdims=True)
        probs = jnp.exp2(scores - top)
        amount = jnp.sum(probs, axis=0, keepdims=True)
        summed = dot(text_vb[:, cols], probs.astype(BF16), TN)
        result[:, cols] = (summed / amount).T.astype(BF16)
        lse[head : head + 1] = top + jnp.log2(amount)
    per_block = 128 // CHUNK

    def project_out(rows, index):
        part[rows] = dot(result[rows], out_weight[1], NT).astype(BF16)
        chain.begin(index * per_block, per_block)

    loop_rows(tokens, 128, project_out)
    chain.drain(0, side.early, side.late)
    side.finish()


def column_cuts(width):
    cuts, low = [], 0
    while low < width:
        high = low + 512 if width - low >= 1024 else width
        cuts.append((low, high))
        low = high
    return cuts


GELU_A = 0.7978845608028654
GELU_B = 0.044715


def mlp_loop(side, tokens, rows_of, inner, second, chain, middle):
    size = 128
    per_block = size // CHUNK
    features, hidden_width = second.shape
    cuts = column_cuts(hidden_width)
    half = features // 2
    blocks = tokens // size

    def step(index, carry):
        rows = pl.ds(pl.multiple_of(index * size, size), size)
        block = rows_of(rows)

        def serve(offset):
            @pl.when(index > 0)
            def _():
                chain.serve(jnp.maximum(index - 1, 0) * per_block + offset)

        served = 0
        for place, (low, high) in enumerate(cuts):
            inner(rows, block, low, high)
            if place % 2 == 1 and served < 2:
                serve(served)
                served += 1
        while served < 2:
            serve(served)
            served += 1
        for part_index in range(2):
            cols = slice(part_index * half, (part_index + 1) * half)
            chain.part[rows, cols] = dot(middle[rows], second[cols], NT).astype(BF16)
            if part_index == 0:
                serve(2)
        chain.begin(index * per_block, per_block)
        serve(3)
        if side.jobs:

            @pl.when(index == 1)
            def _():
                side.early()

            @pl.when(index == blocks - 1)
            def _():
                side.late()

        return carry

    lax.fori_loop(0, blocks, step, 0)
    chain.drain((blocks - 1) * per_block)
    side.finish()


def ffn_kernel(
    side,
    base,
    tot,
    rows_d,
    up,
    rows_f,
    down,
    hidden,
    normal,
    gelu_b,
    slope,
    total,
    part,
    came,
    pair,
    peers,
    sems,
):
    greet(True, side.masks)
    side.start()
    chain = Chain(part, total, (came, pair, peers), sems)
    tokens = hidden.shape[0]
    scale_row = 1.0 + row_of(rows_d, MODS + 4)
    shift_row = row_of(rows_d, MODS + 3)

    def rows_of(rows):
        block = add_branch(base[rows], tot[rows], row_of(rows_d, OUT_BIAS + 1), 1.0)
        hidden[rows] = block
        block = (normed(block)[0] * scale_row + shift_row).astype(BF16)
        normal[rows] = block
        return block

    def inner(rows, block, low, high):
        z = dot(block, up[:, low:high]) + rows_f[:, low:high]
        square = z * z
        tanh = jnp.tanh(GELU_A * z * (1.0 + GELU_B * square))
        side_value = 0.5 * (1.0 + tanh)
        gelu_b[rows, low:high] = (z * side_value).astype(BF16)
        slope[rows, low:high] = (
            side_value
            + 0.5 * z * (1.0 - tanh * tanh) * (GELU_A * (1.0 + 3.0 * GELU_B * square))
        ).astype(BF16)

    mlp_loop(side, tokens, rows_of, inner, down, chain, gelu_b)


def ffn_back_kernel(
    side,
    grad,
    tot,
    rows_d,
    down,
    up,
    slope,
    down_in,
    inner_b,
    total,
    sums,
    bias_sum,
    part,
    came,
    pair,
    peers,
    sems,
):
    greet(True, side.masks)
    side.start()
    chain = Chain(part, total, (came, pair, peers), sems)
    tokens = grad.shape[0]
    sums[...] = jnp.zeros(sums.shape, F32)
    bias_sum[...] = jnp.zeros(bias_sum.shape, F32)

    def rows_of(rows):
        block = grad[rows]
        add_sum(sums, 0, block * (tot[rows].astype(F32) + row_of(rows_d, OUT_BIAS + 2)))
        block = (block * row_of(rows_d, MODS + 5)).astype(BF16)
        down_in[rows] = block
        add_sum(sums, 1, block.astype(F32))
        return block

    def inner(rows, block, low, high):
        cols = (dot(block, down[:, low:high]) * slope[rows, low:high].astype(F32)).astype(BF16)
        inner_b[rows, low:high] = cols
        bias_sum[0:1, low:high] += jnp.sum(cols.astype(F32), axis=0, keepdims=True)

    mlp_loop(side, tokens, rows_of, inner, up, chain, inner_b)


def cross_back_kernel(
    side,
    grad,
    branch,
    hidden,
    rows_d,
    rows_w,
    out_weight,
    query,
    query_b,
    lse,
    slots_q,
    text_kb,
    text_vb,
    weight,
    new_grad,
    out_in,
    text_grad,
    query_grad_b,
    sums,
    width_sums,
    total,
    out_grad,
    query_n,
    slots,
    send_sems,
    recv_sems,
    part,
    came,
    pair,
    peers,
    sems,
):
    greet(True, side.masks)
    side.start()
    chain = Chain(part, total, (came, pair, peers), sems)
    tokens, width = query.shape
    features = grad.shape[1]
    heads = width // HEAD_DIM
    gain = rows_w[GAINS + 2 : GAINS + 3]
    sums[...] = jnp.zeros(sums.shape, F32)
    width_sums[...] = jnp.zeros(width_sums.shape, F32)
    scale_row = 1.0 + row_of(rows_d, MODS + 4)

    def enter(rows, index):
        step = branch[rows].astype(F32)
        back, hat = norm_back(hidden[rows], scale_row, step)
        add_sum(sums, 0, step)
        add_sum(sums, 1, step * hat)
        block = grad[rows] + back
        new_grad[rows] = block
        block = block.astype(BF16)
        out_in[rows] = block
        add_sum(sums, 2, block.astype(F32))
        out_grad[rows] = dot(block, out_weight[1]).astype(BF16)

    loop_rows(tokens, 256, enter)
    side.early_first()
    for head in range(heads):
        cols = head_cols(head)
        query_h, out_grad_h = query_b[:, cols], out_grad[:, cols]
        text_k, text_v = text_kb[:, cols], text_vb[:, cols]
        probs = softmax_back(dot(text_k, query_h, NT), lse[head : head + 1], None)
        prob_grad = dot(text_v, out_grad_h, NT)
        inner = jnp.sum(probs * prob_grad, axis=0, keepdims=True)
        score_b = (probs * (prob_grad - inner) * SCALE).astype(BF16)
        query_n[:, cols] = dot(text_k, score_b, TN).T
        text_grad[0, :, cols] = dot(score_b, query_h)
        text_grad[1, :, cols] = dot(probs.astype(BF16), out_grad_h)
    exchange = Exchange(slots, send_sems, recv_sems)
    exchange.start(stat_rows(query[...] * query_n[...] * gain, 0))
    inverse = inverse_rms(stat_column(slots_q, 0, HEAD_DIM), features)
    exchange.finish()
    term = stat_column(slots, 0, HEAD_DIM) * inverse * inverse * inverse / features
    for head in range(heads):
        cols = head_cols(head)
        width_sums[0:1, cols] = jnp.sum(
            query[:, cols] * query_n[:, cols] * inverse, axis=0, keepdims=True
        )
        block = inverse * gain[:, cols] * query_n[:, cols] - query[:, cols] * term
        block = block.astype(BF16)
        query_grad_b[:, cols] = block
        width_sums[1:2, cols] = jnp.sum(block.astype(F32), axis=0, keepdims=True)
    per_block = 128 // CHUNK

    def leave(rows, index):
        part[rows] = dot(query_grad_b[rows], weight[0], NT).astype(BF16)
        chain.begin(index * per_block, per_block)

    loop_rows(tokens, 128, leave)
    chain.drain(0, side.early_rest, side.late)
    side.finish()


def attend_back_kernel(
    side,
    counts,
    grad,
    branch,
    hidden,
    rows_d,
    tot,
    out_weight,
    query,
    key_value,
    others,
    lse,
    text_grad,
    new_grad,
    out_in,
    sums,
    query_grad,
    key_value_grad,
    text_sum,
    out_grad,
    probs,
    prob_grads,
    away,
    landed,
    text_away,
    text_landed,
    send_sems,
    recv_sems,
):
    greet(False, [1, 2])
    near, far = holders()
    tokens, width = query.shape
    heads = width // HEAD_DIM
    text_rows = text_sum.shape[1]
    sums[...] = jnp.zeros(sums.shape, F32)

    def copy(kind, head):
        return send(
            away.at[kind, head],
            landed.at[kind, head],
            send_sems.at[kind, head],
            recv_sems.at[kind, head],
            dp=far if kind == 1 else near,
        )

    def text_copy(kind):
        return send(
            text_away.at[kind],
            text_landed.at[kind],
            send_sems.at[kind, heads],
            recv_sems.at[kind, heads],
            dp=far if kind == 1 else near,
        )

    place = lax.rem(lax.axis_index("dp"), HOLD)

    def text_part(slot):
        start = pl.multiple_of(flip(place, slot) * text_rows, text_rows)
        return text_grad[:, pl.ds(start, text_rows)]

    text_away[2] = text_part(3).astype(BF16)
    text_copy(2).start()
    text_away[0] = text_part(1).astype(BF16)
    text_copy(0).start()

    def enter(rows, index):
        step = branch[rows].astype(F32)
        back, hat = norm_back(hidden[rows], row_of(rows_d, CROSS_GAIN), step)
        add_sum(sums, 0, step * hat)
        add_sum(sums, 1, step)
        block = grad[rows] + back
        new_grad[rows] = block
        add_sum(sums, 2, block * (tot[rows].astype(F32) + row_of(rows_d, OUT_BIAS)))
        block = (block * row_of(rows_d, MODS + 2)).astype(BF16)
        out_in[rows] = block
        add_sum(sums, 3, block.astype(F32))
        out_grad[rows] = dot(block, out_weight[0]).astype(BF16)

    loop_rows(tokens, 256, enter)
    text_copy(2).wait_recv()
    text_away[1] = (text_part(2) + text_landed[2].astype(F32)).astype(BF16)
    text_copy(1).start()

    for head in range(heads):
        cols = head_cols(head)
        query_h, out_grad_h = query[:, cols], out_grad[:, cols]

        def pair_of(slot, head=head):
            if slot == 0:
                return key_value[head, 0], key_value[head, 1]
            return others[slot - 1, head, 0], others[slot - 1, head, 1]

        inner = jnp.zeros((1, tokens), F32)
        for slot in range(HOLD):
            keys, values = pair_of(slot)
            block = softmax_back(
                dot(keys, query_h, NT),
                lse[head : head + 1],
                below(counts, slot, (tokens, tokens)),
            )
            probs[slot] = block
            block_grad = dot(values, out_grad_h, NT)
            prob_grads[slot] = block_grad
            inner = inner + jnp.sum(block * block_grad, axis=0, keepdims=True)
        query_n = jnp.zeros((HEAD_DIM, tokens), F32)
        for slot in (3, 2, 1, 0):
            keys, values = pair_of(slot)
            block = probs[slot]
            score_b = (block * (prob_grads[slot] - inner) * SCALE).astype(BF16)
            query_n = query_n + dot(keys, score_b, TN)
            key_g = dot(score_b, query_h)
            value_g = dot(block.astype(BF16), out_grad_h)
            if slot == 0:
                key_value_grad[0, :, cols] = key_g
                key_value_grad[1, :, cols] = value_g
            elif slot == 2:
                copy(2, head).wait_recv()
                away[1, head, 0] = (key_g + landed[2, head, 0].astype(F32)).astype(BF16)
                away[1, head, 1] = (value_g + landed[2, head, 1].astype(F32)).astype(BF16)
                copy(1, head).start()
            else:
                away[slot - 1, head, 0] = key_g.astype(BF16)
                away[slot - 1, head, 1] = value_g.astype(BF16)
                copy(slot - 1, head).start()
        query_grad[:, cols] = query_n.T
    text_copy(0).wait_recv()
    text_copy(1).wait_recv()
    text_sum[...] = text_part(0) + text_landed[0].astype(F32) + text_landed[1].astype(F32)
    for head in range(heads):
        cols = head_cols(head)
        copy(0, head).wait_recv()
        copy(1, head).wait_recv()
        for member in range(2):
            key_value_grad[member, :, cols] += landed[0, head, member].astype(F32) + landed[
                1, head, member
            ].astype(F32)
    for kind in range(3):
        text_copy(kind).wait_send()
        for head in range(heads):
            copy(kind, head).wait_send()


def qkv_back_kernel(
    side,
    query_grad,
    key_value_grad,
    text_grad,
    query,
    key,
    text_key,
    slots_in,
    text_slots,
    rows_w,
    cosine,
    sine,
    weight,
    grads_b,
    text_b,
    width_sums,
    total,
    query_n,
    key_n,
    slots,
    send_sems,
    recv_sems,
    part,
    came,
    pair,
    peers,
    sems,
):
    greet(True, side.masks)
    side.start()
    chain = Chain(part, total, (came, pair, peers), sems)
    tokens, width = query.shape
    features = total.shape[1]
    heads = width // HEAD_DIM
    text_rows = text_grad.shape[1]
    place = lax.rem(lax.axis_index("dp"), HOLD)
    mine = pl.ds(pl.multiple_of(place * text_rows, text_rows), text_rows)
    text_k = text_key[mine]
    width_sums[...] = jnp.zeros(width_sums.shape, F32)
    for head in range(heads):
        cols = head_cols(head)
        rows = query_grad[:, cols]
        query_n[:, cols] = rows * cosine[...] - turned(rows * sine[...])
        rows = key_value_grad[0, :, cols]
        key_n[:, cols] = rows * cosine[...] - turned(rows * sine[...])

    def gain(member):
        return rows_w[GAINS + member : GAINS + member + 1]

    exchange = Exchange(slots, send_sems, recv_sems)
    text_terms = stat_rows(text_k * gain(3) * text_grad[0], 2)
    exchange.start(
        stat_rows(query[...] * gain(0) * query_n[...], 0)
        + stat_rows(key[...] * gain(1) * key_n[...], 1)
        + jnp.concatenate([text_terms, jnp.zeros((8, tokens - text_rows), F32)], axis=1)
    )
    query_inv = inverse_rms(stat_column(slots_in, 0, HEAD_DIM), features)
    key_inv = inverse_rms(stat_column(slots_in, 1, HEAD_DIM), features)
    text_inv = inverse_rms(stat_column(text_slots.at[:, :, mine], 0, HEAD_DIM), features)
    side.early_first()
    exchange.finish()

    def cubed(inverse, term):
        return term * inverse * inverse * inverse / features

    query_t = cubed(query_inv, stat_column(slots, 0, HEAD_DIM))
    key_t = cubed(key_inv, stat_column(slots, 1, HEAD_DIM))
    text_t = cubed(text_inv, stat_column(slots.at[:, :, pl.ds(0, text_rows)], 2, HEAD_DIM))

    def back(member, cols, values, inverse, term, grads):
        width_sums[member : member + 1, cols] = jnp.sum(
            values * inverse * grads, axis=0, keepdims=True
        )
        block = inverse * gain(member)[:, cols] * grads - values * term
        block = block.astype(BF16)
        width_sums[4 + member : 5 + member, cols] = jnp.sum(
            block.astype(F32), axis=0, keepdims=True
        )
        return block

    def shifted(cols, member):
        return slice(cols.start + member * width, cols.stop + member * width)

    for head in range(heads):
        cols = head_cols(head)
        grads_b[:, cols] = back(0, cols, query[:, cols], query_inv, query_t, query_n[:, cols])
        grads_b[:, shifted(cols, 1)] = back(
            1, cols, key[:, cols], key_inv, key_t, key_n[:, cols]
        )
        text_b[:, cols] = back(
            3, cols, text_k[:, cols], text_inv, text_t, text_grad[0, :, cols]
        )
    block = key_value_grad[1].astype(BF16)
    grads_b[:, 2 * width :] = block
    width_sums[6:7] = jnp.sum(block.astype(F32), axis=0, keepdims=True)
    block = text_grad[1].astype(BF16)
    text_b[:, width:] = block
    width_sums[8:9] = jnp.sum(block.astype(F32), axis=0, keepdims=True)
    per_block = 128 // CHUNK

    def leave(rows, index):
        part[rows] = (
            dot(grads_b[rows, :width], weight[0], NT)
            + dot(grads_b[rows, width : 2 * width], weight[1], NT)
            + dot(grads_b[rows, 2 * width :], weight[2], NT)
        ).astype(BF16)
        chain.begin(index * per_block, per_block)

    loop_rows(tokens, 128, leave)
    chain.drain(0, side.early_rest, side.late)
    side.finish()


def norm_back_kernel(side, grad, branch, hidden, rows_d, new_grad, sums):
    sums[...] = jnp.zeros(sums.shape, F32)
    scale_row = 1.0 + row_of(rows_d, MODS + 1)

    def enter(rows, index):
        step = branch[rows].astype(F32)
        back, hat = norm_back(hidden[rows], scale_row, step)
        add_sum(sums, 0, step)
        add_sum(sums, 1, step * hat)
        new_grad[rows] = grad[rows] + back

    loop_rows(grad.shape[0], 128, enter)


def scatter_kernel(side):
    greet(False, side.masks)
    side.start()
    side.early()
    side.late()
    side.finish()


def weight_grad(left, right):
    return dot(left, right, TN).astype(BF16)


def per_device(
    latents,
    context,
    time_embed,
    teacher,
    lengths,
    block_order,
    positions,
    self_proj,
    cross_proj,
    out_proj,
    ffn_up,
    ffn_down,
    proj_bias,
    key_bias,
    norm_gains,
    ffn_bias,
    out_bias,
    cross_gain,
    cross_shift,
    modulation,
):
    tokens, features = latents.shape
    width = norm_gains.shape[-1]
    heads = width // HEAD_DIM
    hidden_width = ffn_bias.shape[-1]
    clip_count = time_embed.shape[0]
    text_rows = context.shape[0]
    text_all = text_rows * HOLD
    clip = lax.axis_index("dp") // HOLD
    out_t = jnp.swapaxes(out_proj, 2, 3)
    down_t = jnp.swapaxes(ffn_down, 1, 2)

    rows_d = (tokens, features)
    rows_w = (tokens, width)
    rows_f = (tokens, hidden_width)
    stats = (CHAIN, 8, tokens)
    three = pltpu.SemaphoreType.DMA((CHAIN - 1,))
    chain_scratch = Chain.scratch(tokens, features)
    kv_shape = (heads, 2, tokens, HEAD_DIM)

    pack = (((16, features), F32), ((16, width), F32), ((1, hidden_width), F32))
    results, (self_w,) = run(
        "entry",
        entry_kernel,
        (
            lengths,
            block_order,
            time_embed,
            modulation,
            out_bias,
            cross_gain,
            cross_shift,
            proj_bias,
            key_bias,
            norm_gains,
            ffn_bias,
        ),
        (((HOLD, 8, tokens), F32),) + pack * LAYERS,
        [three, three],
        jobs=[Gather(self_proj, 0)],
        scalars=2,
        micros=25,
    )
    counts = results[0]
    packs = [results[1 + 3 * layer : 4 + 3 * layer] for layer in range(LAYERS)]
    cosine, sine = rope_angles(positions, HEAD_DIM)

    saved = []
    weights = {"self": [self_w], "cross": [], "out": [], "up": [], "down": []}
    sources = {
        "self": self_proj,
        "cross": cross_proj,
        "out": out_t,
        "up": ffn_up,
        "down": down_t,
    }

    def gathers(layer, *names):
        return [Gather(sources[name], layer) for name in names if layer < LAYERS]

    def keep(found, *names):
        for name, item in zip(names, found):
            weights[name].append(item)

    base, tot, before = latents, latents, packs[0][0]
    for layer in range(LAYERS):
        pack_d, pack_w, pack_f = packs[layer]
        names = ("cross", "out") if layer == 0 else ()
        (hidden, a1, sq, sk, q_rot, kv, stat1), found = run(
            "qkv" + str(layer > 0),
            functools.partial(qkv_kernel, layer == 0),
            (base, tot, before, pack_d, pack_w, weights["self"][layer], cosine, sine),
            (
                (rows_d, F32),
                (rows_d, BF16),
                (rows_w, F32),
                (rows_w, F32),
                (rows_w, BF16),
                (kv_shape, BF16),
                (stats, F32),
            ),
            [three, three],
            jobs=gathers(layer, *names),
            micros=15,
        )
        keep(found, *names)
        attended, unused = run(
            "attend" + str(layer > 0),
            functools.partial(attend_kernel, layer == 0),
            (counts, q_rot, kv) + ((context,) if layer == 0 else ()),
            (((HOLD - 1,) + kv_shape, BF16), (rows_w, BF16), ((8, tokens), F32))
            + ((((text_all, features), BF16),) if layer == 0 else ()),
            [
                pltpu.VMEM((heads, HOLD, tokens, tokens), F32),
                pltpu.SemaphoreType.DMA((4 + 2 * heads,)),
                pltpu.SemaphoreType.DMA((4 + 2 * heads,)),
            ],
            micros=30,
        )
        others, o1, lse1 = attended[:3]
        if layer == 0:
            clip_context = attended[3]
        (tot1, ck, ckb, cvb, stat_t), found = run(
            "out_sum",
            out_sum_kernel,
            (o1, weights["out"][layer], clip_context, weights["cross"][layer], pack_w),
            (
                (rows_d, BF16),
                ((text_all, width), F32),
                ((text_all, width), BF16),
                ((text_all, width), BF16),
                ((CHAIN, 8, text_all), F32),
            ),
            [three, three] + chain_scratch,
            jobs=gathers(layer, "up"),
            micros=45,
        )
        keep(found, "up")
        names = ("down",) if layer == LAYERS - 1 else ("down", "self")
        (h1, a3, cq, cqb, o2, lse2, stat2, tot2), found = run(
            "cross",
            cross_kernel,
            (hidden, tot1, pack_d, pack_w, weights["cross"][layer], ckb, cvb)
            + (weights["out"][layer],),
            (
                (rows_d, F32),
                (rows_d, BF16),
                (rows_w, F32),
                (rows_w, BF16),
                (rows_w, BF16),
                ((8, tokens), F32),
                (stats, F32),
                (rows_d, BF16),
            ),
            [three, three] + chain_scratch,
            jobs=gathers(layer, "down") + (gathers(layer + 1, "self")),
            micros=50,
        )
        keep(found, *names)
        (h2, a2, gelu_b, slope, tot3), found = run(
            "ffn",
            ffn_kernel,
            (h1, tot2, pack_d, weights["up"][layer], pack_f, weights["down"][layer]),
            (
                (rows_d, F32),
                (rows_d, BF16),
                (rows_f, BF16),
                (rows_f, BF16),
                (rows_d, BF16),
            ),
            chain_scratch,
            jobs=gathers(layer + 1, "cross", "out"),
            micros=55,
        )
        keep(found, "cross", "out")
        saved.append(
            (hidden, a1, sq, sk, q_rot, kv, stat1, others, o1, lse1, tot1, ck, ckb, cvb, stat_t)
            + (h1, a3, cq, cqb, o2, lse2, stat2, h2, a2, gelu_b, slope, tot3)
        )
        base, tot, before = h2, tot3, pack_d
    output = add_branch(base, tot, before[OUT_BIAS + 2], before[MODS + 5])
    valid = jnp.arange(tokens, dtype=jnp.int32).astype(F32) < counts[0, 0, 0]
    error = jnp.where(valid[:, None], output - teacher.astype(F32), 0.0)
    sse = jnp.sum(error * error)
    grad = error

    pending = []
    reduced = {}

    def scatter_some(names):
        chosen = [item for item in pending if item[0] in names]
        for item in chosen:
            pending.remove(item)
        return [item[0] for item in chosen], [Scatter(item[1]) for item in chosen]

    def keep_sums(names, found):
        for name, item in zip(names, found):
            reduced[name] = item

    sums_d, sums_w, sums_f = [], [], []
    context_part = jnp.zeros(context.shape, F32)
    for layer in reversed(range(LAYERS)):
        (hidden, a1, sq, sk, q_rot, kv, stat1, others, o1, lse1, tot1, ck, ckb, cvb, stat_t) = saved[
            layer
        ][:15]
        (h1, a3, cq, cqb, o2, lse2, stat2, h2, a2, gelu_b, slope, tot3) = saved[layer][15:]
        pack_d, pack_w, pack_f = packs[layer]
        w_self, w_cross, w_out, w_up, w_down = [
            weights[name][layer] for name in ("self", "cross", "out", "up", "down")
        ]
        names, jobs = scatter_some([("self", layer + 1), ("text", layer + 1), ("out0", layer + 1)])
        (dy3, dz, da2, sums3, dz_sum), found = run(
            "ffn_back",
            ffn_back_kernel,
            (grad, tot3, pack_d, w_down, w_up, slope),
            (
                (rows_d, BF16),
                (rows_f, BF16),
                (rows_d, BF16),
                ((8, features), F32),
                ((8, hidden_width), F32),
            ),
            chain_scratch,
            jobs=jobs,
            micros=55,
        )
        keep_sums(names, found)
        pending.append((("up", layer), weight_grad(a2, dz)))
        pending.append((("down", layer), weight_grad(dy3, gelu_b)))
        names, jobs = scatter_some([("up", layer), ("down", layer)])
        (grad, dy2, dct, dcq, sums2, wsums2, da3), found = run(
            "cross_back",
            cross_back_kernel,
            (grad, da2, h2, pack_d, pack_w, w_out, cq, cqb, lse2, stat2, ckb, cvb, w_cross),
            (
                (rows_d, F32),
                (rows_d, BF16),
                ((2, text_all, width), F32),
                (rows_w, BF16),
                ((8, features), F32),
                ((8, width), F32),
                (rows_d, BF16),
            ),
            [
                pltpu.VMEM(rows_w, BF16),
                pltpu.VMEM(rows_w, F32),
                pltpu.VMEM(stats, F32),
                three,
                three,
            ]
            + chain_scratch,
            jobs=jobs,
            micros=60,
        )
        keep_sums(names, found)
        (grad, dy1, sums1, dq_rot, dkv, dtext), unused = run(
            "attend_back",
            attend_back_kernel,
            (counts, grad, da3, h1, pack_d, tot1, w_out, q_rot, kv, others, lse1, dct),
            (
                (rows_d, F32),
                (rows_d, BF16),
                ((8, features), F32),
                (rows_w, F32),
                ((2,) + rows_w, F32),
                ((2, text_rows, width), F32),
            ),
            [
                pltpu.VMEM(rows_w, BF16),
                pltpu.VMEM((HOLD, tokens, tokens), F32),
                pltpu.VMEM((HOLD, tokens, tokens), F32),
                pltpu.VMEM((3,) + kv_shape, BF16),
                pltpu.VMEM((3,) + kv_shape, BF16),
                pltpu.VMEM((3, 2, text_rows, width), BF16),
                pltpu.VMEM((3, 2, text_rows, width), BF16),
                pltpu.SemaphoreType.DMA((3, heads + 1)),
                pltpu.SemaphoreType.DMA((3, heads + 1)),
            ],
            micros=35,
        )
        pending.append((("crossq", layer), weight_grad(a3, dcq)))
        pending.append((("out1", layer), weight_grad(dy2, o2)))
        pending.append((("out0", layer), weight_grad(dy1, o1)))
        names, jobs = scatter_some([("crossq", layer), ("out1", layer)] + [("out0", 0)])
        (ds, dt, wsums1, da1), found = run(
            "qkv_back",
            qkv_back_kernel,
            (dq_rot, dkv, dtext, sq, sk, ck, stat1, stat_t, pack_w, cosine, sine, w_self),
            (
                ((tokens, 3 * width), BF16),
                ((text_rows, 2 * width), BF16),
                ((16, width), F32),
                (rows_d, BF16),
            ),
            [
                pltpu.VMEM(rows_w, F32),
                pltpu.VMEM(rows_w, F32),
                pltpu.VMEM(stats, F32),
                three,
                three,
            ]
            + chain_scratch,
            jobs=jobs,
            micros=50,
        )
        keep_sums(names, found)
        pending.append((("self", layer), weight_grad(a1, ds)))
        pending.append((("text", layer), weight_grad(context, dt)))
        context_part = (
            context_part
            + dot(dt[:, :width], w_cross[1], NT)
            + dot(dt[:, width:], w_cross[2], NT)
        )
        (grad, sums0), unused = run(
            "norm_back",
            norm_back_kernel,
            (grad, da1, hidden, pack_d),
            ((rows_d, F32), ((8, features), F32)),
            remote=False,
            micros=6,
        )
        sums_d = [sums0, sums1, sums2, sums3] + sums_d
        sums_w = [wsums1, wsums2] + sums_w
        sums_f = [dz_sum] + sums_f
    names, jobs = scatter_some([("self", 0), ("text", 0), ("out0", 0)])
    unused, found = run("scatter", scatter_kernel, (), (), jobs=jobs, micros=40)
    keep_sums(names, found)

    sums_d = jnp.stack(sums_d).reshape(LAYERS, 4, 8, features)
    onehot = (jnp.arange(clip_count, dtype=jnp.int32) == clip).astype(F32)
    mod_sums = jnp.stack(
        [
            sums_d[:, 0, 0],
            sums_d[:, 0, 1],
            sums_d[:, 1, 2],
            sums_d[:, 2, 0],
            sums_d[:, 2, 1],
            sums_d[:, 3, 0],
        ],
        axis=1,
    )
    time_sums = onehot[:, None, None] * jnp.sum(mod_sums, axis=0)[None]
    packed_d = jnp.concatenate(
        [
            mod_sums.reshape(-1, features),
            time_sums.reshape(-1, features),
            jnp.stack([sums_d[:, 1, 3], sums_d[:, 2, 2], sums_d[:, 3, 1]], axis=1).reshape(
                -1, features
            ),
            sums_d[:, 1, 0],
            sums_d[:, 1, 1],
            jnp.full((1, features), sse / features, F32),
        ]
    )
    packed_w = jnp.concatenate(sums_w)
    packed_f = jnp.concatenate([item[0:1] for item in sums_f])
    packed_d, packed_w, packed_f = lax.psum(
        (packed_d.astype(BF16), packed_w.astype(BF16), packed_f.astype(BF16)), "dp"
    )
    packed_d, packed_w, packed_f = (
        packed_d.astype(F32),
        packed_w.astype(F32).reshape(LAYERS, 24, width),
        packed_f.astype(F32),
    )
    context_grad = lax.psum(context_part.astype(BF16), "tensor").astype(F32)
    low = 6 * LAYERS
    modulation_grad = packed_d[:low].reshape(LAYERS, 6, features)
    time_grad = packed_d[low : low + 6 * clip_count].reshape(clip_count, 6, features)
    low += 6 * clip_count
    out_bias_grad = packed_d[low : low + 3 * LAYERS].reshape(LAYERS, 3, features)
    low += 3 * LAYERS
    cross_gain_grad = packed_d[low : low + LAYERS]
    cross_shift_grad = packed_d[low + LAYERS : low + 2 * LAYERS]
    loss = jnp.sum(packed_d[low + 2 * LAYERS]) / (jnp.sum(lengths).astype(F32) * features)
    proj_bias_grad = jnp.stack([packed_w[:, row] for row in (4, 6, 17, 7, 8)], axis=1)
    gains_grad = jnp.stack([packed_w[:, row] for row in (0, 1, 16, 3)], axis=1)

    def split(block):
        return jnp.swapaxes(block.reshape(block.shape[0], -1, width), 0, 1)

    self_grad = jnp.stack([split(reduced["self", layer]) for layer in range(LAYERS)])
    cross_grad = jnp.stack(
        [
            jnp.concatenate([reduced["crossq", layer][None], split(reduced["text", layer])])
            for layer in range(LAYERS)
        ]
    )
    out_grad = jnp.stack(
        [
            jnp.stack([reduced["out0", layer].T, reduced["out1", layer].T])
            for layer in range(LAYERS)
        ]
    )
    up_grad = jnp.stack([reduced["up", layer] for layer in range(LAYERS)])
    down_grad = jnp.stack([reduced["down", layer].T for layer in range(LAYERS)])
    return (
        output,
        loss,
        grad,
        context_grad,
        time_grad,
        self_grad,
        cross_grad,
        out_grad,
        up_grad,
        down_grad,
        proj_bias_grad,
        packed_w[:, 5],
        gains_grad,
        packed_f,
        out_bias_grad,
        cross_gain_grad,
        cross_shift_grad,
        modulation_grad,
    )


def solution(mesh):
    COLLECTIVES.clear()
    rows = P("dp", None)
    col_in = P(None, None, "dp", "tensor")
    col_out = P(None, None, "tensor", "dp")
    up, down = P(None, "dp", "tensor"), P(None, "tensor", "dp")
    vec, mat = P(None, "tensor"), P(None, None, "tensor")
    return jax.shard_map(
        per_device,
        mesh=mesh,
        in_specs=(rows, rows, P(), rows, P(), P("dp"), P(None, "dp"))
        + (col_in, col_in, col_out, up, down)
        + (mat, vec, mat, vec, P(), P(), P(), P()),
        out_specs=(rows, P(), rows, rows, P())
        + (col_in, col_in, col_out, up, down)
        + (mat, vec, mat, vec, P(), P(), P(), P()),
        check_vma=False,
    )
```

```python
import functools
import math

import jax
import jax.numpy as jnp
import numpy as np
from jax import lax
from jax.experimental import pallas as pl
from jax.experimental.pallas import tpu as pltpu
from jax.sharding import PartitionSpec as P

BIAS = "bias"
BRANCH = "branch"
CONTEXT = "context"
COSINE = "cosine"
CROSS = "cross"
DOWN = "down"
DP = "dp"
GAIN = "gain"
GELU_B_NAME = "gelu_b"
GRAD = "grad"
HIDDEN = "hidden"
HIDDEN_F = "hidden_f"
KEY = "key"
KEY_VALUE = "key_value"
LOSS = "loss"
MATRIX_GRAD = "matrix_grad"
NEW_GRAD = "new_grad"
NORMAL = "normal"
NORMAL_F = "normal_f"
OTHERS = "others"
OUT = "out"
OUT0 = "out0"
OUTPUT = "output"
QUERY = "query"
QUERY_B = "query_b"
QUERY_GRAD = "query_grad"
QUERY_ROT = "query_rot"
RESULT = "result"
SELF = "self"
SELF_GRAD = "self_grad"
SHIFT = "shift"
SINE = "sine"
SLOPE = "slope"
TENSOR = "tensor"
TEXT = "text"
TEXT_GRAD = "text_grad"
TEXT_KB = "text_kb"
TEXT_MATRIX = "text_matrix"
TEXT_VB = "text_vb"
TEXT_WEIGHT = "text_weight"
UP = "up"
WEIGHT = "weight"
MESH = pl.DeviceIdType.MESH
F32, BF16 = jnp.float32, jnp.bfloat16
NN = (((1,), (0,)), ((), ()))
NT = (((1,), (1,)), ((), ()))
TN = (((0,), (0,)), ((), ()))
HEAD_DIM = 128
HOLD = 4
LAYERS = 2
CHAIN = 4
CHUNK = 32
EPS = 1e-06
LOG2E = math.log2(math.e)
SCALE = 1.0 / math.sqrt(HEAD_DIM)
VMEM_BYTES = 60 * 2**20


def dot(left, right, dims=NN, exact=False):
    precision = lax.Precision.HIGHEST if exact else None
    return lax.dot_general(left, right, dims, precision=precision, preferred_element_type=F32)


def rope_table(head_size):
    third = head_size // 6
    spans = [head_size - 4 * third, 2 * third, 2 * third]
    table = np.zeros((3, head_size), np.float32)
    start_col = 0
    for component in range(3):
        for pair_index in range(spans[component] // 2):
            freq_value = 10000.0 ** (-(2.0 * pair_index) / spans[component])
            table[component, start_col + 2 * pair_index] = freq_value
            table[component, start_col + 2 * pair_index + 1] = freq_value
        start_col += spans[component]
    return table


def signal(**device):
    pl.semaphore_signal(
        pltpu.get_barrier_semaphore(), inc=1, device_id=device, device_id_type=MESH
    )


def bits_of_dp():
    return max(lax.axis_size(DP).bit_length() - 1, 1)


def flip(index, mask):
    result, bit = index, 0
    while mask >> bit:
        if mask >> bit & 1:
            half = 1 << bit
            result = result + half - 2 * half * lax.rem(index // half, 2)
        bit += 1
    return result


def greet(tensor, masks):
    place, me = lax.axis_index(TENSOR), lax.axis_index(DP)
    if tensor:
        for step in range(1, CHAIN):
            signal(tensor=lax.rem(place + step, CHAIN))
    for mask in masks:
        signal(dp=flip(me, mask))
    pl.semaphore_wait(
        pltpu.get_barrier_semaphore(), (CHAIN - 1 if tensor else 0) + len(masks)
    )


def holders():
    me = lax.axis_index(DP)
    return flip(me, 1), flip(me, 2)


def send(src, dst, send_sem, recv_sem, **device):
    return pltpu.make_async_remote_copy(
        src_ref=src,
        dst_ref=dst,
        send_sem=send_sem,
        recv_sem=recv_sem,
        device_id=device,
        device_id_type=MESH,
    )


def masks_over(bits):
    masks = [0]
    for bit in bits:
        masks += [mask | 1 << bit for mask in masks]
    return masks


def halves_of(size):
    cut = (size // 2 + 15) // 16 * 16
    return ((0, cut), (cut, size - cut))


def half_orders(bits):
    rising = list(range(1, bits))
    return (rising, rising[::-1])


class Job:
    phase = 0
    wave = 0
    name = None
    ended = False
    midway = False

    def middle(self):
        pass

    def move(self, target):
        while self.phase < min(target, self.bits - 1):
            self.phase += 1
            self.advance(self.phase)


class Gather(Job):
    def __init__(self, source, layer, name=None, wave=0, held=False):
        self.layer, self.name, self.wave, self.is_held = layer, name, wave, held
        self.operands = [source]
        shape = source.shape[1:]
        self.lead = shape[:-2]
        self.size = shape[-2]
        devices = lax.axis_size(DP)
        self.outs = [(self.lead + (self.size * devices, shape[-1]), source.dtype)]
        self.spaces = [pl.ANY]
        self.bits = bits_of_dp()
        plan = []
        for half, order in enumerate(half_orders(self.bits)):
            for phase, bit in enumerate(order):
                for mask in masks_over(order[:phase]):
                    plan.append((phase, half, bit, mask))
        for mask in masks_over(range(1, self.bits)):
            plan.append((self.bits - 1, None, 0, mask))
        self.plan = plan
        count = len(plan)
        self.scratch = [
            pltpu.SemaphoreType.DMA((count,)),
            pltpu.SemaphoreType.DMA((count,)),
            pltpu.SemaphoreType.DMA,
        ]
        if held:
            self.scratch += [
                pltpu.VMEM(self.outs[0][0], source.dtype),
                pltpu.SemaphoreType.DMA,
            ]

    def key(self):
        return ("gather", self.layer, self.outs[0][0], self.wave, self.is_held)

    def bind(self, sources, outs, scratch):
        self.source = sources[0].at[self.layer]
        self.out = outs[0]
        self.send_sems, self.recv_sems, self.own_sem = scratch[:3]
        self.store = None
        if self.is_held:
            held, sem = scratch[3:]
            self.store = pltpu.make_async_copy(held, self.out, sem)
            self.out = held

    def block(self, ref, index, half):
        low, size = (0, self.size) if half is None else halves_of(self.size)[half]
        start = low if index is None else index * self.size + low
        rows = pl.ds(pl.multiple_of(start, 16), size)
        return ref.at[:, rows] if self.lead else ref.at[rows]

    def copies(self, phase, own=None, only=None):
        me = lax.axis_index(DP)
        for number, (step, half, bit, mask) in enumerate(self.plan):
            if only is not None and mask not in only:
                continue
            if step == phase and own in (None, mask == 0):
                index = flip(me, mask)
                source = (
                    self.block(self.source, None, half)
                    if mask == 0
                    else self.block(self.out, index, half)
                )
                yield send(
                    source,
                    self.block(self.out, index, half),
                    self.send_sems.at[number],
                    self.recv_sems.at[number],
                    dp=flip(me, 1 << bit),
                )

    def own_copy(self):
        me = lax.axis_index(DP)
        return pltpu.make_async_copy(
            self.source, self.block(self.out, me, None), self.own_sem
        )

    def start(self):
        for phase in range(self.bits):
            for copy in self.copies(phase, True):
                copy.start()
        self.own_copy().start()

    def middle(self):
        if self.bits == 3 and not self.midway:
            self.midway = True
            for copy in self.copies(1, True):
                copy.wait_recv()
            for copy in self.copies(2, only=(2, 4)):
                copy.start()

    def advance(self, phase):
        if phase == self.bits - 1 == 2:
            self.middle()
            for copy in self.copies(1, False):
                copy.wait_recv()
            for copy in self.copies(2, only=(6,)):
                copy.start()
            return
        for copy in self.copies(phase - 1):
            copy.wait_recv()
        for copy in self.copies(phase, False):
            copy.start()

    def finish(self):
        for copy in self.copies(self.bits - 1):
            copy.wait_recv()
        for phase in range(self.bits):
            for copy in self.copies(phase):
                copy.wait_send()
        self.own_copy().wait()
        if self.store is not None:
            self.store.start()


class Scatter(Job):
    def __init__(self, source=None, name=None, shape=None):
        self.name = name
        self.operands = [] if source is None else [source]
        shape = source.shape if shape is None else shape
        self.bits = bits_of_dp()
        self.size = shape[0] // lax.axis_size(DP)
        self.width = shape[1]
        self.outs = [((self.size, self.width), F32)]
        self.spaces = [pltpu.VMEM]
        self.slots = 1 << self.bits - 1
        orders = [order[::-1] for order in half_orders(self.bits)]
        plan = [(0, None, 0, mask, mask >> 1) for mask in masks_over(range(1, self.bits))]
        for half, order in enumerate(orders):
            for phase, bit in enumerate(order):
                kept = masks_over(order[phase + 1 :])
                for place, mask in enumerate(kept):
                    plan.append((phase + 1, half, bit, mask, place))
        self.plan = plan
        count = len(plan)
        buffers = [pltpu.VMEM((self.slots, self.size, self.width), BF16)]
        buffers += buffers * len(self.operands)
        for phase in range(1, self.bits):
            places = 1 << self.bits - 1 - phase
            buffers += [
                pltpu.VMEM((places, size, self.width), BF16)
                for _, size in halves_of(self.size)
            ]
        self.scratch = buffers + [
            pltpu.SemaphoreType.DMA((count,)),
            pltpu.SemaphoreType.DMA((count,)),
            pltpu.SemaphoreType.DMA((self.slots,)),
        ]

    def key(self):
        return ("scatter", self.width, len(self.operands))

    def bind(self, sources, outs, scratch):
        self.out = outs[0]
        self.landed, self.own = scratch[0], None
        scratch = scratch[1:]
        if sources:
            self.source, self.own = sources[0], scratch[0]
            scratch = scratch[1:]
        self.parts = scratch[:-3]
        self.send_sems, self.recv_sems, self.own_sems = scratch[-3:]

    def rows(self, index):
        return pl.ds(pl.multiple_of(index * self.size, 16), self.size)

    def held(self, mask, low, size):
        if self.own is not None:
            return self.own.at[mask >> 1, pl.ds(pl.multiple_of(low, 16), size)]
        start = flip(lax.axis_index(DP), mask) * self.size + low
        return self.source.at[pl.ds(pl.multiple_of(start, 16), size)]

    def copies(self, phase):
        me = lax.axis_index(DP)
        for number, (step, half, bit, mask, place) in enumerate(self.plan):
            if step != phase:
                continue
            if phase == 0:
                source = self.source.at[self.rows(flip(me, mask | 1))]
                target = self.landed.at[mask >> 1]
            else:
                low, size = halves_of(self.size)[half]
                source = self.held(mask | 1 << bit, low, size)
                target = self.parts[2 * (phase - 1) + half].at[place]
            yield send(
                source,
                target,
                self.send_sems.at[number],
                self.recv_sems.at[number],
                dp=flip(me, 1 << bit),
            )

    def own_copies(self):
        me = lax.axis_index(DP)
        if self.own is not None:
            for slot in range(self.slots):
                yield pltpu.make_async_copy(
                    self.source.at[self.rows(flip(me, slot << 1))],
                    self.own.at[slot],
                    self.own_sems.at[slot],
                )

    def start(self):
        for copy in self.copies(0):
            copy.start()
        for copy in self.own_copies():
            copy.start()

    def add(self, phase):
        for copy in self.copies(phase):
            copy.wait_recv()
        if phase == 0:
            for copy in self.own_copies():
                copy.wait()
            for slot in range(self.slots):

                def step(rows, index, slot=slot):
                    held = self.held(slot << 1, index * 16, 16)
                    held[...] = held[...] + self.landed[slot, rows]

                loop_rows(self.size, 16, step)
            return
        for number, (step, half, bit, mask, place) in enumerate(self.plan):
            if step == phase:
                low, size = halves_of(self.size)[half]
                part = self.parts[2 * (phase - 1) + half]

                def step(rows, index, mask=mask, place=place, low=low, part=part):
                    held = self.held(mask, low + index * 16, 16)
                    if phase == self.bits - 1:
                        target = pl.ds(pl.multiple_of(low + index * 16, 16), 16)
                        self.out[target] = held[...].astype(F32) + part[place, rows].astype(F32)
                    else:
                        held[...] = held[...] + part[place, rows]

                loop_rows(size, 16, step)

    def advance(self, phase):
        self.add(phase - 1)
        for copy in self.copies(phase):
            copy.start()

    def finish(self):
        self.add(self.bits - 1)
        for phase in range(self.bits):
            for copy in self.copies(phase):
                copy.wait_send()


class Late:
    def __init__(self, name, value, low=None, high=None):
        self.name, self.value, self.low, self.high = name, value, low, high
        shape = value.shape
        if high is not None:
            shape = (high - low,) + shape[1:]
        elif low is not None:
            shape = shape[1:]
        self.scratch = [pltpu.VMEM(shape, value.dtype), pltpu.SemaphoreType.DMA]

    def source(self, ref):
        if self.high is not None:
            return ref.at[self.low : self.high]
        return ref if self.low is None else ref.at[self.low]


class Early:
    def __init__(self, name, shape, kind, over=None):
        self.name, self.shape, self.kind, self.over = name, shape, kind, over
        self.scratch = [pltpu.SemaphoreType.DMA]
        if over is None:
            self.scratch = [pltpu.VMEM(shape, kind)] + self.scratch


class Side:
    def __init__(self, jobs):
        self.jobs = jobs
        self.masks = [1 << bit for bit in range(bits_of_dp())] if jobs else []
        self.loads, self.stores, self.open = {}, {}, []
        self.first_loads = []

    def need(self, *names):
        for name in names:
            self.loads[name].wait()

    def store(self, *names):
        for name in names:
            self.stores[name].start()
            self.open.append(name)

    def start(self, wave=0):
        for job in self.jobs:
            if job.operands and job.wave == wave:
                job.start()
        while self.first_loads:
            self.first_loads.pop(0).wait()

    def launch(self, name, source):
        for job in self.jobs:
            if job.name == name:
                job.source = source
                job.start()

    def move(self, target, *names):
        for job in self.jobs:
            if not names or job.name in names:
                job.move(target)

    def early(self):
        self.move(bits_of_dp() - 2)

    def late(self):
        self.move(bits_of_dp() - 1)

    def middle(self):
        self.early()
        for job in self.jobs:
            job.middle()

    def finish(self, *names):
        for job in self.jobs:
            if not job.ended and (not names or job.name in names):
                job.move(job.bits - 1)
                job.finish()
                job.ended = True

    def close(self):
        for name in self.stores:
            if name not in self.open:
                self.store(name)
        for copy in self.stores.values():
            copy.wait()
        for job in self.jobs:
            if isinstance(job, Gather) and job.store is not None:
                job.store.wait()


class Exchange:
    def __init__(self, slots, send_sems, recv_sems):
        self.slots = slots
        place = lax.axis_index(TENSOR)
        self.place = place
        self.copies = [
            send(
                slots.at[place],
                slots.at[place],
                send_sems.at[step - 1],
                recv_sems.at[step - 1],
                tensor=lax.rem(place + step, CHAIN),
            )
            for step in range(1, CHAIN)
        ]

    def start(self, rows):
        self.slots[self.place] = rows
        for copy in self.copies:
            copy.start()

    def finish(self):
        for copy in self.copies:
            copy.wait()


def stat_rows(squares, row):
    count, width = squares.shape
    ones = jnp.ones((8, width), F32)
    sums = dot(ones, squares, NT, exact=True)
    index = lax.broadcasted_iota(jnp.int32, sums.shape, 0)
    return jnp.where(index == row, sums, 0.0)


def stat_column(slots, row, lanes):
    gathered = jnp.concatenate([slots[place] for place in range(CHAIN)], axis=0)
    index = lax.broadcasted_iota(jnp.int32, (8 * CHAIN, lanes), 0)
    pick = jnp.where(lax.rem(index, 8) == row, 1.0, 0.0)
    return dot(gathered, pick, TN, exact=True)


class Chain:
    def __init__(self, part, total, buffers, sems):
        self.part, self.total = part, total
        self.came, self.pair, self.peers = buffers
        self.sems = sems
        place = lax.axis_index(TENSOR)
        self.is_end = (place == 0) | (place == 3)
        self.is_mid = jnp.logical_not(self.is_end)
        self.inner = jnp.where(place == 0, 1, 2)
        self.outer = jnp.where(place == 1, 0, 3)
        self.peer = 3 - place
        self.chunks = part.shape[0] // CHUNK
        self.closed = False

    @staticmethod
    def scratch(rows, width):
        chunks = rows // CHUNK
        return [pltpu.VMEM((rows, width), BF16)] * 4 + [pltpu.SemaphoreType.DMA((6, chunks))]

    def rows(self, k):
        return pl.ds(pl.multiple_of(k * CHUNK, CHUNK), CHUNK)

    def copy(self, src, dst, kind, k, device):
        return send(
            src.at[self.rows(k)],
            dst.at[self.rows(k)],
            self.sems.at[2 * kind, k],
            self.sems.at[2 * kind + 1, k],
            tensor=device,
        )

    def inward(self, k, device):
        return self.copy(self.part, self.came, 0, k, device)

    def across(self, k):
        return self.copy(self.pair, self.peers, 1, k, self.peer)

    def outward(self, k, device):
        return self.copy(self.total, self.total, 2, k, device)

    def begin(self, low, count):
        @pl.when(self.is_end)
        def _():
            def step(k, carry):
                self.inward(low + k, self.inner).start()
                return carry

            lax.fori_loop(0, count, step, 0)

    def first(self, k):
        self.inward(k, self.outer).wait_recv()
        rows = self.rows(k)
        self.pair[rows] = (self.part[rows].astype(F32) + self.came[rows].astype(F32)).astype(BF16)
        self.across(k).start()

    def second(self, k):
        self.across(k).wait_recv()
        rows = self.rows(k)
        self.total[rows] = (self.pair[rows].astype(F32) + self.peers[rows].astype(F32)).astype(
            BF16
        )
        self.outward(k, self.outer).start()

    def serve(self, k):
        @pl.when(self.is_mid)
        def _():
            self.first(k)

            @pl.when(k > 0)
            def _():
                self.second(jnp.maximum(k - 1, 0))

    def segment(self, low, high, closed, upto):
        @pl.when(self.is_mid)
        def _():
            def both(k, carry):
                self.first(k)

                @pl.when(k > 0)
                def _():
                    self.second(jnp.maximum(k - 1, 0))

                return carry

            lax.fori_loop(low, high, both, 0)
            if high == self.chunks and not self.closed:
                self.second(self.chunks - 1)

        self.closed = self.closed or high == self.chunks

        @pl.when(self.is_end)
        def _():
            def close(k, carry):
                self.inward(k, self.inner).wait_send()
                self.outward(k, self.inner).wait_recv()
                return carry

            lax.fori_loop(closed, upto, close, 0)

    def drain(self, low, early=None, late=None):
        done, last = 0, self.chunks
        if early is not None:
            cut = low + (last - low) // 4
            self.segment(low, cut, done, cut - 1)
            low, done = cut, cut - 1
            early()
        if late is not None:
            cut = low + (last - low) * 5 // 8
            self.segment(low, cut, done, cut - 1)
            low, done = cut, cut - 1
            late()
        self.segment(low, last, done, last)
        self.close()

    def close(self):
        @pl.when(self.is_mid)
        def _():
            def close(k, carry):
                self.across(k).wait_send()
                self.outward(k, self.outer).wait_send()
                return carry

            lax.fori_loop(0, self.chunks, close, 0)


COLLECTIVES = {}


def collective_of(key):
    return COLLECTIVES.setdefault(key, 1 + len(COLLECTIVES))


def run(name, kernel, ins, outs, scratch=(), remote=True, jobs=(), scalars=0, micros=0):
    whole = pl.BlockSpec(memory_space=pltpu.VMEM)
    far = pl.BlockSpec(memory_space=pl.ANY)
    if remote:
        ins = tuple(ins[:scalars]) + tuple(
            item if isinstance(item, Late) else Late(None, item) for item in ins[scalars:]
        )
        outs = tuple(
            item if isinstance(item, Early) or len(item) > 2 else Early(place, *item)
            for place, item in enumerate(outs)
        )
    job_ins = [item for job in jobs for item in job.operands]
    job_outs = [item for job in jobs for item in job.outs]
    job_spaces = [pl.BlockSpec(memory_space=space) for job in jobs for space in job.spaces]
    moved = [item for item in tuple(ins) + tuple(outs) if isinstance(item, (Late, Early))]
    own_scratch = list(scratch) + [item for job in jobs for item in job.scratch]

    def body(*refs):
        side = Side(jobs)
        refs = list(refs)

        def take(count):
            taken = refs[:count]
            del refs[:count]
            return taken

        own_in, side_in = take(len(ins)), take(len(job_ins))
        own_out, side_out = take(len(outs)), take(len(job_outs))
        own = take(len(scratch))
        for job in jobs:
            job.phase, job.ended, job.midway = 0, False, False
            job.bind(
                [side_in.pop(0) for _ in job.operands],
                [side_out.pop(0) for _ in job.outs],
                take(len(job.scratch)),
            )
        for place, item in enumerate(ins):
            if isinstance(item, Late):
                held, sem = take(2)
                copy = pltpu.make_async_copy(item.source(own_in[place]), held, sem)
                copy.start()
                if item.name is None:
                    side.first_loads.append(copy)
                side.loads[item.name] = copy
                own_in[place] = held
        for place, item in enumerate(outs):
            if isinstance(item, Early):
                held = take(1)[0] if item.over is None else own_in[item.over]
                sem = take(1)[0]
                side.stores[item.name] = pltpu.make_async_copy(held, own_out[place], sem)
                own_out[place] = held
        kernel(side, *own_in, *own_out, *own)
        side.close()

    key = (name,) + tuple(job.key() for job in jobs)
    shapes = [
        (item.shape, item.kind) if isinstance(item, Early) else item[:2] for item in outs
    ] + job_outs
    results = pl.pallas_call(
        body,
        out_shape=tuple(jax.ShapeDtypeStruct(shape, kind) for shape, kind in shapes),
        in_specs=[pl.BlockSpec(memory_space=pltpu.SMEM)] * scalars
        + [far if isinstance(item, Late) else whole for item in ins[scalars:]]
        + [far] * len(job_ins),
        out_specs=tuple(
            [far if isinstance(item, Early) or len(item) > 2 else whole for item in outs]
            + job_spaces
        ),
        scratch_shapes=own_scratch + [part for item in moved for part in item.scratch],
        cost_estimate=pl.CostEstimate(
            flops=0, bytes_accessed=micros * 3000000, transcendentals=0
        ),
        compiler_params=pltpu.CompilerParams(
            collective_id=collective_of(key) if remote else None,
            has_side_effects=remote,
            vmem_limit_bytes=VMEM_BYTES,
        ),
    )(*[item.value if isinstance(item, Late) else item for item in ins], *job_ins)
    return results[: len(outs)], results[len(outs) :]


def tiled_grad(left, right, store, serve, size=384):
    for tile in range(left.shape[1] // size):
        cols = slice(tile * size, (tile + 1) * size)
        store(tile, size, dot(left[:, cols], right[...], TN).astype(BF16))
        serve(tile)


def normed(hidden):
    center = hidden - jnp.mean(hidden, axis=-1, keepdims=True)
    inverse = lax.rsqrt(jnp.mean(center * center, axis=-1, keepdims=True) + EPS)
    return center * inverse, inverse


def norm_back(hidden, scale_row, grad):
    hat, inverse = normed(hidden)
    inner = grad * scale_row
    back = inverse * (
        inner
        - jnp.mean(inner, axis=-1, keepdims=True)
        - hat * jnp.mean(inner * hat, axis=-1, keepdims=True)
    )
    return back, hat


def loop_rows(total, size, body):
    def step(index, carry):
        body(pl.ds(pl.multiple_of(index * size, size), size), index)
        return carry

    lax.fori_loop(0, total // size, step, 0)


def add_sum(ref, row, block):
    ref[row : row + 1] += jnp.sum(block, axis=0, keepdims=True)


def turned(rows):
    lane = lax.broadcasted_iota(jnp.int32, rows.shape, 1)
    width = rows.shape[1]
    return jnp.where(
        lax.rem(lane, 2) == 0, -pltpu.roll(rows, width - 1, 1), pltpu.roll(rows, 1, 1)
    )


def head_cols(head):
    return slice(head * HEAD_DIM, (head + 1) * HEAD_DIM)


def inverse_rms(sums, features):
    return lax.rsqrt(sums / features + EPS)


MODS, OUT_BIAS, CROSS_GAIN, CROSS_SHIFT = 0, 6, 9, 10
KEY_BIAS, GAINS = 5, 6


def row_of(ref, index):
    return ref[index : index + 1]


def entry_kernel(
    side,
    lengths,
    block_order,
    time_embed,
    modulation,
    out_bias,
    cross_gain,
    cross_shift,
    proj_bias,
    key_bias,
    norm_gains,
    ffn_bias,
    positions,
    table,
    counts,
    cosine,
    sine,
    *rest,
):
    packs, (send_sems, recv_sems) = rest[:-2], rest[-2:]
    greet(False, side.masks)
    near, far = holders()
    tokens = counts.shape[2]
    clip = lax.axis_index(DP) // HOLD
    mine = (lengths[clip] - block_order[0] * tokens).astype(F32)
    counts[0] = jnp.full(counts.shape[1:], mine, F32)

    def copy(number, source, target, device):
        return send(
            counts.at[source],
            counts.at[target],
            send_sems.at[number],
            recv_sems.at[number],
            dp=device,
        )

    to_near, to_far, onward = copy(0, 0, 1, near), copy(1, 0, 2, far), copy(2, 2, 3, near)
    side.start()
    to_near.start()
    to_far.start()
    for layer in range(LAYERS):
        rows_d, rows_w, rows_f = packs[3 * layer : 3 * layer + 3]
        rows_d[...] = jnp.zeros(rows_d.shape, F32)
        rows_w[...] = jnp.zeros(rows_w.shape, F32)
        for row in range(6):
            embed = jnp.zeros((1, rows_d.shape[1]), F32)
            for index in range(time_embed.shape[1]):
                embed = embed + jnp.where(clip == index, row_of(time_embed.at[row], index), 0.0)
            rows_d[row : row + 1] = row_of(modulation.at[row], layer) + embed
        for row in range(3):
            rows_d[OUT_BIAS + row : OUT_BIAS + row + 1] = row_of(out_bias.at[row], layer)
        rows_d[CROSS_GAIN : CROSS_GAIN + 1] = row_of(cross_gain, layer)
        rows_d[CROSS_SHIFT : CROSS_SHIFT + 1] = row_of(cross_shift, layer)
        for row in range(5):
            rows_w[row : row + 1] = row_of(proj_bias.at[row], layer)
        rows_w[KEY_BIAS : KEY_BIAS + 1] = row_of(key_bias, layer)
        rows_w[GAINS : GAINS + 4] = norm_gains[layer]
        rows_f[...] = row_of(ffn_bias, layer)
    angles = dot(positions[...].astype(F32), table[...], TN, exact=True)
    cosine[...] = jnp.cos(angles)
    sine[...] = jnp.sin(angles)
    to_far.wait_recv()
    onward.start()
    side.early()
    side.late()
    to_near.wait_recv()
    onward.wait_recv()
    for copy in (to_near, to_far, onward):
        copy.wait_send()
    side.finish()


def add_branch(base, tot, bias_row, gate_row):
    return base + (tot.astype(F32) + bias_row) * gate_row


def attend_kernel(
    first,
    side,
    base,
    tot,
    rows_before,
    rows_d,
    rows_w,
    weight,
    cosine,
    sine,
    counts,
    *refs,
):
    refs = list(refs)
    context = refs.pop(0) if first else None
    hidden, normal, query, key, query_rot, key_value, slots = refs[:7]
    others, result, lse = refs[7:10]
    clip_context = refs[10] if first else None
    scores, send_sems, recv_sems, hold_sends, hold_recvs = refs[-5:]
    greet(True, side.masks or [1, 2])
    side.start()
    tokens, width = query.shape
    features = hidden.shape[1]
    heads = width // HEAD_DIM
    scale_row = 1.0 + row_of(rows_d, MODS + 1)
    shift_row = row_of(rows_d, MODS)

    def project(rows, index):
        if first:
            block = base[rows].astype(F32)
        else:
            block = add_branch(
                base[rows], tot[rows], row_of(rows_before, OUT_BIAS + 2), row_of(rows_before, MODS + 5)
            )
        hidden[rows] = block
        block = (normed(block)[0] * scale_row + shift_row).astype(BF16)
        normal[rows] = block
        query[rows] = dot(block, weight[0]) + row_of(rows_w, 0)
        key[rows] = dot(block, weight[1]) + row_of(rows_w, KEY_BIAS)
        value = (dot(block, weight[2]) + row_of(rows_w, 1)).astype(BF16)
        for head in range(heads):
            key_value[head, 1, rows] = value[:, head_cols(head)]

    side.need(WEIGHT)
    loop_rows(tokens, 256, project)
    side.store(HIDDEN, NORMAL, QUERY, KEY)
    exchange = Exchange(slots, send_sems, recv_sems)
    exchange.start(
        stat_rows(query[...] * query[...], 0) + stat_rows(key[...] * key[...], 1)
    )
    side.early()
    near, far = holders()

    def copy(source, target, number, device):
        return send(source, target, hold_sends.at[number], hold_recvs.at[number], dp=device)

    to_near = copy(key_value, others.at[0], 0, near)
    to_far = [
        copy(key_value.at[head], others.at[1, head], 1 + head, far) for head in range(heads)
    ]
    onward = [
        copy(others.at[1, head], others.at[2, head], 1 + heads + head, near)
        for head in range(heads)
    ]
    exchange.finish()
    query_inv = inverse_rms(stat_column(slots, 0, HEAD_DIM), features)
    key_inv = inverse_rms(stat_column(slots, 1, HEAD_DIM), features)
    side.need(COSINE, SINE)
    for head in range(heads):
        cols = head_cols(head)
        rows = key[:, cols] * key_inv * rows_w[GAINS + 1 : GAINS + 2, cols]
        key_value[head, 0] = (rows * cosine[...] + turned(rows) * sine[...]).astype(BF16)
        to_far[head].start()
    to_near.start()
    text = []
    if first:
        place = lax.rem(lax.axis_index(DP), HOLD)
        size = context.shape[0]

        def block(index):
            return clip_context.at[pl.ds(pl.multiple_of(index * size, 16), size)]

        low = 1 + 2 * heads
        clip_context[pl.ds(pl.multiple_of(place * size, 16), size)] = context[...]
        text = [
            copy(block(place), block(place), low, near),
            copy(block(place), block(place), low + 1, far),
            copy(block(flip(place, 2)), block(flip(place, 2)), low + 2, near),
        ]
        text[0].start()
        text[1].start()
    for head in range(heads):
        cols = head_cols(head)
        rows = query[:, cols] * query_inv * rows_w[GAINS : GAINS + 1, cols]
        query_rot[:, cols] = (rows * cosine[...] + turned(rows) * sine[...]).astype(BF16)
    side.store(QUERY_ROT)
    side.middle()

    def score(head, slot, keys):
        block = dot(keys, query_rot[:, head_cols(head)], NT) * (SCALE * LOG2E)
        scores[head, slot] = jnp.where(below(counts, slot, block.shape), block, -1e30)

    for head in range(heads):
        score(head, 0, key_value[head, 0])
    to_near.wait_recv()
    for head in range(heads):
        score(head, 1, others[0, head, 0])
    lse[...] = jnp.zeros(lse.shape, F32)
    for head in range(heads):
        to_far[head].wait_recv()
        onward[head].start()
        if head == 0:
            side.late()
        score(head, 2, others[1, head, 0])
        onward[head].wait_recv()
        score(head, 3, others[2, head, 0])
        top = jnp.max(scores[head, 0], axis=0, keepdims=True)
        for slot in range(1, HOLD):
            top = jnp.maximum(top, jnp.max(scores[head, slot], axis=0, keepdims=True))
        total = jnp.zeros_like(top)
        summed = jnp.zeros((HEAD_DIM, tokens), F32)
        for slot in range(HOLD):
            values = key_value[head, 1] if slot == 0 else others[slot - 1, head, 1]
            probs = jnp.exp2(scores[head, slot] - top)
            total = total + jnp.sum(probs, axis=0, keepdims=True)
            summed = summed + dot(values, probs.astype(BF16), TN)
        result[:, head_cols(head)] = (summed / total).T.astype(BF16)
        lse[head : head + 1] = top + jnp.log2(total)
    if first:
        text[1].wait_recv()
        text[2].start()
        text[0].wait_recv()
        text[2].wait_recv()
    for item in [to_near] + to_far + onward + text:
        item.wait_send()
    side.finish()


def below(counts, slot, shape):
    index = lax.broadcasted_iota(jnp.int32, shape, 0).astype(F32)
    return index < counts[slot, 0:1]


def softmax_back(scores, lse_row, mask):
    probs = jnp.exp2(scores * (SCALE * LOG2E) - lse_row)
    return probs if mask is None else jnp.where(mask, probs, 0.0)


def out_sum_kernel(
    side,
    rows_in,
    weight,
    context,
    text_weight,
    rows_w,
    total,
    text_key,
    text_kb,
    text_vb,
    slots,
    send_sems,
    recv_sems,
    part,
    came,
    pair,
    peers,
    sems,
):
    greet(True, side.masks)
    side.start()
    chain = Chain(part, total, (came, pair, peers), sems)
    tokens, features = total.shape
    per_block = 128 // CHUNK

    def project(rows, index):
        part[rows] = dot(rows_in[rows], weight[...], NT).astype(BF16)
        chain.begin(index * per_block, per_block)

    side.need(OUT)
    loop_rows(tokens, 128, project)
    side.need(CONTEXT, TEXT_WEIGHT)
    text_count, width = text_key.shape
    blocks = text_count // 128

    def text(rows, index):
        block = context[rows]
        text_key[rows] = dot(block, text_weight[0]) + row_of(rows_w, 3)
        chain.serve(2 * index)
        text_vb[rows] = (dot(block, text_weight[1]) + row_of(rows_w, 4)).astype(BF16)
        chain.serve(2 * index + 1)

    loop_rows(text_count, 128, text)
    exchange = Exchange(slots, send_sems, recv_sems)

    def early():
        side.early()
        exchange.start(stat_rows(text_key[...] * text_key[...], 0))

    chain.drain(2 * blocks, early, side.middle)
    exchange.finish()
    text_inv = inverse_rms(stat_column(slots, 0, HEAD_DIM), features)
    for head in range(width // HEAD_DIM):
        cols = head_cols(head)
        text_kb[:, cols] = (
            text_key[:, cols] * text_inv * rows_w[GAINS + 3 : GAINS + 4, cols]
        ).astype(BF16)
    side.finish()


def cross_ffn_kernel(
    gathered,
    side,
    base,
    tot,
    rows_d,
    rows_w,
    rows_f,
    weight,
    text_kb,
    text_vb,
    out_weight,
    up,
    *refs,
):
    refs = list(refs)
    down = side.jobs[0].out if gathered else refs.pop(0)
    hidden, normal, query, query_b, result, lse, slots = refs[:7]
    hidden_f, normal_f, gelu_b, slope, total_f = refs[7:12]
    send_sems, recv_sems, total = refs[12:15]
    part, came, pair, peers, sems = refs[15:20]
    part_f, came_f, pair_f, peers_f, sems_f = refs[20:25]
    greet(True, side.masks)
    side.start()
    chain = Chain(part, total, (came, pair, peers), sems)
    chain_f = Chain(part_f, total_f, (came_f, pair_f, peers_f), sems_f)
    tokens, width = query.shape
    features = hidden.shape[1]
    heads = width // HEAD_DIM

    def project(rows, index):
        block = add_branch(
            base[rows], tot[rows], row_of(rows_d, OUT_BIAS), row_of(rows_d, MODS + 2)
        )
        hidden[rows] = block
        block = normed(block)[0] * row_of(rows_d, CROSS_GAIN) + row_of(rows_d, CROSS_SHIFT)
        block = block.astype(BF16)
        normal[rows] = block
        query[rows] = dot(block, weight[...]) + row_of(rows_w, 2)

    side.need(WEIGHT)
    loop_rows(tokens, 256, project)
    side.store(HIDDEN, NORMAL, QUERY)
    exchange = Exchange(slots, send_sems, recv_sems)
    exchange.start(stat_rows(query[...] * query[...], 0))
    exchange.finish()
    query_inv = inverse_rms(stat_column(slots, 0, HEAD_DIM), features)
    side.need(TEXT_KB, TEXT_VB)
    lse[...] = jnp.zeros(lse.shape, F32)
    for head in range(heads):
        cols = head_cols(head)
        query_b[:, cols] = (
            query[:, cols] * query_inv * rows_w[GAINS + 2 : GAINS + 3, cols]
        ).astype(BF16)
        scores = dot(text_kb[:, cols], query_b[:, cols], NT) * (SCALE * LOG2E)
        top = jnp.max(scores, axis=0, keepdims=True)
        probs = jnp.exp2(scores - top)
        amount = jnp.sum(probs, axis=0, keepdims=True)
        summed = dot(text_vb[:, cols], probs.astype(BF16), TN)
        result[:, cols] = (summed / amount).T.astype(BF16)
        lse[head : head + 1] = top + jnp.log2(amount)
    per_block = 128 // CHUNK

    def project_out(rows, index):
        part[rows] = dot(result[rows], out_weight[...], NT).astype(BF16)
        chain.begin(index * per_block, per_block)

    side.store(QUERY_B, RESULT)
    side.need(OUT)
    loop_rows(tokens, 128, project_out)
    side.move(1, DOWN)
    side.start(1)
    scale_row = 1.0 + row_of(rows_d, MODS + 4)
    shift_row = row_of(rows_d, MODS + 3)

    def rows_of(rows):
        block = add_branch(hidden[rows], total[rows], row_of(rows_d, OUT_BIAS + 1), 1.0)
        hidden_f[rows] = block
        block = (normed(block)[0] * scale_row + shift_row).astype(BF16)
        normal_f[rows] = block
        return block

    def inner(rows, block, low, high):
        z = dot(block, up[:, low:high]) + rows_f[:, low:high]
        square = z * z
        tanh = jnp.tanh(GELU_A * z * (1.0 + GELU_B * square))
        side_value = 0.5 * (1.0 + tanh)
        gelu_b[rows, low:high] = (z * side_value).astype(BF16)
        slope[rows, low:high] = (
            side_value
            + 0.5 * z * (1.0 - tanh * tanh) * (GELU_A * (1.0 + 3.0 * GELU_B * square))
        ).astype(BF16)

    def before_second():
        if gathered:
            side.finish(DOWN)
        else:
            side.need(DOWN)

    def after(left):
        side.store(HIDDEN_F, NORMAL_F, GELU_B_NAME, SLOPE)

    side.need(UP)
    mlp_loop(
        side, tokens, rows_of, inner, down, chain_f, gelu_b, before_second, after, chain
    )


def column_cuts(width):
    cuts, low = [], 0
    while low < width:
        high = low + 512 if width - low >= 1024 else width
        cuts.append((low, high))
        low = high
    return cuts


GELU_A = 0.7978845608028654
GELU_B = 0.044715


def mlp_loop(side, tokens, rows_of, inner, second, chain, middle, before_second, after, feed=None):
    size = 128
    per_block = size // CHUNK
    features, hidden_width = second.shape
    cuts = column_cuts(hidden_width)
    half = features // 2
    blocks = tokens // size
    if feed is not None:

        @pl.when(feed.is_mid)
        def _():
            feed.first(0)
            for k in range(1, per_block):
                feed.first(k)
                feed.second(k - 1)

    def step(index, carry):
        rows = pl.ds(pl.multiple_of(index * size, size), size)
        low = index * per_block

        def serve(offset):
            if feed is None:

                @pl.when(index > 0)
                def _():
                    chain.serve(jnp.maximum(low - per_block, 0) + offset)

                return
            if offset > 0:

                @pl.when(feed.is_mid & (index < blocks - 1))
                def _():
                    ahead = jnp.minimum(low + per_block, feed.chunks - per_block)
                    feed.first(ahead + offset)
                    feed.second(ahead + offset - 1)

            @pl.when(index == blocks - 1)
            def _():
                chain.serve(offset)

        if feed is not None:

            @pl.when(feed.is_mid)
            def _():
                @pl.when(index < blocks - 1)
                def _():
                    feed.first(jnp.minimum(low + per_block, feed.chunks - per_block))

                feed.second(low + per_block - 1)

            @pl.when(feed.is_end)
            def _():
                for offset in range(per_block):
                    feed.inward(low + offset, feed.inner).wait_send()
                    feed.outward(low + offset, feed.inner).wait_recv()

        block = rows_of(rows)
        served = 0
        for place, (left, right) in enumerate(cuts):
            inner(rows, block, left, right)
            if place % 2 == 1 and served < 2:
                serve(served)
                served += 1
        while served < 2:
            serve(served)
            served += 1

        @pl.when(index == 0)
        def _():
            before_second()

        for part_index in range(2):
            cols = slice(part_index * half, (part_index + 1) * half)
            chain.part[rows, cols] = dot(middle[rows], second[cols], NT).astype(BF16)
            if part_index == 0:
                serve(2)
        chain.begin(low, per_block)
        serve(3)
        if side.jobs:
            if feed is None:
                points = ((1, bits_of_dp() - 2), (blocks - 1, bits_of_dp() - 1))
            else:
                points = ((blocks - 1, bits_of_dp() - 2),)
            for point, target in points:

                @pl.when(index == point)
                def _(target=target):
                    side.move(target)

        return carry

    lax.fori_loop(0, blocks, step, 0)
    left = (blocks - 1) * per_block if feed is None else per_block
    left = after(left) or left
    chain.drain(left, None, None if feed is None else side.late)
    if feed is not None:
        feed.close()
    side.finish()


def ffn_back_kernel(
    joined,
    side,
    grad,
    *refs,
):
    refs = list(refs)

    def take(count):
        taken = refs[:count]
        del refs[:count]
        return taken

    if joined:
        branch, hidden, rows_above = take(3)
    else:
        teacher, counts = take(2)
    tot, rows_d, down, up, slope, normal, gelu_b = take(7)
    if joined:
        new_grad, sums_above = take(2)
    else:
        new_grad, output = take(2)
    (total, sums, bias_sum, up_grad, down_grad) = take(5)
    down_in, inner_b, stage, stage_sems, part, came, pair, peers, sems = refs
    greet(True, side.masks)
    side.start()
    chain = Chain(part, total, (came, pair, peers), sems)
    tokens = grad.shape[0]
    sums[...] = jnp.zeros(sums.shape, F32)
    bias_sum[...] = jnp.zeros(bias_sum.shape, F32)
    if joined:
        sums_above[...] = jnp.zeros(sums_above.shape, F32)
        scale_row = 1.0 + row_of(rows_above, MODS + 1)

    def rows_of(rows):
        block = grad[rows]
        if joined:
            step = branch[rows].astype(F32)
            back, hat = norm_back(hidden[rows], scale_row, step)
            add_sum(sums_above, 0, step)
            add_sum(sums_above, 1, step * hat)
            block = block + back
            new_grad[rows] = block
        else:
            block = add_branch(
                block, tot[rows], row_of(rows_d, OUT_BIAS + 2), row_of(rows_d, MODS + 5)
            )
            output[rows] = block
            block = block - teacher[rows].astype(F32)
            place = lax.broadcasted_iota(jnp.int32, (block.shape[0], 1), 0) + rows.start
            block = jnp.where(place.astype(F32) < counts[0, 0:1, 0:1], block, 0.0)
            new_grad[rows] = block
            add_sum(sums, 2, block * block)
        add_sum(sums, 0, block * (tot[rows].astype(F32) + row_of(rows_d, OUT_BIAS + 2)))
        block = (block * row_of(rows_d, MODS + 5)).astype(BF16)
        down_in[rows] = block
        add_sum(sums, 1, block.astype(F32))
        return block

    def inner(rows, block, low, high):
        cols = (dot(block, down[:, low:high]) * slope[rows, low:high].astype(F32)).astype(BF16)
        inner_b[rows, low:high] = cols
        bias_sum[0:1, low:high] += jnp.sum(cols.astype(F32), axis=0, keepdims=True)

    def after(left):
        side.store(NEW_GRAD)
        if not joined:
            side.store(OUTPUT)
        side.need(NORMAL, GELU_B_NAME)
        copies = []

        def keep(target):
            def store(tile, size, block):
                number = len(copies)
                if number >= 2:
                    copies[number - 2].wait()
                stage[number % 2] = block
                copy = pltpu.make_async_copy(
                    stage.at[number % 2],
                    target.at[tile * size : (tile + 1) * size],
                    stage_sems.at[number % 2],
                )
                copy.start()
                copies.append(copy)

            return store

        def serve(tile):
            if left + tile < chain.chunks:
                chain.serve(left + tile)

        tiled_grad(normal, inner_b, keep(up_grad), serve, stage.shape[1])
        chain.segment(chain.chunks, chain.chunks, 0, 0)
        tiled_grad(down_in, gelu_b, keep(down_grad), lambda tile: None, stage.shape[1])
        copies[-2].wait()
        copies[-1].wait()
        return chain.chunks

    side.need(GRAD, DOWN, SLOPE)
    mlp_loop(
        side, tokens, rows_of, inner, up, chain, inner_b, lambda: side.need(UP), after
    )


def cross_back_kernel(
    side,
    grad,
    branch,
    hidden,
    rows_d,
    rows_w,
    out_weight,
    query,
    query_b,
    lse,
    slots_q,
    text_kb,
    text_vb,
    weight,
    normal,
    result,
    new_grad,
    text_grad,
    sums,
    width_sums,
    total,
    matrix_grad,
    out_in,
    query_grad_b,
    out_grad,
    query_n,
    slots,
    send_sems,
    recv_sems,
    part,
    came,
    pair,
    peers,
    sems,
):
    greet(True, side.masks)
    side.start()
    chain = Chain(part, total, (came, pair, peers), sems)
    tokens, width = query.shape
    features = grad.shape[1]
    heads = width // HEAD_DIM
    gain = rows_w[GAINS + 2 : GAINS + 3]
    sums[...] = jnp.zeros(sums.shape, F32)
    width_sums[...] = jnp.zeros(width_sums.shape, F32)
    scale_row = 1.0 + row_of(rows_d, MODS + 4)

    def enter(rows, index):
        step = branch[rows].astype(F32)
        back, hat = norm_back(hidden[rows], scale_row, step)
        add_sum(sums, 0, step)
        add_sum(sums, 1, step * hat)
        block = grad[rows] + back
        new_grad[rows] = block
        block = block.astype(BF16)
        out_in[rows] = block
        add_sum(sums, 2, block.astype(F32))
        out_grad[rows] = dot(block, out_weight[...]).astype(BF16)

    side.need(OUT)
    loop_rows(tokens, 256, enter)
    side.store(NEW_GRAD)
    side.need(QUERY, QUERY_B, TEXT_KB, TEXT_VB)
    for head in range(heads):
        cols = head_cols(head)
        query_h, out_grad_h = query_b[:, cols], out_grad[:, cols]
        text_k, text_v = text_kb[:, cols], text_vb[:, cols]
        probs = softmax_back(dot(text_k, query_h, NT), lse[head : head + 1], None)
        prob_grad = dot(text_v, out_grad_h, NT)
        inner = jnp.sum(probs * prob_grad, axis=0, keepdims=True)
        score_b = (probs * (prob_grad - inner) * SCALE).astype(BF16)
        query_n[:, cols] = dot(text_k, score_b, TN).T
        text_grad[0, :, cols] = dot(score_b, query_h)
        text_grad[1, :, cols] = dot(probs.astype(BF16), out_grad_h)
    exchange = Exchange(slots, send_sems, recv_sems)
    exchange.start(stat_rows(query[...] * query_n[...] * gain, 0))
    inverse = inverse_rms(stat_column(slots_q, 0, HEAD_DIM), features)
    side.move(1)
    exchange.finish()
    term = stat_column(slots, 0, HEAD_DIM) * inverse * inverse * inverse / features
    for head in range(heads):
        cols = head_cols(head)
        width_sums[0:1, cols] = jnp.sum(
            query[:, cols] * query_n[:, cols] * inverse, axis=0, keepdims=True
        )
        block = inverse * gain[:, cols] * query_n[:, cols] - query[:, cols] * term
        block = block.astype(BF16)
        query_grad_b[:, cols] = block
        width_sums[1:2, cols] = jnp.sum(block.astype(F32), axis=0, keepdims=True)
    per_block = 128 // CHUNK

    def leave(rows, index):
        part[rows] = dot(query_grad_b[rows], weight[...], NT).astype(BF16)
        chain.begin(index * per_block, per_block)

    side.store(TEXT_GRAD)
    side.need(WEIGHT)
    loop_rows(tokens, 128, leave)
    side.need(NORMAL, RESULT)

    def keep(low):
        def store(tile, size, block):
            matrix_grad[tile * size : (tile + 1) * size, low : low + width] = block

        return store

    tiled_grad(normal, query_grad_b, keep(0), lambda tile: None if tile % 2 else chain.serve(tile // 2))
    tiled_grad(out_in, result, keep(width), lambda tile: None if tile % 2 else chain.serve(2 + tile // 2))
    side.store(MATRIX_GRAD)
    chain.drain(4, side.late)
    side.finish()


def attend_back_kernel(
    side,
    counts,
    grad,
    branch,
    hidden,
    rows_d,
    tot,
    out_weight,
    query,
    key_value,
    others,
    lse,
    text_grad,
    result,
    new_grad,
    matrix_grad,
    sums,
    query_grad,
    key_value_grad,
    text_sum,
    out_in,
    out_grad,
    probs,
    prob_grads,
    away,
    landed,
    text_away,
    text_landed,
    send_sems,
    recv_sems,
):
    greet(False, [1, 2])
    side.start()
    near, far = holders()
    tokens, width = query.shape
    heads = width // HEAD_DIM
    text_rows = text_sum.shape[1]
    sums[...] = jnp.zeros(sums.shape, F32)

    def copy(kind, head):
        return send(
            away.at[kind, head],
            landed.at[kind, head],
            send_sems.at[kind, head],
            recv_sems.at[kind, head],
            dp=far if kind == 1 else near,
        )

    def text_copy(kind):
        return send(
            text_away.at[kind],
            text_landed.at[kind],
            send_sems.at[kind, heads],
            recv_sems.at[kind, heads],
            dp=far if kind == 1 else near,
        )

    place = lax.rem(lax.axis_index(DP), HOLD)

    def text_part(slot):
        start = pl.multiple_of(flip(place, slot) * text_rows, text_rows)
        return text_grad[:, pl.ds(start, text_rows)]

    text_away[2] = text_part(3).astype(BF16)
    text_copy(2).start()
    text_away[0] = text_part(1).astype(BF16)
    text_copy(0).start()

    def enter(rows, index):
        step = branch[rows].astype(F32)
        back, hat = norm_back(hidden[rows], row_of(rows_d, CROSS_GAIN), step)
        add_sum(sums, 0, step * hat)
        add_sum(sums, 1, step)
        block = grad[rows] + back
        new_grad[rows] = block
        add_sum(sums, 2, block * (tot[rows].astype(F32) + row_of(rows_d, OUT_BIAS)))
        block = (block * row_of(rows_d, MODS + 2)).astype(BF16)
        out_in[rows] = block
        add_sum(sums, 3, block.astype(F32))
        out_grad[rows] = dot(block, out_weight[...]).astype(BF16)

    side.need(OUT)
    loop_rows(tokens, 256, enter)
    side.store(NEW_GRAD)
    side.need(QUERY, KEY_VALUE, OTHERS, RESULT)
    text_copy(2).wait_recv()
    text_away[1] = (text_part(2) + text_landed[2].astype(F32)).astype(BF16)
    text_copy(1).start()

    for head in range(heads):
        cols = head_cols(head)
        query_h, out_grad_h = query[:, cols], out_grad[:, cols]

        def pair_of(slot, head=head):
            if slot == 0:
                return key_value[head, 0], key_value[head, 1]
            return others[slot - 1, head, 0], others[slot - 1, head, 1]

        inner = jnp.zeros((1, tokens), F32)
        for slot in range(HOLD):
            keys, values = pair_of(slot)
            block = softmax_back(
                dot(keys, query_h, NT),
                lse[head : head + 1],
                below(counts, slot, (tokens, tokens)),
            )
            probs[slot] = block
            block_grad = dot(values, out_grad_h, NT)
            prob_grads[slot] = block_grad
            inner = inner + jnp.sum(block * block_grad, axis=0, keepdims=True)
        query_n = jnp.zeros((HEAD_DIM, tokens), F32)
        for slot in (3, 2, 1, 0):
            keys, values = pair_of(slot)
            block = probs[slot]
            score_b = (block * (prob_grads[slot] - inner) * SCALE).astype(BF16)
            query_n = query_n + dot(keys, score_b, TN)
            key_g = dot(score_b, query_h)
            value_g = dot(block.astype(BF16), out_grad_h)
            if slot == 0:
                key_value_grad[0, :, cols] = key_g
                key_value_grad[1, :, cols] = value_g
            elif slot == 2:
                copy(2, head).wait_recv()
                away[1, head, 0] = (key_g + landed[2, head, 0].astype(F32)).astype(BF16)
                away[1, head, 1] = (value_g + landed[2, head, 1].astype(F32)).astype(BF16)
                copy(1, head).start()
            else:
                away[slot - 1, head, 0] = key_g.astype(BF16)
                away[slot - 1, head, 1] = value_g.astype(BF16)
                copy(slot - 1, head).start()
        query_grad[:, cols] = query_n.T
    side.store(QUERY_GRAD)

    def keep(tile, size, block):
        matrix_grad[tile * size : (tile + 1) * size] = block

    tiled_grad(out_in, result, keep, lambda tile: None)
    side.store(MATRIX_GRAD)
    text_copy(0).wait_recv()
    text_copy(1).wait_recv()
    text_sum[...] = text_part(0) + text_landed[0].astype(F32) + text_landed[1].astype(F32)
    for head in range(heads):
        cols = head_cols(head)
        copy(0, head).wait_recv()
        copy(1, head).wait_recv()
        for member in range(2):
            key_value_grad[member, :, cols] += landed[0, head, member].astype(F32) + landed[
                1, head, member
            ].astype(F32)
    for kind in range(3):
        text_copy(kind).wait_send()
        for head in range(heads):
            copy(kind, head).wait_send()


def qkv_back_kernel(
    side,
    query_grad,
    key_value_grad,
    text_grad,
    query,
    key,
    text_key,
    slots_in,
    text_slots,
    rows_w,
    cosine,
    sine,
    weight,
    normal,
    context,
    text_weight,
    context_before,
    width_sums,
    context_part,
    total,
    self_grad,
    text_matrix,
    grads_b,
    text_b,
    query_n,
    key_n,
    slots,
    send_sems,
    recv_sems,
    part,
    came,
    pair,
    peers,
    sems,
):
    greet(True, side.masks)
    side.start()
    chain = Chain(part, total, (came, pair, peers), sems)
    tokens, width = query.shape
    features = total.shape[1]
    heads = width // HEAD_DIM
    text_rows = text_grad.shape[1]
    place = lax.rem(lax.axis_index(DP), HOLD)
    mine = pl.ds(pl.multiple_of(place * text_rows, text_rows), text_rows)
    text_k = text_key[mine]
    width_sums[...] = jnp.zeros(width_sums.shape, F32)
    for head in range(heads):
        cols = head_cols(head)
        rows = query_grad[:, cols]
        query_n[:, cols] = rows * cosine[...] - turned(rows * sine[...])
        rows = key_value_grad[0, :, cols]
        key_n[:, cols] = rows * cosine[...] - turned(rows * sine[...])

    def gain(member):
        return rows_w[GAINS + member : GAINS + member + 1]

    exchange = Exchange(slots, send_sems, recv_sems)
    text_terms = stat_rows(text_k * gain(3) * text_grad[0], 2)
    exchange.start(
        stat_rows(query[...] * gain(0) * query_n[...], 0)
        + stat_rows(key[...] * gain(1) * key_n[...], 1)
        + jnp.concatenate([text_terms, jnp.zeros((8, tokens - text_rows), F32)], axis=1)
    )
    query_inv = inverse_rms(stat_column(slots_in, 0, HEAD_DIM), features)
    key_inv = inverse_rms(stat_column(slots_in, 1, HEAD_DIM), features)
    text_inv = inverse_rms(stat_column(text_slots.at[:, :, mine], 0, HEAD_DIM), features)
    side.move(1)
    exchange.finish()

    def cubed(inverse, term):
        return term * inverse * inverse * inverse / features

    query_t = cubed(query_inv, stat_column(slots, 0, HEAD_DIM))
    key_t = cubed(key_inv, stat_column(slots, 1, HEAD_DIM))
    text_t = cubed(text_inv, stat_column(slots.at[:, :, pl.ds(0, text_rows)], 2, HEAD_DIM))

    def back(member, cols, values, inverse, term, grads):
        width_sums[member : member + 1, cols] = jnp.sum(
            values * inverse * grads, axis=0, keepdims=True
        )
        block = inverse * gain(member)[:, cols] * grads - values * term
        block = block.astype(BF16)
        width_sums[4 + member : 5 + member, cols] = jnp.sum(
            block.astype(F32), axis=0, keepdims=True
        )
        return block

    def shifted(cols, member):
        return slice(cols.start + member * width, cols.stop + member * width)

    for head in range(heads):
        cols = head_cols(head)
        grads_b[:, cols] = back(0, cols, query[:, cols], query_inv, query_t, query_n[:, cols])
        grads_b[:, shifted(cols, 1)] = back(
            1, cols, key[:, cols], key_inv, key_t, key_n[:, cols]
        )
        text_b[:, cols] = back(
            3, cols, text_k[:, cols], text_inv, text_t, text_grad[0, :, cols]
        )
    block = key_value_grad[1].astype(BF16)
    grads_b[:, 2 * width :] = block
    width_sums[6:7] = jnp.sum(block.astype(F32), axis=0, keepdims=True)
    block = text_grad[1].astype(BF16)
    text_b[:, width:] = block
    width_sums[8:9] = jnp.sum(block.astype(F32), axis=0, keepdims=True)
    per_block = 128 // CHUNK

    def leave(rows, index):
        part[rows] = (
            dot(grads_b[rows, :width], weight[0], NT)
            + dot(grads_b[rows, width : 2 * width], weight[1], NT)
            + dot(grads_b[rows, 2 * width :], weight[2], NT)
        ).astype(BF16)
        chain.begin(index * per_block, per_block)

    side.need(WEIGHT)
    loop_rows(tokens, 128, leave)
    side.need(NORMAL, CONTEXT, TEXT_WEIGHT)

    def keep(target):
        def store(tile, size, block):
            target[tile * size : (tile + 1) * size] = block

        return store

    tiled_grad(normal, grads_b, keep(self_grad), chain.serve)
    side.store(SELF_GRAD)
    tiled_grad(context, text_b, keep(text_matrix), lambda tile: None)
    side.store(TEXT_MATRIX)
    chain.serve(4)
    context_part[...] = (
        context_before[...]
        + dot(text_b[:, :width], text_weight[0], NT)
        + dot(text_b[:, width:], text_weight[1], NT)
    )
    chain.drain(5, side.late)
    side.finish()


def small_rows(clips):
    low = 6 * LAYERS + 6 * clips
    places = {BIAS: low, GAIN: low + 3 * LAYERS, SHIFT: low + 4 * LAYERS}
    places[LOSS] = low + 5 * LAYERS
    return places, (low + 5 * LAYERS + 1 + 15) // 16 * 16


def last_kernel(
    clips,
    side,
    context_part,
    grad,
    branch,
    hidden,
    rows_d,
    *refs,
):
    refs = list(refs)

    def take(count):
        taken = refs[:count]
        del refs[:count]
        return taken

    above = take(1)[0]
    small = [take(6) for _ in range(LAYERS)]
    new_grad, total, out_d, out_w, out_f = take(5)
    sums = take(1)[0]
    part, came, pair, peers, sems = take(5)
    bits = bits_of_dp()
    away = [take(3) for _ in range(bits)]
    landed = [take(3) for _ in range(bits)]
    send_sems, recv_sems = take(2)
    greet(True, side.masks)
    side.start()
    me = lax.axis_index(DP)
    clip = me // HOLD
    chain = Chain(part, total, (came, pair, peers), sems)
    part[...] = context_part[...].astype(BF16)
    chain.begin(0, chain.chunks)
    sums[...] = jnp.zeros(sums.shape, F32)
    scale_row = 1.0 + row_of(rows_d, MODS + 1)
    tokens = grad.shape[0]
    size = tokens // chain.chunks
    side.need(GRAD, BRANCH, HIDDEN)

    def enter(rows, index):
        step = branch[rows].astype(F32)
        back, hat = norm_back(hidden[rows], scale_row, step)
        add_sum(sums, 0, step)
        add_sum(sums, 1, step * hat)
        new_grad[rows] = grad[rows] + back
        chain.serve(index)

    loop_rows(tokens, size, enter)
    side.store(NEW_GRAD)
    side.move(1)
    places, count = small_rows(clips)
    out_d[...] = jnp.zeros(out_d.shape, F32)
    out_f[...] = jnp.zeros(out_f.shape, F32)
    time_rows = [jnp.zeros((1, grad.shape[1]), F32) for _ in range(6)]
    for layer in range(LAYERS):
        sums1, sums2, sums3, width1, width2, hidden_sum = small[layer]
        sums0 = sums if layer == 0 else above
        mods = [(sums0, 0), (sums0, 1), (sums1, 2), (sums2, 0), (sums2, 1), (sums3, 0)]
        for row, (ref, index) in enumerate(mods):
            value = row_of(ref, index)
            time_rows[row] = time_rows[row] + value
            out_d[6 * layer + row : 6 * layer + row + 1] = value
        for row, (ref, index) in enumerate([(sums1, 3), (sums2, 2), (sums3, 1)]):
            place = places[BIAS] + 3 * layer + row
            out_d[place : place + 1] = row_of(ref, index)
        place = places[GAIN] + layer
        out_d[place : place + 1] = row_of(sums1, 0)
        place = places[SHIFT] + layer
        out_d[place : place + 1] = row_of(sums1, 1)
        out_w[24 * layer : 24 * layer + 16] = width1[...]
        out_w[24 * layer + 16 : 24 * layer + 24] = width2[...]
        out_f[layer : layer + 1] = row_of(hidden_sum, 0)
    for index in range(clips):
        for row in range(6):
            place = 6 * LAYERS + 6 * index + row
            out_d[place : place + 1] = jnp.where(clip == index, time_rows[row], 0.0)
    out_d[places[LOSS] : places[LOSS] + 1] = row_of(small[LAYERS - 1][2], 2)
    for bit in range(bits):
        copies = []
        for number, ref in enumerate((out_d, out_w, out_f)):
            away[bit][number][...] = ref[...].astype(BF16)
            copy = send(
                away[bit][number],
                landed[bit][number],
                send_sems.at[bit, number],
                recv_sems.at[bit, number],
                dp=flip(me, 1 << bit),
            )
            copy.start()
            copies.append(copy)
        if bit == 0:
            chain.drain(chain.chunks)
        side.move(bit)
        for number, ref in enumerate((out_d, out_w, out_f)):
            copies[number].wait()
            ref[...] = away[bit][number][...].astype(F32) + landed[bit][number][...].astype(F32)
    side.finish()


def unpack_kernel(
    clips, side, lengths, rows_d, rows_w, rows_f, loss, time, bias, key_bias, gains, hidden, out,
    gain, shift, mods
):
    places, count = small_rows(clips)
    for layer in range(LAYERS):
        for row in range(6):
            mods[row, layer : layer + 1] = row_of(rows_d, 6 * layer + row)
        for row in range(3):
            out[row, layer : layer + 1] = row_of(rows_d, places[BIAS] + 3 * layer + row)
        base = 24 * layer
        for row, place in enumerate((4, 6, 17, 7, 8)):
            bias[row, layer : layer + 1] = row_of(rows_w, base + place)
        key_bias[layer : layer + 1] = row_of(rows_w, base + 5)
        for row, place in enumerate((0, 1, 16, 3)):
            gains[layer, row : row + 1] = row_of(rows_w, base + place)
    for index in range(clips):
        for row in range(6):
            time[row, index : index + 1] = row_of(rows_d, 6 * LAYERS + 6 * index + row)
    hidden[...] = rows_f[0:LAYERS]
    gain[...] = rows_d[places[GAIN] : places[GAIN] + LAYERS]
    shift[...] = rows_d[places[SHIFT] : places[SHIFT] + LAYERS]
    count = lengths[0]
    for index in range(1, clips):
        count = count + lengths[index]
    total = jnp.sum(row_of(rows_d, places[LOSS]), axis=1, keepdims=True)
    loss[...] = jnp.broadcast_to(total, loss.shape) / (count.astype(F32) * rows_d.shape[1])


def per_device(
    latents,
    context,
    time_embed,
    teacher,
    lengths,
    block_order,
    positions,
    self_proj,
    cross_proj,
    out_proj,
    ffn_up,
    ffn_down,
    proj_bias,
    key_bias,
    norm_gains,
    ffn_bias,
    out_bias,
    cross_gain,
    cross_shift,
    modulation,
):
    tokens, features = latents.shape
    width = norm_gains.shape[-1]
    heads = width // HEAD_DIM
    hidden_width = ffn_bias.shape[-1]
    clip_count = time_embed.shape[0]
    text_rows = context.shape[0]
    text_all = text_rows * HOLD
    clip = lax.axis_index(DP) // HOLD
    out_t = jnp.swapaxes(out_proj, 2, 3)
    down_t = jnp.swapaxes(ffn_down, 1, 2)

    rows_d = (tokens, features)
    rows_w = (tokens, width)
    rows_f = (tokens, hidden_width)
    stats = (CHAIN, 8, tokens)
    three = pltpu.SemaphoreType.DMA((CHAIN - 1,))
    chain_scratch = Chain.scratch(tokens, features)
    kv_shape = (heads, 2, tokens, HEAD_DIM)

    pack = (((16, features), F32), ((16, width), F32), ((1, hidden_width), F32))
    results, (self_w,) = run(
        "entry",
        entry_kernel,
        (
            lengths,
            block_order,
            jnp.swapaxes(time_embed, 0, 1),
            jnp.swapaxes(modulation, 0, 1),
            jnp.swapaxes(out_bias, 0, 1),
            cross_gain,
            cross_shift,
            jnp.swapaxes(proj_bias, 0, 1),
            key_bias,
            norm_gains,
            ffn_bias,
            positions,
            rope_table(HEAD_DIM),
        ),
        (((HOLD, 8, tokens), F32), ((tokens, HEAD_DIM), F32), ((tokens, HEAD_DIM), F32))
        + pack * LAYERS,
        [three, three],
        jobs=[Gather(self_proj, 0)],
        scalars=2,
        micros=25,
    )
    counts, cosine, sine = results[:3]
    packs = [results[3 + 3 * layer : 6 + 3 * layer] for layer in range(LAYERS)]

    saved = []
    weights = {SELF: [self_w], CROSS: [], OUT: [], UP: [], DOWN: []}
    sources = {
        SELF: self_proj,
        CROSS: cross_proj,
        OUT: out_t,
        UP: ffn_up,
        DOWN: down_t,
    }

    def gathers(layer, *names):
        return [Gather(sources[name], layer) for name in names if layer < LAYERS]

    def keep(found, *names):
        for name, item in zip(names, found):
            weights[name].append(item)

    base, tot, before = latents, latents, packs[0][0]
    for layer in range(LAYERS):
        pack_d, pack_w, pack_f = packs[layer]
        names = (CROSS, OUT) if layer == 0 else ()
        results, found = run(
            "attend" + str(layer > 0),
            functools.partial(attend_kernel, layer == 0),
            (
                base,
                tot,
                before,
                pack_d,
                pack_w,
                Late(WEIGHT, weights[SELF][layer]),
                Late(COSINE, cosine),
                Late(SINE, sine),
                counts,
            )
            + ((context,) if layer == 0 else ()),
            (
                Early(HIDDEN, rows_d, F32),
                Early(NORMAL, rows_d, BF16),
                Early(QUERY, rows_w, F32),
                Early(KEY, rows_w, F32),
                Early(QUERY_ROT, rows_w, BF16),
                (kv_shape, BF16),
                (stats, F32),
                ((HOLD - 1,) + kv_shape, BF16),
                (rows_w, BF16),
                ((8, tokens), F32),
            )
            + ((((text_all, features), BF16),) if layer == 0 else ()),
            [
                pltpu.VMEM((heads, HOLD, tokens, tokens), F32),
                three,
                three,
                pltpu.SemaphoreType.DMA((4 + 2 * heads,)),
                pltpu.SemaphoreType.DMA((4 + 2 * heads,)),
            ],
            jobs=gathers(layer, *names),
            micros=40,
        )
        keep(found, *names)
        hidden, a1, sq, sk, q_rot, kv, stat1, others, o1, lse1 = results[:10]
        if layer == 0:
            clip_context = results[10]
        (tot1, ck, ckb, cvb, stat_t), found = run(
            "out_sum",
            out_sum_kernel,
            (
                o1,
                Late(OUT, weights[OUT][layer], 0),
                Late(CONTEXT, clip_context),
                Late(TEXT_WEIGHT, weights[CROSS][layer], 1, 3),
                pack_w,
            ),
            (
                (rows_d, BF16),
                ((text_all, width), F32),
                ((text_all, width), BF16),
                ((text_all, width), BF16),
                ((CHAIN, 8, text_all), F32),
            ),
            [three, three] + chain_scratch,
            jobs=gathers(layer, UP) + gathers(1, SELF)
            if layer == 0
            else gathers(layer, DOWN),
            micros=45,
        )
        keep(found, *((UP, SELF) if layer == 0 else (DOWN,)))
        gathered = layer == 0
        jobs = [
            Gather(sources[DOWN], 0, name=DOWN, held=True),
            Gather(sources[CROSS], 1, wave=1),
            Gather(sources[OUT], 1, wave=1),
            Gather(sources[UP], 1, wave=1),
        ]
        results, found = run(
            "cross_ffn" + str(gathered),
            functools.partial(cross_ffn_kernel, gathered),
            (
                hidden,
                tot1,
                pack_d,
                pack_w,
                pack_f,
                Late(WEIGHT, weights[CROSS][layer], 0),
                Late(TEXT_KB, ckb),
                Late(TEXT_VB, cvb),
                Late(OUT, weights[OUT][layer], 1),
                Late(UP, weights[UP][layer]),
            )
            + (() if gathered else (Late(DOWN, weights[DOWN][layer]),)),
            (
                Early(HIDDEN, rows_d, F32),
                Early(NORMAL, rows_d, BF16),
                Early(QUERY, rows_w, F32),
                Early(QUERY_B, rows_w, BF16),
                Early(RESULT, rows_w, BF16),
                ((8, tokens), F32),
                (stats, F32),
                Early(HIDDEN_F, rows_d, F32),
                Early(NORMAL_F, rows_d, BF16),
                Early(GELU_B_NAME, rows_f, BF16),
                Early(SLOPE, rows_f, BF16),
                (rows_d, BF16),
            ),
            [three, three, pltpu.VMEM(rows_d, BF16)] + chain_scratch + chain_scratch,
            jobs=jobs if gathered else [],
            micros=90,
        )
        h1, a3, cq, cqb, o2, lse2, stat2, h2, a2, gelu_b, slope, tot3 = results
        if gathered:
            keep(found, DOWN, CROSS, OUT, UP)
        saved.append(
            (hidden, a1, sq, sk, q_rot, kv, stat1, others, o1, lse1, tot1, ck, ckb, cvb, stat_t)
            + (h1, a3, cq, cqb, o2, lse2, stat2, h2, a2, gelu_b, slope, tot3)
        )
        base, tot, before = h2, tot3, pack_d
    grad = base
    reduced = {}
    small = [None] * LAYERS
    context_part = jnp.zeros(context.shape, F32)
    above = None
    for layer in reversed(range(LAYERS)):
        (hidden, a1, sq, sk, q_rot, kv, stat1, others, o1, lse1, tot1, ck, ckb, cvb, stat_t) = saved[
            layer
        ][:15]
        (h1, a3, cq, cqb, o2, lse2, stat2, h2, a2, gelu_b, slope, tot3) = saved[layer][15:]
        pack_d, pack_w, pack_f = packs[layer]
        w_self, w_cross, w_out, w_up, w_down = [
            weights[name][layer] for name in (SELF, CROSS, OUT, UP, DOWN)
        ]
        joined = above is not None
        matrix = (features, hidden_width)
        results, found = run(
            "ffn_back" + str(joined),
            functools.partial(ffn_back_kernel, joined),
            (Late(GRAD, grad),)
            + (above if joined else (teacher, counts))
            + (
                tot3,
                pack_d,
                Late(DOWN, w_down),
                Late(UP, w_up),
                Late(SLOPE, slope),
                Late(NORMAL, a2),
                Late(GELU_B_NAME, gelu_b),
            ),
            (
                Early(NEW_GRAD, rows_d, F32, over=0),
                ((8, features), F32) if joined else Early(OUTPUT, rows_d, F32),
            )
            + (
                (rows_d, BF16),
                ((8, features), F32),
                ((8, hidden_width), F32),
                (matrix, BF16, True),
                (matrix, BF16, True),
            ),
            [
                pltpu.VMEM(rows_d, BF16),
                pltpu.VMEM(rows_f, BF16),
                pltpu.VMEM((2, 256, hidden_width), BF16),
                pltpu.SemaphoreType.DMA((2,)),
            ]
            + chain_scratch,
            jobs=[Scatter(text_matrix), Scatter(self_matrix)] if joined else [],
            micros=60,
        )
        grad = results[0]
        if not joined:
            output = results[1]
        else:
            sums_above = results[1]
            reduced[TEXT, layer + 1], reduced[SELF, layer + 1] = found
        da2, sums3, dz_sum, up_grad, down_grad = results[2:]
        (grad, dct, sums2, wsums2, da3, cross_matrix), found = run(
            "cross_back",
            cross_back_kernel,
            (
                grad,
                da2,
                h2,
                pack_d,
                pack_w,
                Late(OUT, w_out, 1),
                Late(QUERY, cq),
                Late(QUERY_B, cqb),
                lse2,
                stat2,
                Late(TEXT_KB, ckb),
                Late(TEXT_VB, cvb),
                Late(WEIGHT, w_cross, 0),
                Late(NORMAL, a3),
                Late(RESULT, o2),
            ),
            (
                Early(NEW_GRAD, rows_d, F32),
                Early(TEXT_GRAD, (2, text_all, width), F32),
                ((8, features), F32),
                ((8, width), F32),
                (rows_d, BF16),
                Early(MATRIX_GRAD, (features, 2 * width), BF16),
            ),
            [
                pltpu.VMEM(rows_d, BF16),
                pltpu.VMEM(rows_w, BF16),
                pltpu.VMEM(rows_w, BF16),
                pltpu.VMEM(rows_w, F32),
                pltpu.VMEM(stats, F32),
                three,
                three,
            ]
            + chain_scratch,
            jobs=[Scatter(up_grad, UP)],
            micros=60,
        )
        reduced[UP, layer] = found[0]
        (grad, out0, sums1, dq_rot, dkv, dtext), found = run(
            "attend_back",
            attend_back_kernel,
            (
                counts,
                grad,
                da3,
                h1,
                pack_d,
                tot1,
                Late(OUT, w_out, 0),
                Late(QUERY, q_rot),
                Late(KEY_VALUE, kv),
                Late(OTHERS, others),
                lse1,
                dct,
                Late(RESULT, o1),
            ),
            (
                Early(NEW_GRAD, rows_d, F32),
                Early(MATRIX_GRAD, (features, width), BF16),
                ((8, features), F32),
                Early(QUERY_GRAD, rows_w, F32),
                ((2,) + rows_w, F32),
                ((2, text_rows, width), F32),
            ),
            [
                pltpu.VMEM(rows_d, BF16),
                pltpu.VMEM(rows_w, BF16),
                pltpu.VMEM((HOLD, tokens, tokens), F32),
                pltpu.VMEM((HOLD, tokens, tokens), F32),
                pltpu.VMEM((3,) + kv_shape, BF16),
                pltpu.VMEM((3,) + kv_shape, BF16),
                pltpu.VMEM((3, 2, text_rows, width), BF16),
                pltpu.VMEM((3, 2, text_rows, width), BF16),
                pltpu.SemaphoreType.DMA((3, heads + 1)),
                pltpu.SemaphoreType.DMA((3, heads + 1)),
            ],
            micros=35,
        )
        (wsums1, context_part, da1, self_matrix, text_matrix), found = run(
            "qkv_back",
            qkv_back_kernel,
            (
                dq_rot,
                dkv,
                dtext,
                sq,
                sk,
                ck,
                stat1,
                stat_t,
                pack_w,
                cosine,
                sine,
                Late(WEIGHT, w_self),
                Late(NORMAL, a1),
                Late(CONTEXT, context),
                Late(TEXT_WEIGHT, w_cross, 1, 3),
                context_part,
            ),
            (
                ((16, width), F32),
                (context.shape, F32),
                (rows_d, BF16),
                Early(SELF_GRAD, (features, 3 * width), BF16),
                Early(TEXT_MATRIX, (features, 2 * width), BF16),
            ),
            [
                pltpu.VMEM((tokens, 3 * width), BF16),
                pltpu.VMEM((text_rows, 2 * width), BF16),
                pltpu.VMEM(rows_w, F32),
                pltpu.VMEM(rows_w, F32),
                pltpu.VMEM(stats, F32),
                three,
                three,
            ]
            + chain_scratch,
            jobs=[Scatter(down_grad), Scatter(cross_matrix), Scatter(out0)],
            micros=60,
        )
        reduced[DOWN, layer], reduced[CROSS, layer], reduced[OUT0, layer] = found
        small[layer] = (sums1, sums2, sums3, wsums1, wsums2, dz_sum)
        above = (da1, hidden, pack_d)
    places, count = small_rows(clip_count)
    small_shapes = ((count, features), (24 * LAYERS, width), (16, hidden_width))
    travel = [pltpu.VMEM(shape, BF16) for shape in small_shapes]
    bits = bits_of_dp()
    (grad, context_sum, packed_d, packed_w, packed_f), found = run(
        "last",
        functools.partial(last_kernel, clip_count),
        (
            context_part,
            Late(GRAD, grad),
            Late(BRANCH, above[0]),
            Late(HIDDEN, above[1]),
            above[2],
            sums_above,
        )
        + tuple(item for layer in range(LAYERS) for item in small[layer]),
        (Early(NEW_GRAD, rows_d, F32), (context.shape, BF16))
        + tuple((shape, F32) for shape in small_shapes),
        [pltpu.VMEM((8, features), F32)]
        + Chain.scratch(text_rows, features)
        + travel * (2 * bits)
        + [pltpu.SemaphoreType.DMA((bits, 3)), pltpu.SemaphoreType.DMA((bits, 3))],
        jobs=[Scatter(text_matrix), Scatter(self_matrix)],
        micros=30,
    )
    reduced[TEXT, 0], reduced[SELF, 0] = found
    unpacked, unused = run(
        "unpack",
        functools.partial(unpack_kernel, clip_count),
        (lengths, packed_d, packed_w, packed_f),
        (
            ((1, 128), F32),
            ((6, clip_count, features), F32),
            ((5, LAYERS, width), F32),
            ((LAYERS, width), F32),
            ((LAYERS, 4, width), F32),
            ((LAYERS, hidden_width), F32),
            ((3, LAYERS, features), F32),
            ((LAYERS, features), F32),
            ((LAYERS, features), F32),
            ((6, LAYERS, features), F32),
        ),
        remote=False,
        scalars=1,
        micros=3,
    )
    loss, time, bias, key_sums, gain_sums, hidden_sums, out_sums, gain, shift, mods = unpacked
    context_grad = context_sum.astype(F32)

    def split(block):
        return jnp.swapaxes(block.reshape(block.shape[0], -1, width), 0, 1)

    self_grad = jnp.stack([split(reduced[SELF, layer]) for layer in range(LAYERS)])
    cross_grad = jnp.stack(
        [
            jnp.concatenate(
                [split(reduced[CROSS, layer])[:1], split(reduced[TEXT, layer])]
            )
            for layer in range(LAYERS)
        ]
    )
    out_grad = jnp.stack(
        [
            jnp.stack([reduced[OUT0, layer].T, reduced[CROSS, layer][:, width:].T])
            for layer in range(LAYERS)
        ]
    )
    up_grad = jnp.stack([reduced[UP, layer] for layer in range(LAYERS)])
    down_grad = jnp.stack([reduced[DOWN, layer].T for layer in range(LAYERS)])
    return (
        output,
        loss[0, 0],
        grad,
        context_grad,
        jnp.swapaxes(time, 0, 1),
        self_grad,
        cross_grad,
        out_grad,
        up_grad,
        down_grad,
        jnp.swapaxes(bias, 0, 1),
        key_sums,
        gain_sums,
        hidden_sums,
        jnp.swapaxes(out_sums, 0, 1),
        gain,
        shift,
        jnp.swapaxes(mods, 0, 1),
    )


def solution(mesh):
    COLLECTIVES.clear()
    rows = P(DP, None)
    col_in = P(None, None, DP, TENSOR)
    col_out = P(None, None, TENSOR, DP)
    up, down = P(None, DP, TENSOR), P(None, TENSOR, DP)
    vec, mat = P(None, TENSOR), P(None, None, TENSOR)
    return jax.shard_map(
        per_device,
        mesh=mesh,
        in_specs=(rows, rows, P(), rows, P(), P(DP), P(None, DP))
        + (col_in, col_in, col_out, up, down)
        + (mat, vec, mat, vec, P(), P(), P(), P()),
        out_specs=(rows, P(), rows, rows, P())
        + (col_in, col_in, col_out, up, down)
        + (mat, vec, mat, vec, P(), P(), P(), P()),
        check_vma=False,
    )
```

```python
import functools
import math

import jax
import jax.numpy as jnp
import numpy as np
from jax import lax
from jax.experimental import pallas as pl
from jax.experimental.pallas import tpu as pltpu
from jax.sharding import PartitionSpec as P

BEFORE = "before"
BIAS = "bias"
BRANCH = "branch"
CONTEXT = "context"
COSINE = "cosine"
CROSS = "cross"
DOWN = "down"
DP = "dp"
GAIN = "gain"
GELU_B_NAME = "gelu_b"
GRAD = "grad"
HIDDEN = "hidden"
HIDDEN_F = "hidden_f"
KEY = "key"
KEY_VALUE = "key_value"
LOSS = "loss"
MATRIX_GRAD = "matrix_grad"
NEW_GRAD = "new_grad"
NORMAL = "normal"
NORMAL_F = "normal_f"
OTHERS = "others"
OUT = "out"
OUT0 = "out0"
OUTPUT = "output"
QUERY = "query"
QUERY_B = "query_b"
QUERY_GRAD = "query_grad"
QUERY_ROT = "query_rot"
RESULT = "result"
SELF = "self"
SELF_GRAD = "self_grad"
SHIFT = "shift"
SINE = "sine"
SLOPE = "slope"
TENSOR = "tensor"
TEXT = "text"
TEXT_GRAD = "text_grad"
TEXT_KB = "text_kb"
TEXT_MATRIX = "text_matrix"
TEXT_VB = "text_vb"
TEXT_WEIGHT = "text_weight"
UP = "up"
WEIGHT = "weight"
MESH = pl.DeviceIdType.MESH
F32, BF16 = jnp.float32, jnp.bfloat16
NN = (((1,), (0,)), ((), ()))
NT = (((1,), (1,)), ((), ()))
TN = (((0,), (0,)), ((), ()))
HEAD_DIM = 128
HOLD = 4
LAYERS = 2
CHAIN = 4
CHUNK = 32
EPS = 1e-06
LOG2E = math.log2(math.e)
SCALE = 1.0 / math.sqrt(HEAD_DIM)
VMEM_BYTES = 60 * 2**20


def dot(left, right, dims=NN, exact=False):
    precision = lax.Precision.HIGHEST if exact else None
    return lax.dot_general(left, right, dims, precision=precision, preferred_element_type=F32)


def rope_table(head_size):
    third = head_size // 6
    spans = [head_size - 4 * third, 2 * third, 2 * third]
    table = np.zeros((3, head_size), np.float32)
    start_col = 0
    for component in range(3):
        for pair_index in range(spans[component] // 2):
            freq_value = 10000.0 ** (-(2.0 * pair_index) / spans[component])
            table[component, start_col + 2 * pair_index] = freq_value
            table[component, start_col + 2 * pair_index + 1] = freq_value
        start_col += spans[component]
    return table


def signal(**device):
    pl.semaphore_signal(
        pltpu.get_barrier_semaphore(), inc=1, device_id=device, device_id_type=MESH
    )


def bits_of_dp():
    return max(lax.axis_size(DP).bit_length() - 1, 1)


def flip(index, mask):
    result, bit = index, 0
    while mask >> bit:
        if mask >> bit & 1:
            half = 1 << bit
            result = result + half - 2 * half * lax.rem(index // half, 2)
        bit += 1
    return result


def greet(side, tensor, masks):
    place, me = lax.axis_index(TENSOR), lax.axis_index(DP)
    if tensor:
        for step in range(1, CHAIN):
            signal(tensor=lax.rem(place + step, CHAIN))
    for mask in masks:
        signal(dp=flip(me, mask))
    side.load(False)
    pl.semaphore_wait(
        pltpu.get_barrier_semaphore(), (CHAIN - 1 if tensor else 0) + len(masks)
    )


def holders():
    me = lax.axis_index(DP)
    return flip(me, 1), flip(me, 2)


def send(src, dst, send_sem, recv_sem, **device):
    return pltpu.make_async_remote_copy(
        src_ref=src,
        dst_ref=dst,
        send_sem=send_sem,
        recv_sem=recv_sem,
        device_id=device,
        device_id_type=MESH,
    )


def masks_over(bits):
    masks = [0]
    for bit in bits:
        masks += [mask | 1 << bit for mask in masks]
    return masks


def halves_of(size):
    cut = (size // 2 + 15) // 16 * 16
    return ((0, cut), (cut, size - cut))


def half_orders(bits):
    rising = list(range(1, bits))
    return (rising, rising[::-1])


class Job:
    phase = 0
    wave = 0
    name = None
    ended = False
    midway = False

    def middle(self):
        pass

    def move(self, target):
        while self.phase < min(target, self.bits - 1):
            self.phase += 1
            self.advance(self.phase)


class Gather(Job):
    def __init__(self, source, layer, name=None, wave=0, held=False):
        self.layer, self.name, self.wave, self.is_held = layer, name, wave, held
        self.operands = [source]
        shape = source.shape[1:]
        self.lead = shape[:-2]
        self.size = shape[-2]
        devices = lax.axis_size(DP)
        self.outs = [(self.lead + (self.size * devices, shape[-1]), source.dtype)]
        self.spaces = [pl.ANY]
        self.bits = bits_of_dp()
        plan = []
        for half, order in enumerate(half_orders(self.bits)):
            for phase, bit in enumerate(order):
                for mask in masks_over(order[:phase]):
                    plan.append((phase, half, bit, mask))
        for mask in masks_over(range(1, self.bits)):
            plan.append((self.bits - 1, None, 0, mask))
        self.plan = plan
        count = len(plan)
        self.scratch = [
            pltpu.SemaphoreType.DMA((count,)),
            pltpu.SemaphoreType.DMA((count,)),
            pltpu.SemaphoreType.DMA,
        ]
        if held:
            self.scratch += [
                pltpu.VMEM(self.outs[0][0], source.dtype),
                pltpu.SemaphoreType.DMA,
            ]

    def key(self):
        return ("gather", self.layer, self.outs[0][0], self.wave, self.is_held)

    def bind(self, sources, outs, scratch):
        self.source = sources[0].at[self.layer]
        self.out = outs[0]
        self.send_sems, self.recv_sems, self.own_sem = scratch[:3]
        self.store = None
        if self.is_held:
            held, sem = scratch[3:]
            self.store = pltpu.make_async_copy(held, self.out, sem)
            self.out = held

    def block(self, ref, index, half):
        low, size = (0, self.size) if half is None else halves_of(self.size)[half]
        start = low if index is None else index * self.size + low
        rows = pl.ds(pl.multiple_of(start, 16), size)
        return ref.at[:, rows] if self.lead else ref.at[rows]

    def copies(self, phase, own=None, only=None):
        me = lax.axis_index(DP)
        for number, (step, half, bit, mask) in enumerate(self.plan):
            if only is not None and mask not in only:
                continue
            if step == phase and own in (None, mask == 0):
                index = flip(me, mask)
                source = (
                    self.block(self.source, None, half)
                    if mask == 0
                    else self.block(self.out, index, half)
                )
                yield send(
                    source,
                    self.block(self.out, index, half),
                    self.send_sems.at[number],
                    self.recv_sems.at[number],
                    dp=flip(me, 1 << bit),
                )

    def own_copy(self):
        me = lax.axis_index(DP)
        return pltpu.make_async_copy(
            self.source, self.block(self.out, me, None), self.own_sem
        )

    def start(self):
        for phase in range(self.bits):
            for copy in self.copies(phase, True):
                copy.start()
        self.own_copy().start()

    def middle(self):
        if self.bits == 3 and not self.midway:
            self.midway = True
            for copy in self.copies(1, True):
                copy.wait_recv()
            for copy in self.copies(2, only=(2, 4)):
                copy.start()

    def advance(self, phase):
        if phase == self.bits - 1 == 2:
            self.middle()
            for copy in self.copies(1, False):
                copy.wait_recv()
            for copy in self.copies(2, only=(6,)):
                copy.start()
            return
        for copy in self.copies(phase - 1):
            copy.wait_recv()
        for copy in self.copies(phase, False):
            copy.start()

    def finish(self):
        for copy in self.copies(self.bits - 1):
            copy.wait_recv()
        for phase in range(self.bits):
            for copy in self.copies(phase):
                copy.wait_send()
        self.own_copy().wait()
        if self.store is not None:
            self.store.start()


class Scatter(Job):
    def __init__(self, source=None, name=None, shape=None):
        self.name = name
        self.operands = [] if source is None else [source]
        shape = source.shape if shape is None else shape
        self.bits = bits_of_dp()
        self.size = shape[0] // lax.axis_size(DP)
        self.width = shape[1]
        self.outs = [((self.size, self.width), F32)]
        self.spaces = [pltpu.VMEM]
        self.slots = 1 << self.bits - 1
        orders = [order[::-1] for order in half_orders(self.bits)]
        plan = [(0, None, 0, mask, mask >> 1) for mask in masks_over(range(1, self.bits))]
        for half, order in enumerate(orders):
            for phase, bit in enumerate(order):
                kept = masks_over(order[phase + 1 :])
                for place, mask in enumerate(kept):
                    plan.append((phase + 1, half, bit, mask, place))
        self.plan = plan
        count = len(plan)
        buffers = [pltpu.VMEM((self.slots, self.size, self.width), BF16)]
        buffers += buffers * len(self.operands)
        for phase in range(1, self.bits):
            places = 1 << self.bits - 1 - phase
            buffers += [
                pltpu.VMEM((places, size, self.width), BF16)
                for _, size in halves_of(self.size)
            ]
        self.scratch = buffers + [
            pltpu.SemaphoreType.DMA((count,)),
            pltpu.SemaphoreType.DMA((count,)),
            pltpu.SemaphoreType.DMA((self.slots,)),
        ]

    def key(self):
        return ("scatter", self.width, len(self.operands))

    def bind(self, sources, outs, scratch):
        self.out = outs[0]
        self.landed, self.own = scratch[0], None
        scratch = scratch[1:]
        if sources:
            self.source, self.own = sources[0], scratch[0]
            scratch = scratch[1:]
        self.parts = scratch[:-3]
        self.send_sems, self.recv_sems, self.own_sems = scratch[-3:]

    def rows(self, index):
        return pl.ds(pl.multiple_of(index * self.size, 16), self.size)

    def held(self, mask, low, size):
        if self.own is not None:
            return self.own.at[mask >> 1, pl.ds(pl.multiple_of(low, 16), size)]
        start = flip(lax.axis_index(DP), mask) * self.size + low
        return self.source.at[pl.ds(pl.multiple_of(start, 16), size)]

    def copies(self, phase):
        me = lax.axis_index(DP)
        for number, (step, half, bit, mask, place) in enumerate(self.plan):
            if step != phase:
                continue
            if phase == 0:
                source = self.source.at[self.rows(flip(me, mask | 1))]
                target = self.landed.at[mask >> 1]
            else:
                low, size = halves_of(self.size)[half]
                source = self.held(mask | 1 << bit, low, size)
                target = self.parts[2 * (phase - 1) + half].at[place]
            yield send(
                source,
                target,
                self.send_sems.at[number],
                self.recv_sems.at[number],
                dp=flip(me, 1 << bit),
            )

    def own_copies(self):
        me = lax.axis_index(DP)
        if self.own is not None:
            for slot in range(self.slots):
                yield pltpu.make_async_copy(
                    self.source.at[self.rows(flip(me, slot << 1))],
                    self.own.at[slot],
                    self.own_sems.at[slot],
                )

    def start(self):
        for copy in self.copies(0):
            copy.start()
        for copy in self.own_copies():
            copy.start()

    def add(self, phase):
        for copy in self.copies(phase):
            copy.wait_recv()
        if phase == 0:
            for copy in self.own_copies():
                copy.wait()
            for slot in range(self.slots):

                def step(rows, index, slot=slot):
                    held = self.held(slot << 1, index * 16, 16)
                    held[...] = held[...] + self.landed[slot, rows]

                loop_rows(self.size, 16, step)
            return
        for number, (step, half, bit, mask, place) in enumerate(self.plan):
            if step == phase:
                low, size = halves_of(self.size)[half]
                part = self.parts[2 * (phase - 1) + half]

                def step(rows, index, mask=mask, place=place, low=low, part=part):
                    held = self.held(mask, low + index * 16, 16)
                    if phase == self.bits - 1:
                        target = pl.ds(pl.multiple_of(low + index * 16, 16), 16)
                        self.out[target] = held[...].astype(F32) + part[place, rows].astype(F32)
                    else:
                        held[...] = held[...] + part[place, rows]

                loop_rows(size, 16, step)

    def advance(self, phase):
        self.add(phase - 1)
        for copy in self.copies(phase):
            copy.start()

    def finish(self):
        self.add(self.bits - 1)
        for phase in range(self.bits):
            for copy in self.copies(phase):
                copy.wait_send()


class Late:
    def __init__(self, name, value, low=None, high=None, lazy=False):
        self.name, self.value, self.low, self.high = name, value, low, high
        self.lazy = lazy
        shape = value.shape
        if high is not None:
            shape = (high - low,) + shape[1:]
        elif low is not None:
            shape = shape[1:]
        self.scratch = [pltpu.VMEM(shape, value.dtype), pltpu.SemaphoreType.DMA]

    def source(self, ref):
        if self.high is not None:
            return ref.at[self.low : self.high]
        return ref if self.low is None else ref.at[self.low]


class Early:
    def __init__(self, name, shape, kind, over=None):
        self.name, self.shape, self.kind, self.over = name, shape, kind, over
        self.scratch = [pltpu.SemaphoreType.DMA]
        if over is None:
            self.scratch = [pltpu.VMEM(shape, kind)] + self.scratch


class Side:
    def __init__(self, jobs):
        self.jobs = jobs
        self.masks = [1 << bit for bit in range(bits_of_dp())] if jobs else []
        self.loads, self.stores, self.open = {}, {}, []
        self.first_loads, self.waiting = [], []
        self.late_after = False

    def load(self, lazy):
        for item in [item for item in self.waiting if item[0] == lazy]:
            item[1].start()
            self.waiting.remove(item)

    def need(self, *names):
        for name in names:
            self.loads[name].wait()

    def store(self, *names):
        for name in names:
            self.stores[name].start()
            self.open.append(name)

    def start(self, wave=0):
        for job in self.jobs:
            if job.operands and job.wave == wave:
                job.start()
        while self.first_loads:
            self.first_loads.pop(0).wait()
            if not self.first_loads and not self.late_after:
                self.load(True)

    def launch(self, name, source):
        for job in self.jobs:
            if job.name == name:
                job.source = source
                job.start()

    def move(self, target, *names):
        for job in self.jobs:
            if not names or job.name in names:
                job.move(target)

    def early(self):
        self.move(bits_of_dp() - 2)

    def late(self):
        self.move(bits_of_dp() - 1)

    def middle(self):
        self.early()
        for job in self.jobs:
            job.middle()

    def finish(self, *names):
        for job in self.jobs:
            if not job.ended and (not names or job.name in names):
                job.move(job.bits - 1)
                job.finish()
                job.ended = True

    def close(self):
        for name in self.stores:
            if name not in self.open:
                self.store(name)
        for copy in self.stores.values():
            copy.wait()
        for job in self.jobs:
            if isinstance(job, Gather) and job.store is not None:
                job.store.wait()


class Exchange:
    def __init__(self, slots, send_sems, recv_sems):
        self.slots = slots
        place = lax.axis_index(TENSOR)
        self.place = place
        self.copies = [
            send(
                slots.at[place],
                slots.at[place],
                send_sems.at[step - 1],
                recv_sems.at[step - 1],
                tensor=lax.rem(place + step, CHAIN),
            )
            for step in range(1, CHAIN)
        ]

    def start(self, rows):
        self.slots[self.place] = rows
        for copy in self.copies:
            copy.start()

    def finish(self):
        for copy in self.copies:
            copy.wait()


def stat_rows(squares, row):
    count, width = squares.shape
    ones = jnp.ones((8, width), F32)
    sums = dot(ones, squares, NT, exact=True)
    index = lax.broadcasted_iota(jnp.int32, sums.shape, 0)
    return jnp.where(index == row, sums, 0.0)


def stat_column(slots, row, lanes):
    gathered = jnp.concatenate([slots[place] for place in range(CHAIN)], axis=0)
    index = lax.broadcasted_iota(jnp.int32, (8 * CHAIN, lanes), 0)
    pick = jnp.where(lax.rem(index, 8) == row, 1.0, 0.0)
    return dot(gathered, pick, TN, exact=True)


class Chain:
    def __init__(self, part, total, buffers, sems):
        self.part, self.total = part, total
        self.came, self.pair, self.peers = buffers
        self.sems = sems
        place = lax.axis_index(TENSOR)
        self.is_end = (place == 0) | (place == 3)
        self.is_mid = jnp.logical_not(self.is_end)
        self.inner = jnp.where(place == 0, 1, 2)
        self.outer = jnp.where(place == 1, 0, 3)
        self.peer = 3 - place
        self.chunks = part.shape[0] // CHUNK
        self.closed = False

    @staticmethod
    def scratch(rows, width):
        chunks = rows // CHUNK
        return [pltpu.VMEM((rows, width), BF16)] * 4 + [pltpu.SemaphoreType.DMA((6, chunks))]

    def rows(self, k):
        return pl.ds(pl.multiple_of(k * CHUNK, CHUNK), CHUNK)

    def copy(self, src, dst, kind, k, device):
        return send(
            src.at[self.rows(k)],
            dst.at[self.rows(k)],
            self.sems.at[2 * kind, k],
            self.sems.at[2 * kind + 1, k],
            tensor=device,
        )

    def inward(self, k, device):
        return self.copy(self.part, self.came, 0, k, device)

    def across(self, k):
        return self.copy(self.pair, self.peers, 1, k, self.peer)

    def outward(self, k, device):
        return self.copy(self.total, self.total, 2, k, device)

    def begin(self, low, count):
        @pl.when(self.is_end)
        def _():
            def step(k, carry):
                self.inward(low + k, self.inner).start()
                return carry

            lax.fori_loop(0, count, step, 0)

    def first(self, k):
        self.inward(k, self.outer).wait_recv()
        rows = self.rows(k)
        self.pair[rows] = (self.part[rows].astype(F32) + self.came[rows].astype(F32)).astype(BF16)
        self.across(k).start()

    def second(self, k):
        self.across(k).wait_recv()
        rows = self.rows(k)
        self.total[rows] = (self.pair[rows].astype(F32) + self.peers[rows].astype(F32)).astype(
            BF16
        )
        self.outward(k, self.outer).start()

    def serve(self, k):
        @pl.when(self.is_mid)
        def _():
            self.first(k)

            @pl.when(k > 0)
            def _():
                self.second(jnp.maximum(k - 1, 0))

    def segment(self, low, high, closed, upto):
        @pl.when(self.is_mid)
        def _():
            def both(k, carry):
                self.first(k)

                @pl.when(k > 0)
                def _():
                    self.second(jnp.maximum(k - 1, 0))

                return carry

            lax.fori_loop(low, high, both, 0)
            if high == self.chunks and not self.closed:
                self.second(self.chunks - 1)

        self.closed = self.closed or high == self.chunks

        @pl.when(self.is_end)
        def _():
            def close(k, carry):
                self.inward(k, self.inner).wait_send()
                self.outward(k, self.inner).wait_recv()
                return carry

            lax.fori_loop(closed, upto, close, 0)

    def drain(self, low, early=None, late=None):
        done, last = 0, self.chunks
        if early is not None:
            cut = low + (last - low) // 4
            self.segment(low, cut, done, cut - 1)
            low, done = cut, cut - 1
            early()
        if late is not None:
            cut = low + (last - low) * 5 // 8
            self.segment(low, cut, done, cut - 1)
            low, done = cut, cut - 1
            late()
        self.segment(low, last, done, last)
        self.close()

    def close(self):
        @pl.when(self.is_mid)
        def _():
            def close(k, carry):
                self.across(k).wait_send()
                self.outward(k, self.outer).wait_send()
                return carry

            lax.fori_loop(0, self.chunks, close, 0)


COLLECTIVES = {}


def collective_of(key):
    return COLLECTIVES.setdefault(key, 1 + len(COLLECTIVES))


def run(name, kernel, ins, outs, scratch=(), remote=True, jobs=(), scalars=0, micros=0):
    whole = pl.BlockSpec(memory_space=pltpu.VMEM)
    far = pl.BlockSpec(memory_space=pl.ANY)
    if remote:
        ins = tuple(ins[:scalars]) + tuple(
            item if isinstance(item, Late) else Late(None, item) for item in ins[scalars:]
        )
        outs = tuple(
            item if isinstance(item, Early) or len(item) > 2 else Early(place, *item)
            for place, item in enumerate(outs)
        )
    job_ins = [item for job in jobs for item in job.operands]
    job_outs = [item for job in jobs for item in job.outs]
    job_spaces = [pl.BlockSpec(memory_space=space) for job in jobs for space in job.spaces]
    moved = [item for item in tuple(ins) + tuple(outs) if isinstance(item, (Late, Early))]
    own_scratch = list(scratch) + [item for job in jobs for item in job.scratch]

    def body(*refs):
        side = Side(jobs)
        refs = list(refs)

        def take(count):
            taken = refs[:count]
            del refs[:count]
            return taken

        own_in, side_in = take(len(ins)), take(len(job_ins))
        own_out, side_out = take(len(outs)), take(len(job_outs))
        own = take(len(scratch))
        for job in jobs:
            job.phase, job.ended, job.midway = 0, False, False
            job.bind(
                [side_in.pop(0) for _ in job.operands],
                [side_out.pop(0) for _ in job.outs],
                take(len(job.scratch)),
            )
        for place, item in enumerate(ins):
            if isinstance(item, Late):
                held, sem = take(2)
                copy = pltpu.make_async_copy(item.source(own_in[place]), held, sem)
                side.waiting.append((item.lazy, copy))
                if item.name is None:
                    side.first_loads.append(copy)
                side.loads[item.name] = copy
                own_in[place] = held
        for place, item in enumerate(outs):
            if isinstance(item, Early):
                held = take(1)[0] if item.over is None else own_in[item.over]
                sem = take(1)[0]
                side.stores[item.name] = pltpu.make_async_copy(held, own_out[place], sem)
                own_out[place] = held
        if not remote:
            side.load(False)
        kernel(side, *own_in, *own_out, *own)
        side.close()

    key = (name,) + tuple(job.key() for job in jobs)
    shapes = [
        (item.shape, item.kind) if isinstance(item, Early) else item[:2] for item in outs
    ] + job_outs
    results = pl.pallas_call(
        body,
        out_shape=tuple(jax.ShapeDtypeStruct(shape, kind) for shape, kind in shapes),
        in_specs=[pl.BlockSpec(memory_space=pltpu.SMEM)] * scalars
        + [far if isinstance(item, Late) else whole for item in ins[scalars:]]
        + [far] * len(job_ins),
        out_specs=tuple(
            [far if isinstance(item, Early) or len(item) > 2 else whole for item in outs]
            + job_spaces
        ),
        scratch_shapes=own_scratch + [part for item in moved for part in item.scratch],
        cost_estimate=pl.CostEstimate(
            flops=0, bytes_accessed=micros * 3000000, transcendentals=0
        ),
        compiler_params=pltpu.CompilerParams(
            collective_id=collective_of(key) if remote else None,
            has_side_effects=remote,
            vmem_limit_bytes=VMEM_BYTES,
        ),
    )(*[item.value if isinstance(item, Late) else item for item in ins], *job_ins)
    return results[: len(outs)], results[len(outs) :]


def tiled_grad(left, right, store, serve, size=384):
    for tile in range(left.shape[1] // size):
        cols = slice(tile * size, (tile + 1) * size)
        store(tile, size, dot(left[:, cols], right[...], TN).astype(BF16))
        serve(tile)


def normed(hidden):
    center = hidden - jnp.mean(hidden, axis=-1, keepdims=True)
    inverse = lax.rsqrt(jnp.mean(center * center, axis=-1, keepdims=True) + EPS)
    return center * inverse, inverse


def norm_back(hidden, scale_row, grad):
    hat, inverse = normed(hidden)
    inner = grad * scale_row
    back = inverse * (
        inner
        - jnp.mean(inner, axis=-1, keepdims=True)
        - hat * jnp.mean(inner * hat, axis=-1, keepdims=True)
    )
    return back, hat


def loop_rows(total, size, body):
    def step(index, carry):
        body(pl.ds(pl.multiple_of(index * size, size), size), index)
        return carry

    lax.fori_loop(0, total // size, step, 0)


def add_sum(ref, row, block):
    ref[row : row + 1] += jnp.sum(block, axis=0, keepdims=True)


def turned(rows):
    lane = lax.broadcasted_iota(jnp.int32, rows.shape, 1)
    width = rows.shape[1]
    return jnp.where(
        lax.rem(lane, 2) == 0, -pltpu.roll(rows, width - 1, 1), pltpu.roll(rows, 1, 1)
    )


def head_cols(head):
    return slice(head * HEAD_DIM, (head + 1) * HEAD_DIM)


def inverse_rms(sums, features):
    return lax.rsqrt(sums / features + EPS)


MODS, OUT_BIAS, CROSS_GAIN, CROSS_SHIFT = 0, 6, 9, 10
KEY_BIAS, GAINS = 5, 6


def row_of(ref, index):
    return ref[index : index + 1]


def first_kernel(
    side,
    lengths,
    block_order,
    time_embed,
    modulation,
    out_bias,
    cross_gain,
    cross_shift,
    proj_bias,
    key_bias,
    norm_gains,
    ffn_bias,
    positions,
    table,
    base,
    context,
    counts,
    cosine,
    sine,
    nothing,
    *rest,
):
    rest = list(rest)
    packs = rest[: 3 * LAYERS]
    send_sems, recv_sems = rest[-2:]
    rest = rest[3 * LAYERS : -2]
    greet(side, True, side.masks)
    near, far = holders()
    tokens = counts.shape[2]
    clip = lax.axis_index(DP) // HOLD
    mine = (lengths[clip] - block_order[0] * tokens).astype(F32)
    counts[0] = jnp.full(counts.shape[1:], mine, F32)

    def copy(number, source, target, device):
        return send(
            counts.at[source],
            counts.at[target],
            send_sems.at[number],
            recv_sems.at[number],
            dp=device,
        )

    to_near, to_far, onward = copy(0, 0, 1, near), copy(1, 0, 2, far), copy(2, 2, 3, near)
    side.start()
    to_near.start()
    to_far.start()
    for layer in range(LAYERS):
        rows_d, rows_w, rows_f = packs[3 * layer : 3 * layer + 3]
        rows_d[...] = jnp.zeros(rows_d.shape, F32)
        rows_w[...] = jnp.zeros(rows_w.shape, F32)
        for row in range(6):
            embed = jnp.zeros((1, rows_d.shape[1]), F32)
            for index in range(time_embed.shape[1]):
                embed = embed + jnp.where(clip == index, row_of(time_embed.at[row], index), 0.0)
            rows_d[row : row + 1] = row_of(modulation.at[row], layer) + embed
        for row in range(3):
            rows_d[OUT_BIAS + row : OUT_BIAS + row + 1] = row_of(out_bias.at[row], layer)
        rows_d[CROSS_GAIN : CROSS_GAIN + 1] = row_of(cross_gain, layer)
        rows_d[CROSS_SHIFT : CROSS_SHIFT + 1] = row_of(cross_shift, layer)
        for row in range(5):
            rows_w[row : row + 1] = row_of(proj_bias.at[row], layer)
        rows_w[KEY_BIAS : KEY_BIAS + 1] = row_of(key_bias, layer)
        rows_w[GAINS : GAINS + 4] = norm_gains[layer]
        rows_f[...] = row_of(ffn_bias, layer)
    nothing[...] = jnp.zeros(nothing.shape, F32)
    angles = dot(positions[...].astype(F32), table[...], TN, exact=True)
    cosine[...] = jnp.cos(angles)
    sine[...] = jnp.sin(angles)
    to_far.wait_recv()
    onward.start()
    side.move(1, SELF)
    side.start(1)
    to_near.wait_recv()
    onward.wait_recv()
    for copy in (to_near, to_far, onward):
        copy.wait_send()
    side.finish(SELF)
    attend_body(
        side, base, None, None, packs[0], packs[1], side.jobs[0].out, cosine, sine, counts, context, rest
    )


def add_branch(base, tot, bias_row, gate_row):
    return base + (tot.astype(F32) + bias_row) * gate_row


def attend_kernel(
    side, base, tot, rows_before, rows_d, rows_w, weight, cosine, sine, counts, *refs
):
    greet(side, True, [1, 2])
    side.start()
    attend_body(
        side, base, tot, rows_before, rows_d, rows_w, weight, cosine, sine, counts, None, list(refs)
    )


def attend_body(
    side, base, tot, rows_before, rows_d, rows_w, weight, cosine, sine, counts, context, refs
):
    first = context is not None
    hidden, normal, query, key, query_rot, key_value, slots = refs[:7]
    others, result, lse = refs[7:10]
    clip_context = refs[10] if first else None
    scores, send_sems, recv_sems, hold_sends, hold_recvs = refs[-5:]
    tokens, width = query.shape
    features = hidden.shape[1]
    heads = width // HEAD_DIM
    scale_row = 1.0 + row_of(rows_d, MODS + 1)
    shift_row = row_of(rows_d, MODS)

    def project(rows, index):
        if first:
            block = base[rows].astype(F32)
        else:
            block = add_branch(
                base[rows], tot[rows], row_of(rows_before, OUT_BIAS + 2), row_of(rows_before, MODS + 5)
            )
        hidden[rows] = block
        block = (normed(block)[0] * scale_row + shift_row).astype(BF16)
        normal[rows] = block
        query[rows] = dot(block, weight[0]) + row_of(rows_w, 0)
        key[rows] = dot(block, weight[1]) + row_of(rows_w, KEY_BIAS)
        value = (dot(block, weight[2]) + row_of(rows_w, 1)).astype(BF16)
        for head in range(heads):
            key_value[head, 1, rows] = value[:, head_cols(head)]

    if not first:
        side.need(WEIGHT)
    loop_rows(tokens, 256, project)
    side.store(HIDDEN, NORMAL, QUERY, KEY)
    exchange = Exchange(slots, send_sems, recv_sems)
    exchange.start(
        stat_rows(query[...] * query[...], 0) + stat_rows(key[...] * key[...], 1)
    )
    side.early()
    near, far = holders()

    def copy(source, target, number, device):
        return send(source, target, hold_sends.at[number], hold_recvs.at[number], dp=device)

    to_near = copy(key_value, others.at[0], 0, near)
    to_far = [
        copy(key_value.at[head], others.at[1, head], 1 + head, far) for head in range(heads)
    ]
    onward = [
        copy(others.at[1, head], others.at[2, head], 1 + heads + head, near)
        for head in range(heads)
    ]
    exchange.finish()
    query_inv = inverse_rms(stat_column(slots, 0, HEAD_DIM), features)
    key_inv = inverse_rms(stat_column(slots, 1, HEAD_DIM), features)
    if not first:
        side.need(COSINE, SINE)
    for head in range(heads):
        cols = head_cols(head)
        rows = key[:, cols] * key_inv * rows_w[GAINS + 1 : GAINS + 2, cols]
        key_value[head, 0] = (rows * cosine[...] + turned(rows) * sine[...]).astype(BF16)
        to_far[head].start()
    to_near.start()
    text = []
    if first:
        place = lax.rem(lax.axis_index(DP), HOLD)
        size = context.shape[0]

        def block(index):
            return clip_context.at[pl.ds(pl.multiple_of(index * size, 16), size)]

        low = 1 + 2 * heads
        clip_context[pl.ds(pl.multiple_of(place * size, 16), size)] = context[...]
        text = [
            copy(block(place), block(place), low, near),
            copy(block(place), block(place), low + 1, far),
            copy(block(flip(place, 2)), block(flip(place, 2)), low + 2, near),
        ]
        text[0].start()
        text[1].start()
    for head in range(heads):
        cols = head_cols(head)
        rows = query[:, cols] * query_inv * rows_w[GAINS : GAINS + 1, cols]
        query_rot[:, cols] = (rows * cosine[...] + turned(rows) * sine[...]).astype(BF16)
    side.store(QUERY_ROT)
    side.middle()

    def score(head, slot, keys):
        block = dot(keys, query_rot[:, head_cols(head)], NT) * (SCALE * LOG2E)
        scores[head, slot] = jnp.where(below(counts, slot, block.shape), block, -1e30)

    for head in range(heads):
        score(head, 0, key_value[head, 0])
    to_near.wait_recv()
    for head in range(heads):
        score(head, 1, others[0, head, 0])
    lse[...] = jnp.zeros(lse.shape, F32)
    for head in range(heads):
        to_far[head].wait_recv()
        onward[head].start()
        if head == 0:
            side.late()
        score(head, 2, others[1, head, 0])
        onward[head].wait_recv()
        score(head, 3, others[2, head, 0])
        top = jnp.max(scores[head, 0], axis=0, keepdims=True)
        for slot in range(1, HOLD):
            top = jnp.maximum(top, jnp.max(scores[head, slot], axis=0, keepdims=True))
        total = jnp.zeros_like(top)
        summed = jnp.zeros((HEAD_DIM, tokens), F32)
        for slot in range(HOLD):
            values = key_value[head, 1] if slot == 0 else others[slot - 1, head, 1]
            probs = jnp.exp2(scores[head, slot] - top)
            total = total + jnp.sum(probs, axis=0, keepdims=True)
            summed = summed + dot(values, probs.astype(BF16), TN)
        result[:, head_cols(head)] = (summed / total).T.astype(BF16)
        lse[head : head + 1] = top + jnp.log2(total)
    if first:
        text[1].wait_recv()
        text[2].start()
        text[0].wait_recv()
        text[2].wait_recv()
    for item in [to_near] + to_far + onward + text:
        item.wait_send()
    side.finish()


def below(counts, slot, shape):
    index = lax.broadcasted_iota(jnp.int32, shape, 0).astype(F32)
    return index < counts[slot, 0:1]


def softmax_back(scores, lse_row, mask):
    probs = jnp.exp2(scores * (SCALE * LOG2E) - lse_row)
    return probs if mask is None else jnp.where(mask, probs, 0.0)


def out_sum_kernel(
    side,
    rows_in,
    weight,
    context,
    text_weight,
    rows_w,
    total,
    text_key,
    text_kb,
    text_vb,
    slots,
    send_sems,
    recv_sems,
    part,
    came,
    pair,
    peers,
    sems,
):
    greet(side, True, side.masks)
    side.start()
    chain = Chain(part, total, (came, pair, peers), sems)
    tokens, features = total.shape
    per_block = 128 // CHUNK

    def project(rows, index):
        part[rows] = dot(rows_in[rows], weight[...], NT).astype(BF16)
        chain.begin(index * per_block, per_block)

    side.need(OUT)
    loop_rows(tokens, 128, project)
    side.need(CONTEXT, TEXT_WEIGHT)
    text_count, width = text_key.shape
    blocks = text_count // 128

    def text(rows, index):
        block = context[rows]
        text_key[rows] = dot(block, text_weight[0]) + row_of(rows_w, 3)
        chain.serve(2 * index)
        text_vb[rows] = (dot(block, text_weight[1]) + row_of(rows_w, 4)).astype(BF16)
        chain.serve(2 * index + 1)

    loop_rows(text_count, 128, text)
    exchange = Exchange(slots, send_sems, recv_sems)

    def early():
        side.early()
        exchange.start(stat_rows(text_key[...] * text_key[...], 0))

    chain.drain(2 * blocks, early, side.middle)
    exchange.finish()
    text_inv = inverse_rms(stat_column(slots, 0, HEAD_DIM), features)
    for head in range(width // HEAD_DIM):
        cols = head_cols(head)
        text_kb[:, cols] = (
            text_key[:, cols] * text_inv * rows_w[GAINS + 3 : GAINS + 4, cols]
        ).astype(BF16)
    side.finish()


def cross_ffn_kernel(
    gathered,
    side,
    base,
    tot,
    rows_d,
    rows_w,
    rows_f,
    weight,
    text_kb,
    text_vb,
    out_weight,
    up,
    *refs,
):
    refs = list(refs)
    down = side.jobs[0].out if gathered else refs.pop(0)
    hidden, normal, query, query_b, result, lse, slots = refs[:7]
    hidden_f, normal_f, gelu_b, slope, total_f = refs[7:12]
    send_sems, recv_sems, total = refs[12:15]
    part, came, pair, peers, sems = refs[15:20]
    part_f, came_f, pair_f, peers_f, sems_f = refs[20:25]
    greet(side, True, side.masks)
    side.late_after = True
    side.start()
    chain = Chain(part, total, (came, pair, peers), sems)
    chain_f = Chain(part_f, total_f, (came_f, pair_f, peers_f), sems_f)
    tokens, width = query.shape
    features = hidden.shape[1]
    heads = width // HEAD_DIM

    def project(rows, index):
        block = add_branch(
            base[rows], tot[rows], row_of(rows_d, OUT_BIAS), row_of(rows_d, MODS + 2)
        )
        hidden[rows] = block
        block = normed(block)[0] * row_of(rows_d, CROSS_GAIN) + row_of(rows_d, CROSS_SHIFT)
        block = block.astype(BF16)
        normal[rows] = block
        query[rows] = dot(block, weight[...]) + row_of(rows_w, 2)

    side.need(WEIGHT)
    side.load(True)
    loop_rows(tokens, 256, project)
    side.store(HIDDEN, NORMAL, QUERY)
    exchange = Exchange(slots, send_sems, recv_sems)
    exchange.start(stat_rows(query[...] * query[...], 0))
    exchange.finish()
    query_inv = inverse_rms(stat_column(slots, 0, HEAD_DIM), features)
    side.need(TEXT_KB, TEXT_VB)
    lse[...] = jnp.zeros(lse.shape, F32)
    for head in range(heads):
        cols = head_cols(head)
        query_b[:, cols] = (
            query[:, cols] * query_inv * rows_w[GAINS + 2 : GAINS + 3, cols]
        ).astype(BF16)
        scores = dot(text_kb[:, cols], query_b[:, cols], NT) * (SCALE * LOG2E)
        top = jnp.max(scores, axis=0, keepdims=True)
        probs = jnp.exp2(scores - top)
        amount = jnp.sum(probs, axis=0, keepdims=True)
        summed = dot(text_vb[:, cols], probs.astype(BF16), TN)
        result[:, cols] = (summed / amount).T.astype(BF16)
        lse[head : head + 1] = top + jnp.log2(amount)
    per_block = 128 // CHUNK

    def project_out(rows, index):
        part[rows] = dot(result[rows], out_weight[...], NT).astype(BF16)
        chain.begin(index * per_block, per_block)

    side.store(QUERY_B, RESULT)
    side.need(OUT)
    loop_rows(tokens, 128, project_out)
    side.move(1, DOWN)
    side.start(1)
    scale_row = 1.0 + row_of(rows_d, MODS + 4)
    shift_row = row_of(rows_d, MODS + 3)

    def rows_of(rows):
        block = add_branch(hidden[rows], total[rows], row_of(rows_d, OUT_BIAS + 1), 1.0)
        hidden_f[rows] = block
        block = (normed(block)[0] * scale_row + shift_row).astype(BF16)
        normal_f[rows] = block
        return block

    def inner(rows, block, low, high):
        z = dot(block, up[:, low:high]) + rows_f[:, low:high]
        square = z * z
        tanh = jnp.tanh(GELU_A * z * (1.0 + GELU_B * square))
        side_value = 0.5 * (1.0 + tanh)
        gelu_b[rows, low:high] = (z * side_value).astype(BF16)
        slope[rows, low:high] = (
            side_value
            + 0.5 * z * (1.0 - tanh * tanh) * (GELU_A * (1.0 + 3.0 * GELU_B * square))
        ).astype(BF16)

    def before_second():
        if gathered:
            side.finish(DOWN)
        else:
            side.need(DOWN)

    def after(left):
        side.store(HIDDEN_F, NORMAL_F, GELU_B_NAME, SLOPE)

    side.need(UP)
    mlp_loop(
        side, tokens, rows_of, inner, down, chain_f, gelu_b, before_second, after, chain
    )


def column_cuts(width):
    cuts, low = [], 0
    while low < width:
        high = low + 512 if width - low >= 1024 else width
        cuts.append((low, high))
        low = high
    return cuts


GELU_A = 0.7978845608028654
GELU_B = 0.044715


def mlp_loop(side, tokens, rows_of, inner, second, chain, middle, before_second, after, feed=None):
    size = 128
    per_block = size // CHUNK
    features, hidden_width = second.shape
    cuts = column_cuts(hidden_width)
    half = features // 2
    blocks = tokens // size
    if feed is not None:

        @pl.when(feed.is_mid)
        def _():
            feed.first(0)
            for k in range(1, per_block):
                feed.first(k)
                feed.second(k - 1)

    def step(index, carry):
        rows = pl.ds(pl.multiple_of(index * size, size), size)
        low = index * per_block

        def serve(offset):
            if feed is None:

                @pl.when(index > 0)
                def _():
                    chain.serve(jnp.maximum(low - per_block, 0) + offset)

                return
            if offset > 0:

                @pl.when(feed.is_mid & (index < blocks - 1))
                def _():
                    ahead = jnp.minimum(low + per_block, feed.chunks - per_block)
                    feed.first(ahead + offset)
                    feed.second(ahead + offset - 1)

            @pl.when(index == blocks - 1)
            def _():
                chain.serve(offset)

        if feed is not None:

            @pl.when(feed.is_mid)
            def _():
                @pl.when(index < blocks - 1)
                def _():
                    feed.first(jnp.minimum(low + per_block, feed.chunks - per_block))

                feed.second(low + per_block - 1)

            @pl.when(feed.is_end)
            def _():
                for offset in range(per_block):
                    feed.inward(low + offset, feed.inner).wait_send()
                    feed.outward(low + offset, feed.inner).wait_recv()

        block = rows_of(rows)
        served = 0
        for place, (left, right) in enumerate(cuts):
            inner(rows, block, left, right)
            if place % 2 == 1 and served < 2:
                serve(served)
                served += 1
        while served < 2:
            serve(served)
            served += 1

        @pl.when(index == 0)
        def _():
            before_second()

        for part_index in range(2):
            cols = slice(part_index * half, (part_index + 1) * half)
            chain.part[rows, cols] = dot(middle[rows], second[cols], NT).astype(BF16)
            if part_index == 0:
                serve(2)
        chain.begin(low, per_block)
        serve(3)
        if side.jobs:
            if feed is None:
                points = ((1, bits_of_dp() - 2), (blocks - 1, bits_of_dp() - 1))
            else:
                points = ((blocks - 1, bits_of_dp() - 2),)
            for point, target in points:

                @pl.when(index == point)
                def _(target=target):
                    side.move(target)

        return carry

    lax.fori_loop(0, blocks, step, 0)
    left = (blocks - 1) * per_block if feed is None else per_block
    left = after(left) or left
    chain.drain(left, None, None if feed is None else side.late)
    if feed is not None:
        feed.close()
    side.finish()


def ffn_back_kernel(
    joined,
    side,
    grad,
    *refs,
):
    refs = list(refs)

    def take(count):
        taken = refs[:count]
        del refs[:count]
        return taken

    if joined:
        branch, hidden, rows_above = take(3)
    else:
        teacher, counts = take(2)
    tot, rows_d, down, up, slope, normal, gelu_b = take(7)
    if joined:
        new_grad, sums_above = take(2)
    else:
        new_grad, output = take(2)
    (total, sums, bias_sum, up_grad, down_grad) = take(5)
    down_in, inner_b, stage, stage_sems, part, came, pair, peers, sems = refs
    greet(side, True, side.masks)
    side.late_after = True
    side.start()
    chain = Chain(part, total, (came, pair, peers), sems)
    tokens = grad.shape[0]
    sums[...] = jnp.zeros(sums.shape, F32)
    bias_sum[...] = jnp.zeros(bias_sum.shape, F32)
    if joined:
        sums_above[...] = jnp.zeros(sums_above.shape, F32)
        scale_row = 1.0 + row_of(rows_above, MODS + 1)

    def rows_of(rows):
        block = grad[rows]
        if joined:
            step = branch[rows].astype(F32)
            back, hat = norm_back(hidden[rows], scale_row, step)
            add_sum(sums_above, 0, step)
            add_sum(sums_above, 1, step * hat)
            block = block + back
            new_grad[rows] = block
        else:
            block = add_branch(
                block, tot[rows], row_of(rows_d, OUT_BIAS + 2), row_of(rows_d, MODS + 5)
            )
            output[rows] = block
            block = block - teacher[rows].astype(F32)
            place = lax.broadcasted_iota(jnp.int32, (block.shape[0], 1), 0) + rows.start
            block = jnp.where(place.astype(F32) < counts[0, 0:1, 0:1], block, 0.0)
            new_grad[rows] = block
            add_sum(sums, 2, block * block)
        add_sum(sums, 0, block * (tot[rows].astype(F32) + row_of(rows_d, OUT_BIAS + 2)))
        block = (block * row_of(rows_d, MODS + 5)).astype(BF16)
        down_in[rows] = block
        add_sum(sums, 1, block.astype(F32))
        return block

    def inner(rows, block, low, high):
        cols = (dot(block, down[:, low:high]) * slope[rows, low:high].astype(F32)).astype(BF16)
        inner_b[rows, low:high] = cols
        bias_sum[0:1, low:high] += jnp.sum(cols.astype(F32), axis=0, keepdims=True)

    def after(left):
        side.store(NEW_GRAD)
        if not joined:
            side.store(OUTPUT)
        side.need(NORMAL, GELU_B_NAME)
        copies = []

        def keep(target):
            def store(tile, size, block):
                number = len(copies)
                if number >= 2:
                    copies[number - 2].wait()
                stage[number % 2] = block
                copy = pltpu.make_async_copy(
                    stage.at[number % 2],
                    target.at[tile * size : (tile + 1) * size],
                    stage_sems.at[number % 2],
                )
                copy.start()
                copies.append(copy)

            return store

        def serve(tile):
            if left + tile < chain.chunks:
                chain.serve(left + tile)

        tiled_grad(normal, inner_b, keep(up_grad), serve, stage.shape[1])
        chain.segment(chain.chunks, chain.chunks, 0, 0)
        tiled_grad(down_in, gelu_b, keep(down_grad), lambda tile: None, stage.shape[1])
        copies[-2].wait()
        copies[-1].wait()
        return chain.chunks

    side.need(GRAD, DOWN, SLOPE)
    side.load(True)
    mlp_loop(
        side, tokens, rows_of, inner, up, chain, inner_b, lambda: side.need(UP), after
    )


def cross_back_kernel(
    side,
    grad,
    branch,
    hidden,
    rows_d,
    rows_w,
    out_weight,
    query,
    query_b,
    lse,
    slots_q,
    text_kb,
    text_vb,
    weight,
    normal,
    result,
    new_grad,
    text_grad,
    sums,
    width_sums,
    total,
    matrix_grad,
    out_in,
    query_grad_b,
    out_grad,
    query_n,
    slots,
    send_sems,
    recv_sems,
    part,
    came,
    pair,
    peers,
    sems,
):
    greet(side, True, side.masks)
    side.late_after = True
    side.start()
    chain = Chain(part, total, (came, pair, peers), sems)
    tokens, width = query.shape
    features = grad.shape[1]
    heads = width // HEAD_DIM
    gain = rows_w[GAINS + 2 : GAINS + 3]
    sums[...] = jnp.zeros(sums.shape, F32)
    width_sums[...] = jnp.zeros(width_sums.shape, F32)
    scale_row = 1.0 + row_of(rows_d, MODS + 4)

    def enter(rows, index):
        step = branch[rows].astype(F32)
        back, hat = norm_back(hidden[rows], scale_row, step)
        add_sum(sums, 0, step)
        add_sum(sums, 1, step * hat)
        block = grad[rows] + back
        new_grad[rows] = block
        block = block.astype(BF16)
        out_in[rows] = block
        add_sum(sums, 2, block.astype(F32))
        out_grad[rows] = dot(block, out_weight[...]).astype(BF16)

    side.need(OUT)
    side.load(True)
    loop_rows(tokens, 256, enter)
    side.store(NEW_GRAD)
    side.need(QUERY, QUERY_B, TEXT_KB, TEXT_VB)
    for head in range(heads):
        cols = head_cols(head)
        query_h, out_grad_h = query_b[:, cols], out_grad[:, cols]
        text_k, text_v = text_kb[:, cols], text_vb[:, cols]
        probs = softmax_back(dot(text_k, query_h, NT), lse[head : head + 1], None)
        prob_grad = dot(text_v, out_grad_h, NT)
        inner = jnp.sum(probs * prob_grad, axis=0, keepdims=True)
        score_b = (probs * (prob_grad - inner) * SCALE).astype(BF16)
        query_n[:, cols] = dot(text_k, score_b, TN).T
        text_grad[0, :, cols] = dot(score_b, query_h)
        text_grad[1, :, cols] = dot(probs.astype(BF16), out_grad_h)
    exchange = Exchange(slots, send_sems, recv_sems)
    exchange.start(stat_rows(query[...] * query_n[...] * gain, 0))
    inverse = inverse_rms(stat_column(slots_q, 0, HEAD_DIM), features)
    side.move(1)
    exchange.finish()
    term = stat_column(slots, 0, HEAD_DIM) * inverse * inverse * inverse / features
    for head in range(heads):
        cols = head_cols(head)
        width_sums[0:1, cols] = jnp.sum(
            query[:, cols] * query_n[:, cols] * inverse, axis=0, keepdims=True
        )
        block = inverse * gain[:, cols] * query_n[:, cols] - query[:, cols] * term
        block = block.astype(BF16)
        query_grad_b[:, cols] = block
        width_sums[1:2, cols] = jnp.sum(block.astype(F32), axis=0, keepdims=True)
    per_block = 128 // CHUNK

    def leave(rows, index):
        part[rows] = dot(query_grad_b[rows], weight[...], NT).astype(BF16)
        chain.begin(index * per_block, per_block)

    side.store(TEXT_GRAD)
    side.need(WEIGHT)
    loop_rows(tokens, 128, leave)
    side.need(NORMAL, RESULT)

    def keep(low):
        def store(tile, size, block):
            matrix_grad[tile * size : (tile + 1) * size, low : low + width] = block

        return store

    tiled_grad(normal, query_grad_b, keep(0), lambda tile: None if tile % 2 else chain.serve(tile // 2))
    tiled_grad(out_in, result, keep(width), lambda tile: None if tile % 2 else chain.serve(2 + tile // 2))
    side.store(MATRIX_GRAD)
    chain.drain(4, side.late)
    side.finish()


def attend_back_kernel(
    side,
    counts,
    grad,
    branch,
    hidden,
    rows_d,
    tot,
    out_weight,
    query,
    key_value,
    others,
    lse,
    text_grad,
    result,
    new_grad,
    matrix_grad,
    sums,
    query_grad,
    key_value_grad,
    text_sum,
    out_in,
    out_grad,
    probs,
    prob_grads,
    away,
    landed,
    text_away,
    text_landed,
    send_sems,
    recv_sems,
):
    greet(side, False, [1, 2])
    side.start()
    near, far = holders()
    tokens, width = query.shape
    heads = width // HEAD_DIM
    text_rows = text_sum.shape[1]
    sums[...] = jnp.zeros(sums.shape, F32)

    def copy(kind, head):
        return send(
            away.at[kind, head],
            landed.at[kind, head],
            send_sems.at[kind, head],
            recv_sems.at[kind, head],
            dp=far if kind == 1 else near,
        )

    def text_copy(kind):
        return send(
            text_away.at[kind],
            text_landed.at[kind],
            send_sems.at[kind, heads],
            recv_sems.at[kind, heads],
            dp=far if kind == 1 else near,
        )

    place = lax.rem(lax.axis_index(DP), HOLD)

    def text_part(slot):
        start = pl.multiple_of(flip(place, slot) * text_rows, text_rows)
        return text_grad[:, pl.ds(start, text_rows)]

    text_away[2] = text_part(3).astype(BF16)
    text_copy(2).start()
    text_away[0] = text_part(1).astype(BF16)
    text_copy(0).start()

    def enter(rows, index):
        step = branch[rows].astype(F32)
        back, hat = norm_back(hidden[rows], row_of(rows_d, CROSS_GAIN), step)
        add_sum(sums, 0, step * hat)
        add_sum(sums, 1, step)
        block = grad[rows] + back
        new_grad[rows] = block
        add_sum(sums, 2, block * (tot[rows].astype(F32) + row_of(rows_d, OUT_BIAS)))
        block = (block * row_of(rows_d, MODS + 2)).astype(BF16)
        out_in[rows] = block
        add_sum(sums, 3, block.astype(F32))
        out_grad[rows] = dot(block, out_weight[...]).astype(BF16)

    side.need(OUT)
    loop_rows(tokens, 256, enter)
    side.store(NEW_GRAD)
    side.need(QUERY, KEY_VALUE, OTHERS, RESULT)
    text_copy(2).wait_recv()
    text_away[1] = (text_part(2) + text_landed[2].astype(F32)).astype(BF16)
    text_copy(1).start()

    for head in range(heads):
        cols = head_cols(head)
        query_h, out_grad_h = query[:, cols], out_grad[:, cols]

        def pair_of(slot, head=head):
            if slot == 0:
                return key_value[head, 0], key_value[head, 1]
            return others[slot - 1, head, 0], others[slot - 1, head, 1]

        inner = jnp.zeros((1, tokens), F32)
        for slot in range(HOLD):
            keys, values = pair_of(slot)
            block = softmax_back(
                dot(keys, query_h, NT),
                lse[head : head + 1],
                below(counts, slot, (tokens, tokens)),
            )
            probs[slot] = block
            block_grad = dot(values, out_grad_h, NT)
            prob_grads[slot] = block_grad
            inner = inner + jnp.sum(block * block_grad, axis=0, keepdims=True)
        query_n = jnp.zeros((HEAD_DIM, tokens), F32)
        for slot in (3, 2, 1, 0):
            keys, values = pair_of(slot)
            block = probs[slot]
            score_b = (block * (prob_grads[slot] - inner) * SCALE).astype(BF16)
            query_n = query_n + dot(keys, score_b, TN)
            key_g = dot(score_b, query_h)
            value_g = dot(block.astype(BF16), out_grad_h)
            if slot == 0:
                key_value_grad[0, :, cols] = key_g
                key_value_grad[1, :, cols] = value_g
            elif slot == 2:
                copy(2, head).wait_recv()
                away[1, head, 0] = (key_g + landed[2, head, 0].astype(F32)).astype(BF16)
                away[1, head, 1] = (value_g + landed[2, head, 1].astype(F32)).astype(BF16)
                copy(1, head).start()
            else:
                away[slot - 1, head, 0] = key_g.astype(BF16)
                away[slot - 1, head, 1] = value_g.astype(BF16)
                copy(slot - 1, head).start()
        query_grad[:, cols] = query_n.T
    side.store(QUERY_GRAD)

    def keep(tile, size, block):
        matrix_grad[tile * size : (tile + 1) * size] = block

    tiled_grad(out_in, result, keep, lambda tile: None)
    side.store(MATRIX_GRAD)
    text_copy(0).wait_recv()
    text_copy(1).wait_recv()
    text_sum[...] = text_part(0) + text_landed[0].astype(F32) + text_landed[1].astype(F32)
    for head in range(heads):
        cols = head_cols(head)
        copy(0, head).wait_recv()
        copy(1, head).wait_recv()
        for member in range(2):
            key_value_grad[member, :, cols] += landed[0, head, member].astype(F32) + landed[
                1, head, member
            ].astype(F32)
    for kind in range(3):
        text_copy(kind).wait_send()
        for head in range(heads):
            copy(kind, head).wait_send()


def qkv_back_kernel(
    side,
    query_grad,
    key_value_grad,
    text_grad,
    query,
    key,
    text_key,
    slots_in,
    text_slots,
    rows_w,
    cosine,
    sine,
    weight,
    normal,
    context,
    text_weight,
    context_before,
    width_sums,
    context_part,
    total,
    self_grad,
    text_matrix,
    grads_b,
    text_b,
    query_n,
    key_n,
    slots,
    send_sems,
    recv_sems,
    part,
    came,
    pair,
    peers,
    sems,
):
    greet(side, True, side.masks)
    side.start()
    chain = Chain(part, total, (came, pair, peers), sems)
    tokens, width = query.shape
    features = total.shape[1]
    heads = width // HEAD_DIM
    text_rows = text_grad.shape[1]
    place = lax.rem(lax.axis_index(DP), HOLD)
    mine = pl.ds(pl.multiple_of(place * text_rows, text_rows), text_rows)
    text_k = text_key[mine]
    width_sums[...] = jnp.zeros(width_sums.shape, F32)
    for head in range(heads):
        cols = head_cols(head)
        rows = query_grad[:, cols]
        query_n[:, cols] = rows * cosine[...] - turned(rows * sine[...])
        rows = key_value_grad[0, :, cols]
        key_n[:, cols] = rows * cosine[...] - turned(rows * sine[...])

    def gain(member):
        return rows_w[GAINS + member : GAINS + member + 1]

    exchange = Exchange(slots, send_sems, recv_sems)
    text_terms = stat_rows(text_k * gain(3) * text_grad[0], 2)
    exchange.start(
        stat_rows(query[...] * gain(0) * query_n[...], 0)
        + stat_rows(key[...] * gain(1) * key_n[...], 1)
        + jnp.concatenate([text_terms, jnp.zeros((8, tokens - text_rows), F32)], axis=1)
    )
    query_inv = inverse_rms(stat_column(slots_in, 0, HEAD_DIM), features)
    key_inv = inverse_rms(stat_column(slots_in, 1, HEAD_DIM), features)
    text_inv = inverse_rms(stat_column(text_slots.at[:, :, mine], 0, HEAD_DIM), features)
    side.move(1)
    exchange.finish()

    def cubed(inverse, term):
        return term * inverse * inverse * inverse / features

    query_t = cubed(query_inv, stat_column(slots, 0, HEAD_DIM))
    key_t = cubed(key_inv, stat_column(slots, 1, HEAD_DIM))
    text_t = cubed(text_inv, stat_column(slots.at[:, :, pl.ds(0, text_rows)], 2, HEAD_DIM))

    def back(member, cols, values, inverse, term, grads):
        width_sums[member : member + 1, cols] = jnp.sum(
            values * inverse * grads, axis=0, keepdims=True
        )
        block = inverse * gain(member)[:, cols] * grads - values * term
        block = block.astype(BF16)
        width_sums[4 + member : 5 + member, cols] = jnp.sum(
            block.astype(F32), axis=0, keepdims=True
        )
        return block

    def shifted(cols, member):
        return slice(cols.start + member * width, cols.stop + member * width)

    for head in range(heads):
        cols = head_cols(head)
        grads_b[:, cols] = back(0, cols, query[:, cols], query_inv, query_t, query_n[:, cols])
        grads_b[:, shifted(cols, 1)] = back(
            1, cols, key[:, cols], key_inv, key_t, key_n[:, cols]
        )
        text_b[:, cols] = back(
            3, cols, text_k[:, cols], text_inv, text_t, text_grad[0, :, cols]
        )
    block = key_value_grad[1].astype(BF16)
    grads_b[:, 2 * width :] = block
    width_sums[6:7] = jnp.sum(block.astype(F32), axis=0, keepdims=True)
    block = text_grad[1].astype(BF16)
    text_b[:, width:] = block
    width_sums[8:9] = jnp.sum(block.astype(F32), axis=0, keepdims=True)
    per_block = 128 // CHUNK

    def leave(rows, index):
        part[rows] = (
            dot(grads_b[rows, :width], weight[0], NT)
            + dot(grads_b[rows, width : 2 * width], weight[1], NT)
            + dot(grads_b[rows, 2 * width :], weight[2], NT)
        ).astype(BF16)
        chain.begin(index * per_block, per_block)

    side.need(WEIGHT)
    loop_rows(tokens, 128, leave)
    side.need(NORMAL, CONTEXT, TEXT_WEIGHT)

    def keep(target):
        def store(tile, size, block):
            target[tile * size : (tile + 1) * size] = block

        return store

    tiled_grad(normal, grads_b, keep(self_grad), chain.serve)
    side.store(SELF_GRAD)
    tiled_grad(context, text_b, keep(text_matrix), lambda tile: None)
    side.store(TEXT_MATRIX)
    chain.serve(4)
    side.need(BEFORE)
    context_part[...] = (
        context_before[...]
        + dot(text_b[:, :width], text_weight[0], NT)
        + dot(text_b[:, width:], text_weight[1], NT)
    )
    chain.drain(5, side.late)
    side.finish()


def small_rows(clips):
    low = 6 * LAYERS + 6 * clips
    places = {BIAS: low, GAIN: low + 3 * LAYERS, SHIFT: low + 4 * LAYERS}
    places[LOSS] = low + 5 * LAYERS
    return places, (low + 5 * LAYERS + 1 + 15) // 16 * 16


def last_kernel(
    clips,
    side,
    context_part,
    grad,
    branch,
    hidden,
    rows_d,
    *refs,
):
    refs = list(refs)

    def take(count):
        taken = refs[:count]
        del refs[:count]
        return taken

    above = take(1)[0]
    small = [take(6) for _ in range(LAYERS)]
    new_grad, total, out_d, out_w, out_f = take(5)
    sums = take(1)[0]
    part, came, pair, peers, sems = take(5)
    bits = bits_of_dp()
    away = [take(3) for _ in range(bits)]
    landed = [take(3) for _ in range(bits)]
    send_sems, recv_sems = take(2)
    greet(side, True, side.masks)
    side.start()
    me = lax.axis_index(DP)
    clip = me // HOLD
    chain = Chain(part, total, (came, pair, peers), sems)
    part[...] = context_part[...].astype(BF16)
    chain.begin(0, chain.chunks)
    sums[...] = jnp.zeros(sums.shape, F32)
    scale_row = 1.0 + row_of(rows_d, MODS + 1)
    tokens = grad.shape[0]
    size = tokens // chain.chunks
    side.need(GRAD, BRANCH, HIDDEN)

    def enter(rows, index):
        step = branch[rows].astype(F32)
        back, hat = norm_back(hidden[rows], scale_row, step)
        add_sum(sums, 0, step)
        add_sum(sums, 1, step * hat)
        new_grad[rows] = grad[rows] + back
        chain.serve(index)

    loop_rows(tokens, size, enter)
    side.store(NEW_GRAD)
    side.move(1)
    places, count = small_rows(clips)
    out_d[...] = jnp.zeros(out_d.shape, F32)
    out_f[...] = jnp.zeros(out_f.shape, F32)
    time_rows = [jnp.zeros((1, grad.shape[1]), F32) for _ in range(6)]
    for layer in range(LAYERS):
        sums1, sums2, sums3, width1, width2, hidden_sum = small[layer]
        sums0 = sums if layer == 0 else above
        mods = [(sums0, 0), (sums0, 1), (sums1, 2), (sums2, 0), (sums2, 1), (sums3, 0)]
        for row, (ref, index) in enumerate(mods):
            value = row_of(ref, index)
            time_rows[row] = time_rows[row] + value
            out_d[6 * layer + row : 6 * layer + row + 1] = value
        for row, (ref, index) in enumerate([(sums1, 3), (sums2, 2), (sums3, 1)]):
            place = places[BIAS] + 3 * layer + row
            out_d[place : place + 1] = row_of(ref, index)
        place = places[GAIN] + layer
        out_d[place : place + 1] = row_of(sums1, 0)
        place = places[SHIFT] + layer
        out_d[place : place + 1] = row_of(sums1, 1)
        out_w[24 * layer : 24 * layer + 16] = width1[...]
        out_w[24 * layer + 16 : 24 * layer + 24] = width2[...]
        out_f[layer : layer + 1] = row_of(hidden_sum, 0)
    for index in range(clips):
        for row in range(6):
            place = 6 * LAYERS + 6 * index + row
            out_d[place : place + 1] = jnp.where(clip == index, time_rows[row], 0.0)
    out_d[places[LOSS] : places[LOSS] + 1] = row_of(small[LAYERS - 1][2], 2)
    for bit in range(bits):
        copies = []
        for number, ref in enumerate((out_d, out_w, out_f)):
            away[bit][number][...] = ref[...].astype(BF16)
            copy = send(
                away[bit][number],
                landed[bit][number],
                send_sems.at[bit, number],
                recv_sems.at[bit, number],
                dp=flip(me, 1 << bit),
            )
            copy.start()
            copies.append(copy)
        if bit == 0:
            chain.drain(chain.chunks)
        side.move(bit)
        for number, ref in enumerate((out_d, out_w, out_f)):
            copies[number].wait()
            ref[...] = away[bit][number][...].astype(F32) + landed[bit][number][...].astype(F32)
    side.finish()


def unpack_kernel(clips, side, *refs):
    refs = list(refs)

    def take(count):
        taken = refs[:count]
        del refs[:count]
        return taken

    lengths, rows_d, rows_w, rows_f, context_sum = take(5)
    parts = [take(6) for _ in range(LAYERS)]
    whole = take(2)
    loss, time, bias, key_bias, gains, hidden, out, gain, shift, mods = take(10)
    context_grad = take(1)[0]
    self_all, cross_all, out_all, up_all, down_all = take(5)
    whole_out = take(2)
    (sems,) = refs
    width = key_bias.shape[1]
    context_grad[...] = context_sum[...].astype(F32)
    copies = []

    def copy(source, target):
        item = pltpu.make_async_copy(source, target, sems.at[len(copies)])
        item.start()
        copies.append(item)

    for layer in range(LAYERS):
        side.need(*range(6 * layer, 6 * layer + 6))
        up, down, cross, text, self_part, out0 = parts[layer]
        copy(up, up_all.at[layer])
        copy(down, down_all.at[layer])
        for member in range(3):
            copy(self_part.at[:, member * width : (member + 1) * width], self_all.at[layer, member])
        copy(cross.at[:, :width], cross_all.at[layer, 0])
        copy(text.at[:, :width], cross_all.at[layer, 1])
        copy(text.at[:, width:], cross_all.at[layer, 2])
        copy(out0, out_all.at[layer, 0])
        copy(cross.at[:, width:], out_all.at[layer, 1])
    side.need(6 * LAYERS, 6 * LAYERS + 1)
    for source, target in zip(whole, whole_out):
        copy(source, target)
    places, count = small_rows(clips)
    for layer in range(LAYERS):
        for row in range(6):
            mods[row, layer : layer + 1] = row_of(rows_d, 6 * layer + row)
        for row in range(3):
            out[row, layer : layer + 1] = row_of(rows_d, places[BIAS] + 3 * layer + row)
        base = 24 * layer
        for row, place in enumerate((4, 6, 17, 7, 8)):
            bias[row, layer : layer + 1] = row_of(rows_w, base + place)
        key_bias[layer : layer + 1] = row_of(rows_w, base + 5)
        for row, place in enumerate((0, 1, 16, 3)):
            gains[layer, row : row + 1] = row_of(rows_w, base + place)
    for index in range(clips):
        for row in range(6):
            time[row, index : index + 1] = row_of(rows_d, 6 * LAYERS + 6 * index + row)
    hidden[...] = rows_f[0:LAYERS]
    gain[...] = rows_d[places[GAIN] : places[GAIN] + LAYERS]
    shift[...] = rows_d[places[SHIFT] : places[SHIFT] + LAYERS]
    count = lengths[0]
    for index in range(1, clips):
        count = count + lengths[index]
    total = jnp.sum(row_of(rows_d, places[LOSS]), axis=1, keepdims=True)
    loss[...] = jnp.broadcast_to(total, loss.shape) / (count.astype(F32) * rows_d.shape[1])
    for item in copies:
        item.wait()


def per_device(
    latents,
    context,
    time_embed,
    teacher,
    lengths,
    block_order,
    positions,
    self_proj,
    cross_proj,
    out_proj,
    ffn_up,
    ffn_down,
    proj_bias,
    key_bias,
    norm_gains,
    ffn_bias,
    out_bias,
    cross_gain,
    cross_shift,
    modulation,
):
    tokens, features = latents.shape
    width = norm_gains.shape[-1]
    heads = width // HEAD_DIM
    hidden_width = ffn_bias.shape[-1]
    clip_count = time_embed.shape[0]
    text_rows = context.shape[0]
    text_all = text_rows * HOLD
    clip = lax.axis_index(DP) // HOLD
    out_t = jnp.swapaxes(out_proj, 2, 3)
    down_t = jnp.swapaxes(ffn_down, 1, 2)

    rows_d = (tokens, features)
    rows_w = (tokens, width)
    rows_f = (tokens, hidden_width)
    stats = (CHAIN, 8, tokens)
    three = pltpu.SemaphoreType.DMA((CHAIN - 1,))
    chain_scratch = Chain.scratch(tokens, features)
    kv_shape = (heads, 2, tokens, HEAD_DIM)

    pack = (((16, features), F32), ((16, width), F32), ((1, hidden_width), F32))
    attend_outs = (
        Early(HIDDEN, rows_d, F32),
        Early(NORMAL, rows_d, BF16),
        Early(QUERY, rows_w, F32),
        Early(KEY, rows_w, F32),
        Early(QUERY_ROT, rows_w, BF16),
        (kv_shape, BF16),
        (stats, F32),
        ((HOLD - 1,) + kv_shape, BF16),
        (rows_w, BF16),
        ((8, tokens), F32),
    )
    attend_scratch = [
        pltpu.VMEM((heads, HOLD, tokens, tokens), F32),
        three,
        three,
        pltpu.SemaphoreType.DMA((4 + 2 * heads,)),
        pltpu.SemaphoreType.DMA((4 + 2 * heads,)),
    ]
    results, found = run(
        "first",
        first_kernel,
        (
            lengths,
            block_order,
            jnp.swapaxes(time_embed, 0, 1),
            jnp.swapaxes(modulation, 0, 1),
            jnp.swapaxes(out_bias, 0, 1),
            cross_gain,
            cross_shift,
            jnp.swapaxes(proj_bias, 0, 1),
            key_bias,
            norm_gains,
            ffn_bias,
            positions,
            rope_table(HEAD_DIM),
            latents,
            context,
        ),
        (
            ((HOLD, 8, tokens), F32),
            ((tokens, HEAD_DIM), F32),
            ((tokens, HEAD_DIM), F32),
            (context.shape, F32),
        )
        + pack * LAYERS
        + attend_outs
        + (((text_all, features), BF16),),
        attend_scratch + [three, three],
        jobs=[
            Gather(self_proj, 0, name=SELF, held=True),
            Gather(cross_proj, 0, wave=1),
            Gather(out_t, 0, wave=1),
        ],
        scalars=2,
        micros=70,
    )
    counts, cosine, sine, context_part = results[:4]
    packs = [results[4 + 3 * layer : 7 + 3 * layer] for layer in range(LAYERS)]
    attended = results[4 + 3 * LAYERS :]
    clip_context = attended[10]
    weights = {SELF: [found[0]], CROSS: [found[1]], OUT: [found[2]], UP: [], DOWN: []}
    saved = []
    sources = {
        SELF: self_proj,
        CROSS: cross_proj,
        OUT: out_t,
        UP: ffn_up,
        DOWN: down_t,
    }

    def gathers(layer, *names):
        return [Gather(sources[name], layer) for name in names if layer < LAYERS]

    def keep(found, *names):
        for name, item in zip(names, found):
            weights[name].append(item)

    base, tot, before = latents, latents, packs[0][0]
    for layer in range(LAYERS):
        pack_d, pack_w, pack_f = packs[layer]
        if layer > 0:
            attended, unused = run(
                "attend",
                attend_kernel,
                (
                    base,
                    tot,
                    before,
                    pack_d,
                    pack_w,
                    Late(WEIGHT, weights[SELF][layer]),
                    Late(COSINE, cosine, lazy=True),
                    Late(SINE, sine, lazy=True),
                    counts,
                ),
                attend_outs,
                attend_scratch,
                micros=35,
            )
        hidden, a1, sq, sk, q_rot, kv, stat1, others, o1, lse1 = attended[:10]
        (tot1, ck, ckb, cvb, stat_t), found = run(
            "out_sum",
            out_sum_kernel,
            (
                o1,
                Late(OUT, weights[OUT][layer], 0),
                Late(CONTEXT, clip_context, lazy=True),
                Late(TEXT_WEIGHT, weights[CROSS][layer], 1, 3, lazy=True),
                pack_w,
            ),
            (
                (rows_d, BF16),
                ((text_all, width), F32),
                ((text_all, width), BF16),
                ((text_all, width), BF16),
                ((CHAIN, 8, text_all), F32),
            ),
            [three, three] + chain_scratch,
            jobs=gathers(layer, UP) + gathers(1, SELF)
            if layer == 0
            else gathers(layer, DOWN),
            micros=45,
        )
        keep(found, *((UP, SELF) if layer == 0 else (DOWN,)))
        gathered = layer == 0
        jobs = [
            Gather(sources[DOWN], 0, name=DOWN, held=True),
            Gather(sources[CROSS], 1, wave=1),
            Gather(sources[OUT], 1, wave=1),
            Gather(sources[UP], 1, wave=1),
        ]
        results, found = run(
            "cross_ffn" + str(gathered),
            functools.partial(cross_ffn_kernel, gathered),
            (
                hidden,
                tot1,
                pack_d,
                pack_w,
                pack_f,
                Late(WEIGHT, weights[CROSS][layer], 0),
                Late(TEXT_KB, ckb, lazy=True),
                Late(TEXT_VB, cvb, lazy=True),
                Late(OUT, weights[OUT][layer], 1, lazy=True),
                Late(UP, weights[UP][layer], lazy=True),
            )
            + (() if gathered else (Late(DOWN, weights[DOWN][layer], lazy=True),)),
            (
                Early(HIDDEN, rows_d, F32),
                Early(NORMAL, rows_d, BF16),
                Early(QUERY, rows_w, F32),
                Early(QUERY_B, rows_w, BF16),
                Early(RESULT, rows_w, BF16),
                ((8, tokens), F32),
                (stats, F32),
                Early(HIDDEN_F, rows_d, F32),
                Early(NORMAL_F, rows_d, BF16),
                Early(GELU_B_NAME, rows_f, BF16),
                Early(SLOPE, rows_f, BF16),
                (rows_d, BF16),
            ),
            [three, three, pltpu.VMEM(rows_d, BF16)] + chain_scratch + chain_scratch,
            jobs=jobs if gathered else [],
            micros=90,
        )
        h1, a3, cq, cqb, o2, lse2, stat2, h2, a2, gelu_b, slope, tot3 = results
        if gathered:
            keep(found, DOWN, CROSS, OUT, UP)
        saved.append(
            (hidden, a1, sq, sk, q_rot, kv, stat1, others, o1, lse1, tot1, ck, ckb, cvb, stat_t)
            + (h1, a3, cq, cqb, o2, lse2, stat2, h2, a2, gelu_b, slope, tot3)
        )
        base, tot, before = h2, tot3, pack_d
    grad = base
    reduced = {}
    small = [None] * LAYERS
    above = None
    for layer in reversed(range(LAYERS)):
        (hidden, a1, sq, sk, q_rot, kv, stat1, others, o1, lse1, tot1, ck, ckb, cvb, stat_t) = saved[
            layer
        ][:15]
        (h1, a3, cq, cqb, o2, lse2, stat2, h2, a2, gelu_b, slope, tot3) = saved[layer][15:]
        pack_d, pack_w, pack_f = packs[layer]
        w_self, w_cross, w_out, w_up, w_down = [
            weights[name][layer] for name in (SELF, CROSS, OUT, UP, DOWN)
        ]
        joined = above is not None
        matrix = (features, hidden_width)
        results, found = run(
            "ffn_back" + str(joined),
            functools.partial(ffn_back_kernel, joined),
            (Late(GRAD, grad),)
            + (above if joined else (teacher, counts))
            + (
                tot3,
                pack_d,
                Late(DOWN, w_down),
                Late(UP, w_up, lazy=True),
                Late(SLOPE, slope),
                Late(NORMAL, a2, lazy=True),
                Late(GELU_B_NAME, gelu_b, lazy=True),
            ),
            (
                Early(NEW_GRAD, rows_d, F32, over=0),
                ((8, features), F32) if joined else Early(OUTPUT, rows_d, F32),
            )
            + (
                (rows_d, BF16),
                ((8, features), F32),
                ((8, hidden_width), F32),
                (matrix, BF16, True),
                (matrix, BF16, True),
            ),
            [
                pltpu.VMEM(rows_d, BF16),
                pltpu.VMEM(rows_f, BF16),
                pltpu.VMEM((2, 256, hidden_width), BF16),
                pltpu.SemaphoreType.DMA((2,)),
            ]
            + chain_scratch,
            jobs=[Scatter(text_matrix), Scatter(self_matrix)] if joined else [],
            micros=60,
        )
        grad = results[0]
        if not joined:
            output = results[1]
        else:
            sums_above = results[1]
            reduced[TEXT, layer + 1], reduced[SELF, layer + 1] = found
        da2, sums3, dz_sum, up_grad, down_grad = results[2:]
        (grad, dct, sums2, wsums2, da3, cross_matrix), found = run(
            "cross_back",
            cross_back_kernel,
            (
                grad,
                da2,
                h2,
                pack_d,
                pack_w,
                Late(OUT, w_out, 1),
                Late(QUERY, cq, lazy=True),
                Late(QUERY_B, cqb, lazy=True),
                lse2,
                stat2,
                Late(TEXT_KB, ckb, lazy=True),
                Late(TEXT_VB, cvb, lazy=True),
                Late(WEIGHT, w_cross, 0, lazy=True),
                Late(NORMAL, a3, lazy=True),
                Late(RESULT, o2, lazy=True),
            ),
            (
                Early(NEW_GRAD, rows_d, F32),
                Early(TEXT_GRAD, (2, text_all, width), F32),
                ((8, features), F32),
                ((8, width), F32),
                (rows_d, BF16),
                Early(MATRIX_GRAD, (features, 2 * width), BF16),
            ),
            [
                pltpu.VMEM(rows_d, BF16),
                pltpu.VMEM(rows_w, BF16),
                pltpu.VMEM(rows_w, BF16),
                pltpu.VMEM(rows_w, F32),
                pltpu.VMEM(stats, F32),
                three,
                three,
            ]
            + chain_scratch,
            jobs=[Scatter(up_grad, UP)],
            micros=60,
        )
        reduced[UP, layer] = found[0]
        (grad, out0, sums1, dq_rot, dkv, dtext), found = run(
            "attend_back",
            attend_back_kernel,
            (
                counts,
                grad,
                da3,
                h1,
                pack_d,
                tot1,
                Late(OUT, w_out, 0),
                Late(QUERY, q_rot, lazy=True),
                Late(KEY_VALUE, kv, lazy=True),
                Late(OTHERS, others, lazy=True),
                lse1,
                dct,
                Late(RESULT, o1, lazy=True),
            ),
            (
                Early(NEW_GRAD, rows_d, F32),
                Early(MATRIX_GRAD, (features, width), BF16),
                ((8, features), F32),
                Early(QUERY_GRAD, rows_w, F32),
                ((2,) + rows_w, F32),
                ((2, text_rows, width), F32),
            ),
            [
                pltpu.VMEM(rows_d, BF16),
                pltpu.VMEM(rows_w, BF16),
                pltpu.VMEM((HOLD, tokens, tokens), F32),
                pltpu.VMEM((HOLD, tokens, tokens), F32),
                pltpu.VMEM((3,) + kv_shape, BF16),
                pltpu.VMEM((3,) + kv_shape, BF16),
                pltpu.VMEM((3, 2, text_rows, width), BF16),
                pltpu.VMEM((3, 2, text_rows, width), BF16),
                pltpu.SemaphoreType.DMA((3, heads + 1)),
                pltpu.SemaphoreType.DMA((3, heads + 1)),
            ],
            micros=35,
        )
        (wsums1, context_part, da1, self_matrix, text_matrix), found = run(
            "qkv_back",
            qkv_back_kernel,
            (
                dq_rot,
                dkv,
                dtext,
                sq,
                sk,
                ck,
                stat1,
                stat_t,
                pack_w,
                cosine,
                sine,
                Late(WEIGHT, w_self, lazy=True),
                Late(NORMAL, a1, lazy=True),
                Late(CONTEXT, context, lazy=True),
                Late(TEXT_WEIGHT, w_cross, 1, 3, lazy=True),
                Late(BEFORE, context_part, lazy=True),
            ),
            (
                ((16, width), F32),
                (context.shape, F32),
                (rows_d, BF16),
                Early(SELF_GRAD, (features, 3 * width), BF16),
                Early(TEXT_MATRIX, (features, 2 * width), BF16),
            ),
            [
                pltpu.VMEM((tokens, 3 * width), BF16),
                pltpu.VMEM((text_rows, 2 * width), BF16),
                pltpu.VMEM(rows_w, F32),
                pltpu.VMEM(rows_w, F32),
                pltpu.VMEM(stats, F32),
                three,
                three,
            ]
            + chain_scratch,
            jobs=[Scatter(down_grad), Scatter(cross_matrix), Scatter(out0)],
            micros=60,
        )
        reduced[DOWN, layer], reduced[CROSS, layer], reduced[OUT0, layer] = found
        small[layer] = (sums1, sums2, sums3, wsums1, wsums2, dz_sum)
        above = (da1, hidden, pack_d)
    places, count = small_rows(clip_count)
    small_shapes = ((count, features), (24 * LAYERS, width), (16, hidden_width))
    travel = [pltpu.VMEM(shape, BF16) for shape in small_shapes]
    bits = bits_of_dp()
    (grad, context_sum, packed_d, packed_w, packed_f), found = run(
        "last",
        functools.partial(last_kernel, clip_count),
        (
            context_part,
            Late(GRAD, grad),
            Late(BRANCH, above[0]),
            Late(HIDDEN, above[1]),
            above[2],
            sums_above,
        )
        + tuple(item for layer in range(LAYERS) for item in small[layer]),
        (Early(NEW_GRAD, rows_d, F32), (context.shape, BF16))
        + tuple((shape, F32) for shape in small_shapes),
        [pltpu.VMEM((8, features), F32)]
        + Chain.scratch(text_rows, features)
        + travel * (2 * bits)
        + [pltpu.SemaphoreType.DMA((bits, 3)), pltpu.SemaphoreType.DMA((bits, 3))],
        jobs=[Scatter(text_matrix), Scatter(self_matrix)],
        micros=30,
    )
    reduced[TEXT, 0], reduced[SELF, 0] = found
    names = (UP, DOWN, CROSS, TEXT, SELF, OUT0)
    size = features // lax.axis_size(DP)
    far_outs = (
        ((LAYERS, 3, size, width), F32, True),
        ((LAYERS, 3, size, width), F32, True),
        ((LAYERS, 2, size, width), F32, True),
        ((LAYERS, size, hidden_width), F32, True),
        ((LAYERS, size, hidden_width), F32, True),
        (rows_d, F32, True),
        (rows_d, F32, True),
    )
    far_ins = [
        reduced[name, layer] for layer in range(LAYERS) for name in names
    ] + [output, grad]
    unpacked, unused = run(
        "unpack",
        functools.partial(unpack_kernel, clip_count),
        (lengths, packed_d, packed_w, packed_f, context_sum) + tuple(Late(place, item) for place, item in enumerate(far_ins)),
        (
            ((1, 128), F32),
            ((6, clip_count, features), F32),
            ((5, LAYERS, width), F32),
            ((LAYERS, width), F32),
            ((LAYERS, 4, width), F32),
            ((LAYERS, hidden_width), F32),
            ((3, LAYERS, features), F32),
            ((LAYERS, features), F32),
            ((LAYERS, features), F32),
            ((6, LAYERS, features), F32),
            (context.shape, F32),
        )
        + far_outs,
        [pltpu.SemaphoreType.DMA((2 + 10 * LAYERS,))],
        remote=False,
        scalars=1,
        micros=10,
    )
    loss, time, bias, key_sums, gain_sums, hidden_sums, out_sums, gain, shift, mods = unpacked[:10]
    context_grad, self_grad, cross_grad, out_grad, up_grad, down_grad, output, grad = unpacked[10:]
    out_grad = jnp.swapaxes(out_grad, 2, 3)
    down_grad = jnp.swapaxes(down_grad, 1, 2)
    return (
        output,
        loss[0, 0],
        grad,
        context_grad,
        jnp.swapaxes(time, 0, 1),
        self_grad,
        cross_grad,
        out_grad,
        up_grad,
        down_grad,
        jnp.swapaxes(bias, 0, 1),
        key_sums,
        gain_sums,
        hidden_sums,
        jnp.swapaxes(out_sums, 0, 1),
        gain,
        shift,
        jnp.swapaxes(mods, 0, 1),
    )


def solution(mesh):
    COLLECTIVES.clear()
    rows = P(DP, None)
    col_in = P(None, None, DP, TENSOR)
    col_out = P(None, None, TENSOR, DP)
    up, down = P(None, DP, TENSOR), P(None, TENSOR, DP)
    vec, mat = P(None, TENSOR), P(None, None, TENSOR)
    return jax.shard_map(
        per_device,
        mesh=mesh,
        in_specs=(rows, rows, P(), rows, P(), P(DP), P(None, DP))
        + (col_in, col_in, col_out, up, down)
        + (mat, vec, mat, vec, P(), P(), P(), P()),
        out_specs=(rows, P(), rows, rows, P())
        + (col_in, col_in, col_out, up, down)
        + (mat, vec, mat, vec, P(), P(), P(), P()),
        check_vma=False,
    )
```

```python
import functools
import math

import jax
import jax.numpy as jnp
import numpy as np
from jax import lax
from jax.experimental import pallas as pl
from jax.experimental.pallas import tpu as pltpu
from jax.sharding import PartitionSpec as P

BEFORE = "before"
BIAS = "bias"
BRANCH = "branch"
CONTEXT = "context"
COSINE = "cosine"
CROSS = "cross"
DOWN = "down"
DP = "dp"
GAIN = "gain"
GELU_B_NAME = "gelu_b"
GRAD = "grad"
HIDDEN = "hidden"
HIDDEN_F = "hidden_f"
KEY = "key"
KEY_VALUE = "key_value"
LOSS = "loss"
MATRIX_GRAD = "matrix_grad"
NEW_GRAD = "new_grad"
NORMAL = "normal"
NORMAL_F = "normal_f"
OTHERS = "others"
OUT = "out"
OUT0 = "out0"
OUTPUT = "output"
QUERY = "query"
QUERY_B = "query_b"
QUERY_GRAD = "query_grad"
QUERY_ROT = "query_rot"
RESULT = "result"
SELF = "self"
SELF_GRAD = "self_grad"
SHIFT = "shift"
SINE = "sine"
SLOPE = "slope"
TENSOR = "tensor"
TEXT = "text"
TEXT_GRAD = "text_grad"
TEXT_KB = "text_kb"
TEXT_MATRIX = "text_matrix"
TEXT_VB = "text_vb"
TEXT_WEIGHT = "text_weight"
UP = "up"
WEIGHT = "weight"
MESH = pl.DeviceIdType.MESH
F32, BF16 = jnp.float32, jnp.bfloat16
NN = (((1,), (0,)), ((), ()))
NT = (((1,), (1,)), ((), ()))
TN = (((0,), (0,)), ((), ()))
HEAD_DIM = 128
HOLD = 4
LAYERS = 2
CHAIN = 4
CHUNK = 32
EPS = 1e-06
LOG2E = math.log2(math.e)
SCALE = 1.0 / math.sqrt(HEAD_DIM)
VMEM_BYTES = 60 * 2**20


def dot(left, right, dims=NN, exact=False):
    precision = lax.Precision.HIGHEST if exact else None
    return lax.dot_general(left, right, dims, precision=precision, preferred_element_type=F32)


def rope_table(head_size):
    third = head_size // 6
    spans = [head_size - 4 * third, 2 * third, 2 * third]
    table = np.zeros((3, head_size), np.float32)
    start_col = 0
    for component in range(3):
        for pair_index in range(spans[component] // 2):
            freq_value = 10000.0 ** (-(2.0 * pair_index) / spans[component])
            table[component, start_col + 2 * pair_index] = freq_value
            table[component, start_col + 2 * pair_index + 1] = freq_value
        start_col += spans[component]
    return table


def signal(**device):
    pl.semaphore_signal(
        pltpu.get_barrier_semaphore(), inc=1, device_id=device, device_id_type=MESH
    )


def bits_of_dp():
    return max(lax.axis_size(DP).bit_length() - 1, 1)


def flip(index, mask):
    result, bit = index, 0
    while mask >> bit:
        if mask >> bit & 1:
            half = 1 << bit
            result = result + half - 2 * half * lax.rem(index // half, 2)
        bit += 1
    return result


def greet(side, tensor, masks):
    place, me = lax.axis_index(TENSOR), lax.axis_index(DP)
    if tensor:
        for step in range(1, CHAIN):
            signal(tensor=lax.rem(place + step, CHAIN))
    for mask in masks:
        signal(dp=flip(me, mask))
    side.load(False)
    pl.semaphore_wait(
        pltpu.get_barrier_semaphore(), (CHAIN - 1 if tensor else 0) + len(masks)
    )


def holders():
    me = lax.axis_index(DP)
    return flip(me, 1), flip(me, 2)


def send(src, dst, send_sem, recv_sem, **device):
    return pltpu.make_async_remote_copy(
        src_ref=src,
        dst_ref=dst,
        send_sem=send_sem,
        recv_sem=recv_sem,
        device_id=device,
        device_id_type=MESH,
    )


def masks_over(bits):
    masks = [0]
    for bit in bits:
        masks += [mask | 1 << bit for mask in masks]
    return masks


def halves_of(size):
    cut = (size // 2 + 15) // 16 * 16
    return ((0, cut), (cut, size - cut))


def half_orders(bits):
    rising = list(range(1, bits))
    return (rising, rising[::-1])


class Job:
    phase = 0
    wave = 0
    name = None
    ended = False
    midway = False

    def middle(self):
        pass

    def move(self, target):
        while self.phase < min(target, self.bits - 1):
            self.phase += 1
            self.advance(self.phase)


class Gather(Job):
    def __init__(self, source, layer, name=None, wave=0, held=False, skewed=False):
        self.layer, self.name, self.wave, self.is_held = layer, name, wave, held
        self.operands = [source]
        shape = source.shape[1:]
        self.lead = shape[:-2]
        self.size = shape[-2]
        devices = lax.axis_size(DP)
        self.outs = [(self.lead + (self.size * devices, shape[-1]), source.dtype)]
        self.spaces = [pl.ANY]
        self.bits = bits_of_dp()
        plan = []
        orders = half_orders(self.bits)
        if skewed:
            orders = (orders[0], orders[0])
        for half, order in enumerate(orders):
            for phase, bit in enumerate(order):
                for mask in masks_over(order[:phase]):
                    plan.append((phase, half, bit, mask))
        for mask in masks_over(range(1, self.bits)):
            plan.append((self.bits - 1, None, 0, mask))
        self.plan = plan
        count = len(plan)
        self.scratch = [
            pltpu.SemaphoreType.DMA((count,)),
            pltpu.SemaphoreType.DMA((count,)),
            pltpu.SemaphoreType.DMA,
        ]
        if held:
            self.scratch += [
                pltpu.VMEM(self.outs[0][0], source.dtype),
                pltpu.SemaphoreType.DMA,
            ]

    def key(self):
        return ("gather", self.layer, self.outs[0][0], self.wave, self.is_held)

    def bind(self, sources, outs, scratch):
        self.source = sources[0].at[self.layer]
        self.out = outs[0]
        self.send_sems, self.recv_sems, self.own_sem = scratch[:3]
        self.store = None
        if self.is_held:
            held, sem = scratch[3:]
            self.store = pltpu.make_async_copy(held, self.out, sem)
            self.out = held

    def block(self, ref, index, half):
        low, size = (0, self.size) if half is None else halves_of(self.size)[half]
        start = low if index is None else index * self.size + low
        rows = pl.ds(pl.multiple_of(start, 16), size)
        return ref.at[:, rows] if self.lead else ref.at[rows]

    def copies(self, phase, own=None, only=None):
        me = lax.axis_index(DP)
        for number, (step, half, bit, mask) in enumerate(self.plan):
            if only is not None and mask not in only:
                continue
            if step == phase and own in (None, mask == 0):
                index = flip(me, mask)
                source = (
                    self.block(self.source, None, half)
                    if mask == 0
                    else self.block(self.out, index, half)
                )
                yield send(
                    source,
                    self.block(self.out, index, half),
                    self.send_sems.at[number],
                    self.recv_sems.at[number],
                    dp=flip(me, 1 << bit),
                )

    def own_copy(self):
        me = lax.axis_index(DP)
        return pltpu.make_async_copy(
            self.source, self.block(self.out, me, None), self.own_sem
        )

    def start(self):
        for phase in range(self.bits):
            for copy in self.copies(phase, True):
                copy.start()
        self.own_copy().start()

    def middle(self):
        if self.bits == 3 and not self.midway:
            self.midway = True
            for copy in self.copies(1, True):
                copy.wait_recv()
            for copy in self.copies(2, only=(2, 4)):
                copy.start()

    def advance(self, phase):
        if phase == self.bits - 1 == 2:
            self.middle()
            for copy in self.copies(1, False):
                copy.wait_recv()
            for copy in self.copies(2, only=(6,)):
                copy.start()
            return
        for copy in self.copies(phase - 1):
            copy.wait_recv()
        for copy in self.copies(phase, False):
            copy.start()

    def finish(self):
        for copy in self.copies(self.bits - 1):
            copy.wait_recv()
        for phase in range(self.bits):
            for copy in self.copies(phase):
                copy.wait_send()
        self.own_copy().wait()
        if self.store is not None:
            self.store.start()


class Scatter(Job):
    def __init__(self, source=None, name=None, shape=None):
        self.name = name
        self.operands = [] if source is None else [source]
        shape = source.shape if shape is None else shape
        self.bits = bits_of_dp()
        self.size = shape[0] // lax.axis_size(DP)
        self.width = shape[1]
        self.outs = [((self.size, self.width), F32)]
        self.spaces = [pltpu.VMEM]
        self.slots = 1 << self.bits - 1
        orders = [order[::-1] for order in half_orders(self.bits)]
        plan = [(0, None, 0, mask, mask >> 1) for mask in masks_over(range(1, self.bits))]
        for half, order in enumerate(orders):
            for phase, bit in enumerate(order):
                kept = masks_over(order[phase + 1 :])
                for place, mask in enumerate(kept):
                    plan.append((phase + 1, half, bit, mask, place))
        self.plan = plan
        count = len(plan)
        buffers = [pltpu.VMEM((self.slots, self.size, self.width), BF16)]
        buffers += buffers * len(self.operands)
        for phase in range(1, self.bits):
            places = 1 << self.bits - 1 - phase
            buffers += [
                pltpu.VMEM((places, size, self.width), BF16)
                for _, size in halves_of(self.size)
            ]
        self.scratch = buffers + [
            pltpu.SemaphoreType.DMA((count,)),
            pltpu.SemaphoreType.DMA((count,)),
            pltpu.SemaphoreType.DMA((self.slots,)),
        ]

    def key(self):
        return ("scatter", self.width, len(self.operands))

    def bind(self, sources, outs, scratch):
        self.out = outs[0]
        self.landed, self.own = scratch[0], None
        scratch = scratch[1:]
        if sources:
            self.source, self.own = sources[0], scratch[0]
            scratch = scratch[1:]
        self.parts = scratch[:-3]
        self.send_sems, self.recv_sems, self.own_sems = scratch[-3:]

    def rows(self, index):
        return pl.ds(pl.multiple_of(index * self.size, 16), self.size)

    def held(self, mask, low, size):
        if self.own is not None:
            return self.own.at[mask >> 1, pl.ds(pl.multiple_of(low, 16), size)]
        start = flip(lax.axis_index(DP), mask) * self.size + low
        return self.source.at[pl.ds(pl.multiple_of(start, 16), size)]

    def copies(self, phase):
        me = lax.axis_index(DP)
        for number, (step, half, bit, mask, place) in enumerate(self.plan):
            if step != phase:
                continue
            if phase == 0:
                source = self.source.at[self.rows(flip(me, mask | 1))]
                target = self.landed.at[mask >> 1]
            else:
                low, size = halves_of(self.size)[half]
                source = self.held(mask | 1 << bit, low, size)
                target = self.parts[2 * (phase - 1) + half].at[place]
            yield send(
                source,
                target,
                self.send_sems.at[number],
                self.recv_sems.at[number],
                dp=flip(me, 1 << bit),
            )

    def own_copies(self):
        me = lax.axis_index(DP)
        if self.own is not None:
            for slot in range(self.slots):
                yield pltpu.make_async_copy(
                    self.source.at[self.rows(flip(me, slot << 1))],
                    self.own.at[slot],
                    self.own_sems.at[slot],
                )

    def start(self):
        for copy in self.copies(0):
            copy.start()
        for copy in self.own_copies():
            copy.start()

    def add(self, phase):
        for copy in self.copies(phase):
            copy.wait_recv()
        if phase == 0:
            for copy in self.own_copies():
                copy.wait()
            for slot in range(self.slots):

                def step(rows, index, slot=slot):
                    held = self.held(slot << 1, index * 16, 16)
                    held[...] = held[...] + self.landed[slot, rows]

                loop_rows(self.size, 16, step)
            return
        for number, (step, half, bit, mask, place) in enumerate(self.plan):
            if step == phase:
                low, size = halves_of(self.size)[half]
                part = self.parts[2 * (phase - 1) + half]

                def step(rows, index, mask=mask, place=place, low=low, part=part):
                    held = self.held(mask, low + index * 16, 16)
                    if phase == self.bits - 1:
                        target = pl.ds(pl.multiple_of(low + index * 16, 16), 16)
                        self.out[target] = held[...].astype(F32) + part[place, rows].astype(F32)
                    else:
                        held[...] = held[...] + part[place, rows]

                loop_rows(size, 16, step)

    def advance(self, phase):
        self.add(phase - 1)
        for copy in self.copies(phase):
            copy.start()

    def finish(self):
        self.add(self.bits - 1)
        for phase in range(self.bits):
            for copy in self.copies(phase):
                copy.wait_send()


class Late:
    def __init__(self, name, value, low=None, high=None, lazy=False):
        self.name, self.value, self.low, self.high = name, value, low, high
        self.lazy = lazy
        shape = value.shape
        if high is not None:
            shape = (high - low,) + shape[1:]
        elif low is not None:
            shape = shape[1:]
        self.scratch = [pltpu.VMEM(shape, value.dtype), pltpu.SemaphoreType.DMA]

    def source(self, ref):
        if self.high is not None:
            return ref.at[self.low : self.high]
        return ref if self.low is None else ref.at[self.low]


class Early:
    def __init__(self, name, shape, kind, over=None):
        self.name, self.shape, self.kind, self.over = name, shape, kind, over
        self.scratch = [pltpu.SemaphoreType.DMA]
        if over is None:
            self.scratch = [pltpu.VMEM(shape, kind)] + self.scratch


class Side:
    def __init__(self, jobs):
        self.jobs = jobs
        self.masks = [1 << bit for bit in range(bits_of_dp())] if jobs else []
        self.loads, self.stores, self.open = {}, {}, []
        self.first_loads, self.waiting = [], []
        self.late_after = False

    def load(self, lazy):
        for item in [item for item in self.waiting if item[0] == lazy]:
            item[1].start()
            self.waiting.remove(item)

    def need(self, *names):
        for name in names:
            self.loads[name].wait()

    def store(self, *names):
        for name in names:
            self.stores[name].start()
            self.open.append(name)

    def start(self, wave=0):
        for job in self.jobs:
            if job.operands and job.wave == wave:
                job.start()
        while self.first_loads:
            self.first_loads.pop(0).wait()
            if not self.first_loads and not self.late_after:
                self.load(True)

    def launch(self, name, source):
        for job in self.jobs:
            if job.name == name:
                job.source = source
                job.start()

    def move(self, target, *names):
        for job in self.jobs:
            if not names or job.name in names:
                job.move(target)

    def early(self):
        self.move(bits_of_dp() - 2)

    def late(self):
        self.move(bits_of_dp() - 1)

    def middle(self):
        self.early()
        for job in self.jobs:
            job.middle()

    def finish(self, *names):
        for job in self.jobs:
            if not job.ended and (not names or job.name in names):
                job.move(job.bits - 1)
                job.finish()
                job.ended = True

    def close(self):
        for name in self.stores:
            if name not in self.open:
                self.store(name)
        for copy in self.stores.values():
            copy.wait()
        for job in self.jobs:
            if isinstance(job, Gather) and job.store is not None:
                job.store.wait()


class Exchange:
    def __init__(self, slots, send_sems, recv_sems):
        self.slots = slots
        place = lax.axis_index(TENSOR)
        self.place = place
        self.copies = [
            send(
                slots.at[place],
                slots.at[place],
                send_sems.at[step - 1],
                recv_sems.at[step - 1],
                tensor=lax.rem(place + step, CHAIN),
            )
            for step in range(1, CHAIN)
        ]

    def start(self, rows):
        self.slots[self.place] = rows
        for copy in self.copies:
            copy.start()

    def finish(self):
        for copy in self.copies:
            copy.wait()


def stat_rows(squares, row):
    count, width = squares.shape
    ones = jnp.ones((8, width), F32)
    sums = dot(ones, squares, NT, exact=True)
    index = lax.broadcasted_iota(jnp.int32, sums.shape, 0)
    return jnp.where(index == row, sums, 0.0)


def stat_column(slots, row, lanes):
    gathered = jnp.concatenate([slots[place] for place in range(CHAIN)], axis=0)
    index = lax.broadcasted_iota(jnp.int32, (8 * CHAIN, lanes), 0)
    pick = jnp.where(lax.rem(index, 8) == row, 1.0, 0.0)
    return dot(gathered, pick, TN, exact=True)


class Chain:
    def __init__(self, part, total, buffers, sems):
        self.part, self.total = part, total
        self.came, self.pair, self.peers = buffers
        self.sems = sems
        place = lax.axis_index(TENSOR)
        self.is_end = (place == 0) | (place == 3)
        self.is_mid = jnp.logical_not(self.is_end)
        self.inner = jnp.where(place == 0, 1, 2)
        self.outer = jnp.where(place == 1, 0, 3)
        self.peer = 3 - place
        self.chunks = part.shape[0] // CHUNK
        self.closed = False

    @staticmethod
    def scratch(rows, width):
        chunks = rows // CHUNK
        return [pltpu.VMEM((rows, width), BF16)] * 4 + [pltpu.SemaphoreType.DMA((6, chunks))]

    def rows(self, k):
        return pl.ds(pl.multiple_of(k * CHUNK, CHUNK), CHUNK)

    def copy(self, src, dst, kind, k, device):
        return send(
            src.at[self.rows(k)],
            dst.at[self.rows(k)],
            self.sems.at[2 * kind, k],
            self.sems.at[2 * kind + 1, k],
            tensor=device,
        )

    def inward(self, k, device):
        return self.copy(self.part, self.came, 0, k, device)

    def across(self, k):
        return self.copy(self.pair, self.peers, 1, k, self.peer)

    def outward(self, k, device):
        return self.copy(self.total, self.total, 2, k, device)

    def begin(self, low, count):
        @pl.when(self.is_end)
        def _():
            def step(k, carry):
                self.inward(low + k, self.inner).start()
                return carry

            lax.fori_loop(0, count, step, 0)

    def first(self, k):
        self.inward(k, self.outer).wait_recv()
        rows = self.rows(k)
        self.pair[rows] = (self.part[rows].astype(F32) + self.came[rows].astype(F32)).astype(BF16)
        self.across(k).start()

    def second(self, k):
        self.across(k).wait_recv()
        rows = self.rows(k)
        self.total[rows] = (self.pair[rows].astype(F32) + self.peers[rows].astype(F32)).astype(
            BF16
        )
        self.outward(k, self.outer).start()

    def serve(self, k):
        @pl.when(self.is_mid)
        def _():
            self.first(k)

            @pl.when(k > 0)
            def _():
                self.second(jnp.maximum(k - 1, 0))

    def segment(self, low, high, closed, upto):
        @pl.when(self.is_mid)
        def _():
            def both(k, carry):
                self.first(k)

                @pl.when(k > 0)
                def _():
                    self.second(jnp.maximum(k - 1, 0))

                return carry

            lax.fori_loop(low, high, both, 0)
            if high == self.chunks and not self.closed:
                self.second(self.chunks - 1)

        self.closed = self.closed or high == self.chunks

        @pl.when(self.is_end)
        def _():
            def close(k, carry):
                self.inward(k, self.inner).wait_send()
                self.outward(k, self.inner).wait_recv()
                return carry

            lax.fori_loop(closed, upto, close, 0)

    def drain(self, low, early=None, late=None):
        done, last = 0, self.chunks
        if early is not None:
            cut = low + (last - low) // 4
            self.segment(low, cut, done, cut - 1)
            low, done = cut, cut - 1
            early()
        if late is not None:
            cut = low + (last - low) * 5 // 8
            self.segment(low, cut, done, cut - 1)
            low, done = cut, cut - 1
            late()
        self.segment(low, last, done, last)
        self.close()

    def close(self):
        @pl.when(self.is_mid)
        def _():
            def close(k, carry):
                self.across(k).wait_send()
                self.outward(k, self.outer).wait_send()
                return carry

            lax.fori_loop(0, self.chunks, close, 0)


COLLECTIVES = {}


def collective_of(key):
    return COLLECTIVES.setdefault(key, 1 + len(COLLECTIVES))


def run(name, kernel, ins, outs, scratch=(), remote=True, jobs=(), scalars=0, micros=0):
    whole = pl.BlockSpec(memory_space=pltpu.VMEM)
    far = pl.BlockSpec(memory_space=pl.ANY)
    if remote:
        ins = tuple(ins[:scalars]) + tuple(
            item if isinstance(item, Late) else Late(None, item) for item in ins[scalars:]
        )
        outs = tuple(
            item if isinstance(item, Early) or len(item) > 2 else Early(place, *item)
            for place, item in enumerate(outs)
        )
    job_ins = [item for job in jobs for item in job.operands]
    job_outs = [item for job in jobs for item in job.outs]
    job_spaces = [pl.BlockSpec(memory_space=space) for job in jobs for space in job.spaces]
    moved = [item for item in tuple(ins) + tuple(outs) if isinstance(item, (Late, Early))]
    own_scratch = list(scratch) + [item for job in jobs for item in job.scratch]

    def body(*refs):
        side = Side(jobs)
        refs = list(refs)

        def take(count):
            taken = refs[:count]
            del refs[:count]
            return taken

        own_in, side_in = take(len(ins)), take(len(job_ins))
        own_out, side_out = take(len(outs)), take(len(job_outs))
        own = take(len(scratch))
        for job in jobs:
            job.phase, job.ended, job.midway = 0, False, False
            job.bind(
                [side_in.pop(0) for _ in job.operands],
                [side_out.pop(0) for _ in job.outs],
                take(len(job.scratch)),
            )
        for place, item in enumerate(ins):
            if isinstance(item, Late):
                held, sem = take(2)
                copy = pltpu.make_async_copy(item.source(own_in[place]), held, sem)
                side.waiting.append((item.lazy, copy))
                if item.name is None:
                    side.first_loads.append(copy)
                side.loads[item.name] = copy
                own_in[place] = held
        for place, item in enumerate(outs):
            if isinstance(item, Early):
                held = take(1)[0] if item.over is None else own_in[item.over]
                sem = take(1)[0]
                side.stores[item.name] = pltpu.make_async_copy(held, own_out[place], sem)
                own_out[place] = held
        if not remote:
            side.load(False)
        kernel(side, *own_in, *own_out, *own)
        side.close()

    key = (name,) + tuple(job.key() for job in jobs)
    shapes = [
        (item.shape, item.kind) if isinstance(item, Early) else item[:2] for item in outs
    ] + job_outs
    results = pl.pallas_call(
        body,
        out_shape=tuple(jax.ShapeDtypeStruct(shape, kind) for shape, kind in shapes),
        in_specs=[pl.BlockSpec(memory_space=pltpu.SMEM)] * scalars
        + [far if isinstance(item, Late) else whole for item in ins[scalars:]]
        + [far] * len(job_ins),
        out_specs=tuple(
            [far if isinstance(item, Early) or len(item) > 2 else whole for item in outs]
            + job_spaces
        ),
        scratch_shapes=own_scratch + [part for item in moved for part in item.scratch],
        cost_estimate=pl.CostEstimate(
            flops=0, bytes_accessed=micros * 3000000, transcendentals=0
        ),
        compiler_params=pltpu.CompilerParams(
            collective_id=collective_of(key) if remote else None,
            has_side_effects=remote,
            vmem_limit_bytes=VMEM_BYTES,
        ),
    )(*[item.value if isinstance(item, Late) else item for item in ins], *job_ins)
    return results[: len(outs)], results[len(outs) :]


def tiled_grad(left, right, store, serve, size=384):
    for tile in range(left.shape[1] // size):
        cols = slice(tile * size, (tile + 1) * size)
        store(tile, size, dot(left[:, cols], right[...], TN).astype(BF16))
        serve(tile)


def normed(hidden):
    center = hidden - jnp.mean(hidden, axis=-1, keepdims=True)
    inverse = lax.rsqrt(jnp.mean(center * center, axis=-1, keepdims=True) + EPS)
    return center * inverse, inverse


def norm_back(hidden, scale_row, grad):
    hat, inverse = normed(hidden)
    inner = grad * scale_row
    back = inverse * (
        inner
        - jnp.mean(inner, axis=-1, keepdims=True)
        - hat * jnp.mean(inner * hat, axis=-1, keepdims=True)
    )
    return back, hat


def loop_rows(total, size, body):
    def step(index, carry):
        body(pl.ds(pl.multiple_of(index * size, size), size), index)
        return carry

    lax.fori_loop(0, total // size, step, 0)


def add_sum(ref, row, block):
    ref[row : row + 1] += jnp.sum(block, axis=0, keepdims=True)


def turned(rows):
    lane = lax.broadcasted_iota(jnp.int32, rows.shape, 1)
    width = rows.shape[1]
    return jnp.where(
        lax.rem(lane, 2) == 0, -pltpu.roll(rows, width - 1, 1), pltpu.roll(rows, 1, 1)
    )


def head_cols(head):
    return slice(head * HEAD_DIM, (head + 1) * HEAD_DIM)


def inverse_rms(sums, features):
    return lax.rsqrt(sums / features + EPS)


MODS, OUT_BIAS, CROSS_GAIN, CROSS_SHIFT = 0, 6, 9, 10
KEY_BIAS, GAINS = 5, 6


def row_of(ref, index):
    return ref[index : index + 1]


def first_kernel(
    side,
    lengths,
    block_order,
    time_embed,
    modulation,
    out_bias,
    cross_gain,
    cross_shift,
    proj_bias,
    key_bias,
    norm_gains,
    ffn_bias,
    positions,
    table,
    base,
    counts,
    cosine,
    sine,
    nothing,
    *rest,
):
    rest = list(rest)
    packs = rest[: 3 * LAYERS]
    send_sems, recv_sems = rest[-2:]
    rest = rest[3 * LAYERS : -2]
    greet(side, True, side.masks)
    near, far = holders()
    tokens = counts.shape[2]
    clip = lax.axis_index(DP) // HOLD
    mine = (lengths[clip] - block_order[0] * tokens).astype(F32)
    counts[0] = jnp.full(counts.shape[1:], mine, F32)

    def copy(number, source, target, device):
        return send(
            counts.at[source],
            counts.at[target],
            send_sems.at[number],
            recv_sems.at[number],
            dp=device,
        )

    to_near, to_far, onward = copy(0, 0, 1, near), copy(1, 0, 2, far), copy(2, 2, 3, near)
    side.start()
    to_near.start()
    to_far.start()
    for layer in range(LAYERS):
        rows_d, rows_w, rows_f = packs[3 * layer : 3 * layer + 3]
        rows_d[...] = jnp.zeros(rows_d.shape, F32)
        rows_w[...] = jnp.zeros(rows_w.shape, F32)
        for row in range(6):
            embed = jnp.zeros((1, rows_d.shape[1]), F32)
            for index in range(time_embed.shape[1]):
                embed = embed + jnp.where(clip == index, row_of(time_embed.at[row], index), 0.0)
            rows_d[row : row + 1] = row_of(modulation.at[row], layer) + embed
        for row in range(3):
            rows_d[OUT_BIAS + row : OUT_BIAS + row + 1] = row_of(out_bias.at[row], layer)
        rows_d[CROSS_GAIN : CROSS_GAIN + 1] = row_of(cross_gain, layer)
        rows_d[CROSS_SHIFT : CROSS_SHIFT + 1] = row_of(cross_shift, layer)
        for row in range(5):
            rows_w[row : row + 1] = row_of(proj_bias.at[row], layer)
        rows_w[KEY_BIAS : KEY_BIAS + 1] = row_of(key_bias, layer)
        rows_w[GAINS : GAINS + 4] = norm_gains[layer]
        rows_f[...] = row_of(ffn_bias, layer)
    nothing[...] = jnp.zeros(nothing.shape, F32)
    angles = dot(positions[...].astype(F32), table[...], TN, exact=True)
    cosine[...] = jnp.cos(angles)
    sine[...] = jnp.sin(angles)
    to_far.wait_recv()
    onward.start()
    side.move(1, SELF)
    side.start(1)
    to_near.wait_recv()
    onward.wait_recv()
    for copy in (to_near, to_far, onward):
        copy.wait_send()
    side.finish(SELF)
    attend_body(
        side, base, None, None, packs[0], packs[1], side.jobs[0].out, cosine, sine, counts, True, rest
    )


def add_branch(base, tot, bias_row, gate_row):
    return base + (tot.astype(F32) + bias_row) * gate_row


def attend_kernel(
    side, base, tot, rows_before, rows_d, rows_w, weight, cosine, sine, counts, *refs
):
    greet(side, True, [1, 2])
    side.start()
    attend_body(
        side, base, tot, rows_before, rows_d, rows_w, weight, cosine, sine, counts, False, list(refs)
    )


def attend_body(
    side, base, tot, rows_before, rows_d, rows_w, weight, cosine, sine, counts, first, refs
):
    hidden, normal, query, key, query_rot, key_value, slots = refs[:7]
    others, result, lse = refs[7:10]
    scores, send_sems, recv_sems, hold_sends, hold_recvs = refs[-5:]
    tokens, width = query.shape
    features = hidden.shape[1]
    heads = width // HEAD_DIM
    scale_row = 1.0 + row_of(rows_d, MODS + 1)
    shift_row = row_of(rows_d, MODS)

    def project(rows, index):
        if first:
            block = base[rows].astype(F32)
        else:
            block = add_branch(
                base[rows], tot[rows], row_of(rows_before, OUT_BIAS + 2), row_of(rows_before, MODS + 5)
            )
        hidden[rows] = block
        block = (normed(block)[0] * scale_row + shift_row).astype(BF16)
        normal[rows] = block
        query[rows] = dot(block, weight[0]) + row_of(rows_w, 0)
        key[rows] = dot(block, weight[1]) + row_of(rows_w, KEY_BIAS)
        value = (dot(block, weight[2]) + row_of(rows_w, 1)).astype(BF16)
        for head in range(heads):
            key_value[head, 1, rows] = value[:, head_cols(head)]

    if not first:
        side.need(WEIGHT)
    loop_rows(tokens, 256, project)
    side.store(HIDDEN, NORMAL, QUERY, KEY)
    near, far = holders()

    def copy(source, target, number, device):
        return send(source, target, hold_sends.at[number], hold_recvs.at[number], dp=device)

    to_near = copy(key_value, others.at[0], 0, near)
    values_far, keys_far = [
        [
            copy(
                key_value.at[head, member],
                others.at[1, head, member],
                1 + (1 + member) * heads + head,
                far,
            )
            for head in range(heads)
        ]
        for member in (1, 0)
    ]
    onward = [
        copy(others.at[1, head], others.at[2, head], 1 + head, near) for head in range(heads)
    ]
    for item in values_far:
        item.start()
    exchange = Exchange(slots, send_sems, recv_sems)
    exchange.start(
        stat_rows(query[...] * query[...], 0) + stat_rows(key[...] * key[...], 1)
    )
    side.early()
    exchange.finish()
    query_inv = inverse_rms(stat_column(slots, 0, HEAD_DIM), features)
    key_inv = inverse_rms(stat_column(slots, 1, HEAD_DIM), features)
    if not first:
        side.need(COSINE, SINE)
    for head in range(heads):
        cols = head_cols(head)
        rows = key[:, cols] * key_inv * rows_w[GAINS + 1 : GAINS + 2, cols]
        key_value[head, 0] = (rows * cosine[...] + turned(rows) * sine[...]).astype(BF16)
        keys_far[head].start()
    to_near.start()
    for head in range(heads):
        cols = head_cols(head)
        rows = query[:, cols] * query_inv * rows_w[GAINS : GAINS + 1, cols]
        query_rot[:, cols] = (rows * cosine[...] + turned(rows) * sine[...]).astype(BF16)
    side.store(QUERY_ROT)
    side.middle()

    def score(head, slot, keys):
        block = dot(keys, query_rot[:, head_cols(head)], NT) * (SCALE * LOG2E)
        scores[head, slot] = jnp.where(below(counts, slot, block.shape), block, -1e30)

    for head in range(heads):
        score(head, 0, key_value[head, 0])
    to_near.wait_recv()
    for head in range(heads):
        score(head, 1, others[0, head, 0])
    lse[...] = jnp.zeros(lse.shape, F32)
    for head in range(heads):
        values_far[head].wait_recv()
        keys_far[head].wait_recv()
        onward[head].start()
        if head == 0:
            side.late()
        score(head, 2, others[1, head, 0])
        onward[head].wait_recv()
        score(head, 3, others[2, head, 0])
        top = jnp.max(scores[head, 0], axis=0, keepdims=True)
        for slot in range(1, HOLD):
            top = jnp.maximum(top, jnp.max(scores[head, slot], axis=0, keepdims=True))
        total = jnp.zeros_like(top)
        summed = jnp.zeros((HEAD_DIM, tokens), F32)
        for slot in range(HOLD):
            values = key_value[head, 1] if slot == 0 else others[slot - 1, head, 1]
            probs = jnp.exp2(scores[head, slot] - top)
            total = total + jnp.sum(probs, axis=0, keepdims=True)
            summed = summed + dot(values, probs.astype(BF16), TN)
        result[:, head_cols(head)] = (summed / total).T.astype(BF16)
        lse[head : head + 1] = top + jnp.log2(total)
    for item in [to_near] + values_far + keys_far + onward:
        item.wait_send()
    side.finish()


def below(counts, slot, shape):
    index = lax.broadcasted_iota(jnp.int32, shape, 0).astype(F32)
    return index < counts[slot, 0:1]


def softmax_back(scores, lse_row, mask):
    probs = jnp.exp2(scores * (SCALE * LOG2E) - lse_row)
    return probs if mask is None else jnp.where(mask, probs, 0.0)


def out_sum_kernel(
    first,
    side,
    rows_in,
    weight,
    context,
    text_weight,
    rows_w,
    total,
    text_key,
    text_kb,
    text_vb,
    slots,
    *refs,
):
    refs = list(refs)
    own, arrived = context, []
    if first:
        context = refs.pop(0)
        clip_sends, clip_recvs = refs[-2:]
        refs = refs[:-2]
    send_sems, recv_sems, part, came, pair, peers, sems = refs
    greet(side, True, side.masks)
    if first:
        near, far = holders()
        place = lax.rem(lax.axis_index(DP), HOLD)
        size = own.shape[0]

        def block(index):
            return context.at[pl.ds(pl.multiple_of(index * size, 16), size)]

        def copy(number, index, device):
            return send(
                block(index), block(index), clip_sends.at[number], clip_recvs.at[number], dp=device
            )

        arrived = [copy(0, place, near), copy(1, place, far), copy(2, flip(place, 2), near)]
        side.need(CONTEXT)
        context[pl.ds(pl.multiple_of(place * size, 16), size)] = own[...]
        arrived[1].start()
        arrived[0].start()
    side.start()
    chain = Chain(part, total, (came, pair, peers), sems)
    tokens, features = total.shape
    per_block = 128 // CHUNK

    def project(rows, index):
        part[rows] = dot(rows_in[rows], weight[...], NT).astype(BF16)
        chain.begin(index * per_block, per_block)

    side.need(OUT)
    loop_rows(tokens, 128, project)
    low = 0
    if first:
        low = 4
        chain.segment(0, low, 0, 0)
        arrived[1].wait_recv()
        arrived[2].start()
        arrived[0].wait_recv()
        arrived[2].wait_recv()
        for item in arrived:
            item.wait_send()
    else:
        side.need(CONTEXT)
    side.need(TEXT_WEIGHT)
    text_count, width = text_key.shape
    blocks = text_count // 128

    def text(rows, index):
        block = context[rows]
        text_key[rows] = dot(block, text_weight[0]) + row_of(rows_w, 3)
        chain.serve(low + 2 * index)
        text_vb[rows] = (dot(block, text_weight[1]) + row_of(rows_w, 4)).astype(BF16)
        chain.serve(low + 2 * index + 1)

    loop_rows(text_count, 128, text)
    exchange = Exchange(slots, send_sems, recv_sems)

    def early():
        side.early()
        exchange.start(stat_rows(text_key[...] * text_key[...], 0))

    chain.drain(low + 2 * blocks, early, side.middle)
    exchange.finish()
    text_inv = inverse_rms(stat_column(slots, 0, HEAD_DIM), features)
    for head in range(width // HEAD_DIM):
        cols = head_cols(head)
        text_kb[:, cols] = (
            text_key[:, cols] * text_inv * rows_w[GAINS + 3 : GAINS + 4, cols]
        ).astype(BF16)
    side.finish()


def cross_ffn_kernel(
    gathered,
    side,
    base,
    tot,
    rows_d,
    rows_w,
    rows_f,
    weight,
    text_kb,
    text_vb,
    out_weight,
    up,
    *refs,
):
    refs = list(refs)
    down = side.jobs[0].out if gathered else refs.pop(0)
    hidden, normal, query, query_b, result, lse, slots = refs[:7]
    hidden_f, normal_f, gelu_b, slope, total_f = refs[7:12]
    send_sems, recv_sems, total = refs[12:15]
    part, came, pair, peers, sems = refs[15:20]
    part_f, came_f, pair_f, peers_f, sems_f = refs[20:25]
    greet(side, True, side.masks)
    side.late_after = True
    side.start()
    chain = Chain(part, total, (came, pair, peers), sems)
    chain_f = Chain(part_f, total_f, (came_f, pair_f, peers_f), sems_f)
    tokens, width = query.shape
    features = hidden.shape[1]
    heads = width // HEAD_DIM

    def project(rows, index):
        block = add_branch(
            base[rows], tot[rows], row_of(rows_d, OUT_BIAS), row_of(rows_d, MODS + 2)
        )
        hidden[rows] = block
        block = normed(block)[0] * row_of(rows_d, CROSS_GAIN) + row_of(rows_d, CROSS_SHIFT)
        block = block.astype(BF16)
        normal[rows] = block
        query[rows] = dot(block, weight[...]) + row_of(rows_w, 2)

    side.need(WEIGHT)
    side.load(True)
    loop_rows(tokens, 256, project)
    side.store(HIDDEN, NORMAL, QUERY)
    exchange = Exchange(slots, send_sems, recv_sems)
    exchange.start(stat_rows(query[...] * query[...], 0))
    exchange.finish()
    query_inv = inverse_rms(stat_column(slots, 0, HEAD_DIM), features)
    side.need(TEXT_KB, TEXT_VB)
    lse[...] = jnp.zeros(lse.shape, F32)
    for head in range(heads):
        cols = head_cols(head)
        query_b[:, cols] = (
            query[:, cols] * query_inv * rows_w[GAINS + 2 : GAINS + 3, cols]
        ).astype(BF16)
        scores = dot(text_kb[:, cols], query_b[:, cols], NT) * (SCALE * LOG2E)
        top = jnp.max(scores, axis=0, keepdims=True)
        probs = jnp.exp2(scores - top)
        amount = jnp.sum(probs, axis=0, keepdims=True)
        summed = dot(text_vb[:, cols], probs.astype(BF16), TN)
        result[:, cols] = (summed / amount).T.astype(BF16)
        lse[head : head + 1] = top + jnp.log2(amount)
    per_block = 128 // CHUNK

    def project_out(rows, index):
        part[rows] = dot(result[rows], out_weight[...], NT).astype(BF16)
        chain.begin(index * per_block, per_block)

    side.store(QUERY_B, RESULT)
    side.need(OUT)
    loop_rows(tokens, 128, project_out)
    side.move(1, DOWN)
    side.start(1)
    scale_row = 1.0 + row_of(rows_d, MODS + 4)
    shift_row = row_of(rows_d, MODS + 3)

    def rows_of(rows):
        block = add_branch(hidden[rows], total[rows], row_of(rows_d, OUT_BIAS + 1), 1.0)
        hidden_f[rows] = block
        block = (normed(block)[0] * scale_row + shift_row).astype(BF16)
        normal_f[rows] = block
        return block

    def inner(rows, block, low, high):
        z = dot(block, up[:, low:high]) + rows_f[:, low:high]
        square = z * z
        tanh = jnp.tanh(GELU_A * z * (1.0 + GELU_B * square))
        side_value = 0.5 * (1.0 + tanh)
        gelu_b[rows, low:high] = (z * side_value).astype(BF16)
        slope[rows, low:high] = (
            side_value
            + 0.5 * z * (1.0 - tanh * tanh) * (GELU_A * (1.0 + 3.0 * GELU_B * square))
        ).astype(BF16)

    def before_second():
        if gathered:
            side.finish(DOWN)
        else:
            side.need(DOWN)

    def after(left):
        side.store(HIDDEN_F, NORMAL_F, GELU_B_NAME, SLOPE)

    side.need(UP)
    mlp_loop(
        side, tokens, rows_of, inner, down, chain_f, gelu_b, before_second, after, chain
    )


def column_cuts(width):
    cuts, low = [], 0
    while low < width:
        high = low + 512 if width - low >= 1024 else width
        cuts.append((low, high))
        low = high
    return cuts


GELU_A = 0.7978845608028654
GELU_B = 0.044715


def mlp_loop(side, tokens, rows_of, inner, second, chain, middle, before_second, after, feed=None):
    size = 128
    per_block = size // CHUNK
    features, hidden_width = second.shape
    cuts = column_cuts(hidden_width)
    half = features // 2
    blocks = tokens // size
    if feed is not None:

        @pl.when(feed.is_mid)
        def _():
            feed.first(0)
            for k in range(1, per_block):
                feed.first(k)
                feed.second(k - 1)

    def step(index, carry):
        rows = pl.ds(pl.multiple_of(index * size, size), size)
        low = index * per_block

        def serve(offset):
            if feed is None:

                @pl.when(index > 0)
                def _():
                    chain.serve(jnp.maximum(low - per_block, 0) + offset)

                return
            if offset > 0:

                @pl.when(feed.is_mid & (index < blocks - 1))
                def _():
                    ahead = jnp.minimum(low + per_block, feed.chunks - per_block)
                    feed.first(ahead + offset)
                    feed.second(ahead + offset - 1)

            @pl.when(index == blocks - 1)
            def _():
                chain.serve(offset)

        if feed is not None:

            @pl.when(feed.is_mid)
            def _():
                @pl.when(index < blocks - 1)
                def _():
                    feed.first(jnp.minimum(low + per_block, feed.chunks - per_block))

                feed.second(low + per_block - 1)

            @pl.when(feed.is_end)
            def _():
                for offset in range(per_block):
                    feed.inward(low + offset, feed.inner).wait_send()
                    feed.outward(low + offset, feed.inner).wait_recv()

        block = rows_of(rows)
        served = 0
        for place, (left, right) in enumerate(cuts):
            inner(rows, block, left, right)
            if place % 2 == 1 and served < 2:
                serve(served)
                served += 1
        while served < 2:
            serve(served)
            served += 1

        @pl.when(index == 0)
        def _():
            before_second()

        for part_index in range(2):
            cols = slice(part_index * half, (part_index + 1) * half)
            chain.part[rows, cols] = dot(middle[rows], second[cols], NT).astype(BF16)
            if part_index == 0:
                serve(2)
        chain.begin(low, per_block)
        serve(3)
        if side.jobs:
            if feed is None:
                points = ((1, bits_of_dp() - 2), (blocks - 1, bits_of_dp() - 1))
            else:
                points = ((blocks - 1, bits_of_dp() - 2),)
            for point, target in points:

                @pl.when(index == point)
                def _(target=target):
                    side.move(target)

        return carry

    lax.fori_loop(0, blocks, step, 0)
    left = (blocks - 1) * per_block if feed is None else per_block
    left = after(left) or left
    chain.drain(left, None, None if feed is None else side.late)
    if feed is not None:
        feed.close()
    side.finish()


def ffn_back_kernel(
    joined,
    side,
    grad,
    *refs,
):
    refs = list(refs)

    def take(count):
        taken = refs[:count]
        del refs[:count]
        return taken

    if joined:
        branch, hidden, rows_above = take(3)
    else:
        teacher, counts = take(2)
    tot, rows_d, down, up, slope, normal, gelu_b = take(7)
    if joined:
        new_grad, sums_above = take(2)
    else:
        new_grad, output = take(2)
    (total, sums, bias_sum, up_grad, down_grad) = take(5)
    down_in, inner_b, stage, stage_sems, part, came, pair, peers, sems = refs
    greet(side, True, side.masks)
    side.late_after = True
    side.start()
    chain = Chain(part, total, (came, pair, peers), sems)
    tokens = grad.shape[0]
    sums[...] = jnp.zeros(sums.shape, F32)
    bias_sum[...] = jnp.zeros(bias_sum.shape, F32)
    if joined:
        sums_above[...] = jnp.zeros(sums_above.shape, F32)
        scale_row = 1.0 + row_of(rows_above, MODS + 1)

    def rows_of(rows):
        block = grad[rows]
        if joined:
            step = branch[rows].astype(F32)
            back, hat = norm_back(hidden[rows], scale_row, step)
            add_sum(sums_above, 0, step)
            add_sum(sums_above, 1, step * hat)
            block = block + back
            new_grad[rows] = block
        else:
            block = add_branch(
                block, tot[rows], row_of(rows_d, OUT_BIAS + 2), row_of(rows_d, MODS + 5)
            )
            output[rows] = block
            block = block - teacher[rows].astype(F32)
            place = lax.broadcasted_iota(jnp.int32, (block.shape[0], 1), 0) + rows.start
            block = jnp.where(place.astype(F32) < counts[0, 0:1, 0:1], block, 0.0)
            new_grad[rows] = block
            add_sum(sums, 2, block * block)
        add_sum(sums, 0, block * (tot[rows].astype(F32) + row_of(rows_d, OUT_BIAS + 2)))
        block = (block * row_of(rows_d, MODS + 5)).astype(BF16)
        down_in[rows] = block
        add_sum(sums, 1, block.astype(F32))
        return block

    def inner(rows, block, low, high):
        cols = (dot(block, down[:, low:high]) * slope[rows, low:high].astype(F32)).astype(BF16)
        inner_b[rows, low:high] = cols
        bias_sum[0:1, low:high] += jnp.sum(cols.astype(F32), axis=0, keepdims=True)

    def after(left):
        side.store(NEW_GRAD)
        if not joined:
            side.store(OUTPUT)
        side.need(NORMAL, GELU_B_NAME)
        copies = []

        def keep(target):
            def store(tile, size, block):
                number = len(copies)
                if number >= 2:
                    copies[number - 2].wait()
                stage[number % 2] = block
                copy = pltpu.make_async_copy(
                    stage.at[number % 2],
                    target.at[tile * size : (tile + 1) * size],
                    stage_sems.at[number % 2],
                )
                copy.start()
                copies.append(copy)

            return store

        def serve(tile):
            if left + tile < chain.chunks:
                chain.serve(left + tile)

        tiled_grad(normal, inner_b, keep(up_grad), serve, stage.shape[1])
        chain.segment(chain.chunks, chain.chunks, 0, 0)
        tiled_grad(down_in, gelu_b, keep(down_grad), lambda tile: None, stage.shape[1])
        copies[-2].wait()
        copies[-1].wait()
        return chain.chunks

    side.need(GRAD, DOWN, SLOPE)
    side.load(True)
    mlp_loop(
        side, tokens, rows_of, inner, up, chain, inner_b, lambda: side.need(UP), after
    )


def cross_back_kernel(
    side,
    grad,
    branch,
    hidden,
    rows_d,
    rows_w,
    out_weight,
    query,
    query_b,
    lse,
    slots_q,
    text_kb,
    text_vb,
    weight,
    normal,
    result,
    new_grad,
    text_grad,
    sums,
    width_sums,
    total,
    matrix_grad,
    out_in,
    query_grad_b,
    out_grad,
    query_n,
    slots,
    send_sems,
    recv_sems,
    part,
    came,
    pair,
    peers,
    sems,
):
    greet(side, True, side.masks)
    side.late_after = True
    side.start()
    chain = Chain(part, total, (came, pair, peers), sems)
    tokens, width = query.shape
    features = grad.shape[1]
    heads = width // HEAD_DIM
    gain = rows_w[GAINS + 2 : GAINS + 3]
    sums[...] = jnp.zeros(sums.shape, F32)
    width_sums[...] = jnp.zeros(width_sums.shape, F32)
    scale_row = 1.0 + row_of(rows_d, MODS + 4)

    def enter(rows, index):
        step = branch[rows].astype(F32)
        back, hat = norm_back(hidden[rows], scale_row, step)
        add_sum(sums, 0, step)
        add_sum(sums, 1, step * hat)
        block = grad[rows] + back
        new_grad[rows] = block
        block = block.astype(BF16)
        out_in[rows] = block
        add_sum(sums, 2, block.astype(F32))
        out_grad[rows] = dot(block, out_weight[...]).astype(BF16)

    side.need(OUT)
    side.load(True)
    loop_rows(tokens, 256, enter)
    side.store(NEW_GRAD)
    side.need(QUERY, QUERY_B, TEXT_KB, TEXT_VB)
    for head in range(heads):
        cols = head_cols(head)
        query_h, out_grad_h = query_b[:, cols], out_grad[:, cols]
        text_k, text_v = text_kb[:, cols], text_vb[:, cols]
        probs = softmax_back(dot(text_k, query_h, NT), lse[head : head + 1], None)
        prob_grad = dot(text_v, out_grad_h, NT)
        inner = jnp.sum(probs * prob_grad, axis=0, keepdims=True)
        score_b = (probs * (prob_grad - inner) * SCALE).astype(BF16)
        query_n[:, cols] = dot(text_k, score_b, TN).T
        text_grad[0, :, cols] = dot(score_b, query_h)
        text_grad[1, :, cols] = dot(probs.astype(BF16), out_grad_h)
    exchange = Exchange(slots, send_sems, recv_sems)
    exchange.start(stat_rows(query[...] * query_n[...] * gain, 0))
    inverse = inverse_rms(stat_column(slots_q, 0, HEAD_DIM), features)
    side.move(1)
    exchange.finish()
    term = stat_column(slots, 0, HEAD_DIM) * inverse * inverse * inverse / features
    for head in range(heads):
        cols = head_cols(head)
        width_sums[0:1, cols] = jnp.sum(
            query[:, cols] * query_n[:, cols] * inverse, axis=0, keepdims=True
        )
        block = inverse * gain[:, cols] * query_n[:, cols] - query[:, cols] * term
        block = block.astype(BF16)
        query_grad_b[:, cols] = block
        width_sums[1:2, cols] = jnp.sum(block.astype(F32), axis=0, keepdims=True)
    per_block = 128 // CHUNK

    def leave(rows, index):
        part[rows] = dot(query_grad_b[rows], weight[...], NT).astype(BF16)
        chain.begin(index * per_block, per_block)

    side.store(TEXT_GRAD)
    side.need(WEIGHT)
    loop_rows(tokens, 128, leave)
    side.need(NORMAL, RESULT)

    def keep(low):
        def store(tile, size, block):
            matrix_grad[tile * size : (tile + 1) * size, low : low + width] = block

        return store

    tiled_grad(normal, query_grad_b, keep(0), lambda tile: None if tile % 2 else chain.serve(tile // 2))
    tiled_grad(out_in, result, keep(width), lambda tile: None if tile % 2 else chain.serve(2 + tile // 2))
    side.store(MATRIX_GRAD)
    chain.drain(4, side.late)
    side.finish()


def attend_back_kernel(
    side,
    counts,
    grad,
    branch,
    hidden,
    rows_d,
    tot,
    out_weight,
    query,
    key_value,
    others,
    lse,
    text_grad,
    result,
    new_grad,
    matrix_grad,
    sums,
    query_grad,
    key_value_grad,
    text_sum,
    out_in,
    out_grad,
    probs,
    prob_grads,
    away,
    landed,
    text_away,
    text_landed,
    send_sems,
    recv_sems,
):
    greet(side, False, [1, 2])
    side.start()
    near, far = holders()
    tokens, width = query.shape
    heads = width // HEAD_DIM
    text_rows = text_sum.shape[1]
    sums[...] = jnp.zeros(sums.shape, F32)

    def copy(kind, head):
        return send(
            away.at[kind, head],
            landed.at[kind, head],
            send_sems.at[kind, head],
            recv_sems.at[kind, head],
            dp=far if kind == 1 else near,
        )

    def text_copy(kind):
        return send(
            text_away.at[kind],
            text_landed.at[kind],
            send_sems.at[kind, heads],
            recv_sems.at[kind, heads],
            dp=far if kind == 1 else near,
        )

    place = lax.rem(lax.axis_index(DP), HOLD)

    def text_part(slot):
        start = pl.multiple_of(flip(place, slot) * text_rows, text_rows)
        return text_grad[:, pl.ds(start, text_rows)]

    text_away[2] = text_part(3).astype(BF16)
    text_copy(2).start()
    text_away[0] = text_part(1).astype(BF16)
    text_copy(0).start()

    def enter(rows, index):
        step = branch[rows].astype(F32)
        back, hat = norm_back(hidden[rows], row_of(rows_d, CROSS_GAIN), step)
        add_sum(sums, 0, step * hat)
        add_sum(sums, 1, step)
        block = grad[rows] + back
        new_grad[rows] = block
        add_sum(sums, 2, block * (tot[rows].astype(F32) + row_of(rows_d, OUT_BIAS)))
        block = (block * row_of(rows_d, MODS + 2)).astype(BF16)
        out_in[rows] = block
        add_sum(sums, 3, block.astype(F32))
        out_grad[rows] = dot(block, out_weight[...]).astype(BF16)

    side.need(OUT)
    loop_rows(tokens, 256, enter)
    side.store(NEW_GRAD)
    side.need(QUERY, KEY_VALUE, OTHERS, RESULT)
    text_copy(2).wait_recv()
    text_away[1] = (text_part(2) + text_landed[2].astype(F32)).astype(BF16)
    text_copy(1).start()

    for head in range(heads):
        cols = head_cols(head)
        query_h, out_grad_h = query[:, cols], out_grad[:, cols]

        def pair_of(slot, head=head):
            if slot == 0:
                return key_value[head, 0], key_value[head, 1]
            return others[slot - 1, head, 0], others[slot - 1, head, 1]

        inner = jnp.zeros((1, tokens), F32)
        for slot in range(HOLD):
            keys, values = pair_of(slot)
            block = softmax_back(
                dot(keys, query_h, NT),
                lse[head : head + 1],
                below(counts, slot, (tokens, tokens)),
            )
            probs[slot] = block
            block_grad = dot(values, out_grad_h, NT)
            prob_grads[slot] = block_grad
            inner = inner + jnp.sum(block * block_grad, axis=0, keepdims=True)
        query_n = jnp.zeros((HEAD_DIM, tokens), F32)
        for slot in (3, 2, 1, 0):
            keys, values = pair_of(slot)
            block = probs[slot]
            score_b = (block * (prob_grads[slot] - inner) * SCALE).astype(BF16)
            query_n = query_n + dot(keys, score_b, TN)
            key_g = dot(score_b, query_h)
            value_g = dot(block.astype(BF16), out_grad_h)
            if slot == 0:
                key_value_grad[0, :, cols] = key_g
                key_value_grad[1, :, cols] = value_g
            elif slot == 2:
                copy(2, head).wait_recv()
                away[1, head, 0] = (key_g + landed[2, head, 0].astype(F32)).astype(BF16)
                away[1, head, 1] = (value_g + landed[2, head, 1].astype(F32)).astype(BF16)
                copy(1, head).start()
            else:
                away[slot - 1, head, 0] = key_g.astype(BF16)
                away[slot - 1, head, 1] = value_g.astype(BF16)
                copy(slot - 1, head).start()
        query_grad[:, cols] = query_n.T
    side.store(QUERY_GRAD)

    def keep(tile, size, block):
        matrix_grad[tile * size : (tile + 1) * size] = block

    tiled_grad(out_in, result, keep, lambda tile: None)
    side.store(MATRIX_GRAD)
    text_copy(0).wait_recv()
    text_copy(1).wait_recv()
    text_sum[...] = text_part(0) + text_landed[0].astype(F32) + text_landed[1].astype(F32)
    for head in range(heads):
        cols = head_cols(head)
        copy(0, head).wait_recv()
        copy(1, head).wait_recv()
        for member in range(2):
            key_value_grad[member, :, cols] += landed[0, head, member].astype(F32) + landed[
                1, head, member
            ].astype(F32)
    for kind in range(3):
        text_copy(kind).wait_send()
        for head in range(heads):
            copy(kind, head).wait_send()


def qkv_back_kernel(
    side,
    query_grad,
    key_value_grad,
    text_grad,
    query,
    key,
    text_key,
    slots_in,
    text_slots,
    rows_w,
    cosine,
    sine,
    weight,
    normal,
    context,
    text_weight,
    context_before,
    width_sums,
    context_part,
    total,
    self_grad,
    text_matrix,
    grads_b,
    text_b,
    query_n,
    key_n,
    slots,
    send_sems,
    recv_sems,
    part,
    came,
    pair,
    peers,
    sems,
):
    greet(side, True, side.masks)
    side.start()
    chain = Chain(part, total, (came, pair, peers), sems)
    tokens, width = query.shape
    features = total.shape[1]
    heads = width // HEAD_DIM
    text_rows = text_grad.shape[1]
    place = lax.rem(lax.axis_index(DP), HOLD)
    mine = pl.ds(pl.multiple_of(place * text_rows, text_rows), text_rows)
    text_k = text_key[mine]
    width_sums[...] = jnp.zeros(width_sums.shape, F32)
    for head in range(heads):
        cols = head_cols(head)
        rows = query_grad[:, cols]
        query_n[:, cols] = rows * cosine[...] - turned(rows * sine[...])
        rows = key_value_grad[0, :, cols]
        key_n[:, cols] = rows * cosine[...] - turned(rows * sine[...])

    def gain(member):
        return rows_w[GAINS + member : GAINS + member + 1]

    exchange = Exchange(slots, send_sems, recv_sems)
    text_terms = stat_rows(text_k * gain(3) * text_grad[0], 2)
    exchange.start(
        stat_rows(query[...] * gain(0) * query_n[...], 0)
        + stat_rows(key[...] * gain(1) * key_n[...], 1)
        + jnp.concatenate([text_terms, jnp.zeros((8, tokens - text_rows), F32)], axis=1)
    )
    query_inv = inverse_rms(stat_column(slots_in, 0, HEAD_DIM), features)
    key_inv = inverse_rms(stat_column(slots_in, 1, HEAD_DIM), features)
    text_inv = inverse_rms(stat_column(text_slots.at[:, :, mine], 0, HEAD_DIM), features)
    side.move(1)
    exchange.finish()

    def cubed(inverse, term):
        return term * inverse * inverse * inverse / features

    query_t = cubed(query_inv, stat_column(slots, 0, HEAD_DIM))
    key_t = cubed(key_inv, stat_column(slots, 1, HEAD_DIM))
    text_t = cubed(text_inv, stat_column(slots.at[:, :, pl.ds(0, text_rows)], 2, HEAD_DIM))

    def back(member, cols, values, inverse, term, grads):
        width_sums[member : member + 1, cols] = jnp.sum(
            values * inverse * grads, axis=0, keepdims=True
        )
        block = inverse * gain(member)[:, cols] * grads - values * term
        block = block.astype(BF16)
        width_sums[4 + member : 5 + member, cols] = jnp.sum(
            block.astype(F32), axis=0, keepdims=True
        )
        return block

    def shifted(cols, member):
        return slice(cols.start + member * width, cols.stop + member * width)

    for head in range(heads):
        cols = head_cols(head)
        grads_b[:, cols] = back(0, cols, query[:, cols], query_inv, query_t, query_n[:, cols])
        grads_b[:, shifted(cols, 1)] = back(
            1, cols, key[:, cols], key_inv, key_t, key_n[:, cols]
        )
        text_b[:, cols] = back(
            3, cols, text_k[:, cols], text_inv, text_t, text_grad[0, :, cols]
        )
    block = key_value_grad[1].astype(BF16)
    grads_b[:, 2 * width :] = block
    width_sums[6:7] = jnp.sum(block.astype(F32), axis=0, keepdims=True)
    block = text_grad[1].astype(BF16)
    text_b[:, width:] = block
    width_sums[8:9] = jnp.sum(block.astype(F32), axis=0, keepdims=True)
    per_block = 128 // CHUNK

    def leave(rows, index):
        part[rows] = (
            dot(grads_b[rows, :width], weight[0], NT)
            + dot(grads_b[rows, width : 2 * width], weight[1], NT)
            + dot(grads_b[rows, 2 * width :], weight[2], NT)
        ).astype(BF16)
        chain.begin(index * per_block, per_block)

    side.need(WEIGHT)
    loop_rows(tokens, 128, leave)
    side.need(NORMAL, CONTEXT, TEXT_WEIGHT)

    def keep(target):
        def store(tile, size, block):
            target[tile * size : (tile + 1) * size] = block

        return store

    tiled_grad(normal, grads_b, keep(self_grad), chain.serve)
    side.store(SELF_GRAD)
    tiled_grad(context, text_b, keep(text_matrix), lambda tile: None)
    side.store(TEXT_MATRIX)
    chain.serve(4)
    side.need(BEFORE)
    context_part[...] = (
        context_before[...]
        + dot(text_b[:, :width], text_weight[0], NT)
        + dot(text_b[:, width:], text_weight[1], NT)
    )
    chain.drain(5, side.late)
    side.finish()


def small_rows(clips):
    low = 6 * LAYERS + 6 * clips
    places = {BIAS: low, GAIN: low + 3 * LAYERS, SHIFT: low + 4 * LAYERS}
    places[LOSS] = low + 5 * LAYERS
    return places, (low + 5 * LAYERS + 1 + 15) // 16 * 16


def last_kernel(
    clips,
    side,
    context_part,
    grad,
    branch,
    hidden,
    rows_d,
    *refs,
):
    refs = list(refs)

    def take(count):
        taken = refs[:count]
        del refs[:count]
        return taken

    above = take(1)[0]
    small = [take(6) for _ in range(LAYERS)]
    new_grad, total, out_d, out_w, out_f = take(5)
    sums = take(1)[0]
    part, came, pair, peers, sems = take(5)
    bits = bits_of_dp()
    away = [take(3) for _ in range(bits)]
    landed = [take(3) for _ in range(bits)]
    send_sems, recv_sems = take(2)
    greet(side, True, side.masks)
    side.start()
    me = lax.axis_index(DP)
    clip = me // HOLD
    chain = Chain(part, total, (came, pair, peers), sems)
    part[...] = context_part[...].astype(BF16)
    chain.begin(0, chain.chunks)
    sums[...] = jnp.zeros(sums.shape, F32)
    scale_row = 1.0 + row_of(rows_d, MODS + 1)
    tokens = grad.shape[0]
    size = tokens // chain.chunks
    side.need(GRAD, BRANCH, HIDDEN)

    def enter(rows, index):
        step = branch[rows].astype(F32)
        back, hat = norm_back(hidden[rows], scale_row, step)
        add_sum(sums, 0, step)
        add_sum(sums, 1, step * hat)
        new_grad[rows] = grad[rows] + back
        chain.serve(index)

    loop_rows(tokens, size, enter)
    side.store(NEW_GRAD)
    side.move(1)
    places, count = small_rows(clips)
    out_d[...] = jnp.zeros(out_d.shape, F32)
    out_f[...] = jnp.zeros(out_f.shape, F32)
    time_rows = [jnp.zeros((1, grad.shape[1]), F32) for _ in range(6)]
    for layer in range(LAYERS):
        sums1, sums2, sums3, width1, width2, hidden_sum = small[layer]
        sums0 = sums if layer == 0 else above
        mods = [(sums0, 0), (sums0, 1), (sums1, 2), (sums2, 0), (sums2, 1), (sums3, 0)]
        for row, (ref, index) in enumerate(mods):
            value = row_of(ref, index)
            time_rows[row] = time_rows[row] + value
            out_d[6 * layer + row : 6 * layer + row + 1] = value
        for row, (ref, index) in enumerate([(sums1, 3), (sums2, 2), (sums3, 1)]):
            place = places[BIAS] + 3 * layer + row
            out_d[place : place + 1] = row_of(ref, index)
        place = places[GAIN] + layer
        out_d[place : place + 1] = row_of(sums1, 0)
        place = places[SHIFT] + layer
        out_d[place : place + 1] = row_of(sums1, 1)
        out_w[24 * layer : 24 * layer + 16] = width1[...]
        out_w[24 * layer + 16 : 24 * layer + 24] = width2[...]
        out_f[layer : layer + 1] = row_of(hidden_sum, 0)
    for index in range(clips):
        for row in range(6):
            place = 6 * LAYERS + 6 * index + row
            out_d[place : place + 1] = jnp.where(clip == index, time_rows[row], 0.0)
    out_d[places[LOSS] : places[LOSS] + 1] = row_of(small[LAYERS - 1][2], 2)
    for bit in range(bits):
        copies = []
        for number, ref in enumerate((out_d, out_w, out_f)):
            away[bit][number][...] = ref[...].astype(BF16)
            copy = send(
                away[bit][number],
                landed[bit][number],
                send_sems.at[bit, number],
                recv_sems.at[bit, number],
                dp=flip(me, 1 << bit),
            )
            copy.start()
            copies.append(copy)
        if bit == 0:
            chain.drain(chain.chunks)
        side.move(bit)
        for number, ref in enumerate((out_d, out_w, out_f)):
            copies[number].wait()
            ref[...] = away[bit][number][...].astype(F32) + landed[bit][number][...].astype(F32)
    side.finish()


def unpack_kernel(clips, side, *refs):
    refs = list(refs)

    def take(count):
        taken = refs[:count]
        del refs[:count]
        return taken

    lengths, rows_d, rows_w, rows_f, context_sum = take(5)
    parts = [take(6) for _ in range(LAYERS)]
    whole = take(2)
    loss, time, bias, key_bias, gains, hidden, out, gain, shift, mods = take(10)
    context_grad = take(1)[0]
    self_all, cross_all, out_all, up_all, down_all = take(5)
    whole_out = take(2)
    (sems,) = refs
    width = key_bias.shape[1]
    context_grad[...] = context_sum[...].astype(F32)
    copies = []

    def copy(source, target):
        item = pltpu.make_async_copy(source, target, sems.at[len(copies)])
        item.start()
        copies.append(item)

    for layer in range(LAYERS):
        side.need(*range(6 * layer, 6 * layer + 6))
        up, down, cross, text, self_part, out0 = parts[layer]
        copy(up, up_all.at[layer])
        copy(down, down_all.at[layer])
        for member in range(3):
            copy(self_part.at[:, member * width : (member + 1) * width], self_all.at[layer, member])
        copy(cross.at[:, :width], cross_all.at[layer, 0])
        copy(text.at[:, :width], cross_all.at[layer, 1])
        copy(text.at[:, width:], cross_all.at[layer, 2])
        copy(out0, out_all.at[layer, 0])
        copy(cross.at[:, width:], out_all.at[layer, 1])
    side.need(6 * LAYERS, 6 * LAYERS + 1)
    for source, target in zip(whole, whole_out):
        copy(source, target)
    places, count = small_rows(clips)
    for layer in range(LAYERS):
        for row in range(6):
            mods[row, layer : layer + 1] = row_of(rows_d, 6 * layer + row)
        for row in range(3):
            out[row, layer : layer + 1] = row_of(rows_d, places[BIAS] + 3 * layer + row)
        base = 24 * layer
        for row, place in enumerate((4, 6, 17, 7, 8)):
            bias[row, layer : layer + 1] = row_of(rows_w, base + place)
        key_bias[layer : layer + 1] = row_of(rows_w, base + 5)
        for row, place in enumerate((0, 1, 16, 3)):
            gains[layer, row : row + 1] = row_of(rows_w, base + place)
    for index in range(clips):
        for row in range(6):
            time[row, index : index + 1] = row_of(rows_d, 6 * LAYERS + 6 * index + row)
    hidden[...] = rows_f[0:LAYERS]
    gain[...] = rows_d[places[GAIN] : places[GAIN] + LAYERS]
    shift[...] = rows_d[places[SHIFT] : places[SHIFT] + LAYERS]
    count = lengths[0]
    for index in range(1, clips):
        count = count + lengths[index]
    total = jnp.sum(row_of(rows_d, places[LOSS]), axis=1, keepdims=True)
    loss[...] = jnp.broadcast_to(total, loss.shape) / (count.astype(F32) * rows_d.shape[1])
    for item in copies:
        item.wait()


def per_device(
    latents,
    context,
    time_embed,
    teacher,
    lengths,
    block_order,
    positions,
    self_proj,
    cross_proj,
    out_proj,
    ffn_up,
    ffn_down,
    proj_bias,
    key_bias,
    norm_gains,
    ffn_bias,
    out_bias,
    cross_gain,
    cross_shift,
    modulation,
):
    tokens, features = latents.shape
    width = norm_gains.shape[-1]
    heads = width // HEAD_DIM
    hidden_width = ffn_bias.shape[-1]
    clip_count = time_embed.shape[0]
    text_rows = context.shape[0]
    text_all = text_rows * HOLD
    clip = lax.axis_index(DP) // HOLD
    out_t = jnp.swapaxes(out_proj, 2, 3)
    down_t = jnp.swapaxes(ffn_down, 1, 2)

    rows_d = (tokens, features)
    rows_w = (tokens, width)
    rows_f = (tokens, hidden_width)
    stats = (CHAIN, 8, tokens)
    three = pltpu.SemaphoreType.DMA((CHAIN - 1,))
    chain_scratch = Chain.scratch(tokens, features)
    kv_shape = (heads, 2, tokens, HEAD_DIM)

    pack = (((16, features), F32), ((16, width), F32), ((1, hidden_width), F32))
    attend_outs = (
        Early(HIDDEN, rows_d, F32),
        Early(NORMAL, rows_d, BF16),
        Early(QUERY, rows_w, F32),
        Early(KEY, rows_w, F32),
        Early(QUERY_ROT, rows_w, BF16),
        (kv_shape, BF16),
        (stats, F32),
        ((HOLD - 1,) + kv_shape, BF16),
        (rows_w, BF16),
        ((8, tokens), F32),
    )
    attend_scratch = [
        pltpu.VMEM((heads, HOLD, tokens, tokens), F32),
        three,
        three,
        pltpu.SemaphoreType.DMA((1 + 3 * heads,)),
        pltpu.SemaphoreType.DMA((1 + 3 * heads,)),
    ]
    results, found = run(
        "first",
        first_kernel,
        (
            lengths,
            block_order,
            jnp.swapaxes(time_embed, 0, 1),
            jnp.swapaxes(modulation, 0, 1),
            jnp.swapaxes(out_bias, 0, 1),
            cross_gain,
            cross_shift,
            jnp.swapaxes(proj_bias, 0, 1),
            key_bias,
            norm_gains,
            ffn_bias,
            positions,
            rope_table(HEAD_DIM),
            latents,
        ),
        (
            ((HOLD, 8, tokens), F32),
            ((tokens, HEAD_DIM), F32),
            ((tokens, HEAD_DIM), F32),
            (context.shape, F32),
        )
        + pack * LAYERS
        + attend_outs,
        attend_scratch + [three, three],
        jobs=[
            Gather(self_proj, 0, name=SELF, held=True),
            Gather(cross_proj, 0, wave=1, skewed=True),
            Gather(out_t, 0, wave=1, skewed=True),
        ],
        scalars=2,
        micros=70,
    )
    counts, cosine, sine, context_part = results[:4]
    packs = [results[4 + 3 * layer : 7 + 3 * layer] for layer in range(LAYERS)]
    attended = results[4 + 3 * LAYERS :]
    weights = {SELF: [found[0]], CROSS: [found[1]], OUT: [found[2]], UP: [], DOWN: []}
    saved = []
    sources = {
        SELF: self_proj,
        CROSS: cross_proj,
        OUT: out_t,
        UP: ffn_up,
        DOWN: down_t,
    }

    def gathers(layer, *names):
        return [Gather(sources[name], layer) for name in names if layer < LAYERS]

    def keep(found, *names):
        for name, item in zip(names, found):
            weights[name].append(item)

    base, tot, before = latents, latents, packs[0][0]
    for layer in range(LAYERS):
        pack_d, pack_w, pack_f = packs[layer]
        if layer > 0:
            attended, unused = run(
                "attend",
                attend_kernel,
                (
                    base,
                    tot,
                    before,
                    pack_d,
                    pack_w,
                    Late(WEIGHT, weights[SELF][layer]),
                    Late(COSINE, cosine, lazy=True),
                    Late(SINE, sine, lazy=True),
                    counts,
                ),
                attend_outs,
                attend_scratch,
                micros=35,
            )
        hidden, a1, sq, sk, q_rot, kv, stat1, others, o1, lse1 = attended[:10]
        results, found = run(
            "out_sum" + str(layer),
            functools.partial(out_sum_kernel, layer == 0),
            (
                o1,
                Late(OUT, weights[OUT][layer], 0),
                Late(CONTEXT, context) if layer == 0 else Late(CONTEXT, clip_context, lazy=True),
                Late(TEXT_WEIGHT, weights[CROSS][layer], 1, 3, lazy=True),
                pack_w,
            ),
            (
                (rows_d, BF16),
                ((text_all, width), F32),
                ((text_all, width), BF16),
                ((text_all, width), BF16),
                ((CHAIN, 8, text_all), F32),
            )
            + ((((text_all, features), BF16),) if layer == 0 else ()),
            [three, three] + chain_scratch + ([three, three] if layer == 0 else []),
            jobs=gathers(layer, UP) + [Gather(self_proj, 1)]
            if layer == 0
            else gathers(layer, DOWN),
            micros=45,
        )
        keep(found, *((UP, SELF) if layer == 0 else (DOWN,)))
        tot1, ck, ckb, cvb, stat_t = results[:5]
        if layer == 0:
            clip_context = results[5]
        gathered = layer == 0
        jobs = [
            Gather(sources[DOWN], 0, name=DOWN, held=True),
            Gather(sources[CROSS], 1, wave=1),
            Gather(sources[OUT], 1, wave=1),
            Gather(sources[UP], 1, wave=1),
        ]
        results, found = run(
            "cross_ffn" + str(gathered),
            functools.partial(cross_ffn_kernel, gathered),
            (
                hidden,
                tot1,
                pack_d,
                pack_w,
                pack_f,
                Late(WEIGHT, weights[CROSS][layer], 0),
                Late(TEXT_KB, ckb, lazy=True),
                Late(TEXT_VB, cvb, lazy=True),
                Late(OUT, weights[OUT][layer], 1, lazy=True),
                Late(UP, weights[UP][layer], lazy=True),
            )
            + (() if gathered else (Late(DOWN, weights[DOWN][layer], lazy=True),)),
            (
                Early(HIDDEN, rows_d, F32),
                Early(NORMAL, rows_d, BF16),
                Early(QUERY, rows_w, F32),
                Early(QUERY_B, rows_w, BF16),
                Early(RESULT, rows_w, BF16),
                ((8, tokens), F32),
                (stats, F32),
                Early(HIDDEN_F, rows_d, F32),
                Early(NORMAL_F, rows_d, BF16),
                Early(GELU_B_NAME, rows_f, BF16),
                Early(SLOPE, rows_f, BF16),
                (rows_d, BF16),
            ),
            [three, three, pltpu.VMEM(rows_d, BF16)] + chain_scratch + chain_scratch,
            jobs=jobs if gathered else [],
            micros=90,
        )
        h1, a3, cq, cqb, o2, lse2, stat2, h2, a2, gelu_b, slope, tot3 = results
        if gathered:
            keep(found, DOWN, CROSS, OUT, UP)
        saved.append(
            (hidden, a1, sq, sk, q_rot, kv, stat1, others, o1, lse1, tot1, ck, ckb, cvb, stat_t)
            + (h1, a3, cq, cqb, o2, lse2, stat2, h2, a2, gelu_b, slope, tot3)
        )
        base, tot, before = h2, tot3, pack_d
    grad = base
    reduced = {}
    small = [None] * LAYERS
    above = None
    for layer in reversed(range(LAYERS)):
        (hidden, a1, sq, sk, q_rot, kv, stat1, others, o1, lse1, tot1, ck, ckb, cvb, stat_t) = saved[
            layer
        ][:15]
        (h1, a3, cq, cqb, o2, lse2, stat2, h2, a2, gelu_b, slope, tot3) = saved[layer][15:]
        pack_d, pack_w, pack_f = packs[layer]
        w_self, w_cross, w_out, w_up, w_down = [
            weights[name][layer] for name in (SELF, CROSS, OUT, UP, DOWN)
        ]
        joined = above is not None
        matrix = (features, hidden_width)
        results, found = run(
            "ffn_back" + str(joined),
            functools.partial(ffn_back_kernel, joined),
            (Late(GRAD, grad),)
            + (above if joined else (teacher, counts))
            + (
                tot3,
                pack_d,
                Late(DOWN, w_down),
                Late(UP, w_up, lazy=True),
                Late(SLOPE, slope),
                Late(NORMAL, a2, lazy=True),
                Late(GELU_B_NAME, gelu_b, lazy=True),
            ),
            (
                Early(NEW_GRAD, rows_d, F32, over=0),
                ((8, features), F32) if joined else Early(OUTPUT, rows_d, F32),
            )
            + (
                (rows_d, BF16),
                ((8, features), F32),
                ((8, hidden_width), F32),
                (matrix, BF16, True),
                (matrix, BF16, True),
            ),
            [
                pltpu.VMEM(rows_d, BF16),
                pltpu.VMEM(rows_f, BF16),
                pltpu.VMEM((2, 256, hidden_width), BF16),
                pltpu.SemaphoreType.DMA((2,)),
            ]
            + chain_scratch,
            jobs=[Scatter(text_matrix), Scatter(self_matrix)] if joined else [],
            micros=60,
        )
        grad = results[0]
        if not joined:
            output = results[1]
        else:
            sums_above = results[1]
            reduced[TEXT, layer + 1], reduced[SELF, layer + 1] = found
        da2, sums3, dz_sum, up_grad, down_grad = results[2:]
        (grad, dct, sums2, wsums2, da3, cross_matrix), found = run(
            "cross_back",
            cross_back_kernel,
            (
                grad,
                da2,
                h2,
                pack_d,
                pack_w,
                Late(OUT, w_out, 1),
                Late(QUERY, cq, lazy=True),
                Late(QUERY_B, cqb, lazy=True),
                lse2,
                stat2,
                Late(TEXT_KB, ckb, lazy=True),
                Late(TEXT_VB, cvb, lazy=True),
                Late(WEIGHT, w_cross, 0, lazy=True),
                Late(NORMAL, a3, lazy=True),
                Late(RESULT, o2, lazy=True),
            ),
            (
                Early(NEW_GRAD, rows_d, F32),
                Early(TEXT_GRAD, (2, text_all, width), F32),
                ((8, features), F32),
                ((8, width), F32),
                (rows_d, BF16),
                Early(MATRIX_GRAD, (features, 2 * width), BF16),
            ),
            [
                pltpu.VMEM(rows_d, BF16),
                pltpu.VMEM(rows_w, BF16),
                pltpu.VMEM(rows_w, BF16),
                pltpu.VMEM(rows_w, F32),
                pltpu.VMEM(stats, F32),
                three,
                three,
            ]
            + chain_scratch,
            jobs=[Scatter(up_grad, UP)],
            micros=60,
        )
        reduced[UP, layer] = found[0]
        (grad, out0, sums1, dq_rot, dkv, dtext), found = run(
            "attend_back",
            attend_back_kernel,
            (
                counts,
                grad,
                da3,
                h1,
                pack_d,
                tot1,
                Late(OUT, w_out, 0),
                Late(QUERY, q_rot, lazy=True),
                Late(KEY_VALUE, kv, lazy=True),
                Late(OTHERS, others, lazy=True),
                lse1,
                dct,
                Late(RESULT, o1, lazy=True),
            ),
            (
                Early(NEW_GRAD, rows_d, F32),
                Early(MATRIX_GRAD, (features, width), BF16),
                ((8, features), F32),
                Early(QUERY_GRAD, rows_w, F32),
                ((2,) + rows_w, F32),
                ((2, text_rows, width), F32),
            ),
            [
                pltpu.VMEM(rows_d, BF16),
                pltpu.VMEM(rows_w, BF16),
                pltpu.VMEM((HOLD, tokens, tokens), F32),
                pltpu.VMEM((HOLD, tokens, tokens), F32),
                pltpu.VMEM((3,) + kv_shape, BF16),
                pltpu.VMEM((3,) + kv_shape, BF16),
                pltpu.VMEM((3, 2, text_rows, width), BF16),
                pltpu.VMEM((3, 2, text_rows, width), BF16),
                pltpu.SemaphoreType.DMA((3, heads + 1)),
                pltpu.SemaphoreType.DMA((3, heads + 1)),
            ],
            micros=35,
        )
        (wsums1, context_part, da1, self_matrix, text_matrix), found = run(
            "qkv_back",
            qkv_back_kernel,
            (
                dq_rot,
                dkv,
                dtext,
                sq,
                sk,
                ck,
                stat1,
                stat_t,
                pack_w,
                cosine,
                sine,
                Late(WEIGHT, w_self, lazy=True),
                Late(NORMAL, a1, lazy=True),
                Late(CONTEXT, context, lazy=True),
                Late(TEXT_WEIGHT, w_cross, 1, 3, lazy=True),
                Late(BEFORE, context_part, lazy=True),
            ),
            (
                ((16, width), F32),
                (context.shape, F32),
                (rows_d, BF16),
                Early(SELF_GRAD, (features, 3 * width), BF16),
                Early(TEXT_MATRIX, (features, 2 * width), BF16),
            ),
            [
                pltpu.VMEM((tokens, 3 * width), BF16),
                pltpu.VMEM((text_rows, 2 * width), BF16),
                pltpu.VMEM(rows_w, F32),
                pltpu.VMEM(rows_w, F32),
                pltpu.VMEM(stats, F32),
                three,
                three,
            ]
            + chain_scratch,
            jobs=[Scatter(down_grad), Scatter(cross_matrix), Scatter(out0)],
            micros=60,
        )
        reduced[DOWN, layer], reduced[CROSS, layer], reduced[OUT0, layer] = found
        small[layer] = (sums1, sums2, sums3, wsums1, wsums2, dz_sum)
        above = (da1, hidden, pack_d)
    places, count = small_rows(clip_count)
    small_shapes = ((count, features), (24 * LAYERS, width), (16, hidden_width))
    travel = [pltpu.VMEM(shape, BF16) for shape in small_shapes]
    bits = bits_of_dp()
    (grad, context_sum, packed_d, packed_w, packed_f), found = run(
        "last",
        functools.partial(last_kernel, clip_count),
        (
            context_part,
            Late(GRAD, grad),
            Late(BRANCH, above[0]),
            Late(HIDDEN, above[1]),
            above[2],
            sums_above,
        )
        + tuple(item for layer in range(LAYERS) for item in small[layer]),
        (Early(NEW_GRAD, rows_d, F32), (context.shape, BF16))
        + tuple((shape, F32) for shape in small_shapes),
        [pltpu.VMEM((8, features), F32)]
        + Chain.scratch(text_rows, features)
        + travel * (2 * bits)
        + [pltpu.SemaphoreType.DMA((bits, 3)), pltpu.SemaphoreType.DMA((bits, 3))],
        jobs=[Scatter(text_matrix), Scatter(self_matrix)],
        micros=30,
    )
    reduced[TEXT, 0], reduced[SELF, 0] = found
    names = (UP, DOWN, CROSS, TEXT, SELF, OUT0)
    size = features // lax.axis_size(DP)
    far_outs = (
        ((LAYERS, 3, size, width), F32, True),
        ((LAYERS, 3, size, width), F32, True),
        ((LAYERS, 2, size, width), F32, True),
        ((LAYERS, size, hidden_width), F32, True),
        ((LAYERS, size, hidden_width), F32, True),
        (rows_d, F32, True),
        (rows_d, F32, True),
    )
    far_ins = [
        reduced[name, layer] for layer in range(LAYERS) for name in names
    ] + [output, grad]
    unpacked, unused = run(
        "unpack",
        functools.partial(unpack_kernel, clip_count),
        (lengths, packed_d, packed_w, packed_f, context_sum) + tuple(Late(place, item) for place, item in enumerate(far_ins)),
        (
            ((1, 128), F32),
            ((6, clip_count, features), F32),
            ((5, LAYERS, width), F32),
            ((LAYERS, width), F32),
            ((LAYERS, 4, width), F32),
            ((LAYERS, hidden_width), F32),
            ((3, LAYERS, features), F32),
            ((LAYERS, features), F32),
            ((LAYERS, features), F32),
            ((6, LAYERS, features), F32),
            (context.shape, F32),
        )
        + far_outs,
        [pltpu.SemaphoreType.DMA((2 + 10 * LAYERS,))],
        remote=False,
        scalars=1,
        micros=10,
    )
    loss, time, bias, key_sums, gain_sums, hidden_sums, out_sums, gain, shift, mods = unpacked[:10]
    context_grad, self_grad, cross_grad, out_grad, up_grad, down_grad, output, grad = unpacked[10:]
    out_grad = jnp.swapaxes(out_grad, 2, 3)
    down_grad = jnp.swapaxes(down_grad, 1, 2)
    return (
        output,
        loss[0, 0],
        grad,
        context_grad,
        jnp.swapaxes(time, 0, 1),
        self_grad,
        cross_grad,
        out_grad,
        up_grad,
        down_grad,
        jnp.swapaxes(bias, 0, 1),
        key_sums,
        gain_sums,
        hidden_sums,
        jnp.swapaxes(out_sums, 0, 1),
        gain,
        shift,
        jnp.swapaxes(mods, 0, 1),
    )


def solution(mesh):
    COLLECTIVES.clear()
    rows = P(DP, None)
    col_in = P(None, None, DP, TENSOR)
    col_out = P(None, None, TENSOR, DP)
    up, down = P(None, DP, TENSOR), P(None, TENSOR, DP)
    vec, mat = P(None, TENSOR), P(None, None, TENSOR)
    return jax.shard_map(
        per_device,
        mesh=mesh,
        in_specs=(rows, rows, P(), rows, P(), P(DP), P(None, DP))
        + (col_in, col_in, col_out, up, down)
        + (mat, vec, mat, vec, P(), P(), P(), P()),
        out_specs=(rows, P(), rows, rows, P())
        + (col_in, col_in, col_out, up, down)
        + (mat, vec, mat, vec, P(), P(), P(), P()),
        check_vma=False,
    )
```

```python
import functools
import math

import jax
import jax.numpy as jnp
import numpy as np
from jax import lax
from jax.experimental import pallas as pl
from jax.experimental.pallas import tpu as pltpu
from jax.sharding import PartitionSpec as P

BEFORE = "before"
BIAS = "bias"
BRANCH = "branch"
CONTEXT = "context"
COSINE = "cosine"
CROSS = "cross"
DOWN = "down"
DP = "dp"
GAIN = "gain"
GELU_B_NAME = "gelu_b"
GRAD = "grad"
HIDDEN = "hidden"
HIDDEN_F = "hidden_f"
KEY = "key"
KEY_VALUE = "key_value"
LOSS = "loss"
MATRIX_GRAD = "matrix_grad"
NEW_GRAD = "new_grad"
NORMAL = "normal"
NORMAL_F = "normal_f"
OTHERS = "others"
OUT = "out"
OUT0 = "out0"
OUTPUT = "output"
QUERY = "query"
QUERY_B = "query_b"
QUERY_GRAD = "query_grad"
QUERY_ROT = "query_rot"
RESULT = "result"
SELF = "self"
SELF_GRAD = "self_grad"
SHIFT = "shift"
SINE = "sine"
SLOPE = "slope"
TENSOR = "tensor"
TEXT = "text"
TEXT_GRAD = "text_grad"
TEXT_KB = "text_kb"
TEXT_MATRIX = "text_matrix"
TEXT_VB = "text_vb"
TEXT_WEIGHT = "text_weight"
UP = "up"
WEIGHT = "weight"
MESH = pl.DeviceIdType.MESH
F32, BF16 = jnp.float32, jnp.bfloat16
NN = (((1,), (0,)), ((), ()))
NT = (((1,), (1,)), ((), ()))
TN = (((0,), (0,)), ((), ()))
HEAD_DIM = 128
HOLD = 4
LAYERS = 2
CHAIN = 4
CHUNK = 32
EPS = 1e-06
LOG2E = math.log2(math.e)
SCALE = 1.0 / math.sqrt(HEAD_DIM)
VMEM_BYTES = 60 * 2**20


def dot(left, right, dims=NN, exact=False):
    precision = lax.Precision.HIGHEST if exact else None
    return lax.dot_general(left, right, dims, precision=precision, preferred_element_type=F32)


def rope_table(head_size):
    third = head_size // 6
    spans = [head_size - 4 * third, 2 * third, 2 * third]
    table = np.zeros((3, head_size), np.float32)
    start_col = 0
    for component in range(3):
        for pair_index in range(spans[component] // 2):
            freq_value = 10000.0 ** (-(2.0 * pair_index) / spans[component])
            table[component, start_col + 2 * pair_index] = freq_value
            table[component, start_col + 2 * pair_index + 1] = freq_value
        start_col += spans[component]
    return table


def signal(**device):
    pl.semaphore_signal(
        pltpu.get_barrier_semaphore(), inc=1, device_id=device, device_id_type=MESH
    )


def bits_of_dp():
    return max(lax.axis_size(DP).bit_length() - 1, 1)


def flip(index, mask):
    result, bit = index, 0
    while mask >> bit:
        if mask >> bit & 1:
            half = 1 << bit
            result = result + half - 2 * half * lax.rem(index // half, 2)
        bit += 1
    return result


def greet(side, tensor, masks):
    place, me = lax.axis_index(TENSOR), lax.axis_index(DP)
    if tensor:
        for step in range(1, CHAIN):
            signal(tensor=lax.rem(place + step, CHAIN))
    for mask in masks:
        signal(dp=flip(me, mask))
    side.load(False)
    pl.semaphore_wait(
        pltpu.get_barrier_semaphore(), (CHAIN - 1 if tensor else 0) + len(masks)
    )


def holders():
    me = lax.axis_index(DP)
    return flip(me, 1), flip(me, 2)


def send(src, dst, send_sem, recv_sem, **device):
    return pltpu.make_async_remote_copy(
        src_ref=src,
        dst_ref=dst,
        send_sem=send_sem,
        recv_sem=recv_sem,
        device_id=device,
        device_id_type=MESH,
    )


def masks_over(bits):
    masks = [0]
    for bit in bits:
        masks += [mask | 1 << bit for mask in masks]
    return masks


def halves_of(size):
    cut = (size // 2 + 15) // 16 * 16
    return ((0, cut), (cut, size - cut))


def half_orders(bits):
    rising = list(range(1, bits))
    return (rising, rising[::-1])


class Job:
    phase = 0
    wave = 0
    name = None
    ended = False
    midway = False

    def middle(self):
        pass

    def move(self, target):
        while self.phase < min(target, self.bits - 1):
            self.phase += 1
            self.advance(self.phase)


class Gather(Job):
    def __init__(self, source, layer, name=None, wave=0, held=False, skewed=False):
        self.layer, self.name, self.wave, self.is_held = layer, name, wave, held
        self.operands = [source]
        shape = source.shape[1:]
        self.lead = shape[:-2]
        self.size = shape[-2]
        devices = lax.axis_size(DP)
        self.outs = [(self.lead + (self.size * devices, shape[-1]), source.dtype)]
        self.spaces = [pl.ANY]
        self.bits = bits_of_dp()
        plan = []
        orders = half_orders(self.bits)
        if skewed:
            orders = (orders[0], orders[0])
        for half, order in enumerate(orders):
            for phase, bit in enumerate(order):
                for mask in masks_over(order[:phase]):
                    plan.append((phase, half, bit, mask))
        for mask in masks_over(range(1, self.bits)):
            plan.append((self.bits - 1, None, 0, mask))
        self.plan = plan
        count = len(plan)
        self.scratch = [
            pltpu.SemaphoreType.DMA((count,)),
            pltpu.SemaphoreType.DMA((count,)),
            pltpu.SemaphoreType.DMA,
        ]
        if held:
            self.scratch += [
                pltpu.VMEM(self.outs[0][0], source.dtype),
                pltpu.SemaphoreType.DMA,
            ]

    def key(self):
        return ("gather", self.layer, self.outs[0][0], self.wave, self.is_held)

    def bind(self, sources, outs, scratch):
        self.source = sources[0].at[self.layer]
        self.out = outs[0]
        self.send_sems, self.recv_sems, self.own_sem = scratch[:3]
        self.store = None
        if self.is_held:
            held, sem = scratch[3:]
            self.store = pltpu.make_async_copy(held, self.out, sem)
            self.out = held

    def block(self, ref, index, half):
        low, size = (0, self.size) if half is None else halves_of(self.size)[half]
        start = low if index is None else index * self.size + low
        rows = pl.ds(pl.multiple_of(start, 16), size)
        return ref.at[:, rows] if self.lead else ref.at[rows]

    def copies(self, phase, own=None, only=None):
        me = lax.axis_index(DP)
        for number, (step, half, bit, mask) in enumerate(self.plan):
            if only is not None and mask not in only:
                continue
            if step == phase and own in (None, mask == 0):
                index = flip(me, mask)
                source = (
                    self.block(self.source, None, half)
                    if mask == 0
                    else self.block(self.out, index, half)
                )
                yield send(
                    source,
                    self.block(self.out, index, half),
                    self.send_sems.at[number],
                    self.recv_sems.at[number],
                    dp=flip(me, 1 << bit),
                )

    def own_copy(self):
        me = lax.axis_index(DP)
        return pltpu.make_async_copy(
            self.source, self.block(self.out, me, None), self.own_sem
        )

    def start(self):
        for phase in range(self.bits):
            for copy in self.copies(phase, True):
                copy.start()
        self.own_copy().start()

    def middle(self):
        if self.bits == 3 and not self.midway:
            self.midway = True
            for copy in self.copies(1, True):
                copy.wait_recv()
            for copy in self.copies(2, only=(2, 4)):
                copy.start()

    def advance(self, phase):
        if phase == self.bits - 1 == 2:
            self.middle()
            for copy in self.copies(1, False):
                copy.wait_recv()
            for copy in self.copies(2, only=(6,)):
                copy.start()
            return
        for copy in self.copies(phase - 1):
            copy.wait_recv()
        for copy in self.copies(phase, False):
            copy.start()

    def finish(self):
        for copy in self.copies(self.bits - 1):
            copy.wait_recv()
        for phase in range(self.bits):
            for copy in self.copies(phase):
                copy.wait_send()
        self.own_copy().wait()
        if self.store is not None:
            self.store.start()


class Scatter(Job):
    def __init__(self, source=None, name=None, shape=None):
        self.name = name
        self.operands = [] if source is None else [source]
        shape = source.shape if shape is None else shape
        self.bits = bits_of_dp()
        self.size = shape[0] // lax.axis_size(DP)
        self.width = shape[1]
        self.outs = [((self.size, self.width), F32)]
        self.spaces = [pltpu.VMEM]
        self.slots = 1 << self.bits - 1
        orders = [order[::-1] for order in half_orders(self.bits)]
        plan = [(0, None, 0, mask, mask >> 1) for mask in masks_over(range(1, self.bits))]
        for half, order in enumerate(orders):
            for phase, bit in enumerate(order):
                kept = masks_over(order[phase + 1 :])
                for place, mask in enumerate(kept):
                    plan.append((phase + 1, half, bit, mask, place))
        self.plan = plan
        count = len(plan)
        buffers = [pltpu.VMEM((self.slots, self.size, self.width), BF16)]
        buffers += buffers * len(self.operands)
        for phase in range(1, self.bits):
            places = 1 << self.bits - 1 - phase
            buffers += [
                pltpu.VMEM((places, size, self.width), BF16)
                for _, size in halves_of(self.size)
            ]
        self.scratch = buffers + [
            pltpu.SemaphoreType.DMA((count,)),
            pltpu.SemaphoreType.DMA((count,)),
            pltpu.SemaphoreType.DMA((self.slots,)),
        ]

    def key(self):
        return ("scatter", self.width, len(self.operands))

    def bind(self, sources, outs, scratch):
        self.out = outs[0]
        self.landed, self.own = scratch[0], None
        scratch = scratch[1:]
        if sources:
            self.source, self.own = sources[0], scratch[0]
            scratch = scratch[1:]
        self.parts = scratch[:-3]
        self.send_sems, self.recv_sems, self.own_sems = scratch[-3:]

    def rows(self, index):
        return pl.ds(pl.multiple_of(index * self.size, 16), self.size)

    def held(self, mask, low, size):
        if self.own is not None:
            return self.own.at[mask >> 1, pl.ds(pl.multiple_of(low, 16), size)]
        start = flip(lax.axis_index(DP), mask) * self.size + low
        return self.source.at[pl.ds(pl.multiple_of(start, 16), size)]

    def copies(self, phase):
        me = lax.axis_index(DP)
        for number, (step, half, bit, mask, place) in enumerate(self.plan):
            if step != phase:
                continue
            if phase == 0:
                source = self.source.at[self.rows(flip(me, mask | 1))]
                target = self.landed.at[mask >> 1]
            else:
                low, size = halves_of(self.size)[half]
                source = self.held(mask | 1 << bit, low, size)
                target = self.parts[2 * (phase - 1) + half].at[place]
            yield send(
                source,
                target,
                self.send_sems.at[number],
                self.recv_sems.at[number],
                dp=flip(me, 1 << bit),
            )

    def own_copies(self):
        me = lax.axis_index(DP)
        if self.own is not None:
            for slot in range(self.slots):
                yield pltpu.make_async_copy(
                    self.source.at[self.rows(flip(me, slot << 1))],
                    self.own.at[slot],
                    self.own_sems.at[slot],
                )

    def start(self):
        for copy in self.copies(0):
            copy.start()
        for copy in self.own_copies():
            copy.start()

    def add(self, phase):
        for copy in self.copies(phase):
            copy.wait_recv()
        if phase == 0:
            for copy in self.own_copies():
                copy.wait()
            for slot in range(self.slots):

                def step(rows, index, slot=slot):
                    held = self.held(slot << 1, index * 16, 16)
                    held[...] = held[...] + self.landed[slot, rows]

                loop_rows(self.size, 16, step)
            return
        for number, (step, half, bit, mask, place) in enumerate(self.plan):
            if step == phase:
                low, size = halves_of(self.size)[half]
                part = self.parts[2 * (phase - 1) + half]

                def step(rows, index, mask=mask, place=place, low=low, part=part):
                    held = self.held(mask, low + index * 16, 16)
                    if phase == self.bits - 1:
                        target = pl.ds(pl.multiple_of(low + index * 16, 16), 16)
                        self.out[target] = held[...].astype(F32) + part[place, rows].astype(F32)
                    else:
                        held[...] = held[...] + part[place, rows]

                loop_rows(size, 16, step)

    def advance(self, phase):
        self.add(phase - 1)
        for copy in self.copies(phase):
            copy.start()

    def finish(self):
        self.add(self.bits - 1)
        for phase in range(self.bits):
            for copy in self.copies(phase):
                copy.wait_send()


class Late:
    def __init__(self, name, value, low=None, high=None, lazy=False):
        self.name, self.value, self.low, self.high = name, value, low, high
        self.lazy = lazy
        shape = value.shape
        if high is not None:
            shape = (high - low,) + shape[1:]
        elif low is not None:
            shape = shape[1:]
        self.scratch = [pltpu.VMEM(shape, value.dtype), pltpu.SemaphoreType.DMA]

    def source(self, ref):
        if self.high is not None:
            return ref.at[self.low : self.high]
        return ref if self.low is None else ref.at[self.low]


class Early:
    def __init__(self, name, shape, kind, over=None):
        self.name, self.shape, self.kind, self.over = name, shape, kind, over
        self.scratch = [pltpu.SemaphoreType.DMA]
        if over is None:
            self.scratch = [pltpu.VMEM(shape, kind)] + self.scratch


class Side:
    def __init__(self, jobs):
        self.jobs = jobs
        self.masks = [1 << bit for bit in range(bits_of_dp())] if jobs else []
        self.loads, self.stores, self.open = {}, {}, []
        self.first_loads, self.waiting = [], []
        self.late_after = False

    def load(self, lazy):
        for item in [item for item in self.waiting if item[0] == lazy]:
            item[1].start()
            self.waiting.remove(item)

    def need(self, *names):
        for name in names:
            self.loads[name].wait()

    def store(self, *names):
        for name in names:
            self.stores[name].start()
            self.open.append(name)

    def start(self, wave=0):
        for job in self.jobs:
            if job.operands and job.wave == wave:
                job.start()
        while self.first_loads:
            self.first_loads.pop(0).wait()
            if not self.first_loads and not self.late_after:
                self.load(True)

    def launch(self, name, source):
        for job in self.jobs:
            if job.name == name:
                job.source = source
                job.start()

    def move(self, target, *names):
        for job in self.jobs:
            if not names or job.name in names:
                job.move(target)

    def early(self):
        self.move(bits_of_dp() - 2)

    def late(self):
        self.move(bits_of_dp() - 1)

    def middle(self):
        self.early()
        for job in self.jobs:
            job.middle()

    def finish(self, *names):
        for job in self.jobs:
            if not job.ended and (not names or job.name in names):
                job.move(job.bits - 1)
                job.finish()
                job.ended = True

    def close(self):
        for name in self.stores:
            if name not in self.open:
                self.store(name)
        for copy in self.stores.values():
            copy.wait()
        for job in self.jobs:
            if isinstance(job, Gather) and job.store is not None:
                job.store.wait()


class Exchange:
    def __init__(self, slots, send_sems, recv_sems):
        self.slots = slots
        place = lax.axis_index(TENSOR)
        self.place = place
        self.copies = [
            send(
                slots.at[place],
                slots.at[place],
                send_sems.at[step - 1],
                recv_sems.at[step - 1],
                tensor=lax.rem(place + step, CHAIN),
            )
            for step in range(1, CHAIN)
        ]

    def start(self, rows):
        self.slots[self.place] = rows
        for copy in self.copies:
            copy.start()

    def finish(self):
        for copy in self.copies:
            copy.wait()


def stat_rows(squares, row):
    count, width = squares.shape
    ones = jnp.ones((8, width), F32)
    sums = dot(ones, squares, NT, exact=True)
    index = lax.broadcasted_iota(jnp.int32, sums.shape, 0)
    return jnp.where(index == row, sums, 0.0)


def stat_column(slots, row, lanes):
    gathered = jnp.concatenate([slots[place] for place in range(CHAIN)], axis=0)
    index = lax.broadcasted_iota(jnp.int32, (8 * CHAIN, lanes), 0)
    pick = jnp.where(lax.rem(index, 8) == row, 1.0, 0.0)
    return dot(gathered, pick, TN, exact=True)


class Chain:
    def __init__(self, part, total, buffers, sems):
        self.part, self.total = part, total
        self.came, self.pair, self.peers = buffers
        self.sems = sems
        place = lax.axis_index(TENSOR)
        self.is_end = (place == 0) | (place == 3)
        self.is_mid = jnp.logical_not(self.is_end)
        self.inner = jnp.where(place == 0, 1, 2)
        self.outer = jnp.where(place == 1, 0, 3)
        self.peer = 3 - place
        self.chunks = part.shape[0] // CHUNK
        self.closed = False

    @staticmethod
    def scratch(rows, width):
        chunks = rows // CHUNK
        return [pltpu.VMEM((rows, width), BF16)] * 4 + [pltpu.SemaphoreType.DMA((6, chunks))]

    def rows(self, k):
        return pl.ds(pl.multiple_of(k * CHUNK, CHUNK), CHUNK)

    def copy(self, src, dst, kind, k, device):
        return send(
            src.at[self.rows(k)],
            dst.at[self.rows(k)],
            self.sems.at[2 * kind, k],
            self.sems.at[2 * kind + 1, k],
            tensor=device,
        )

    def inward(self, k, device):
        return self.copy(self.part, self.came, 0, k, device)

    def across(self, k):
        return self.copy(self.pair, self.peers, 1, k, self.peer)

    def outward(self, k, device):
        return self.copy(self.total, self.total, 2, k, device)

    def begin(self, low, count):
        @pl.when(self.is_end)
        def _():
            def step(k, carry):
                self.inward(low + k, self.inner).start()
                return carry

            lax.fori_loop(0, count, step, 0)

    def first(self, k):
        self.inward(k, self.outer).wait_recv()
        rows = self.rows(k)
        self.pair[rows] = (self.part[rows].astype(F32) + self.came[rows].astype(F32)).astype(BF16)
        self.across(k).start()

    def second(self, k):
        self.across(k).wait_recv()
        rows = self.rows(k)
        self.total[rows] = (self.pair[rows].astype(F32) + self.peers[rows].astype(F32)).astype(
            BF16
        )
        self.outward(k, self.outer).start()

    def serve(self, k):
        @pl.when(self.is_mid)
        def _():
            self.first(k)

            @pl.when(k > 0)
            def _():
                self.second(jnp.maximum(k - 1, 0))

    def segment(self, low, high, closed, upto):
        @pl.when(self.is_mid)
        def _():
            def both(k, carry):
                self.first(k)

                @pl.when(k > 0)
                def _():
                    self.second(jnp.maximum(k - 1, 0))

                return carry

            lax.fori_loop(low, high, both, 0)
            if high == self.chunks and not self.closed:
                self.second(self.chunks - 1)

        self.closed = self.closed or high == self.chunks

        @pl.when(self.is_end)
        def _():
            def close(k, carry):
                self.inward(k, self.inner).wait_send()
                self.outward(k, self.inner).wait_recv()
                return carry

            lax.fori_loop(closed, upto, close, 0)

    def drain(self, low, early=None, late=None):
        done, last = 0, self.chunks
        if early is not None:
            cut = low + (last - low) // 4
            self.segment(low, cut, done, cut - 1)
            low, done = cut, cut - 1
            early()
        if late is not None:
            cut = low + (last - low) * 5 // 8
            self.segment(low, cut, done, cut - 1)
            low, done = cut, cut - 1
            late()
        self.segment(low, last, done, last)
        self.close()

    def close(self):
        @pl.when(self.is_mid)
        def _():
            def close(k, carry):
                self.across(k).wait_send()
                self.outward(k, self.outer).wait_send()
                return carry

            lax.fori_loop(0, self.chunks, close, 0)


COLLECTIVES = {}


def collective_of(key):
    return COLLECTIVES.setdefault(key, 1 + len(COLLECTIVES))


def run(name, kernel, ins, outs, scratch=(), remote=True, jobs=(), scalars=0, micros=0):
    whole = pl.BlockSpec(memory_space=pltpu.VMEM)
    far = pl.BlockSpec(memory_space=pl.ANY)
    if remote:
        ins = tuple(ins[:scalars]) + tuple(
            item if isinstance(item, Late) else Late(None, item) for item in ins[scalars:]
        )
        outs = tuple(
            item if isinstance(item, Early) or len(item) > 2 else Early(place, *item)
            for place, item in enumerate(outs)
        )
    job_ins = [item for job in jobs for item in job.operands]
    job_outs = [item for job in jobs for item in job.outs]
    job_spaces = [pl.BlockSpec(memory_space=space) for job in jobs for space in job.spaces]
    moved = [item for item in tuple(ins) + tuple(outs) if isinstance(item, (Late, Early))]
    own_scratch = list(scratch) + [item for job in jobs for item in job.scratch]

    def body(*refs):
        side = Side(jobs)
        refs = list(refs)

        def take(count):
            taken = refs[:count]
            del refs[:count]
            return taken

        own_in, side_in = take(len(ins)), take(len(job_ins))
        own_out, side_out = take(len(outs)), take(len(job_outs))
        own = take(len(scratch))
        for job in jobs:
            job.phase, job.ended, job.midway = 0, False, False
            job.bind(
                [side_in.pop(0) for _ in job.operands],
                [side_out.pop(0) for _ in job.outs],
                take(len(job.scratch)),
            )
        for place, item in enumerate(ins):
            if isinstance(item, Late):
                held, sem = take(2)
                copy = pltpu.make_async_copy(item.source(own_in[place]), held, sem)
                side.waiting.append((item.lazy, copy))
                if item.name is None:
                    side.first_loads.append(copy)
                side.loads[item.name] = copy
                own_in[place] = held
        for place, item in enumerate(outs):
            if isinstance(item, Early):
                held = take(1)[0] if item.over is None else own_in[item.over]
                sem = take(1)[0]
                side.stores[item.name] = pltpu.make_async_copy(held, own_out[place], sem)
                own_out[place] = held
        if not remote:
            side.load(False)
        kernel(side, *own_in, *own_out, *own)
        side.close()

    key = (name,) + tuple(job.key() for job in jobs)
    shapes = [
        (item.shape, item.kind) if isinstance(item, Early) else item[:2] for item in outs
    ] + job_outs
    results = pl.pallas_call(
        body,
        out_shape=tuple(jax.ShapeDtypeStruct(shape, kind) for shape, kind in shapes),
        in_specs=[pl.BlockSpec(memory_space=pltpu.SMEM)] * scalars
        + [far if isinstance(item, Late) else whole for item in ins[scalars:]]
        + [far] * len(job_ins),
        out_specs=tuple(
            [far if isinstance(item, Early) or len(item) > 2 else whole for item in outs]
            + job_spaces
        ),
        scratch_shapes=own_scratch + [part for item in moved for part in item.scratch],
        cost_estimate=pl.CostEstimate(
            flops=0, bytes_accessed=micros * 3000000, transcendentals=0
        ),
        compiler_params=pltpu.CompilerParams(
            collective_id=collective_of(key) if remote else None,
            has_side_effects=remote,
            vmem_limit_bytes=VMEM_BYTES,
        ),
    )(*[item.value if isinstance(item, Late) else item for item in ins], *job_ins)
    return results[: len(outs)], results[len(outs) :]


def tiled_grad(left, right, store, serve, size=384):
    for tile in range(left.shape[1] // size):
        cols = slice(tile * size, (tile + 1) * size)
        store(tile, size, dot(left[:, cols], right[...], TN).astype(BF16))
        serve(tile)


def normed(hidden):
    center = hidden - jnp.mean(hidden, axis=-1, keepdims=True)
    inverse = lax.rsqrt(jnp.mean(center * center, axis=-1, keepdims=True) + EPS)
    return center * inverse, inverse


def norm_back(hidden, scale_row, grad):
    hat, inverse = normed(hidden)
    inner = grad * scale_row
    back = inverse * (
        inner
        - jnp.mean(inner, axis=-1, keepdims=True)
        - hat * jnp.mean(inner * hat, axis=-1, keepdims=True)
    )
    return back, hat


def loop_rows(total, size, body):
    def step(index, carry):
        body(pl.ds(pl.multiple_of(index * size, size), size), index)
        return carry

    lax.fori_loop(0, total // size, step, 0)


def add_sum(ref, row, block):
    ref[row : row + 1] += jnp.sum(block, axis=0, keepdims=True)


def turned(rows):
    lane = lax.broadcasted_iota(jnp.int32, rows.shape, 1)
    width = rows.shape[1]
    return jnp.where(
        lax.rem(lane, 2) == 0, -pltpu.roll(rows, width - 1, 1), pltpu.roll(rows, 1, 1)
    )


def head_cols(head):
    return slice(head * HEAD_DIM, (head + 1) * HEAD_DIM)


def inverse_rms(sums, features):
    return lax.rsqrt(sums / features + EPS)


MODS, OUT_BIAS, CROSS_GAIN, CROSS_SHIFT = 0, 6, 9, 10
KEY_BIAS, GAINS = 5, 6


def row_of(ref, index):
    return ref[index : index + 1]


def first_kernel(
    side,
    lengths,
    block_order,
    time_embed,
    modulation,
    out_bias,
    cross_gain,
    cross_shift,
    proj_bias,
    key_bias,
    norm_gains,
    ffn_bias,
    positions,
    table,
    base,
    counts,
    cosine,
    sine,
    nothing,
    *rest,
):
    rest = list(rest)
    packs = rest[: 3 * LAYERS]
    send_sems, recv_sems = rest[-2:]
    rest = rest[3 * LAYERS : -2]
    greet(side, True, side.masks)
    near, far = holders()
    tokens = counts.shape[2]
    clip = lax.axis_index(DP) // HOLD
    mine = (lengths[clip] - block_order[0] * tokens).astype(F32)
    counts[0] = jnp.full(counts.shape[1:], mine, F32)

    def copy(number, source, target, device):
        return send(
            counts.at[source],
            counts.at[target],
            send_sems.at[number],
            recv_sems.at[number],
            dp=device,
        )

    to_near, to_far, onward = copy(0, 0, 1, near), copy(1, 0, 2, far), copy(2, 2, 3, near)
    side.start()
    to_near.start()
    to_far.start()
    for layer in range(LAYERS):
        rows_d, rows_w, rows_f = packs[3 * layer : 3 * layer + 3]
        rows_d[...] = jnp.zeros(rows_d.shape, F32)
        rows_w[...] = jnp.zeros(rows_w.shape, F32)
        for row in range(6):
            embed = jnp.zeros((1, rows_d.shape[1]), F32)
            for index in range(time_embed.shape[1]):
                embed = embed + jnp.where(clip == index, row_of(time_embed.at[row], index), 0.0)
            rows_d[row : row + 1] = row_of(modulation.at[row], layer) + embed
        for row in range(3):
            rows_d[OUT_BIAS + row : OUT_BIAS + row + 1] = row_of(out_bias.at[row], layer)
        rows_d[CROSS_GAIN : CROSS_GAIN + 1] = row_of(cross_gain, layer)
        rows_d[CROSS_SHIFT : CROSS_SHIFT + 1] = row_of(cross_shift, layer)
        for row in range(5):
            rows_w[row : row + 1] = row_of(proj_bias.at[row], layer)
        rows_w[KEY_BIAS : KEY_BIAS + 1] = row_of(key_bias, layer)
        rows_w[GAINS : GAINS + 4] = norm_gains[layer]
        rows_f[...] = row_of(ffn_bias, layer)
    nothing[...] = jnp.zeros(nothing.shape, F32)
    angles = dot(positions[...].astype(F32), table[...], TN, exact=True)
    cosine[...] = jnp.cos(angles)
    sine[...] = jnp.sin(angles)
    to_far.wait_recv()
    onward.start()
    side.move(1, SELF)
    side.start(1)
    to_near.wait_recv()
    onward.wait_recv()
    for copy in (to_near, to_far, onward):
        copy.wait_send()
    side.finish(SELF)
    attend_body(
        side, base, None, None, packs[0], packs[1], side.jobs[0].out, cosine, sine, counts, True, rest
    )


def add_branch(base, tot, bias_row, gate_row):
    return base + (tot.astype(F32) + bias_row) * gate_row


def attend_kernel(
    side, base, tot, rows_before, rows_d, rows_w, weight, cosine, sine, counts, *refs
):
    greet(side, True, [1, 2])
    side.start()
    attend_body(
        side, base, tot, rows_before, rows_d, rows_w, weight, cosine, sine, counts, False, list(refs)
    )


def attend_body(
    side, base, tot, rows_before, rows_d, rows_w, weight, cosine, sine, counts, first, refs
):
    hidden, normal, query, key, query_rot, key_value, slots = refs[:7]
    others, result, lse = refs[7:10]
    scores, send_sems, recv_sems, hold_sends, hold_recvs = refs[-5:]
    tokens, width = query.shape
    features = hidden.shape[1]
    heads = width // HEAD_DIM
    scale_row = 1.0 + row_of(rows_d, MODS + 1)
    shift_row = row_of(rows_d, MODS)

    def project(rows, index):
        if first:
            block = base[rows].astype(F32)
        else:
            block = add_branch(
                base[rows], tot[rows], row_of(rows_before, OUT_BIAS + 2), row_of(rows_before, MODS + 5)
            )
        hidden[rows] = block
        block = (normed(block)[0] * scale_row + shift_row).astype(BF16)
        normal[rows] = block
        query[rows] = dot(block, weight[0]) + row_of(rows_w, 0)
        key[rows] = dot(block, weight[1]) + row_of(rows_w, KEY_BIAS)
        value = (dot(block, weight[2]) + row_of(rows_w, 1)).astype(BF16)
        for head in range(heads):
            key_value[head, 1, rows] = value[:, head_cols(head)]

    if not first:
        side.need(WEIGHT)
    loop_rows(tokens, 256, project)
    side.store(HIDDEN, NORMAL, QUERY, KEY)
    near, far = holders()

    def copy(source, target, number, device):
        return send(source, target, hold_sends.at[number], hold_recvs.at[number], dp=device)

    to_near = copy(key_value, others.at[0], 0, near)
    values_far, keys_far = [
        [
            copy(
                key_value.at[head, member],
                others.at[1, head, member],
                1 + (1 + member) * heads + head,
                far,
            )
            for head in range(heads)
        ]
        for member in (1, 0)
    ]
    onward = [
        copy(others.at[1, head], others.at[2, head], 1 + head, near) for head in range(heads)
    ]
    for item in values_far:
        item.start()
    exchange = Exchange(slots, send_sems, recv_sems)
    exchange.start(
        stat_rows(query[...] * query[...], 0) + stat_rows(key[...] * key[...], 1)
    )
    side.early()
    exchange.finish()
    query_inv = inverse_rms(stat_column(slots, 0, HEAD_DIM), features)
    key_inv = inverse_rms(stat_column(slots, 1, HEAD_DIM), features)
    if not first:
        side.need(COSINE, SINE)
    for head in range(heads):
        cols = head_cols(head)
        rows = key[:, cols] * key_inv * rows_w[GAINS + 1 : GAINS + 2, cols]
        key_value[head, 0] = (rows * cosine[...] + turned(rows) * sine[...]).astype(BF16)
        keys_far[head].start()
    to_near.start()
    for head in range(heads):
        cols = head_cols(head)
        rows = query[:, cols] * query_inv * rows_w[GAINS : GAINS + 1, cols]
        query_rot[:, cols] = (rows * cosine[...] + turned(rows) * sine[...]).astype(BF16)
    side.store(QUERY_ROT)
    side.middle()

    def score(head, slot, keys):
        block = dot(keys, query_rot[:, head_cols(head)], NT) * (SCALE * LOG2E)
        scores[head, slot] = jnp.where(below(counts, slot, block.shape), block, -1e30)

    for head in range(heads):
        score(head, 0, key_value[head, 0])
    to_near.wait_recv()
    for head in range(heads):
        score(head, 1, others[0, head, 0])
    lse[...] = jnp.zeros(lse.shape, F32)
    for head in range(heads):
        values_far[head].wait_recv()
        keys_far[head].wait_recv()
        onward[head].start()
        if head == 0:
            side.late()
        score(head, 2, others[1, head, 0])
        onward[head].wait_recv()
        score(head, 3, others[2, head, 0])
        top = jnp.max(scores[head, 0], axis=0, keepdims=True)
        for slot in range(1, HOLD):
            top = jnp.maximum(top, jnp.max(scores[head, slot], axis=0, keepdims=True))
        total = jnp.zeros_like(top)
        summed = jnp.zeros((HEAD_DIM, tokens), F32)
        for slot in range(HOLD):
            values = key_value[head, 1] if slot == 0 else others[slot - 1, head, 1]
            probs = jnp.exp2(scores[head, slot] - top)
            total = total + jnp.sum(probs, axis=0, keepdims=True)
            summed = summed + dot(values, probs.astype(BF16), TN)
        result[:, head_cols(head)] = (summed / total).T.astype(BF16)
        lse[head : head + 1] = top + jnp.log2(total)
    for item in [to_near] + values_far + keys_far + onward:
        item.wait_send()
    side.finish()


def below(counts, slot, shape):
    index = lax.broadcasted_iota(jnp.int32, shape, 0).astype(F32)
    return index < counts[slot, 0:1]


def softmax_back(scores, lse_row, mask):
    probs = jnp.exp2(scores * (SCALE * LOG2E) - lse_row)
    return probs if mask is None else jnp.where(mask, probs, 0.0)


def out_sum_kernel(
    first,
    side,
    rows_in,
    weight,
    context,
    text_weight,
    rows_w,
    total,
    text_key,
    text_kb,
    text_vb,
    slots,
    *refs,
):
    refs = list(refs)
    own, arrived = context, []
    if first:
        context = refs.pop(0)
        clip_sends, clip_recvs = refs[-2:]
        refs = refs[:-2]
    send_sems, recv_sems, part, came, pair, peers, sems = refs
    greet(side, True, side.masks)
    if first:
        near, far = holders()
        place = lax.rem(lax.axis_index(DP), HOLD)
        size = own.shape[0]

        def block(index):
            return context.at[pl.ds(pl.multiple_of(index * size, 16), size)]

        def copy(number, index, device):
            return send(
                block(index), block(index), clip_sends.at[number], clip_recvs.at[number], dp=device
            )

        arrived = [copy(0, place, near), copy(1, place, far), copy(2, flip(place, 2), near)]
        side.need(CONTEXT)
        context[pl.ds(pl.multiple_of(place * size, 16), size)] = own[...]
        arrived[1].start()
        arrived[0].start()
    side.start()
    chain = Chain(part, total, (came, pair, peers), sems)
    tokens, features = total.shape
    per_block = 128 // CHUNK

    def project(rows, index):
        part[rows] = dot(rows_in[rows], weight[...], NT).astype(BF16)
        chain.begin(index * per_block, per_block)

    side.need(OUT)
    loop_rows(tokens, 128, project)
    low = 0
    if first:
        low = 4
        chain.segment(0, low, 0, 0)
        arrived[1].wait_recv()
        arrived[2].start()
        arrived[0].wait_recv()
        arrived[2].wait_recv()
        for item in arrived:
            item.wait_send()
    else:
        side.need(CONTEXT)
    side.need(TEXT_WEIGHT)
    text_count, width = text_key.shape
    blocks = text_count // 128

    def text(rows, index):
        block = context[rows]
        text_key[rows] = dot(block, text_weight[0]) + row_of(rows_w, 3)
        chain.serve(low + 2 * index)
        text_vb[rows] = (dot(block, text_weight[1]) + row_of(rows_w, 4)).astype(BF16)
        chain.serve(low + 2 * index + 1)

    loop_rows(text_count, 128, text)
    exchange = Exchange(slots, send_sems, recv_sems)

    def early():
        side.early()
        exchange.start(stat_rows(text_key[...] * text_key[...], 0))

    chain.drain(low + 2 * blocks, early, side.middle)
    exchange.finish()
    text_inv = inverse_rms(stat_column(slots, 0, HEAD_DIM), features)
    for head in range(width // HEAD_DIM):
        cols = head_cols(head)
        text_kb[:, cols] = (
            text_key[:, cols] * text_inv * rows_w[GAINS + 3 : GAINS + 4, cols]
        ).astype(BF16)
    side.finish()


def cross_ffn_kernel(
    gathered,
    side,
    base,
    tot,
    rows_d,
    rows_w,
    rows_f,
    weight,
    text_kb,
    text_vb,
    out_weight,
    up,
    *refs,
):
    refs = list(refs)
    down = side.jobs[0].out if gathered else refs.pop(0)
    hidden, normal, query, query_b, result, lse, slots = refs[:7]
    hidden_f, normal_f, gelu_b, slope, total_f = refs[7:12]
    send_sems, recv_sems, total = refs[12:15]
    part, came, pair, peers, sems = refs[15:20]
    part_f, came_f, pair_f, peers_f, sems_f = refs[20:25]
    greet(side, True, side.masks)
    side.late_after = True
    side.start()
    chain = Chain(part, total, (came, pair, peers), sems)
    chain_f = Chain(part_f, total_f, (came_f, pair_f, peers_f), sems_f)
    tokens, width = query.shape
    features = hidden.shape[1]
    heads = width // HEAD_DIM

    def project(rows, index):
        block = add_branch(
            base[rows], tot[rows], row_of(rows_d, OUT_BIAS), row_of(rows_d, MODS + 2)
        )
        hidden[rows] = block
        block = normed(block)[0] * row_of(rows_d, CROSS_GAIN) + row_of(rows_d, CROSS_SHIFT)
        block = block.astype(BF16)
        normal[rows] = block
        query[rows] = dot(block, weight[...]) + row_of(rows_w, 2)

    side.need(WEIGHT)
    side.load(True)
    loop_rows(tokens, 256, project)
    side.store(HIDDEN, NORMAL, QUERY)
    exchange = Exchange(slots, send_sems, recv_sems)
    exchange.start(stat_rows(query[...] * query[...], 0))
    exchange.finish()
    query_inv = inverse_rms(stat_column(slots, 0, HEAD_DIM), features)
    side.need(TEXT_KB, TEXT_VB)
    lse[...] = jnp.zeros(lse.shape, F32)
    for head in range(heads):
        cols = head_cols(head)
        query_b[:, cols] = (
            query[:, cols] * query_inv * rows_w[GAINS + 2 : GAINS + 3, cols]
        ).astype(BF16)
        scores = dot(text_kb[:, cols], query_b[:, cols], NT) * (SCALE * LOG2E)
        top = jnp.max(scores, axis=0, keepdims=True)
        probs = jnp.exp2(scores - top)
        amount = jnp.sum(probs, axis=0, keepdims=True)
        summed = dot(text_vb[:, cols], probs.astype(BF16), TN)
        result[:, cols] = (summed / amount).T.astype(BF16)
        lse[head : head + 1] = top + jnp.log2(amount)
    per_block = 128 // CHUNK

    def project_out(rows, index):
        part[rows] = dot(result[rows], out_weight[...], NT).astype(BF16)
        chain.begin(index * per_block, per_block)

    side.store(QUERY_B, RESULT)
    side.need(OUT)
    loop_rows(tokens, 128, project_out)
    side.move(1, DOWN)
    side.start(1)
    scale_row = 1.0 + row_of(rows_d, MODS + 4)
    shift_row = row_of(rows_d, MODS + 3)

    def rows_of(rows):
        block = add_branch(hidden[rows], total[rows], row_of(rows_d, OUT_BIAS + 1), 1.0)
        hidden_f[rows] = block
        block = (normed(block)[0] * scale_row + shift_row).astype(BF16)
        normal_f[rows] = block
        return block

    def inner(rows, block, low, high):
        z = dot(block, up[:, low:high]) + rows_f[:, low:high]
        square = z * z
        tanh = jnp.tanh(GELU_A * z * (1.0 + GELU_B * square))
        side_value = 0.5 * (1.0 + tanh)
        gelu_b[rows, low:high] = (z * side_value).astype(BF16)
        slope[rows, low:high] = (
            side_value
            + 0.5 * z * (1.0 - tanh * tanh) * (GELU_A * (1.0 + 3.0 * GELU_B * square))
        ).astype(BF16)

    def before_second():
        if gathered:
            side.finish(DOWN)
        else:
            side.need(DOWN)

    def after(left):
        side.store(HIDDEN_F, NORMAL_F, GELU_B_NAME, SLOPE)

    side.need(UP)
    mlp_loop(
        side, tokens, rows_of, inner, down, chain_f, gelu_b, before_second, after, chain
    )


def column_cuts(width):
    cuts, low = [], 0
    while low < width:
        high = low + 512 if width - low >= 1024 else width
        cuts.append((low, high))
        low = high
    return cuts


GELU_A = 0.7978845608028654
GELU_B = 0.044715


def mlp_loop(side, tokens, rows_of, inner, second, chain, middle, before_second, after, feed=None):
    size = 128
    per_block = size // CHUNK
    features, hidden_width = second.shape
    cuts = column_cuts(hidden_width)
    half = features // 2
    blocks = tokens // size
    if feed is not None:

        @pl.when(feed.is_mid)
        def _():
            feed.first(0)
            for k in range(1, per_block):
                feed.first(k)
                feed.second(k - 1)

    def step(index, carry):
        rows = pl.ds(pl.multiple_of(index * size, size), size)
        low = index * per_block

        def serve(offset):
            if feed is None:

                @pl.when(index > 0)
                def _():
                    chain.serve(jnp.maximum(low - per_block, 0) + offset)

                return
            if offset > 0:

                @pl.when(feed.is_mid & (index < blocks - 1))
                def _():
                    ahead = jnp.minimum(low + per_block, feed.chunks - per_block)
                    feed.first(ahead + offset)
                    feed.second(ahead + offset - 1)

            @pl.when(index == blocks - 1)
            def _():
                chain.serve(offset)

        if feed is not None:

            @pl.when(feed.is_mid)
            def _():
                @pl.when(index < blocks - 1)
                def _():
                    feed.first(jnp.minimum(low + per_block, feed.chunks - per_block))

                feed.second(low + per_block - 1)

            @pl.when(feed.is_end)
            def _():
                for offset in range(per_block):
                    feed.inward(low + offset, feed.inner).wait_send()
                    feed.outward(low + offset, feed.inner).wait_recv()

        block = rows_of(rows)
        served = 0
        for place, (left, right) in enumerate(cuts):
            inner(rows, block, left, right)
            if place % 2 == 1 and served < 2:
                serve(served)
                served += 1
        while served < 2:
            serve(served)
            served += 1

        @pl.when(index == 0)
        def _():
            before_second()

        for part_index in range(2):
            cols = slice(part_index * half, (part_index + 1) * half)
            chain.part[rows, cols] = dot(middle[rows], second[cols], NT).astype(BF16)
            if part_index == 0:
                serve(2)
        chain.begin(low, per_block)
        serve(3)
        if side.jobs:
            if feed is None:
                points = ((1, bits_of_dp() - 2), (blocks - 1, bits_of_dp() - 1))
            else:
                points = ((blocks - 1, bits_of_dp() - 2),)
            for point, target in points:

                @pl.when(index == point)
                def _(target=target):
                    side.move(target)

        return carry

    lax.fori_loop(0, blocks, step, 0)
    left = (blocks - 1) * per_block if feed is None else per_block
    left = after(left) or left
    chain.drain(left, None, None if feed is None else side.late)
    if feed is not None:
        feed.close()
    side.finish()


def ffn_back_kernel(
    joined,
    side,
    grad,
    *refs,
):
    refs = list(refs)

    def take(count):
        taken = refs[:count]
        del refs[:count]
        return taken

    if joined:
        branch, hidden, rows_above = take(3)
    else:
        teacher, counts = take(2)
    tot, rows_d, down, up, slope, normal, gelu_b = take(7)
    if joined:
        new_grad, sums_above = take(2)
    else:
        new_grad, output = take(2)
    (total, sums, bias_sum, up_grad, down_grad) = take(5)
    down_in, inner_b, stage, stage_sems, part, came, pair, peers, sems = refs
    greet(side, True, side.masks)
    side.late_after = True
    side.start()
    chain = Chain(part, total, (came, pair, peers), sems)
    tokens = grad.shape[0]
    sums[...] = jnp.zeros(sums.shape, F32)
    bias_sum[...] = jnp.zeros(bias_sum.shape, F32)
    if joined:
        sums_above[...] = jnp.zeros(sums_above.shape, F32)
        scale_row = 1.0 + row_of(rows_above, MODS + 1)

    def rows_of(rows):
        block = grad[rows]
        if joined:
            step = branch[rows].astype(F32)
            back, hat = norm_back(hidden[rows], scale_row, step)
            add_sum(sums_above, 0, step)
            add_sum(sums_above, 1, step * hat)
            block = block + back
            new_grad[rows] = block
        else:
            block = add_branch(
                block, tot[rows], row_of(rows_d, OUT_BIAS + 2), row_of(rows_d, MODS + 5)
            )
            output[rows] = block
            block = block - teacher[rows].astype(F32)
            place = lax.broadcasted_iota(jnp.int32, (block.shape[0], 1), 0) + rows.start
            block = jnp.where(place.astype(F32) < counts[0, 0:1, 0:1], block, 0.0)
            new_grad[rows] = block
            add_sum(sums, 2, block * block)
        add_sum(sums, 0, block * (tot[rows].astype(F32) + row_of(rows_d, OUT_BIAS + 2)))
        block = (block * row_of(rows_d, MODS + 5)).astype(BF16)
        down_in[rows] = block
        add_sum(sums, 1, block.astype(F32))
        return block

    def inner(rows, block, low, high):
        cols = (dot(block, down[:, low:high]) * slope[rows, low:high].astype(F32)).astype(BF16)
        inner_b[rows, low:high] = cols
        bias_sum[0:1, low:high] += jnp.sum(cols.astype(F32), axis=0, keepdims=True)

    def after(left):
        side.store(NEW_GRAD)
        if not joined:
            side.store(OUTPUT)
        side.need(NORMAL, GELU_B_NAME)
        copies = []

        def keep(target):
            def store(tile, size, block):
                number = len(copies)
                if number >= 2:
                    copies[number - 2].wait()
                stage[number % 2] = block
                copy = pltpu.make_async_copy(
                    stage.at[number % 2],
                    target.at[tile * size : (tile + 1) * size],
                    stage_sems.at[number % 2],
                )
                copy.start()
                copies.append(copy)

            return store

        def serve(tile):
            if left + tile < chain.chunks:
                chain.serve(left + tile)

        tiled_grad(normal, inner_b, keep(up_grad), serve, stage.shape[1])
        chain.segment(chain.chunks, chain.chunks, 0, 0)
        tiled_grad(down_in, gelu_b, keep(down_grad), lambda tile: None, stage.shape[1])
        copies[-2].wait()
        copies[-1].wait()
        return chain.chunks

    side.need(GRAD, DOWN, SLOPE)
    side.load(True)
    mlp_loop(
        side, tokens, rows_of, inner, up, chain, inner_b, lambda: side.need(UP), after
    )


def cross_back_kernel(
    side,
    grad,
    branch,
    hidden,
    rows_d,
    rows_w,
    out_weight,
    query,
    query_b,
    lse,
    slots_q,
    text_kb,
    text_vb,
    weight,
    normal,
    result,
    new_grad,
    text_grad,
    sums,
    width_sums,
    total,
    matrix_grad,
    out_in,
    query_grad_b,
    out_grad,
    query_n,
    slots,
    send_sems,
    recv_sems,
    part,
    came,
    pair,
    peers,
    sems,
):
    greet(side, True, side.masks)
    side.late_after = True
    side.start()
    chain = Chain(part, total, (came, pair, peers), sems)
    tokens, width = query.shape
    features = grad.shape[1]
    heads = width // HEAD_DIM
    gain = rows_w[GAINS + 2 : GAINS + 3]
    sums[...] = jnp.zeros(sums.shape, F32)
    width_sums[...] = jnp.zeros(width_sums.shape, F32)
    scale_row = 1.0 + row_of(rows_d, MODS + 4)

    def enter(rows, index):
        step = branch[rows].astype(F32)
        back, hat = norm_back(hidden[rows], scale_row, step)
        add_sum(sums, 0, step)
        add_sum(sums, 1, step * hat)
        block = grad[rows] + back
        new_grad[rows] = block
        block = block.astype(BF16)
        out_in[rows] = block
        add_sum(sums, 2, block.astype(F32))
        out_grad[rows] = dot(block, out_weight[...]).astype(BF16)

    side.need(OUT)
    side.load(True)
    loop_rows(tokens, 256, enter)
    side.store(NEW_GRAD)
    side.need(QUERY, QUERY_B, TEXT_KB, TEXT_VB)
    for head in range(heads):
        cols = head_cols(head)
        query_h, out_grad_h = query_b[:, cols], out_grad[:, cols]
        text_k, text_v = text_kb[:, cols], text_vb[:, cols]
        probs = softmax_back(dot(text_k, query_h, NT), lse[head : head + 1], None)
        prob_grad = dot(text_v, out_grad_h, NT)
        inner = jnp.sum(probs * prob_grad, axis=0, keepdims=True)
        score_b = (probs * (prob_grad - inner) * SCALE).astype(BF16)
        query_n[:, cols] = dot(text_k, score_b, TN).T
        text_grad[0, :, cols] = dot(score_b, query_h)
        text_grad[1, :, cols] = dot(probs.astype(BF16), out_grad_h)
    exchange = Exchange(slots, send_sems, recv_sems)
    exchange.start(stat_rows(query[...] * query_n[...] * gain, 0))
    inverse = inverse_rms(stat_column(slots_q, 0, HEAD_DIM), features)
    side.move(1)
    exchange.finish()
    term = stat_column(slots, 0, HEAD_DIM) * inverse * inverse * inverse / features
    for head in range(heads):
        cols = head_cols(head)
        width_sums[0:1, cols] = jnp.sum(
            query[:, cols] * query_n[:, cols] * inverse, axis=0, keepdims=True
        )
        block = inverse * gain[:, cols] * query_n[:, cols] - query[:, cols] * term
        block = block.astype(BF16)
        query_grad_b[:, cols] = block
        width_sums[1:2, cols] = jnp.sum(block.astype(F32), axis=0, keepdims=True)
    per_block = 128 // CHUNK

    def leave(rows, index):
        part[rows] = dot(query_grad_b[rows], weight[...], NT).astype(BF16)
        chain.begin(index * per_block, per_block)

    side.store(TEXT_GRAD)
    side.need(WEIGHT)
    loop_rows(tokens, 128, leave)
    side.need(NORMAL, RESULT)

    def keep(low):
        def store(tile, size, block):
            matrix_grad[tile * size : (tile + 1) * size, low : low + width] = block

        return store

    tiled_grad(normal, query_grad_b, keep(0), lambda tile: None if tile % 2 else chain.serve(tile // 2))
    tiled_grad(out_in, result, keep(width), lambda tile: None if tile % 2 else chain.serve(2 + tile // 2))
    side.store(MATRIX_GRAD)
    chain.drain(4, side.late)
    side.finish()


def attend_back_kernel(
    side,
    counts,
    grad,
    branch,
    hidden,
    rows_d,
    tot,
    out_weight,
    query,
    key_value,
    others,
    lse,
    text_grad,
    result,
    new_grad,
    matrix_grad,
    sums,
    query_grad,
    key_value_grad,
    text_sum,
    out_in,
    out_grad,
    probs,
    prob_grads,
    away,
    landed,
    text_away,
    text_landed,
    send_sems,
    recv_sems,
):
    greet(side, False, [1, 2])
    side.start()
    near, far = holders()
    tokens, width = query.shape
    heads = width // HEAD_DIM
    text_rows = text_sum.shape[1]
    sums[...] = jnp.zeros(sums.shape, F32)

    def copy(kind, head, member):
        return send(
            away.at[kind, head, member],
            landed.at[kind, head, member],
            send_sems.at[kind, member * heads + head],
            recv_sems.at[kind, member * heads + head],
            dp=far if kind == 1 else near,
        )

    def text_copy(kind):
        return send(
            text_away.at[kind],
            text_landed.at[kind],
            send_sems.at[kind, 2 * heads],
            recv_sems.at[kind, 2 * heads],
            dp=far if kind == 1 else near,
        )

    place = lax.rem(lax.axis_index(DP), HOLD)

    def text_part(slot):
        start = pl.multiple_of(flip(place, slot) * text_rows, text_rows)
        return text_grad[:, pl.ds(start, text_rows)]

    text_away[2] = text_part(3).astype(BF16)
    text_copy(2).start()
    text_away[0] = text_part(1).astype(BF16)
    text_copy(0).start()

    def enter(rows, index):
        step = branch[rows].astype(F32)
        back, hat = norm_back(hidden[rows], row_of(rows_d, CROSS_GAIN), step)
        add_sum(sums, 0, step * hat)
        add_sum(sums, 1, step)
        block = grad[rows] + back
        new_grad[rows] = block
        add_sum(sums, 2, block * (tot[rows].astype(F32) + row_of(rows_d, OUT_BIAS)))
        block = (block * row_of(rows_d, MODS + 2)).astype(BF16)
        out_in[rows] = block
        add_sum(sums, 3, block.astype(F32))
        out_grad[rows] = dot(block, out_weight[...]).astype(BF16)

    side.need(OUT)
    loop_rows(tokens, 256, enter)
    side.store(NEW_GRAD)
    side.need(QUERY, KEY_VALUE, OTHERS, RESULT)
    text_copy(2).wait_recv()
    text_away[1] = (text_part(2) + text_landed[2].astype(F32)).astype(BF16)
    text_copy(1).start()

    for head in range(heads):
        cols = head_cols(head)
        query_h, out_grad_h = query[:, cols], out_grad[:, cols]

        def pair_of(slot, head=head):
            if slot == 0:
                return key_value[head, 0], key_value[head, 1]
            return others[slot - 1, head, 0], others[slot - 1, head, 1]

        def share(slot, member, block, head=head, cols=cols):
            if slot == 0:
                key_value_grad[member, :, cols] = block
                return
            if slot == 2:
                copy(2, head, member).wait_recv()
                block = block + landed[2, head, member].astype(F32)
            away[slot - 1, head, member] = block.astype(BF16)
            copy(slot - 1, head, member).start()

        inner = jnp.zeros((1, tokens), F32)
        for slot in (3, 2, 1, 0):
            keys, values = pair_of(slot)
            block = softmax_back(
                dot(keys, query_h, NT),
                lse[head : head + 1],
                below(counts, slot, (tokens, tokens)),
            )
            probs[slot] = block
            block_grad = dot(values, out_grad_h, NT)
            prob_grads[slot] = block_grad
            inner = inner + jnp.sum(block * block_grad, axis=0, keepdims=True)
            share(slot, 1, dot(block.astype(BF16), out_grad_h))
        query_n = jnp.zeros((HEAD_DIM, tokens), F32)
        for slot in (3, 2, 1, 0):
            keys, values = pair_of(slot)
            block = probs[slot]
            score_b = (block * (prob_grads[slot] - inner) * SCALE).astype(BF16)
            query_n = query_n + dot(keys, score_b, TN)
            share(slot, 0, dot(score_b, query_h))
        query_grad[:, cols] = query_n.T
    side.store(QUERY_GRAD)

    def keep(tile, size, block):
        matrix_grad[tile * size : (tile + 1) * size] = block

    tiled_grad(out_in, result, keep, lambda tile: None)
    side.store(MATRIX_GRAD)
    text_copy(0).wait_recv()
    text_copy(1).wait_recv()
    text_sum[...] = text_part(0) + text_landed[0].astype(F32) + text_landed[1].astype(F32)
    for head in range(heads):
        cols = head_cols(head)
        for member in range(2):
            copy(0, head, member).wait_recv()
            copy(1, head, member).wait_recv()
            key_value_grad[member, :, cols] += landed[0, head, member].astype(F32) + landed[
                1, head, member
            ].astype(F32)
    for kind in range(3):
        text_copy(kind).wait_send()
        for head in range(heads):
            for member in range(2):
                copy(kind, head, member).wait_send()


def qkv_back_kernel(
    side,
    query_grad,
    key_value_grad,
    text_grad,
    query,
    key,
    text_key,
    slots_in,
    text_slots,
    rows_w,
    cosine,
    sine,
    weight,
    normal,
    context,
    text_weight,
    context_before,
    width_sums,
    context_part,
    total,
    self_grad,
    text_matrix,
    grads_b,
    text_b,
    query_n,
    key_n,
    slots,
    send_sems,
    recv_sems,
    part,
    came,
    pair,
    peers,
    sems,
):
    greet(side, True, side.masks)
    side.start()
    chain = Chain(part, total, (came, pair, peers), sems)
    tokens, width = query.shape
    features = total.shape[1]
    heads = width // HEAD_DIM
    text_rows = text_grad.shape[1]
    place = lax.rem(lax.axis_index(DP), HOLD)
    mine = pl.ds(pl.multiple_of(place * text_rows, text_rows), text_rows)
    text_k = text_key[mine]
    width_sums[...] = jnp.zeros(width_sums.shape, F32)
    for head in range(heads):
        cols = head_cols(head)
        rows = query_grad[:, cols]
        query_n[:, cols] = rows * cosine[...] - turned(rows * sine[...])
        rows = key_value_grad[0, :, cols]
        key_n[:, cols] = rows * cosine[...] - turned(rows * sine[...])

    def gain(member):
        return rows_w[GAINS + member : GAINS + member + 1]

    exchange = Exchange(slots, send_sems, recv_sems)
    text_terms = stat_rows(text_k * gain(3) * text_grad[0], 2)
    exchange.start(
        stat_rows(query[...] * gain(0) * query_n[...], 0)
        + stat_rows(key[...] * gain(1) * key_n[...], 1)
        + jnp.concatenate([text_terms, jnp.zeros((8, tokens - text_rows), F32)], axis=1)
    )
    query_inv = inverse_rms(stat_column(slots_in, 0, HEAD_DIM), features)
    key_inv = inverse_rms(stat_column(slots_in, 1, HEAD_DIM), features)
    text_inv = inverse_rms(stat_column(text_slots.at[:, :, mine], 0, HEAD_DIM), features)
    side.move(1)
    exchange.finish()

    def cubed(inverse, term):
        return term * inverse * inverse * inverse / features

    query_t = cubed(query_inv, stat_column(slots, 0, HEAD_DIM))
    key_t = cubed(key_inv, stat_column(slots, 1, HEAD_DIM))
    text_t = cubed(text_inv, stat_column(slots.at[:, :, pl.ds(0, text_rows)], 2, HEAD_DIM))

    def back(member, cols, values, inverse, term, grads):
        width_sums[member : member + 1, cols] = jnp.sum(
            values * inverse * grads, axis=0, keepdims=True
        )
        block = inverse * gain(member)[:, cols] * grads - values * term
        block = block.astype(BF16)
        width_sums[4 + member : 5 + member, cols] = jnp.sum(
            block.astype(F32), axis=0, keepdims=True
        )
        return block

    def shifted(cols, member):
        return slice(cols.start + member * width, cols.stop + member * width)

    for head in range(heads):
        cols = head_cols(head)
        grads_b[:, cols] = back(0, cols, query[:, cols], query_inv, query_t, query_n[:, cols])
        grads_b[:, shifted(cols, 1)] = back(
            1, cols, key[:, cols], key_inv, key_t, key_n[:, cols]
        )
        text_b[:, cols] = back(
            3, cols, text_k[:, cols], text_inv, text_t, text_grad[0, :, cols]
        )
    block = key_value_grad[1].astype(BF16)
    grads_b[:, 2 * width :] = block
    width_sums[6:7] = jnp.sum(block.astype(F32), axis=0, keepdims=True)
    block = text_grad[1].astype(BF16)
    text_b[:, width:] = block
    width_sums[8:9] = jnp.sum(block.astype(F32), axis=0, keepdims=True)
    per_block = 128 // CHUNK

    def leave(rows, index):
        part[rows] = (
            dot(grads_b[rows, :width], weight[0], NT)
            + dot(grads_b[rows, width : 2 * width], weight[1], NT)
            + dot(grads_b[rows, 2 * width :], weight[2], NT)
        ).astype(BF16)
        chain.begin(index * per_block, per_block)

    side.need(WEIGHT)
    loop_rows(tokens, 128, leave)
    side.need(NORMAL, CONTEXT, TEXT_WEIGHT)

    def keep(target):
        def store(tile, size, block):
            target[tile * size : (tile + 1) * size] = block

        return store

    tiled_grad(normal, grads_b, keep(self_grad), chain.serve)
    side.store(SELF_GRAD)
    tiled_grad(context, text_b, keep(text_matrix), lambda tile: None)
    side.store(TEXT_MATRIX)
    chain.serve(4)
    side.need(BEFORE)
    context_part[...] = (
        context_before[...]
        + dot(text_b[:, :width], text_weight[0], NT)
        + dot(text_b[:, width:], text_weight[1], NT)
    )
    chain.drain(5, side.late)
    side.finish()


def small_rows(clips):
    low = 6 * LAYERS + 6 * clips
    places = {BIAS: low, GAIN: low + 3 * LAYERS, SHIFT: low + 4 * LAYERS}
    places[LOSS] = low + 5 * LAYERS
    return places, (low + 5 * LAYERS + 1 + 15) // 16 * 16


def last_kernel(
    clips,
    side,
    context_part,
    grad,
    branch,
    hidden,
    rows_d,
    *refs,
):
    refs = list(refs)

    def take(count):
        taken = refs[:count]
        del refs[:count]
        return taken

    above = take(1)[0]
    small = [take(6) for _ in range(LAYERS)]
    new_grad, total, out_d, out_w, out_f = take(5)
    sums = take(1)[0]
    part, came, pair, peers, sems = take(5)
    bits = bits_of_dp()
    away = [take(3) for _ in range(bits)]
    landed = [take(3) for _ in range(bits)]
    send_sems, recv_sems = take(2)
    greet(side, True, side.masks)
    side.start()
    me = lax.axis_index(DP)
    clip = me // HOLD
    chain = Chain(part, total, (came, pair, peers), sems)
    part[...] = context_part[...].astype(BF16)
    chain.begin(0, chain.chunks)
    sums[...] = jnp.zeros(sums.shape, F32)
    scale_row = 1.0 + row_of(rows_d, MODS + 1)
    tokens = grad.shape[0]
    size = tokens // chain.chunks
    side.need(GRAD, BRANCH, HIDDEN)

    def enter(rows, index):
        step = branch[rows].astype(F32)
        back, hat = norm_back(hidden[rows], scale_row, step)
        add_sum(sums, 0, step)
        add_sum(sums, 1, step * hat)
        new_grad[rows] = grad[rows] + back
        chain.serve(index)

    loop_rows(tokens, size, enter)
    side.store(NEW_GRAD)
    side.move(1)
    places, count = small_rows(clips)
    out_d[...] = jnp.zeros(out_d.shape, F32)
    out_f[...] = jnp.zeros(out_f.shape, F32)
    time_rows = [jnp.zeros((1, grad.shape[1]), F32) for _ in range(6)]
    for layer in range(LAYERS):
        sums1, sums2, sums3, width1, width2, hidden_sum = small[layer]
        sums0 = sums if layer == 0 else above
        mods = [(sums0, 0), (sums0, 1), (sums1, 2), (sums2, 0), (sums2, 1), (sums3, 0)]
        for row, (ref, index) in enumerate(mods):
            value = row_of(ref, index)
            time_rows[row] = time_rows[row] + value
            out_d[6 * layer + row : 6 * layer + row + 1] = value
        for row, (ref, index) in enumerate([(sums1, 3), (sums2, 2), (sums3, 1)]):
            place = places[BIAS] + 3 * layer + row
            out_d[place : place + 1] = row_of(ref, index)
        place = places[GAIN] + layer
        out_d[place : place + 1] = row_of(sums1, 0)
        place = places[SHIFT] + layer
        out_d[place : place + 1] = row_of(sums1, 1)
        out_w[24 * layer : 24 * layer + 16] = width1[...]
        out_w[24 * layer + 16 : 24 * layer + 24] = width2[...]
        out_f[layer : layer + 1] = row_of(hidden_sum, 0)
    for index in range(clips):
        for row in range(6):
            place = 6 * LAYERS + 6 * index + row
            out_d[place : place + 1] = jnp.where(clip == index, time_rows[row], 0.0)
    out_d[places[LOSS] : places[LOSS] + 1] = row_of(small[LAYERS - 1][2], 2)
    for bit in range(bits):
        copies = []
        for number, ref in enumerate((out_d, out_w, out_f)):
            away[bit][number][...] = ref[...].astype(BF16)
            copy = send(
                away[bit][number],
                landed[bit][number],
                send_sems.at[bit, number],
                recv_sems.at[bit, number],
                dp=flip(me, 1 << bit),
            )
            copy.start()
            copies.append(copy)
        if bit == 0:
            chain.drain(chain.chunks)
        side.move(bit)
        for number, ref in enumerate((out_d, out_w, out_f)):
            copies[number].wait()
            ref[...] = away[bit][number][...].astype(F32) + landed[bit][number][...].astype(F32)
    side.finish()


def unpack_kernel(clips, side, *refs):
    refs = list(refs)

    def take(count):
        taken = refs[:count]
        del refs[:count]
        return taken

    lengths, rows_d, rows_w, rows_f, context_sum = take(5)
    parts = [take(6) for _ in range(LAYERS)]
    whole = take(2)
    loss, time, bias, key_bias, gains, hidden, out, gain, shift, mods = take(10)
    context_grad = take(1)[0]
    self_all, cross_all, out_all, up_all, down_all = take(5)
    whole_out = take(2)
    (sems,) = refs
    width = key_bias.shape[1]
    context_grad[...] = context_sum[...].astype(F32)
    copies = []

    def copy(source, target):
        item = pltpu.make_async_copy(source, target, sems.at[len(copies)])
        item.start()
        copies.append(item)

    for layer in range(LAYERS):
        side.need(*range(6 * layer, 6 * layer + 6))
        up, down, cross, text, self_part, out0 = parts[layer]
        copy(up, up_all.at[layer])
        copy(down, down_all.at[layer])
        for member in range(3):
            copy(self_part.at[:, member * width : (member + 1) * width], self_all.at[layer, member])
        copy(cross.at[:, :width], cross_all.at[layer, 0])
        copy(text.at[:, :width], cross_all.at[layer, 1])
        copy(text.at[:, width:], cross_all.at[layer, 2])
        copy(out0, out_all.at[layer, 0])
        copy(cross.at[:, width:], out_all.at[layer, 1])
    side.need(6 * LAYERS, 6 * LAYERS + 1)
    for source, target in zip(whole, whole_out):
        copy(source, target)
    places, count = small_rows(clips)
    for layer in range(LAYERS):
        for row in range(6):
            mods[row, layer : layer + 1] = row_of(rows_d, 6 * layer + row)
        for row in range(3):
            out[row, layer : layer + 1] = row_of(rows_d, places[BIAS] + 3 * layer + row)
        base = 24 * layer
        for row, place in enumerate((4, 6, 17, 7, 8)):
            bias[row, layer : layer + 1] = row_of(rows_w, base + place)
        key_bias[layer : layer + 1] = row_of(rows_w, base + 5)
        for row, place in enumerate((0, 1, 16, 3)):
            gains[layer, row : row + 1] = row_of(rows_w, base + place)
    for index in range(clips):
        for row in range(6):
            time[row, index : index + 1] = row_of(rows_d, 6 * LAYERS + 6 * index + row)
    hidden[...] = rows_f[0:LAYERS]
    gain[...] = rows_d[places[GAIN] : places[GAIN] + LAYERS]
    shift[...] = rows_d[places[SHIFT] : places[SHIFT] + LAYERS]
    count = lengths[0]
    for index in range(1, clips):
        count = count + lengths[index]
    total = jnp.sum(row_of(rows_d, places[LOSS]), axis=1, keepdims=True)
    loss[...] = jnp.broadcast_to(total, loss.shape) / (count.astype(F32) * rows_d.shape[1])
    for item in copies:
        item.wait()


def per_device(
    latents,
    context,
    time_embed,
    teacher,
    lengths,
    block_order,
    positions,
    self_proj,
    cross_proj,
    out_proj,
    ffn_up,
    ffn_down,
    proj_bias,
    key_bias,
    norm_gains,
    ffn_bias,
    out_bias,
    cross_gain,
    cross_shift,
    modulation,
):
    tokens, features = latents.shape
    width = norm_gains.shape[-1]
    heads = width // HEAD_DIM
    hidden_width = ffn_bias.shape[-1]
    clip_count = time_embed.shape[0]
    text_rows = context.shape[0]
    text_all = text_rows * HOLD
    clip = lax.axis_index(DP) // HOLD
    out_t = jnp.swapaxes(out_proj, 2, 3)
    down_t = jnp.swapaxes(ffn_down, 1, 2)

    rows_d = (tokens, features)
    rows_w = (tokens, width)
    rows_f = (tokens, hidden_width)
    stats = (CHAIN, 8, tokens)
    three = pltpu.SemaphoreType.DMA((CHAIN - 1,))
    chain_scratch = Chain.scratch(tokens, features)
    kv_shape = (heads, 2, tokens, HEAD_DIM)

    pack = (((16, features), F32), ((16, width), F32), ((1, hidden_width), F32))
    attend_outs = (
        Early(HIDDEN, rows_d, F32),
        Early(NORMAL, rows_d, BF16),
        Early(QUERY, rows_w, F32),
        Early(KEY, rows_w, F32),
        Early(QUERY_ROT, rows_w, BF16),
        (kv_shape, BF16),
        (stats, F32),
        ((HOLD - 1,) + kv_shape, BF16),
        (rows_w, BF16),
        ((8, tokens), F32),
    )
    attend_scratch = [
        pltpu.VMEM((heads, HOLD, tokens, tokens), F32),
        three,
        three,
        pltpu.SemaphoreType.DMA((1 + 3 * heads,)),
        pltpu.SemaphoreType.DMA((1 + 3 * heads,)),
    ]
    results, found = run(
        "first",
        first_kernel,
        (
            lengths,
            block_order,
            jnp.swapaxes(time_embed, 0, 1),
            jnp.swapaxes(modulation, 0, 1),
            jnp.swapaxes(out_bias, 0, 1),
            cross_gain,
            cross_shift,
            jnp.swapaxes(proj_bias, 0, 1),
            key_bias,
            norm_gains,
            ffn_bias,
            positions,
            rope_table(HEAD_DIM),
            latents,
        ),
        (
            ((HOLD, 8, tokens), F32),
            ((tokens, HEAD_DIM), F32),
            ((tokens, HEAD_DIM), F32),
            (context.shape, F32),
        )
        + pack * LAYERS
        + attend_outs,
        attend_scratch + [three, three],
        jobs=[
            Gather(self_proj, 0, name=SELF, held=True),
            Gather(cross_proj, 0, wave=1, skewed=True),
            Gather(out_t, 0, wave=1, skewed=True),
        ],
        scalars=2,
        micros=70,
    )
    counts, cosine, sine, context_part = results[:4]
    packs = [results[4 + 3 * layer : 7 + 3 * layer] for layer in range(LAYERS)]
    attended = results[4 + 3 * LAYERS :]
    weights = {SELF: [found[0]], CROSS: [found[1]], OUT: [found[2]], UP: [], DOWN: []}
    saved = []
    sources = {
        SELF: self_proj,
        CROSS: cross_proj,
        OUT: out_t,
        UP: ffn_up,
        DOWN: down_t,
    }

    def gathers(layer, *names):
        return [Gather(sources[name], layer) for name in names if layer < LAYERS]

    def keep(found, *names):
        for name, item in zip(names, found):
            weights[name].append(item)

    base, tot, before = latents, latents, packs[0][0]
    for layer in range(LAYERS):
        pack_d, pack_w, pack_f = packs[layer]
        if layer > 0:
            attended, unused = run(
                "attend",
                attend_kernel,
                (
                    base,
                    tot,
                    before,
                    pack_d,
                    pack_w,
                    Late(WEIGHT, weights[SELF][layer]),
                    Late(COSINE, cosine, lazy=True),
                    Late(SINE, sine, lazy=True),
                    counts,
                ),
                attend_outs,
                attend_scratch,
                micros=35,
            )
        hidden, a1, sq, sk, q_rot, kv, stat1, others, o1, lse1 = attended[:10]
        results, found = run(
            "out_sum" + str(layer),
            functools.partial(out_sum_kernel, layer == 0),
            (
                o1,
                Late(OUT, weights[OUT][layer], 0),
                Late(CONTEXT, context) if layer == 0 else Late(CONTEXT, clip_context, lazy=True),
                Late(TEXT_WEIGHT, weights[CROSS][layer], 1, 3, lazy=True),
                pack_w,
            ),
            (
                (rows_d, BF16),
                ((text_all, width), F32),
                ((text_all, width), BF16),
                ((text_all, width), BF16),
                ((CHAIN, 8, text_all), F32),
            )
            + ((((text_all, features), BF16),) if layer == 0 else ()),
            [three, three] + chain_scratch + ([three, three] if layer == 0 else []),
            jobs=gathers(layer, UP) + [Gather(self_proj, 1)]
            if layer == 0
            else gathers(layer, DOWN),
            micros=45,
        )
        keep(found, *((UP, SELF) if layer == 0 else (DOWN,)))
        tot1, ck, ckb, cvb, stat_t = results[:5]
        if layer == 0:
            clip_context = results[5]
        gathered = layer == 0
        jobs = [
            Gather(sources[DOWN], 0, name=DOWN, held=True),
            Gather(sources[CROSS], 1, wave=1),
            Gather(sources[OUT], 1, wave=1),
            Gather(sources[UP], 1, wave=1),
        ]
        results, found = run(
            "cross_ffn" + str(gathered),
            functools.partial(cross_ffn_kernel, gathered),
            (
                hidden,
                tot1,
                pack_d,
                pack_w,
                pack_f,
                Late(WEIGHT, weights[CROSS][layer], 0),
                Late(TEXT_KB, ckb, lazy=True),
                Late(TEXT_VB, cvb, lazy=True),
                Late(OUT, weights[OUT][layer], 1, lazy=True),
                Late(UP, weights[UP][layer], lazy=True),
            )
            + (() if gathered else (Late(DOWN, weights[DOWN][layer], lazy=True),)),
            (
                Early(HIDDEN, rows_d, F32),
                Early(NORMAL, rows_d, BF16),
                Early(QUERY, rows_w, F32),
                Early(QUERY_B, rows_w, BF16),
                Early(RESULT, rows_w, BF16),
                ((8, tokens), F32),
                (stats, F32),
                Early(HIDDEN_F, rows_d, F32),
                Early(NORMAL_F, rows_d, BF16),
                Early(GELU_B_NAME, rows_f, BF16),
                Early(SLOPE, rows_f, BF16),
                (rows_d, BF16),
            ),
            [three, three, pltpu.VMEM(rows_d, BF16)] + chain_scratch + chain_scratch,
            jobs=jobs if gathered else [],
            micros=90,
        )
        h1, a3, cq, cqb, o2, lse2, stat2, h2, a2, gelu_b, slope, tot3 = results
        if gathered:
            keep(found, DOWN, CROSS, OUT, UP)
        saved.append(
            (hidden, a1, sq, sk, q_rot, kv, stat1, others, o1, lse1, tot1, ck, ckb, cvb, stat_t)
            + (h1, a3, cq, cqb, o2, lse2, stat2, h2, a2, gelu_b, slope, tot3)
        )
        base, tot, before = h2, tot3, pack_d
    grad = base
    reduced = {}
    small = [None] * LAYERS
    above = None
    for layer in reversed(range(LAYERS)):
        (hidden, a1, sq, sk, q_rot, kv, stat1, others, o1, lse1, tot1, ck, ckb, cvb, stat_t) = saved[
            layer
        ][:15]
        (h1, a3, cq, cqb, o2, lse2, stat2, h2, a2, gelu_b, slope, tot3) = saved[layer][15:]
        pack_d, pack_w, pack_f = packs[layer]
        w_self, w_cross, w_out, w_up, w_down = [
            weights[name][layer] for name in (SELF, CROSS, OUT, UP, DOWN)
        ]
        joined = above is not None
        matrix = (features, hidden_width)
        results, found = run(
            "ffn_back" + str(joined),
            functools.partial(ffn_back_kernel, joined),
            (Late(GRAD, grad),)
            + (above if joined else (teacher, counts))
            + (
                tot3,
                pack_d,
                Late(DOWN, w_down),
                Late(UP, w_up, lazy=True),
                Late(SLOPE, slope),
                Late(NORMAL, a2, lazy=True),
                Late(GELU_B_NAME, gelu_b, lazy=True),
            ),
            (
                Early(NEW_GRAD, rows_d, F32, over=0),
                ((8, features), F32) if joined else Early(OUTPUT, rows_d, F32),
            )
            + (
                (rows_d, BF16),
                ((8, features), F32),
                ((8, hidden_width), F32),
                (matrix, BF16, True),
                (matrix, BF16, True),
            ),
            [
                pltpu.VMEM(rows_d, BF16),
                pltpu.VMEM(rows_f, BF16),
                pltpu.VMEM((2, 256, hidden_width), BF16),
                pltpu.SemaphoreType.DMA((2,)),
            ]
            + chain_scratch,
            jobs=[Scatter(text_matrix), Scatter(self_matrix)] if joined else [],
            micros=60,
        )
        grad = results[0]
        if not joined:
            output = results[1]
        else:
            sums_above = results[1]
            reduced[TEXT, layer + 1], reduced[SELF, layer + 1] = found
        da2, sums3, dz_sum, up_grad, down_grad = results[2:]
        (grad, dct, sums2, wsums2, da3, cross_matrix), found = run(
            "cross_back",
            cross_back_kernel,
            (
                grad,
                da2,
                h2,
                pack_d,
                pack_w,
                Late(OUT, w_out, 1),
                Late(QUERY, cq, lazy=True),
                Late(QUERY_B, cqb, lazy=True),
                lse2,
                stat2,
                Late(TEXT_KB, ckb, lazy=True),
                Late(TEXT_VB, cvb, lazy=True),
                Late(WEIGHT, w_cross, 0, lazy=True),
                Late(NORMAL, a3, lazy=True),
                Late(RESULT, o2, lazy=True),
            ),
            (
                Early(NEW_GRAD, rows_d, F32),
                Early(TEXT_GRAD, (2, text_all, width), F32),
                ((8, features), F32),
                ((8, width), F32),
                (rows_d, BF16),
                Early(MATRIX_GRAD, (features, 2 * width), BF16),
            ),
            [
                pltpu.VMEM(rows_d, BF16),
                pltpu.VMEM(rows_w, BF16),
                pltpu.VMEM(rows_w, BF16),
                pltpu.VMEM(rows_w, F32),
                pltpu.VMEM(stats, F32),
                three,
                three,
            ]
            + chain_scratch,
            jobs=[Scatter(up_grad, UP)],
            micros=60,
        )
        reduced[UP, layer] = found[0]
        (grad, out0, sums1, dq_rot, dkv, dtext), found = run(
            "attend_back",
            attend_back_kernel,
            (
                counts,
                grad,
                da3,
                h1,
                pack_d,
                tot1,
                Late(OUT, w_out, 0),
                Late(QUERY, q_rot, lazy=True),
                Late(KEY_VALUE, kv, lazy=True),
                Late(OTHERS, others, lazy=True),
                lse1,
                dct,
                Late(RESULT, o1, lazy=True),
            ),
            (
                Early(NEW_GRAD, rows_d, F32),
                Early(MATRIX_GRAD, (features, width), BF16),
                ((8, features), F32),
                Early(QUERY_GRAD, rows_w, F32),
                ((2,) + rows_w, F32),
                ((2, text_rows, width), F32),
            ),
            [
                pltpu.VMEM(rows_d, BF16),
                pltpu.VMEM(rows_w, BF16),
                pltpu.VMEM((HOLD, tokens, tokens), F32),
                pltpu.VMEM((HOLD, tokens, tokens), F32),
                pltpu.VMEM((3,) + kv_shape, BF16),
                pltpu.VMEM((3,) + kv_shape, BF16),
                pltpu.VMEM((3, 2, text_rows, width), BF16),
                pltpu.VMEM((3, 2, text_rows, width), BF16),
                pltpu.SemaphoreType.DMA((3, 2 * heads + 1)),
                pltpu.SemaphoreType.DMA((3, 2 * heads + 1)),
            ],
            micros=35,
        )
        (wsums1, context_part, da1, self_matrix, text_matrix), found = run(
            "qkv_back",
            qkv_back_kernel,
            (
                dq_rot,
                dkv,
                dtext,
                sq,
                sk,
                ck,
                stat1,
                stat_t,
                pack_w,
                cosine,
                sine,
                Late(WEIGHT, w_self, lazy=True),
                Late(NORMAL, a1, lazy=True),
                Late(CONTEXT, context, lazy=True),
                Late(TEXT_WEIGHT, w_cross, 1, 3, lazy=True),
                Late(BEFORE, context_part, lazy=True),
            ),
            (
                ((16, width), F32),
                (context.shape, F32),
                (rows_d, BF16),
                Early(SELF_GRAD, (features, 3 * width), BF16),
                Early(TEXT_MATRIX, (features, 2 * width), BF16),
            ),
            [
                pltpu.VMEM((tokens, 3 * width), BF16),
                pltpu.VMEM((text_rows, 2 * width), BF16),
                pltpu.VMEM(rows_w, F32),
                pltpu.VMEM(rows_w, F32),
                pltpu.VMEM(stats, F32),
                three,
                three,
            ]
            + chain_scratch,
            jobs=[Scatter(down_grad), Scatter(cross_matrix), Scatter(out0)],
            micros=60,
        )
        reduced[DOWN, layer], reduced[CROSS, layer], reduced[OUT0, layer] = found
        small[layer] = (sums1, sums2, sums3, wsums1, wsums2, dz_sum)
        above = (da1, hidden, pack_d)
    places, count = small_rows(clip_count)
    small_shapes = ((count, features), (24 * LAYERS, width), (16, hidden_width))
    travel = [pltpu.VMEM(shape, BF16) for shape in small_shapes]
    bits = bits_of_dp()
    (grad, context_sum, packed_d, packed_w, packed_f), found = run(
        "last",
        functools.partial(last_kernel, clip_count),
        (
            context_part,
            Late(GRAD, grad),
            Late(BRANCH, above[0]),
            Late(HIDDEN, above[1]),
            above[2],
            sums_above,
        )
        + tuple(item for layer in range(LAYERS) for item in small[layer]),
        (Early(NEW_GRAD, rows_d, F32), (context.shape, BF16))
        + tuple((shape, F32) for shape in small_shapes),
        [pltpu.VMEM((8, features), F32)]
        + Chain.scratch(text_rows, features)
        + travel * (2 * bits)
        + [pltpu.SemaphoreType.DMA((bits, 3)), pltpu.SemaphoreType.DMA((bits, 3))],
        jobs=[Scatter(text_matrix), Scatter(self_matrix)],
        micros=30,
    )
    reduced[TEXT, 0], reduced[SELF, 0] = found
    names = (UP, DOWN, CROSS, TEXT, SELF, OUT0)
    size = features // lax.axis_size(DP)
    far_outs = (
        ((LAYERS, 3, size, width), F32, True),
        ((LAYERS, 3, size, width), F32, True),
        ((LAYERS, 2, size, width), F32, True),
        ((LAYERS, size, hidden_width), F32, True),
        ((LAYERS, size, hidden_width), F32, True),
        (rows_d, F32, True),
        (rows_d, F32, True),
    )
    far_ins = [
        reduced[name, layer] for layer in range(LAYERS) for name in names
    ] + [output, grad]
    unpacked, unused = run(
        "unpack",
        functools.partial(unpack_kernel, clip_count),
        (lengths, packed_d, packed_w, packed_f, context_sum) + tuple(Late(place, item) for place, item in enumerate(far_ins)),
        (
            ((1, 128), F32),
            ((6, clip_count, features), F32),
            ((5, LAYERS, width), F32),
            ((LAYERS, width), F32),
            ((LAYERS, 4, width), F32),
            ((LAYERS, hidden_width), F32),
            ((3, LAYERS, features), F32),
            ((LAYERS, features), F32),
            ((LAYERS, features), F32),
            ((6, LAYERS, features), F32),
            (context.shape, F32),
        )
        + far_outs,
        [pltpu.SemaphoreType.DMA((2 + 10 * LAYERS,))],
        remote=False,
        scalars=1,
        micros=10,
    )
    loss, time, bias, key_sums, gain_sums, hidden_sums, out_sums, gain, shift, mods = unpacked[:10]
    context_grad, self_grad, cross_grad, out_grad, up_grad, down_grad, output, grad = unpacked[10:]
    out_grad = jnp.swapaxes(out_grad, 2, 3)
    down_grad = jnp.swapaxes(down_grad, 1, 2)
    return (
        output,
        loss[0, 0],
        grad,
        context_grad,
        jnp.swapaxes(time, 0, 1),
        self_grad,
        cross_grad,
        out_grad,
        up_grad,
        down_grad,
        jnp.swapaxes(bias, 0, 1),
        key_sums,
        gain_sums,
        hidden_sums,
        jnp.swapaxes(out_sums, 0, 1),
        gain,
        shift,
        jnp.swapaxes(mods, 0, 1),
    )


def solution(mesh):
    COLLECTIVES.clear()
    rows = P(DP, None)
    col_in = P(None, None, DP, TENSOR)
    col_out = P(None, None, TENSOR, DP)
    up, down = P(None, DP, TENSOR), P(None, TENSOR, DP)
    vec, mat = P(None, TENSOR), P(None, None, TENSOR)
    return jax.shard_map(
        per_device,
        mesh=mesh,
        in_specs=(rows, rows, P(), rows, P(), P(DP), P(None, DP))
        + (col_in, col_in, col_out, up, down)
        + (mat, vec, mat, vec, P(), P(), P(), P()),
        out_specs=(rows, P(), rows, rows, P())
        + (col_in, col_in, col_out, up, down)
        + (mat, vec, mat, vec, P(), P(), P(), P()),
        check_vma=False,
    )
```
